32 devices in a mesh: dp: 8 (over y, x, core), seq: 4 (over z).
Axes of the slice: x: 2, y: 2, z: 4, core: 2. Of those that a mesh axis runs over, the one named last changes fastest.
Arguments:
- hidden: bfloat16 [8, 1024, 1536], P('dp', 'seq'), may hold values from -6 to 6
- pad_mask: int32 [8, 1024], P('dp', 'seq'), may hold values 0 or 1
- timestep: int32 [8], P('dp'), may hold values from 0 to 999
- input_weight: bfloat16 [1536, 6144], P(('dp', 'seq')), may hold values from -0.15625 to 0.15625
- select_weight: bfloat16 [3072, 128], P(('dp', 'seq')), may hold values from -0.109375 to 0.109375
- step_weight: bfloat16 [96, 3072], P(None, ('dp', 'seq')), may hold values from -0.625 to 0.625
- output_weight: bfloat16 [3072, 1536], P(None, ('dp', 'seq')), may hold values from -0.109375 to 0.109375
- decay_forward: bfloat16 [3072, 16], P(('dp', 'seq')), may hold values from -8 to 0.69921875
- decay_reverse: bfloat16 [3072, 16], P(('dp', 'seq')), may hold values from -8 to 0.69921875
- filter_weight: bfloat16 [4, 3072], P(None, ('dp', 'seq')), may hold values from -3 to 3
- filter_bias: bfloat16 [3072], P(('dp', 'seq')), may hold values from -3 to 3
- step_bias: bfloat16 [3072], P(('dp', 'seq')), may hold values from -4 to -1
- modulation_weight: bfloat16 [256, 4608], P(('dp', 'seq')), may hold values from -0.375 to 0.375
- modulation_bias: bfloat16 [4608], P(('dp', 'seq')), may hold values from -3 to 3
- cotangent: bfloat16 [8, 1024, 1536], P('dp', 'seq'), may hold values from -6 to 6
Outputs:
- block_out: bfloat16 [8, 1024, 1536], P('dp', 'seq')
- grad_hidden: bfloat16 [8, 1024, 1536], P('dp', 'seq')
- grad_input_weight: float32 [1536, 6144], P(('dp', 'seq'))
- grad_select_weight: float32 [3072, 128], P(('dp', 'seq'))
- grad_step_weight: float32 [96, 3072], P(None, ('dp', 'seq'))
- grad_output_weight: float32 [3072, 1536], P(None, ('dp', 'seq'))
- grad_decay_forward: float32 [3072, 16], P(('dp', 'seq'))
- grad_decay_reverse: float32 [3072, 16], P(('dp', 'seq'))
- grad_filter_weight: float32 [4, 3072], P(None, ('dp', 'seq'))
- grad_filter_bias: float32 [3072], P(('dp', 'seq'))
- grad_step_bias: float32 [3072], P(('dp', 'seq'))
- grad_modulation_weight: float32 [256, 4608], P(('dp', 'seq'))
- grad_modulation_bias: float32 [4608], P(('dp', 'seq'))
The draws below stay inside these ranges and needn't reach their ends.
All inputs are finite; a program needn't handle non-finite values. No bound on the sum of `pad_mask` on one device may be relied on, other than what follows from the above.
Results may differ from the reference program's by a relative error of at most 0.01.
Values may be sent and summed in bfloat16 or wider, within the bound.
A program may use at most 184 MiB of HBM per device.

```python
import math
import jax
import jax.numpy as jnp
from jax import lax

D = 1536
INNER = 3072
STATE = 16
RANK = 96
KERNEL = 4
FREQ = 256
SEQ_LEN = 1024
ITEMS = 8


def place_ends(values, key, low, largest):
    shape = values.shape
    place = [jax.random.randint(jax.random.fold_in(key, axis), (), 0, shape[axis]) for axis in range(len(shape))]
    values = values.at[tuple(place)].set(low)
    longest = shape.index(max(shape))
    place[longest] = (place[longest] + 1) % shape[longest]
    return values.at[tuple(place)].set(largest)


def block_levels(key, shape, cuts, smallest, high):
    def one(axis_at, blocks):
        heights = jax.random.uniform(jax.random.fold_in(jax.random.fold_in(key, 6), axis_at), (blocks,), jnp.float32, smallest / len(cuts), high / len(cuts))
        return jnp.repeat(jnp.exp(heights), shape[axis_at] // blocks).reshape((-1,) + (1,) * (len(shape) - axis_at - 1))

    gain = one(*cuts[0])
    for cut in cuts[1:]:
        gain = gain * one(*cut)
    return gain


def noise(own_key, shape, width, limit, cuts=(), kind=jnp.bfloat16):
    drawn = jax.random.normal(own_key, shape, jnp.float32) * width
    if len(cuts) > 0:
        drawn = block_levels(own_key, shape, cuts, -0.22, 0.18) * drawn
    return jnp.clip(drawn, min=-limit, max=limit).astype(kind)


def setup_inputs(seed: int = 0) -> dict:
    key_list = jax.random.split(jax.random.key(seed), 16)
    return {
        "hidden": noise(key_list[0], (ITEMS, SEQ_LEN, D), 1.0, 6.0, ((0, 8), (1, 4))),
        "pad_mask": place_ends((jax.random.randint(key_list[1], (ITEMS, SEQ_LEN), 0, 8) < 7).astype(jnp.int32), jax.random.fold_in(key_list[1], 1), 0, 1),
        "timestep": place_ends(jax.random.randint(key_list[2], (ITEMS,), 0, 1000), jax.random.fold_in(key_list[2], 1), 0, 999).astype(jnp.int32),
        "input_weight": noise(key_list[3], (D, 2 * INNER), D ** -0.5, 0.15625, ((0, 32),)),
        "select_weight": noise(key_list[4], (INNER, RANK + 2 * STATE), INNER ** -0.5, 0.109375, ((0, 32),)),
        "step_weight": noise(key_list[5], (RANK, INNER), RANK ** -0.5, 0.625, ((1, 32),)),
        "output_weight": noise(key_list[6], (INNER, D), INNER ** -0.5, 0.109375, ((1, 32),)),
        "decay_forward": jnp.clip(-8.0 + 8.699219 * jax.random.uniform(key_list[7], (INNER, STATE), jnp.float32) ** block_levels(key_list[7], (INNER, STATE), ((0, 32),), -0.2, 0.2), -8.0, 0.69921875).astype(jnp.bfloat16),
        "decay_reverse": jnp.clip(-8.0 + 8.699219 * jax.random.uniform(key_list[8], (INNER, STATE), jnp.float32) ** block_levels(key_list[8], (INNER, STATE), ((0, 32),), -0.2, 0.2), -8.0, 0.69921875).astype(jnp.bfloat16),
        "filter_weight": noise(key_list[9], (KERNEL, INNER), KERNEL ** -0.5, 3.0, ((1, 32),)),
        "filter_bias": noise(key_list[10], (INNER,), 0.5, 3.0, ((0, 32),)),
        "step_bias": jnp.clip(-4.0 + 3.0 * jax.random.uniform(key_list[11], (INNER,), jnp.float32) ** block_levels(key_list[11], (INNER,), ((0, 32),), -0.2, 0.2), -4.0, -1.0).astype(jnp.bfloat16),
        "modulation_weight": noise(key_list[12], (FREQ, 3 * D), FREQ ** -0.5, 0.375, ((0, 32),)),
        "modulation_bias": noise(key_list[13], (3 * D,), 0.5, 3.0, ((0, 32),)),
        "cotangent": noise(key_list[14], (ITEMS, SEQ_LEN, D), 1.0, 6.0, ((0, 8), (1, 4))),
    }


EPS = 1e-06
HIGHEST = lax.Precision.HIGHEST

@jax.custom_vjp
def low(v):
    return lax.optimization_barrier(v.astype(jnp.bfloat16)).astype(jnp.float32)

@jax.custom_vjp
def low_back(v):
    return v

def low_keep(v):
    return (low(v), None)

def low_pass(kept, grad):
    return (grad,)

def back_keep(v):
    return (v, None)

def back_low(kept, grad):
    return (low(grad),)
low.defvjp(low_keep, low_pass)
low_back.defvjp(back_keep, back_low)

def frequency_embed(timestep_one):
    half_width = FREQ // 2
    counter = jnp.arange(half_width, dtype=jnp.float32)
    frequency = jnp.exp(counter * (-math.log(10000.0) / half_width))
    angles = timestep_one.astype(jnp.float32) * frequency
    return jnp.concatenate([jnp.cos(angles), jnp.sin(angles)])

def selective(steps, drives, b_rows, c_rows, log_rate):
    rates = -jnp.exp(log_rate)

    def advance(current, pieces):
        step_now, drive_now, b_now, c_now = pieces
        current = jnp.exp(step_now[:, None] * rates) * current + (step_now * drive_now)[:, None] * b_now[None, :]
        return (current, lax.optimization_barrier(jnp.sum(current * c_now[None, :], axis=1)))
    initial = jnp.zeros((INNER, STATE), jnp.float32)
    unused, outputs = lax.scan(advance, initial, (steps, drives, b_rows, c_rows))
    return outputs

def item_forward(params, hidden_row, mask_row, timestep_one):
    input_weight, select_weight, step_weight, output_weight, decay_forward, decay_reverse, filter_weight, filter_bias, step_bias, modulation_weight, modulation_bias = params
    embedded = low(jax.nn.silu(frequency_embed(timestep_one)))
    modulation = jnp.dot(embedded, modulation_weight, precision=HIGHEST) + modulation_bias
    shifts = modulation[:D]
    scales = modulation[D:2 * D]
    gate_scale = modulation[2 * D:]
    centered = hidden_row - lax.optimization_barrier(jnp.mean(hidden_row, axis=1, keepdims=True))
    variance = lax.optimization_barrier(jnp.mean(centered * centered, axis=1, keepdims=True))
    normed = centered * lax.rsqrt(variance + EPS)
    modded = low(normed * (1.0 + scales) + shifts)
    projected = low_back(jnp.dot(modded, input_weight, precision=HIGHEST))
    keeper = mask_row.astype(jnp.float32)[:, None]
    inner_part = low(projected[:, :INNER]) * keeper
    gate_branch = projected[:, INNER:]
    padded = jnp.concatenate([jnp.zeros((KERNEL - 1, INNER), jnp.float32), inner_part], axis=0)
    filtered = jnp.zeros((SEQ_LEN, INNER), jnp.float32) + filter_bias
    for offset in range(KERNEL):
        filtered = filtered + filter_weight[offset] * padded[offset:offset + SEQ_LEN]
    active = low(jax.nn.silu(filtered))
    selected = low_back(jnp.dot(active, select_weight, precision=HIGHEST))
    low_rank = low(selected[:, :RANK])
    b_rows = selected[:, RANK:RANK + STATE]
    c_rows = selected[:, RANK + STATE:]
    steps = jax.nn.softplus(low_back(jnp.dot(low_rank, step_weight, precision=HIGHEST)) + step_bias)
    mixed_forward = selective(steps, active, b_rows, c_rows, decay_forward)
    mixed_reverse = jnp.flip(selective(jnp.flip(steps, 0), jnp.flip(active, 0), jnp.flip(b_rows, 0), jnp.flip(c_rows, 0), decay_reverse), 0)
    merged = mixed_forward + mixed_reverse
    gated = low(merged * jax.nn.silu(gate_branch))
    branch = low_back(jnp.dot(gated, output_weight, precision=HIGHEST))
    return hidden_row + gate_scale * keeper * branch

def reference(hidden, pad_mask, timestep, input_weight, select_weight, step_weight, output_weight, decay_forward, decay_reverse, filter_weight, filter_bias, step_bias, modulation_weight, modulation_bias, cotangent):
    params = (input_weight.astype(jnp.float32), select_weight.astype(jnp.float32), step_weight.astype(jnp.float32), output_weight.astype(jnp.float32), decay_forward.astype(jnp.float32), decay_reverse.astype(jnp.float32), filter_weight.astype(jnp.float32), filter_bias.astype(jnp.float32), step_bias.astype(jnp.float32), modulation_weight.astype(jnp.float32), modulation_bias.astype(jnp.float32))

    def forward(hidden_all, params_all):

        def one_item(pieces):
            return item_forward(params_all, pieces[0], pieces[1], pieces[2])
        return lax.map(jax.checkpoint(one_item), (hidden_all, pad_mask, timestep))
    result, pullback = jax.vjp(forward, hidden.astype(jnp.float32), params)
    grad_hidden, grads = pullback(cotangent.astype(jnp.float32))
    return (result.astype(jnp.bfloat16), grad_hidden.astype(jnp.bfloat16), grads[0], grads[1], grads[2], grads[3], grads[4], grads[5], grads[6], grads[7], grads[8], grads[9], grads[10])
```

```python
import functools
import math

import jax
import jax.numpy as jnp
from jax import lax
from jax.experimental import pallas as pl
from jax.experimental.pallas import tpu as pltpu
from jax.sharding import PartitionSpec as P

FREQ = 256
EPS = 1e-06
HIGHEST = lax.Precision.HIGHEST
LOG2E = 1.4426950408889634
SUB = 16
F32, BF = jnp.float32, jnp.bfloat16

def wide(block, lanes):
    return jnp.concatenate([block] * (lanes // 128), axis=1) if lanes > 128 else block

def fwd_kernel(step_ref, u_ref, rate_ref, bb_ref, cblk_ref, y_ref, s_ref, carry_ref, *, flip):
    rows, lanes = step_ref.shape
    chunk = pl.program_id(1)
    @pl.when(pl.program_id(0) == 0)
    def _():
        carry_ref[chunk] = jnp.zeros(carry_ref.shape[1:], F32)
    rates = rate_ref[...]
    def sub(i, state):
        at = rows // SUB - 1 - i if flip else i
        base = pl.multiple_of(at * SUB, SUB)
        for k in range(SUB):
            j = SUB - 1 - k if flip else k
            row = step_ref[pl.ds(base + j, 1), :]
            u = u_ref[pl.ds(base + j, 1), :]
            state = jnp.exp2(row * rates) * state + u * wide(bb_ref[base + j], lanes)
            s_ref[pl.ds(pl.multiple_of((base + j) * 16, 16), 16), :] = state.astype(BF)
        block = s_ref[pl.ds(pl.multiple_of(base * 16, 256), 256), :]
        y_ref[pl.ds(base, SUB), :] = jnp.dot(cblk_ref[pl.ds(base, SUB), :], block, preferred_element_type=F32)
        return state
    carry_ref[chunk] = lax.fori_loop(0, rows // SUB, sub, carry_ref[chunk])

def fwd_scan(steps, u, rates2, bb, cblk, flip, tile=128, width=384):
    length, lanes = steps.shape
    blocks, chunks = length // tile, lanes // width
    order = (lambda t: blocks - 1 - t) if flip else (lambda t: t)
    return pl.pallas_call(
        functools.partial(fwd_kernel, flip=flip),
        grid=(blocks, chunks),
        in_specs=[
            pl.BlockSpec((tile, width), lambda t, c: (order(t), c)),
            pl.BlockSpec((tile, width), lambda t, c: (order(t), c)),
            pl.BlockSpec((16, width), lambda t, c: (0, c)),
            pl.BlockSpec((tile, 16, 128), lambda t, c: (order(t), 0, 0)),
            pl.BlockSpec((tile, 256), lambda t, c: (order(t), 0)),
        ],
        out_specs=[
            pl.BlockSpec((tile, width), lambda t, c: (order(t), c)),
            pl.BlockSpec((tile * 16, width), lambda t, c: (order(t), c)),
        ],
        out_shape=[jax.ShapeDtypeStruct((length, lanes), F32), jax.ShapeDtypeStruct((length * 16, lanes), BF)],
        scratch_shapes=[pltpu.VMEM((chunks, 16, width), F32)],
        compiler_params=pltpu.CompilerParams(vmem_limit_bytes=48 * 2**20, dimension_semantics=("arbitrary", "arbitrary")),
        name="fwd_scan",
    )(steps, u, rates2, bb, cblk)

def bwd_kernel(step_ref, u_ref, gy_ref, rate_ref, bb_ref, cb_ref, bblk_ref, s_ref, sprev_ref,
               dlog_ref, adjb_ref, bg_ref, cg_ref, rg_ref, carry_ref, a_ref, l_ref, *, flip):
    rows, lanes = step_ref.shape
    t, chunk = pl.program_id(0), pl.program_id(1)
    last = pl.num_programs(0) - 1
    @pl.when(t == 0)
    def _():
        carry_ref[chunk] = jnp.zeros(carry_ref.shape[1:], F32)
        rg_ref[chunk] = jnp.zeros(rg_ref.shape[1:], F32)
    @pl.when(chunk == 0)
    def _():
        bg_ref[...] = jnp.zeros(bg_ref.shape, F32)
        cg_ref[...] = jnp.zeros(cg_ref.shape, F32)
    rates = rate_ref[...]
    ones = (lax.broadcasted_iota(jnp.int32, (SUB, 256), 0) == lax.broadcasted_iota(jnp.int32, (SUB, 256), 1) // 16)
    onesb = ones.astype(BF)
    subs = rows // SUB
    def sub(i, both):
        passed, rg = both
        at = i if flip else subs - 1 - i
        base = pl.multiple_of(at * SUB, SUB)
        for k in range(SUB):
            j = k if flip else SUB - 1 - k
            row = step_ref[pl.ds(base + j, 1), :]
            g = gy_ref[pl.ds(base + j, 1), :]
            adj = g * wide(cb_ref[base + j], lanes) + passed
            passed = jnp.exp2(row * rates) * adj
            if flip:
                before = base + j + 1
                edge = (j == SUB - 1)
                inner = s_ref[pl.ds(pl.multiple_of(jnp.minimum(before, rows - 1) * 16, 16), 16), :] if edge else s_ref[pl.ds(pl.multiple_of(before * 16, 16), 16), :]
                if edge:
                    outer = jnp.where(t == last, jnp.zeros_like(inner), sprev_ref[...])
                    inner = jnp.where(before == rows, outer, inner)
            else:
                before = base + j - 1
                edge = (j == 0)
                inner = s_ref[pl.ds(pl.multiple_of(jnp.maximum(before, 0) * 16, 16), 16), :] if edge else s_ref[pl.ds(pl.multiple_of(before * 16, 16), 16), :]
                if edge:
                    outer = jnp.where(t == last, jnp.zeros_like(inner), sprev_ref[...])
                    inner = jnp.where(before < 0, outer, inner)
            lg = passed * inner.astype(F32)
            rg = rg + lg * row
            a_ref[j * 16:(j + 1) * 16, :] = adj.astype(BF)
            l_ref[j * 16:(j + 1) * 16, :] = (lg * rates).astype(BF)
        a = a_ref[...]
        here = pl.ds(base, SUB)
        dlog_ref[here, :] = jnp.dot(onesb, l_ref[...], preferred_element_type=F32)
        adjb_ref[here, :] = jnp.dot(bblk_ref[here, :], a, preferred_element_type=F32)
        nt = (((1,), (1,)), ((), ()))
        bgd = lax.dot_general(u_ref[here, :].astype(BF), a, nt, preferred_element_type=F32)
        sblk = s_ref[pl.ds(pl.multiple_of(base * 16, 256), 256), :]
        cgd = lax.dot_general(gy_ref[here, :].astype(BF), sblk, nt, preferred_element_type=F32)
        zero = jnp.zeros_like(bgd)
        bg_ref[pl.ds(at, 1), :] += jnp.sum(jnp.where(ones, bgd, zero), axis=0, keepdims=True)
        cg_ref[pl.ds(at, 1), :] += jnp.sum(jnp.where(ones, cgd, zero), axis=0, keepdims=True)
        return passed, rg
    passed, rg = lax.fori_loop(0, subs, sub, (carry_ref[chunk], rg_ref[chunk]))
    carry_ref[chunk] = passed
    rg_ref[chunk] = rg

def bwd_scan(steps, u, gy, rates2, bb, cb, bblk, states, flip, tile=128, width=384):
    length, lanes = steps.shape
    blocks, chunks = length // tile, lanes // width
    order = (lambda t: t) if flip else (lambda t: blocks - 1 - t)
    if flip:
        prev = lambda t: jnp.minimum((t + 1) * tile, length - 1)
    else:
        prev = lambda t: jnp.maximum((blocks - 1 - t) * tile - 1, 0)
    row = pl.BlockSpec((tile, width), lambda t, c: (order(t), c))
    bc = pl.BlockSpec((tile, 16, 128), lambda t, c: (order(t), 0, 0))
    blk = pl.BlockSpec((tile, 256), lambda t, c: (order(t), 0))
    diag = pl.BlockSpec((tile // 16, 256), lambda t, c: (order(t), 0))
    return pl.pallas_call(
        functools.partial(bwd_kernel, flip=flip),
        grid=(blocks, chunks),
        in_specs=[row, row, row, pl.BlockSpec((16, width), lambda t, c: (0, c)), bc, bc, blk,
            pl.BlockSpec((tile * 16, width), lambda t, c: (order(t), c)),
            pl.BlockSpec((16, width), lambda t, c: (prev(t), c))],
        out_specs=[row, row, diag, diag, pl.BlockSpec((chunks, 16, width), lambda t, c: (0, 0, 0))],
        out_shape=[jax.ShapeDtypeStruct((length, lanes), F32), jax.ShapeDtypeStruct((length, lanes), F32),
            jax.ShapeDtypeStruct((length // 16, 256), F32), jax.ShapeDtypeStruct((length // 16, 256), F32),
            jax.ShapeDtypeStruct((chunks, 16, width), F32)],
        scratch_shapes=[pltpu.VMEM((chunks, 16, width), F32), pltpu.VMEM((256, width), BF), pltpu.VMEM((256, width), BF)],
        compiler_params=pltpu.CompilerParams(vmem_limit_bytes=48 * 2**20, dimension_semantics=("arbitrary", "arbitrary")),
        name="bwd_scan",
    )(steps, u, gy, rates2, bb, cb, bblk, states, states)

def blockdiag(rows):
    length = rows.shape[0]
    eye = (jnp.arange(length)[:, None] % 16) == (jnp.arange(256)[None, :] // 16)
    return jnp.where(eye, jnp.tile(rows, (1, 16)), 0).astype(BF)

def lanes_of(rows):
    return jnp.broadcast_to(rows[:, :, None], rows.shape + (128,))


def frequency_embed(timestep):
    half_width = FREQ // 2
    counter = jnp.arange(half_width, dtype=F32)
    frequency = jnp.exp(counter * (-math.log(10000.0) / half_width))
    angles = timestep.astype(F32)[:, None] * frequency[None, :]
    return jnp.concatenate([jnp.cos(angles), jnp.sin(angles)], axis=1)


def dot(a, b):
    return jnp.dot(a, b, preferred_element_type=F32)


def dot_nt(a, b):
    return lax.dot_general(a, b, (((1,), (1,)), ((), ())), preferred_element_type=F32)


def dot_tn(a, b):
    return lax.dot_general(a, b, (((0,), (0,)), ((), ())), preferred_element_type=F32)


def body(
    hidden,
    pad_mask,
    timestep,
    input_weight,
    select_weight,
    step_weight,
    output_weight,
    decay_forward,
    decay_reverse,
    filter_weight,
    filter_bias,
    step_bias,
    modulation_weight,
    modulation_bias,
    cotangent,
):
    ns, nd = lax.axis_size("seq"), lax.axis_size("dp")
    q, d = lax.axis_index("seq"), lax.axis_index("dp")
    every = ("dp", "seq")
    local_len, width = hidden.shape[1:]
    length = local_len * ns
    inner = output_weight.shape[0]
    part = inner // ns
    rank = step_weight.shape[0]
    state = decay_forward.shape[1]
    taps = filter_weight.shape[0]
    rows_in = input_weight.shape[0]
    units = select_weight.shape[0]

    hid = lax.all_gather(hidden[0], "seq", axis=0, tiled=True)
    mask = lax.all_gather(pad_mask[0].astype(BF), "seq", axis=0, tiled=True).astype(F32)[:, None]
    win = input_weight.reshape(rows_in, 2, ns, part).transpose(2, 0, 1, 3).reshape(ns, rows_in, 2 * part)
    win = lax.all_to_all(win, "seq", 0, 0)
    win = lax.all_gather(win, "dp", axis=0, tiled=False).reshape(width, 2 * part)
    wout = output_weight.T.reshape(-1, ns, part).transpose(1, 0, 2)
    wout = lax.all_to_all(wout, "seq", 0, 0)
    wout = lax.all_gather(wout, "dp", axis=0, tiled=False).reshape(width, part)
    pack = jnp.concatenate(
        [select_weight, step_weight.T, decay_forward, decay_reverse, filter_weight.T,
         filter_bias[:, None], step_bias[:, None]], axis=1)
    used = pack.shape[1]
    pack = jnp.pad(pack, ((0, 0), (0, -used % 128)))
    pack = lax.all_gather(pack, every, axis=0, tiled=True)
    pack = lax.dynamic_slice_in_dim(pack, q * part, part, 0)
    cuts = []
    at = 0
    for size in (rank + 2 * state, rank, state, state, taps, 1, 1):
        cuts.append((at, at + size))
        at += size
    select_q, step_q, log_f, log_r, filt, fbias, sbias = [pack[:, a:b] for a, b in cuts]
    step_q = step_q.T
    modw = lax.all_gather(modulation_weight, every, axis=0, tiled=True)
    modb = lax.all_gather(modulation_bias, every, axis=0, tiled=True)
    cot = lax.all_gather(cotangent[0], "seq", axis=0, tiled=True)

    embedded = jax.nn.silu(frequency_embed(timestep)).astype(BF)
    modulation = dot(embedded, modw) + modb.astype(F32)
    shifts = modulation[:, :width]
    scales = modulation[:, width : 2 * width]
    gate_scale = modulation[:, 2 * width :]

    def norm(x):
        x = x.astype(F32)
        centered = x - jnp.mean(x, axis=1, keepdims=True)
        inverse = lax.rsqrt(jnp.mean(centered * centered, axis=1, keepdims=True) + EPS)
        return centered * inverse, inverse

    modded = (norm(hid)[0] * (1.0 + scales) + shifts).astype(BF)
    projected = dot(modded, win)
    inner_part = projected[:, :part].astype(BF).astype(F32) * mask
    gate_branch = projected[:, part:]
    filt32 = filt.astype(F32)
    padded = jnp.pad(inner_part, ((taps - 1, 0), (0, 0)))
    filtered = fbias.astype(F32).T
    for k in range(taps):
        filtered = filtered + filt32[:, k][None, :] * padded[k : k + length]
    sigma_filter = jax.nn.sigmoid(filtered)
    active = (filtered * sigma_filter).astype(BF)
    active32 = active.astype(F32)
    selected = lax.psum(dot(active, select_q), "seq")
    low_rank = selected[:, :rank].astype(BF)
    b_rows = selected[:, rank : rank + state]
    c_rows = selected[:, rank + state :]
    pre_steps = dot(low_rank, step_q) + sbias.astype(F32).T
    steps = jax.nn.softplus(pre_steps)
    rates_f = -jnp.exp(log_f.astype(F32)).T
    rates_r = -jnp.exp(log_r.astype(F32)).T
    drive = steps * active32
    bb, cb = lanes_of(b_rows), lanes_of(c_rows)
    bblk, cblk = blockdiag(b_rows), blockdiag(c_rows)
    mixed_f, states_f = fwd_scan(steps, drive, rates_f * LOG2E, bb, cblk, False)
    mixed_r, states_r = fwd_scan(steps, drive, rates_r * LOG2E, bb, cblk, True)
    merged = mixed_f + mixed_r
    sigma_gate = jax.nn.sigmoid(gate_branch)
    silu_gate = gate_branch * sigma_gate
    gated = (merged * silu_gate).astype(BF)
    branch = lax.psum_scatter(dot_nt(gated, wout), "seq", scatter_dimension=0, tiled=True)

    mask_here = pad_mask[0].astype(F32)[:, None]
    cot_here = cotangent[0].astype(F32)
    block_out = (hidden[0].astype(F32) + gate_scale * mask_here * branch).astype(BF)
    grad_gate = jnp.sum(mask_here * cot_here * branch, axis=0)

    grad_branch = (cot.astype(F32) * gate_scale * mask).astype(BF)
    grad_gated = dot(grad_branch, wout)
    grad_merged = grad_gated * silu_gate
    grad_gate_branch = grad_gated * merged * sigma_gate * (1.0 + gate_branch * (1.0 - sigma_gate))
    dlog_f, adjb_f, bg_f, cg_f, rg_f = bwd_scan(
        steps, drive, grad_merged, rates_f * LOG2E, bb, cb, bblk, states_f, False)
    dlog_r, adjb_r, bg_r, cg_r, rg_r = bwd_scan(
        steps, drive, grad_merged, rates_r * LOG2E, bb, cb, bblk, states_r, True)
    adjb = adjb_f + adjb_r
    grad_steps = (dlog_f + dlog_r) * (1.0 / LOG2E) + active32 * adjb
    grad_b = (bg_f + bg_r).reshape(length, state)
    grad_c = (cg_f + cg_r).reshape(length, state)
    grad_decay_f = rg_f.transpose(1, 0, 2).reshape(state, part) * rates_f
    grad_decay_r = rg_r.transpose(1, 0, 2).reshape(state, part) * rates_r
    grad_pre = grad_steps * jax.nn.sigmoid(pre_steps)
    grad_step_bias = jnp.sum(grad_pre, axis=0)
    grad_pre_low = grad_pre.astype(BF)
    grad_step_t = dot_tn(grad_pre_low, low_rank)
    grad_low_rank = dot_nt(grad_pre_low, step_q)
    grad_selected = lax.psum(jnp.concatenate([grad_low_rank, grad_b, grad_c], axis=1), "seq").astype(BF)
    grad_select = dot_tn(active, grad_selected)
    grad_active = steps * adjb + dot_nt(grad_selected, select_q)
    grad_filtered = grad_active * sigma_filter * (1.0 + filtered * (1.0 - sigma_filter))
    extended = jnp.pad(grad_filtered, ((0, taps - 1), (0, 0)))
    grad_inner = jnp.zeros_like(grad_filtered)
    filter_rows = []
    for k in range(taps):
        lead = taps - 1 - k
        grad_inner = grad_inner + filt32[:, k][None, :] * extended[lead : lead + length]
        filter_rows.append(jnp.sum(grad_filtered * padded[k : k + length], axis=0))
    grad_filter_bias = jnp.sum(grad_filtered, axis=0)
    grad_projected = jnp.concatenate([grad_inner * mask, grad_gate_branch], axis=1).astype(BF)
    grad_modded = lax.psum_scatter(dot_nt(grad_projected, win), "seq", scatter_dimension=0, tiled=True)

    normed, inverse = norm(hidden[0])
    grad_shifts = jnp.sum(grad_modded, axis=0)
    grad_scales = jnp.sum(grad_modded * normed, axis=0)
    grad_normed = grad_modded * (1.0 + scales)
    grad_hidden = cot_here + inverse * (
        grad_normed
        - jnp.mean(grad_normed, axis=1, keepdims=True)
        - normed * jnp.mean(grad_normed * normed, axis=1, keepdims=True)
    )

    def home(grad, cols):
        got = lax.psum_scatter(grad, "dp", scatter_dimension=0, tiled=True)
        got = got.reshape(ns, -1, cols)
        return lax.all_to_all(got, "seq", 0, 0)

    g_in = home(dot_tn(modded, grad_projected), 2 * part)
    g_in = g_in.reshape(ns, rows_in, 2, part).transpose(1, 2, 0, 3).reshape(rows_in, 2 * inner)
    g_out = home(dot_tn(grad_branch, gated), part).transpose(1, 0, 2).reshape(-1, inner).T
    small = jnp.concatenate(
        [grad_select, grad_step_t, grad_decay_f.T, grad_decay_r.T, jnp.stack(filter_rows, axis=1),
         grad_filter_bias[:, None], grad_step_bias[:, None]], axis=1)
    small = jnp.pad(small, ((0, 0), (0, -used % 128)))
    small = lax.psum_scatter(small, "dp", scatter_dimension=0, tiled=True)
    small = lax.ppermute(small, every, [(a * ns + b, b * nd + a) for a in range(nd) for b in range(ns)])
    gs_select, gs_step, gs_f, gs_r, gs_filter, gs_fbias, gs_sbias = [small[:, a:b] for a, b in cuts]
    grad_mod = jnp.concatenate([grad_shifts, grad_scales, grad_gate, embedded[0].astype(F32)])
    grad_mod = lax.all_gather(grad_mod, every, axis=0, tiled=False).reshape(nd, ns, -1)
    embeds = grad_mod[:, 0, 3 * width :]
    grad_mod = jnp.sum(grad_mod[:, :, : 3 * width], axis=1)
    me = d * ns + q
    mine = lax.dynamic_slice_in_dim(embeds, me * modulation_weight.shape[0], modulation_weight.shape[0], 1)
    g_modw = lax.dot_general(mine, grad_mod, (((0,), (0,)), ((), ())), precision=HIGHEST)
    g_modb = lax.dynamic_slice_in_dim(
        jnp.sum(grad_mod, axis=0), me * modulation_bias.shape[0], modulation_bias.shape[0], 0)
    return (
        block_out[None],
        grad_hidden.astype(BF)[None],
        g_in,
        gs_select,
        gs_step.T,
        g_out,
        gs_f,
        gs_r,
        gs_filter.T,
        gs_fbias[:, 0],
        gs_sbias[:, 0],
        g_modw,
        g_modb,
    )


def solution(mesh):
    return jax.shard_map(
        body,
        mesh=mesh,
        in_specs=(
            P("dp", "seq", None),
            P("dp", "seq"),
            P("dp"),
            P(("dp", "seq"), None),
            P(("dp", "seq"), None),
            P(None, ("dp", "seq")),
            P(None, ("dp", "seq")),
            P(("dp", "seq"), None),
            P(("dp", "seq"), None),
            P(None, ("dp", "seq")),
            P(("dp", "seq")),
            P(("dp", "seq")),
            P(("dp", "seq"), None),
            P(("dp", "seq")),
            P("dp", "seq", None),
        ),
        out_specs=(
            P("dp", "seq", None),
            P("dp", "seq", None),
            P(("dp", "seq"), None),
            P(("dp", "seq"), None),
            P(None, ("dp", "seq")),
            P(None, ("dp", "seq")),
            P(("dp", "seq"), None),
            P(("dp", "seq"), None),
            P(None, ("dp", "seq")),
            P(("dp", "seq")),
            P(("dp", "seq")),
            P(("dp", "seq"), None),
            P(("dp", "seq")),
        ),
        check_vma=False,
    )
```

```python
import functools
import math

import jax
import jax.numpy as jnp
from jax import lax
from jax.experimental import pallas as pl
from jax.experimental.pallas import tpu as pltpu
from jax.sharding import PartitionSpec as P

FREQ = 256
EPS = 1e-06
HIGHEST = lax.Precision.HIGHEST
LOG2E = 1.4426950408889634
SUB = 16
F32, BF = jnp.float32, jnp.bfloat16

def wide(block, lanes):
    return jnp.concatenate([block] * (lanes // 128), axis=1) if lanes > 128 else block

def fwd_kernel(step_ref, u_ref, rate_ref, bb_ref, cblk_ref, y_ref, s_ref, carry_ref, *, flip):
    rows, lanes = step_ref.shape
    chunk = pl.program_id(1)
    @pl.when(pl.program_id(0) == 0)
    def _():
        carry_ref[chunk] = jnp.zeros(carry_ref.shape[1:], F32)
    rates = rate_ref[...]
    def sub(i, state):
        at = rows // SUB - 1 - i if flip else i
        base = pl.multiple_of(at * SUB, SUB)
        for k in range(SUB):
            j = SUB - 1 - k if flip else k
            row = step_ref[pl.ds(base + j, 1), :]
            u = u_ref[pl.ds(base + j, 1), :]
            state = jnp.exp2(row * rates) * state + u * wide(bb_ref[base + j], lanes)
            s_ref[pl.ds(pl.multiple_of((base + j) * 16, 16), 16), :] = state.astype(BF)
        block = s_ref[pl.ds(pl.multiple_of(base * 16, 256), 256), :]
        y_ref[pl.ds(base, SUB), :] = jnp.dot(cblk_ref[pl.ds(base, SUB), :], block, preferred_element_type=F32)
        return state
    carry_ref[chunk] = lax.fori_loop(0, rows // SUB, sub, carry_ref[chunk])

def fwd_scan(steps, u, rates2, bb, cblk, flip, tile=128, width=384):
    length, lanes = steps.shape
    blocks, chunks = length // tile, lanes // width
    order = (lambda t: blocks - 1 - t) if flip else (lambda t: t)
    return pl.pallas_call(
        functools.partial(fwd_kernel, flip=flip),
        grid=(blocks, chunks),
        in_specs=[
            pl.BlockSpec((tile, width), lambda t, c: (order(t), c)),
            pl.BlockSpec((tile, width), lambda t, c: (order(t), c)),
            pl.BlockSpec((16, width), lambda t, c: (0, c)),
            pl.BlockSpec((tile, 16, 128), lambda t, c: (order(t), 0, 0)),
            pl.BlockSpec((tile, 256), lambda t, c: (order(t), 0)),
        ],
        out_specs=[
            pl.BlockSpec((tile, width), lambda t, c: (order(t), c)),
            pl.BlockSpec((tile * 16, width), lambda t, c: (order(t), c)),
        ],
        out_shape=[jax.ShapeDtypeStruct((length, lanes), F32), jax.ShapeDtypeStruct((length * 16, lanes), BF)],
        scratch_shapes=[pltpu.VMEM((chunks, 16, width), F32)],
        compiler_params=pltpu.CompilerParams(vmem_limit_bytes=48 * 2**20, dimension_semantics=("arbitrary", "arbitrary")),
        name="fwd_scan",
    )(steps, u, rates2, bb, cblk)

def bwd_kernel(step_ref, u_ref, gy_ref, rate_ref, bb_ref, cb_ref, bblk_ref, s_ref, sprev_ref,
               dlog_ref, adjb_ref, bg_ref, cg_ref, rg_ref, carry_ref, a_ref, l_ref, *, flip):
    rows, lanes = step_ref.shape
    t, chunk = pl.program_id(0), pl.program_id(1)
    last = pl.num_programs(0) - 1
    @pl.when(t == 0)
    def _():
        carry_ref[chunk] = jnp.zeros(carry_ref.shape[1:], F32)
        rg_ref[chunk] = jnp.zeros(rg_ref.shape[1:], F32)
    @pl.when(chunk == 0)
    def _():
        bg_ref[...] = jnp.zeros(bg_ref.shape, F32)
        cg_ref[...] = jnp.zeros(cg_ref.shape, F32)
    rates = rate_ref[...]
    ones = (lax.broadcasted_iota(jnp.int32, (SUB, 256), 0) == lax.broadcasted_iota(jnp.int32, (SUB, 256), 1) // 16)
    onesb = ones.astype(BF)
    subs = rows // SUB
    def sub(i, both):
        passed, rg = both
        at = i if flip else subs - 1 - i
        base = pl.multiple_of(at * SUB, SUB)
        for k in range(SUB):
            j = k if flip else SUB - 1 - k
            row = step_ref[pl.ds(base + j, 1), :]
            g = gy_ref[pl.ds(base + j, 1), :]
            adj = g * wide(cb_ref[base + j], lanes) + passed
            passed = jnp.exp2(row * rates) * adj
            if flip:
                before = base + j + 1
                edge = (j == SUB - 1)
                inner = s_ref[pl.ds(pl.multiple_of(jnp.minimum(before, rows - 1) * 16, 16), 16), :] if edge else s_ref[pl.ds(pl.multiple_of(before * 16, 16), 16), :]
                if edge:
                    outer = jnp.where(t == last, jnp.zeros_like(inner), sprev_ref[...])
                    inner = jnp.where(before == rows, outer, inner)
            else:
                before = base + j - 1
                edge = (j == 0)
                inner = s_ref[pl.ds(pl.multiple_of(jnp.maximum(before, 0) * 16, 16), 16), :] if edge else s_ref[pl.ds(pl.multiple_of(before * 16, 16), 16), :]
                if edge:
                    outer = jnp.where(t == last, jnp.zeros_like(inner), sprev_ref[...])
                    inner = jnp.where(before < 0, outer, inner)
            lg = passed * inner.astype(F32)
            rg = rg + lg * row
            a_ref[j * 16:(j + 1) * 16, :] = adj.astype(BF)
            l_ref[j * 16:(j + 1) * 16, :] = (lg * rates).astype(BF)
        a = a_ref[...]
        here = pl.ds(base, SUB)
        dlog_ref[here, :] = jnp.dot(onesb, l_ref[...], preferred_element_type=F32)
        adjb_ref[here, :] = jnp.dot(bblk_ref[here, :], a, preferred_element_type=F32)
        nt = (((1,), (1,)), ((), ()))
        bgd = lax.dot_general(u_ref[here, :].astype(BF), a, nt, preferred_element_type=F32)
        sblk = s_ref[pl.ds(pl.multiple_of(base * 16, 256), 256), :]
        cgd = lax.dot_general(gy_ref[here, :].astype(BF), sblk, nt, preferred_element_type=F32)
        zero = jnp.zeros_like(bgd)
        bg_ref[pl.ds(at, 1), :] += jnp.sum(jnp.where(ones, bgd, zero), axis=0, keepdims=True)
        cg_ref[pl.ds(at, 1), :] += jnp.sum(jnp.where(ones, cgd, zero), axis=0, keepdims=True)
        return passed, rg
    passed, rg = lax.fori_loop(0, subs, sub, (carry_ref[chunk], rg_ref[chunk]))
    carry_ref[chunk] = passed
    rg_ref[chunk] = rg

def bwd_scan(steps, u, gy, rates2, bb, cb, bblk, states, flip, tile=128, width=384):
    length, lanes = steps.shape
    blocks, chunks = length // tile, lanes // width
    order = (lambda t: t) if flip else (lambda t: blocks - 1 - t)
    if flip:
        prev = lambda t: jnp.minimum((t + 1) * tile, length - 1)
    else:
        prev = lambda t: jnp.maximum((blocks - 1 - t) * tile - 1, 0)
    row = pl.BlockSpec((tile, width), lambda t, c: (order(t), c))
    bc = pl.BlockSpec((tile, 16, 128), lambda t, c: (order(t), 0, 0))
    blk = pl.BlockSpec((tile, 256), lambda t, c: (order(t), 0))
    diag = pl.BlockSpec((tile // 16, 256), lambda t, c: (order(t), 0))
    return pl.pallas_call(
        functools.partial(bwd_kernel, flip=flip),
        grid=(blocks, chunks),
        in_specs=[row, row, row, pl.BlockSpec((16, width), lambda t, c: (0, c)), bc, bc, blk,
            pl.BlockSpec((tile * 16, width), lambda t, c: (order(t), c)),
            pl.BlockSpec((16, width), lambda t, c: (prev(t), c))],
        out_specs=[row, row, diag, diag, pl.BlockSpec((chunks, 16, width), lambda t, c: (0, 0, 0))],
        out_shape=[jax.ShapeDtypeStruct((length, lanes), F32), jax.ShapeDtypeStruct((length, lanes), F32),
            jax.ShapeDtypeStruct((length // 16, 256), F32), jax.ShapeDtypeStruct((length // 16, 256), F32),
            jax.ShapeDtypeStruct((chunks, 16, width), F32)],
        scratch_shapes=[pltpu.VMEM((chunks, 16, width), F32), pltpu.VMEM((256, width), BF), pltpu.VMEM((256, width), BF)],
        compiler_params=pltpu.CompilerParams(vmem_limit_bytes=48 * 2**20, dimension_semantics=("arbitrary", "arbitrary")),
        name="bwd_scan",
    )(steps, u, gy, rates2, bb, cb, bblk, states, states)

def blockdiag(rows):
    length = rows.shape[0]
    eye = (jnp.arange(length)[:, None] % 16) == (jnp.arange(256)[None, :] // 16)
    return jnp.where(eye, jnp.tile(rows, (1, 16)), 0).astype(BF)

def lanes_of(rows):
    return jnp.broadcast_to(rows[:, :, None], rows.shape + (128,))


MESH = pl.DeviceIdType.MESH
VMEM = pl.BlockSpec(memory_space=pltpu.VMEM)
HBM = pl.BlockSpec(memory_space=pl.ANY)
DMA = pltpu.SemaphoreType.DMA


def send(src, dst, out_sem, in_sem, to):
    return pltpu.make_async_remote_copy(
        src_ref=src, dst_ref=dst, send_sem=out_sem, recv_sem=in_sem, device_id=to, device_id_type=MESH)


def greet(devices):
    bar = pltpu.get_barrier_semaphore()
    for to in devices:
        pl.semaphore_signal(bar, inc=1, device_id=to, device_id_type=MESH)
    pl.semaphore_wait(bar, len(devices))


def column_sum_kernel(ns, p_ref, o_ref, land, s1, r1, s2, r2):
    d, q = lax.axis_index("dp"), lax.axis_index("seq")
    others = [lax.rem(q + k, ns) for k in range(1, ns)]
    greet([(d, t) for t in others])
    for k, t in enumerate(others):
        send(p_ref.at[t], land.at[q], s1.at[k], r1.at[q], (d, t)).start()
    total = p_ref[q]
    for k, t in enumerate(others):
        send(p_ref.at[t], land.at[t], s1.at[k], r1.at[t], (d, t)).wait_recv()
        total = total + land[t]
    o_ref[q] = total.astype(o_ref.dtype)
    for k, t in enumerate(others):
        send(o_ref.at[q], o_ref.at[q], s2.at[k], r2.at[q], (d, t)).start()
    for k, t in enumerate(others):
        send(o_ref.at[t], o_ref.at[t], s2.at[k], r2.at[t], (d, t)).wait_recv()
    for k, t in enumerate(others):
        send(p_ref.at[t], land.at[q], s1.at[k], r1.at[q], (d, t)).wait_send()
        send(o_ref.at[q], o_ref.at[q], s2.at[k], r2.at[q], (d, t)).wait_send()


def column_sum(partial, ns, out_dtype, cid):
    rows, lanes = partial.shape
    block = (ns, rows // ns, lanes)
    out = pl.pallas_call(
        functools.partial(column_sum_kernel, ns),
        out_shape=jax.ShapeDtypeStruct(block, out_dtype),
        in_specs=[VMEM], out_specs=VMEM,
        scratch_shapes=[pltpu.VMEM(block, partial.dtype), DMA((ns,)), DMA((ns,)), DMA((ns,)), DMA((ns,))],
        compiler_params=pltpu.CompilerParams(
            collective_id=cid, has_side_effects=True, vmem_limit_bytes=32 * 2**20),
        name="column_sum",
    )(partial.reshape(block))
    return out.reshape(rows, lanes)


def mod_gather_kernel(nd, ns, g_ref, o_ref, land, s1, r1, s2, r2):
    d, q = lax.axis_index("dp"), lax.axis_index("seq")
    others = [lax.rem(q + k, ns) for k in range(1, ns)]
    peers = [lax.rem(d + k, nd) for k in range(1, nd)]
    greet([(d, t) for t in others] + [(e, q) for e in peers])
    for k, t in enumerate(others):
        send(g_ref, land.at[q], s1.at[k], r1.at[q], (d, t)).start()
    total = g_ref[...]
    for k, t in enumerate(others):
        send(g_ref, land.at[t], s1.at[k], r1.at[t], (d, t)).wait_recv()
        total = total + land[t]
    o_ref[d] = total
    for k, e in enumerate(peers):
        send(o_ref.at[d], o_ref.at[d], s2.at[k], r2.at[d], (e, q)).start()
    for k, e in enumerate(peers):
        send(o_ref.at[e], o_ref.at[e], s2.at[k], r2.at[e], (e, q)).wait_recv()
    for k, t in enumerate(others):
        send(g_ref, land.at[q], s1.at[k], r1.at[q], (d, t)).wait_send()
    for k, e in enumerate(peers):
        send(o_ref.at[d], o_ref.at[d], s2.at[k], r2.at[d], (e, q)).wait_send()


def mod_gather(g, nd, ns, cid):
    rows, lanes = g.shape
    return pl.pallas_call(
        functools.partial(mod_gather_kernel, nd, ns),
        out_shape=jax.ShapeDtypeStruct((nd, rows, lanes), F32),
        in_specs=[VMEM], out_specs=VMEM,
        scratch_shapes=[pltpu.VMEM((ns, rows, lanes), F32), DMA((ns,)), DMA((ns,)), DMA((nd,)), DMA((nd,))],
        compiler_params=pltpu.CompilerParams(
            collective_id=cid, has_side_effects=True, vmem_limit_bytes=32 * 2**20),
        name="mod_gather",
    )(g)


def home_kernel(nd, ns, nsub, g_ref, sm_ref, gm_ref, f_ref, so_ref, out_ref,
                pair, plane, spair, splane, ssum, up, down,
                sa, ra, sb, rb, sc, rc, ta, ra2, tb, rb2, tc, rc2, su, ru, sd, rd):
    d, q = lax.axis_index("dp"), lax.axis_index("seq")
    nc = nd // 2
    chip, core = d // 2, lax.rem(d, 2)
    mate = chip * 2 + 1 - core
    chips = [lax.rem(chip + k, nc) for k in range(1, nc)]
    others = [lax.rem(q + k, ns) for k in range(1, ns)]
    spread = nd // ns
    final_to = (spread * q + d // ns, lax.rem(d, ns))
    mine = d * ns + q
    final_from = (lax.rem(mine, nd), mine // nd)
    stays = jnp.logical_and(final_to[0] == d, final_to[1] == q)
    bar = pltpu.get_barrier_semaphore()
    friends = [(mate, q)] + [(c * 2 + core, q) for c in chips] + [(d, t) for t in others]
    for to in friends:
        pl.semaphore_signal(bar, inc=1, device_id=to, device_id_type=MESH)
    @pl.when(jnp.logical_not(stays))
    def _():
        pl.semaphore_signal(bar, inc=1, device_id=final_from, device_id_type=MESH)
        pl.semaphore_wait(bar, len(friends) + 1)
    @pl.when(stays)
    def _():
        pl.semaphore_wait(bar, len(friends))

    def first(c):
        return send(g_ref.at[c * 2 + 1 - core], pair.at[c], sa.at[c], ra.at[c], (mate, q))

    def first_small(c):
        return send(sm_ref.at[c * 2 + 1 - core], spair.at[c], ta.at[c], ra2.at[c], (mate, q))

    order = chips + [chip]
    for c in order:
        first(c).start()
        first_small(c).start()

    def rise(t, s, src):
        return send(src, up.at[t, s], su.at[t, s], ru.at[t, s], (d, q + 1))

    def sink(t, s, src):
        return send(src, down.at[t, s], sd.at[t, s], rd.at[t, s], (d, q - 1))

    def added(land, t, s):
        land[t, s] = (land[t, s].astype(F32) + gm_ref[t, s].astype(F32)).astype(BF)

    def step_up(t, s):
        @pl.when(q < t)
        def _():
            @pl.when(q == 0)
            def _():
                rise(t, s, gm_ref.at[t, s]).start()
            @pl.when(q > 0)
            def _():
                rise(t, s, up.at[t, s]).wait_recv()
                added(up, t, s)
                rise(t, s, up.at[t, s]).start()

    def step_down(t, s):
        @pl.when(q > t)
        def _():
            @pl.when(q == ns - 1)
            def _():
                sink(t, s, gm_ref.at[t, s]).start()
            @pl.when(q < ns - 1)
            def _():
                sink(t, s, down.at[t, s]).wait_recv()
                added(down, t, s)
                sink(t, s, down.at[t, s]).start()

    steps = [(k, s) for k in range(ns - 1) for s in range(nsub)]
    middle = len(steps) * 2 // 3

    def walk(some):
        for k, s in some:
            step_up(ns - 1 - k, s)
            step_down(k, s)

    def second(c, src):
        return send(pair.at[c], plane.at[src], sb.at[c], rb.at[src], (c * 2 + core, q))

    def second_small(c, src):
        return send(spair.at[c], splane.at[src], tb.at[c], rb2.at[src], (c * 2 + core, q))

    walk(steps[:1])
    for c in order:
        first(c).wait_recv()
        @pl.loop(0, ns)
        def _(t):
            pair[c, t] = (pair[c, t].astype(F32) + g_ref[c * 2 + core, t].astype(F32)).astype(BF)
        first_small(c).wait_recv()
        spair[c] = spair[c] + sm_ref[c * 2 + core]
        if c is not chip:
            second(c, chip).start()
            second_small(c, chip).start()
    walk(steps[1:middle])

    for c in chips:
        second(c, c).wait_recv()
        second_small(c, c).wait_recv()
    @pl.loop(0, ns)
    def _(t):
        total = pair[chip, t].astype(F32)
        for c in chips:
            total = total + plane[c, t].astype(F32)
        pair[chip, t] = total.astype(BF)
    small = spair[chip]
    for c in chips:
        small = small + splane[c]
    ssum[...] = small

    def third(t, src):
        return send(pair.at[chip, t], f_ref.at[src], sc.at[t], rc.at[src], (d, t))

    last = send(ssum, so_ref, tc, rc2, final_to)
    @pl.when(stays)
    def _():
        so_ref[...] = ssum[...]
    @pl.when(jnp.logical_not(stays))
    def _():
        last.start()
    for t in others:
        third(t, q).start()
    f_ref[q] = pair[chip, q]
    walk(steps[middle:])

    for s in range(nsub):
        total = gm_ref[q, s].astype(F32)
        out_ref[s] = total
        @pl.when(q > 0)
        def _():
            rise(q, s, gm_ref.at[q, s]).wait_recv()
            out_ref[s] += up[q, s].astype(F32)
        @pl.when(q < ns - 1)
        def _():
            sink(q, s, gm_ref.at[q, s]).wait_recv()
            out_ref[s] += down[q, s].astype(F32)
    for t in others:
        third(t, t).wait_recv()
    @pl.when(jnp.logical_not(stays))
    def _():
        last.wait_recv()
        last.wait_send()
    for c in order:
        first(c).wait_send()
        first_small(c).wait_send()
    for c in chips:
        second(c, chip).wait_send()
        second_small(c, chip).wait_send()
    for t in others:
        third(t, q).wait_send()
    for k, s in steps:
        t = ns - 1 - k
        @pl.when(q < t)
        def _():
            rise(t, s, gm_ref.at[t, s]).wait_send()
        @pl.when(q > k)
        def _():
            sink(k, s, gm_ref.at[k, s]).wait_send()


def home(g, small, gm, nd, ns, cid):
    rows, cols = g.shape[2:]
    nc, nsub = nd // 2, 4
    length, width = gm.shape
    part = length // ns // nsub
    v = small.shape[1:]
    gm = gm.reshape(ns, nsub, part, width)
    f, so, out = pl.pallas_call(
        functools.partial(home_kernel, nd, ns, nsub),
        out_shape=[
            jax.ShapeDtypeStruct((ns, rows, cols), BF),
            jax.ShapeDtypeStruct(v, F32),
            jax.ShapeDtypeStruct((nsub, part, width), F32),
        ],
        in_specs=[VMEM] * 3, out_specs=[VMEM] * 3,
        scratch_shapes=[
            pltpu.VMEM((nc, ns, rows, cols), BF), pltpu.VMEM((nc, ns, rows, cols), BF),
            pltpu.VMEM((nc,) + v, F32), pltpu.VMEM((nc,) + v, F32), pltpu.VMEM(v, F32),
            pltpu.VMEM((ns, nsub, part, width), BF), pltpu.VMEM((ns, nsub, part, width), BF),
            DMA((nc,)), DMA((nc,)), DMA((nc,)), DMA((nc,)), DMA((ns,)), DMA((ns,)),
            DMA((nc,)), DMA((nc,)), DMA((nc,)), DMA((nc,)), DMA(()), DMA(()),
            DMA((ns, nsub)), DMA((ns, nsub)), DMA((ns, nsub)), DMA((ns, nsub)),
        ],
        compiler_params=pltpu.CompilerParams(
            collective_id=cid, has_side_effects=True, vmem_limit_bytes=56 * 2**20),
        name="home",
    )(g, small, gm)
    return f, so, out.reshape(length // ns, width)


def frequency_embed(timestep):
    half_width = FREQ // 2
    counter = jnp.arange(half_width, dtype=F32)
    frequency = jnp.exp(counter * (-math.log(10000.0) / half_width))
    angles = timestep.astype(F32)[:, None] * frequency[None, :]
    return jnp.concatenate([jnp.cos(angles), jnp.sin(angles)], axis=1)


def dot(a, b):
    return jnp.dot(a, b, preferred_element_type=F32)


def dot_nt(a, b):
    return lax.dot_general(a, b, (((1,), (1,)), ((), ())), preferred_element_type=F32)


def dot_tn(a, b):
    return lax.dot_general(a, b, (((0,), (0,)), ((), ())), preferred_element_type=F32)


def body(
    hidden,
    pad_mask,
    timestep,
    input_weight,
    select_weight,
    step_weight,
    output_weight,
    decay_forward,
    decay_reverse,
    filter_weight,
    filter_bias,
    step_bias,
    modulation_weight,
    modulation_bias,
    cotangent,
):
    ns, nd = lax.axis_size("seq"), lax.axis_size("dp")
    q, d = lax.axis_index("seq"), lax.axis_index("dp")
    every = ("dp", "seq")
    local_len, width = hidden.shape[1:]
    length = local_len * ns
    inner = output_weight.shape[0]
    part = inner // ns
    rank = step_weight.shape[0]
    state = decay_forward.shape[1]
    taps = filter_weight.shape[0]
    rows_in = input_weight.shape[0]
    lanes = select_weight.shape[1]

    hid = lax.all_gather(hidden[0], "seq", axis=0, tiled=True)
    mask = lax.all_gather(pad_mask[0].astype(BF), "seq", axis=0, tiled=True).astype(F32)[:, None]
    win = input_weight.reshape(rows_in, 2, ns, part).transpose(2, 0, 1, 3).reshape(ns, rows_in, 2 * part)
    win = lax.all_to_all(win, "seq", 0, 0)
    win = lax.all_gather(win, "dp", axis=0, tiled=False).reshape(width, 2 * part)
    wout = output_weight.T.reshape(-1, ns, part).transpose(1, 0, 2)
    wout = lax.all_to_all(wout, "seq", 0, 0)
    wout = lax.all_gather(wout, "dp", axis=0, tiled=False).reshape(width, part)
    pack = jnp.concatenate(
        [select_weight, step_weight.T, decay_forward, decay_reverse, filter_weight.T,
         filter_bias[:, None], step_bias[:, None]], axis=1)
    used = pack.shape[1]
    pack = jnp.pad(pack, ((0, 0), (0, -used % 128)))
    pack = lax.all_gather(pack, every, axis=0, tiled=True)
    pack = lax.dynamic_slice_in_dim(pack, q * part, part, 0)
    cuts = []
    at = 0
    for size in (rank + 2 * state, rank, state, state, taps, 1, 1):
        cuts.append((at, at + size))
        at += size
    select_q, step_q, log_f, log_r, filt, fbias, sbias = [pack[:, a:b] for a, b in cuts]
    step_q = step_q.T
    modw = lax.all_gather(modulation_weight, every, axis=0, tiled=True)
    modb = lax.all_gather(modulation_bias, every, axis=0, tiled=True)
    cot = lax.all_gather(cotangent[0], "seq", axis=0, tiled=True)

    embedded = jax.nn.silu(frequency_embed(timestep)).astype(BF)
    modulation = dot(embedded, modw) + modb.astype(F32)
    shifts = modulation[:, :width]
    scales = modulation[:, width : 2 * width]
    gate_scale = modulation[:, 2 * width :]

    def norm(x):
        x = x.astype(F32)
        centered = x - jnp.mean(x, axis=1, keepdims=True)
        inverse = lax.rsqrt(jnp.mean(centered * centered, axis=1, keepdims=True) + EPS)
        return centered * inverse, inverse

    modded = (norm(hid)[0] * (1.0 + scales) + shifts).astype(BF)
    projected = dot(modded, win)
    inner_part = projected[:, :part].astype(BF).astype(F32) * mask
    gate_branch = projected[:, part:]
    filt32 = filt.astype(F32)
    padded = jnp.pad(inner_part, ((taps - 1, 0), (0, 0)))
    filtered = fbias.astype(F32).T
    for k in range(taps):
        filtered = filtered + filt32[:, k][None, :] * padded[k : k + length]
    sigma_filter = jax.nn.sigmoid(filtered)
    active = (filtered * sigma_filter).astype(BF)
    active32 = active.astype(F32)
    selected = column_sum(dot(active, select_q), ns, BF, 0)
    low_rank = selected[:, :rank].astype(BF)
    b_rows = selected[:, rank : rank + state].astype(F32)
    c_rows = selected[:, rank + state :].astype(F32)
    pre_steps = dot(low_rank, step_q) + sbias.astype(F32).T
    steps = jax.nn.softplus(pre_steps)
    rates_f = -jnp.exp(log_f.astype(F32)).T
    rates_r = -jnp.exp(log_r.astype(F32)).T
    drive = steps * active32
    bb, cb = lanes_of(b_rows), lanes_of(c_rows)
    bblk, cblk = blockdiag(b_rows), blockdiag(c_rows)
    mixed_f, states_f = fwd_scan(steps, drive, rates_f * LOG2E, bb, cblk, False)
    mixed_r, states_r = fwd_scan(steps, drive, rates_r * LOG2E, bb, cblk, True)
    merged = mixed_f + mixed_r
    sigma_gate = jax.nn.sigmoid(gate_branch)
    silu_gate = gate_branch * sigma_gate
    gated = (merged * silu_gate).astype(BF)
    branch = lax.psum_scatter(dot_nt(gated, wout), "seq", scatter_dimension=0, tiled=True)

    mask_here = pad_mask[0].astype(F32)[:, None]
    cot_here = cotangent[0].astype(F32)
    block_out = (hidden[0].astype(F32) + gate_scale * mask_here * branch).astype(BF)
    grad_gate = jnp.sum(mask_here * cot_here * branch, axis=0)

    grad_branch = (cot.astype(F32) * gate_scale * mask).astype(BF)
    grad_gated = dot(grad_branch, wout)
    grad_merged = grad_gated * silu_gate
    grad_gate_branch = grad_gated * merged * sigma_gate * (1.0 + gate_branch * (1.0 - sigma_gate))
    dlog_f, adjb_f, bg_f, cg_f, rg_f = bwd_scan(
        steps, drive, grad_merged, rates_f * LOG2E, bb, cb, bblk, states_f, False)
    dlog_r, adjb_r, bg_r, cg_r, rg_r = bwd_scan(
        steps, drive, grad_merged, rates_r * LOG2E, bb, cb, bblk, states_r, True)
    adjb = adjb_f + adjb_r
    grad_steps = (dlog_f + dlog_r) * (1.0 / LOG2E) + active32 * adjb
    grad_b = (bg_f + bg_r).reshape(length, state)
    grad_c = (cg_f + cg_r).reshape(length, state)
    grad_decay_f = rg_f.transpose(1, 0, 2).reshape(state, part) * rates_f
    grad_decay_r = rg_r.transpose(1, 0, 2).reshape(state, part) * rates_r
    grad_pre = grad_steps * jax.nn.sigmoid(pre_steps)
    grad_step_bias = jnp.sum(grad_pre, axis=0)
    grad_pre_low = grad_pre.astype(BF)
    grad_step_t = dot_tn(grad_pre_low, low_rank)
    grad_low_rank = dot_nt(grad_pre_low, step_q)
    grad_selected = column_sum(jnp.concatenate([grad_low_rank, grad_b, grad_c], axis=1), ns, BF, 1)
    grad_select = dot_tn(active, grad_selected)
    grad_active = steps * adjb + dot_nt(grad_selected, select_q)
    grad_filtered = grad_active * sigma_filter * (1.0 + filtered * (1.0 - sigma_filter))
    extended = jnp.pad(grad_filtered, ((0, taps - 1), (0, 0)))
    grad_inner = jnp.zeros_like(grad_filtered)
    filter_rows = []
    for k in range(taps):
        lead = taps - 1 - k
        grad_inner = grad_inner + filt32[:, k][None, :] * extended[lead : lead + length]
        filter_rows.append(jnp.sum(grad_filtered * padded[k : k + length], axis=0))
    grad_filter_bias = jnp.sum(grad_filtered, axis=0)
    grad_projected = jnp.concatenate([grad_inner * mask, grad_gate_branch], axis=1).astype(BF)
    units = part // nd
    fil = jnp.stack(filter_rows + [grad_filter_bias, grad_step_bias])
    fil = fil.reshape(-1, nd, units).transpose(1, 0, 2)
    fil = jnp.pad(fil, ((0, 0), (0, 16 - fil.shape[1]), (0, lanes - units)))
    mid = jnp.concatenate([grad_step_t, grad_decay_f.T, grad_decay_r.T], axis=1)
    small = jnp.concatenate([grad_select.reshape(nd, units, lanes), mid.reshape(nd, units, lanes), fil], axis=1)
    grads = jnp.concatenate([dot_tn(modded, grad_projected), dot_tn(grad_branch, gated)], axis=1)
    grads = grads.astype(BF).reshape(nd, ns, rows_in, 3 * part)
    grads = jnp.pad(grads, ((0, 0), (0, 0), (0, -rows_in % 16), (0, 0)))
    grads, small, grad_modded = home(grads, small, dot_nt(grad_projected, win).astype(BF), nd, ns, 2)
    grads = grads[:, :rows_in].astype(F32)
    g_in = grads[:, :, : 2 * part].reshape(ns, rows_in, 2, part).transpose(1, 2, 0, 3).reshape(rows_in, 2 * inner)
    g_out = grads[:, :, 2 * part :].transpose(1, 0, 2).reshape(rows_in, inner).T
    gs_select = small[:units]
    mid = small[units : 2 * units]
    gs_step, gs_f, gs_r = mid[:, :rank], mid[:, rank : rank + state], mid[:, rank + state :]
    fil = small[2 * units :, :units]

    normed, inverse = norm(hidden[0])
    grad_shifts = jnp.sum(grad_modded, axis=0)
    grad_scales = jnp.sum(grad_modded * normed, axis=0)
    grad_normed = grad_modded * (1.0 + scales)
    grad_hidden = cot_here + inverse * (
        grad_normed
        - jnp.mean(grad_normed, axis=1, keepdims=True)
        - normed * jnp.mean(grad_normed * normed, axis=1, keepdims=True)
    )

    grad_mod = jnp.concatenate([grad_shifts, grad_scales, grad_gate, embedded[0].astype(F32) / ns])
    grad_mod = jnp.pad(grad_mod, (0, -grad_mod.shape[0] % 1024)).reshape(-1, 128)
    grad_mod = mod_gather(grad_mod, nd, ns, 3).reshape(nd, -1)
    embeds = grad_mod[:, 3 * width : 3 * width + FREQ]
    grad_mod = grad_mod[:, : 3 * width]
    me = d * ns + q
    mine = lax.dynamic_slice_in_dim(embeds, me * modulation_weight.shape[0], modulation_weight.shape[0], 1)
    g_modw = lax.dot_general(mine, grad_mod, (((0,), (0,)), ((), ())), precision=HIGHEST)
    g_modb = lax.dynamic_slice_in_dim(
        jnp.sum(grad_mod, axis=0), me * modulation_bias.shape[0], modulation_bias.shape[0], 0)
    return (
        block_out[None],
        grad_hidden.astype(BF)[None],
        g_in,
        gs_select,
        gs_step.T,
        g_out,
        gs_f,
        gs_r,
        fil[:taps],
        fil[taps],
        fil[taps + 1],
        g_modw,
        g_modb,
    )


def solution(mesh):
    return jax.shard_map(
        body,
        mesh=mesh,
        in_specs=(
            P("dp", "seq", None),
            P("dp", "seq"),
            P("dp"),
            P(("dp", "seq"), None),
            P(("dp", "seq"), None),
            P(None, ("dp", "seq")),
            P(None, ("dp", "seq")),
            P(("dp", "seq"), None),
            P(("dp", "seq"), None),
            P(None, ("dp", "seq")),
            P(("dp", "seq")),
            P(("dp", "seq")),
            P(("dp", "seq"), None),
            P(("dp", "seq")),
            P("dp", "seq", None),
        ),
        out_specs=(
            P("dp", "seq", None),
            P("dp", "seq", None),
            P(("dp", "seq"), None),
            P(("dp", "seq"), None),
            P(None, ("dp", "seq")),
            P(None, ("dp", "seq")),
            P(("dp", "seq"), None),
            P(("dp", "seq"), None),
            P(None, ("dp", "seq")),
            P(("dp", "seq")),
            P(("dp", "seq")),
            P(("dp", "seq"), None),
            P(("dp", "seq")),
        ),
        check_vma=False,
    )
```

```python
import functools
import math

import jax
import jax.numpy as jnp
from jax import lax
from jax.experimental import pallas as pl
from jax.experimental.pallas import tpu as pltpu
from jax.sharding import PartitionSpec as P

FREQ = 256
EPS = 1e-06
HIGHEST = lax.Precision.HIGHEST
LOG2E = 1.4426950408889634
SUB = 16
F32, BF = jnp.float32, jnp.bfloat16

def wide(block, lanes):
    return jnp.concatenate([block] * (lanes // 128), axis=1) if lanes > 128 else block

def fwd_kernel(step_ref, u_ref, rate_ref, bb_ref, cblk_ref, y_ref, s_ref, carry_ref, *, flip):
    rows, lanes = step_ref.shape
    chunk = pl.program_id(1)
    @pl.when(pl.program_id(0) == 0)
    def _():
        carry_ref[chunk] = jnp.zeros(carry_ref.shape[1:], F32)
    rates = rate_ref[...]
    def sub(i, state):
        at = rows // SUB - 1 - i if flip else i
        base = pl.multiple_of(at * SUB, SUB)
        for k in range(SUB):
            j = SUB - 1 - k if flip else k
            row = step_ref[pl.ds(base + j, 1), :]
            u = u_ref[pl.ds(base + j, 1), :]
            state = jnp.exp2(row * rates) * state + u * wide(bb_ref[base + j], lanes)
            s_ref[pl.ds(pl.multiple_of((base + j) * 16, 16), 16), :] = state.astype(BF)
        block = s_ref[pl.ds(pl.multiple_of(base * 16, 256), 256), :]
        y_ref[pl.ds(base, SUB), :] = jnp.dot(cblk_ref[pl.ds(base, SUB), :], block, preferred_element_type=F32)
        return state
    carry_ref[chunk] = lax.fori_loop(0, rows // SUB, sub, carry_ref[chunk])

def fwd_scan(steps, u, rates2, bb, cblk, flip, tile=128, width=384):
    length, lanes = steps.shape
    blocks, chunks = length // tile, lanes // width
    order = (lambda t: blocks - 1 - t) if flip else (lambda t: t)
    return pl.pallas_call(
        functools.partial(fwd_kernel, flip=flip),
        grid=(blocks, chunks),
        in_specs=[
            pl.BlockSpec((tile, width), lambda t, c: (order(t), c)),
            pl.BlockSpec((tile, width), lambda t, c: (order(t), c)),
            pl.BlockSpec((16, width), lambda t, c: (0, c)),
            pl.BlockSpec((tile, 16, 128), lambda t, c: (order(t), 0, 0)),
            pl.BlockSpec((tile, 256), lambda t, c: (order(t), 0)),
        ],
        out_specs=[
            pl.BlockSpec((tile, width), lambda t, c: (order(t), c)),
            pl.BlockSpec((tile * 16, width), lambda t, c: (order(t), c)),
        ],
        out_shape=[jax.ShapeDtypeStruct((length, lanes), F32), jax.ShapeDtypeStruct((length * 16, lanes), BF)],
        scratch_shapes=[pltpu.VMEM((chunks, 16, width), F32)],
        compiler_params=pltpu.CompilerParams(vmem_limit_bytes=48 * 2**20, dimension_semantics=("arbitrary", "arbitrary")),
        name="fwd_scan",
    )(steps, u, rates2, bb, cblk)

def bwd_kernel(step_ref, u_ref, gy_ref, rate_ref, bb_ref, cb_ref, bblk_ref, s_ref, sprev_ref,
               dlog_ref, adjb_ref, bg_ref, cg_ref, rg_ref, carry_ref, a_ref, l_ref, *, flip):
    rows, lanes = step_ref.shape
    t, chunk = pl.program_id(0), pl.program_id(1)
    last = pl.num_programs(0) - 1
    @pl.when(t == 0)
    def _():
        carry_ref[chunk] = jnp.zeros(carry_ref.shape[1:], F32)
        rg_ref[chunk] = jnp.zeros(rg_ref.shape[1:], F32)
    @pl.when(chunk == 0)
    def _():
        bg_ref[...] = jnp.zeros(bg_ref.shape, F32)
        cg_ref[...] = jnp.zeros(cg_ref.shape, F32)
    rates = rate_ref[...]
    ones = (lax.broadcasted_iota(jnp.int32, (SUB, 256), 0) == lax.broadcasted_iota(jnp.int32, (SUB, 256), 1) // 16)
    onesb = ones.astype(BF)
    subs = rows // SUB
    def sub(i, both):
        passed, rg = both
        at = i if flip else subs - 1 - i
        base = pl.multiple_of(at * SUB, SUB)
        for k in range(SUB):
            j = k if flip else SUB - 1 - k
            row = step_ref[pl.ds(base + j, 1), :]
            g = gy_ref[pl.ds(base + j, 1), :]
            adj = g * wide(cb_ref[base + j], lanes) + passed
            passed = jnp.exp2(row * rates) * adj
            if flip:
                before = base + j + 1
                edge = (j == SUB - 1)
                inner = s_ref[pl.ds(pl.multiple_of(jnp.minimum(before, rows - 1) * 16, 16), 16), :] if edge else s_ref[pl.ds(pl.multiple_of(before * 16, 16), 16), :]
                if edge:
                    outer = jnp.where(t == last, jnp.zeros_like(inner), sprev_ref[...])
                    inner = jnp.where(before == rows, outer, inner)
            else:
                before = base + j - 1
                edge = (j == 0)
                inner = s_ref[pl.ds(pl.multiple_of(jnp.maximum(before, 0) * 16, 16), 16), :] if edge else s_ref[pl.ds(pl.multiple_of(before * 16, 16), 16), :]
                if edge:
                    outer = jnp.where(t == last, jnp.zeros_like(inner), sprev_ref[...])
                    inner = jnp.where(before < 0, outer, inner)
            lg = passed * inner.astype(F32)
            rg = rg + lg * row
            a_ref[j * 16:(j + 1) * 16, :] = adj.astype(BF)
            l_ref[j * 16:(j + 1) * 16, :] = (lg * rates).astype(BF)
        a = a_ref[...]
        here = pl.ds(base, SUB)
        dlog_ref[here, :] = jnp.dot(onesb, l_ref[...], preferred_element_type=F32)
        adjb_ref[here, :] = jnp.dot(bblk_ref[here, :], a, preferred_element_type=F32)
        nt = (((1,), (1,)), ((), ()))
        bgd = lax.dot_general(u_ref[here, :].astype(BF), a, nt, preferred_element_type=F32)
        sblk = s_ref[pl.ds(pl.multiple_of(base * 16, 256), 256), :]
        cgd = lax.dot_general(gy_ref[here, :].astype(BF), sblk, nt, preferred_element_type=F32)
        zero = jnp.zeros_like(bgd)
        bg_ref[pl.ds(at, 1), :] += jnp.sum(jnp.where(ones, bgd, zero), axis=0, keepdims=True)
        cg_ref[pl.ds(at, 1), :] += jnp.sum(jnp.where(ones, cgd, zero), axis=0, keepdims=True)
        return passed, rg
    passed, rg = lax.fori_loop(0, subs, sub, (carry_ref[chunk], rg_ref[chunk]))
    carry_ref[chunk] = passed
    rg_ref[chunk] = rg

def bwd_scan(steps, u, gy, rates2, bb, cb, bblk, states, flip, tile=128, width=384):
    length, lanes = steps.shape
    blocks, chunks = length // tile, lanes // width
    order = (lambda t: t) if flip else (lambda t: blocks - 1 - t)
    if flip:
        prev = lambda t: jnp.minimum((t + 1) * tile, length - 1)
    else:
        prev = lambda t: jnp.maximum((blocks - 1 - t) * tile - 1, 0)
    row = pl.BlockSpec((tile, width), lambda t, c: (order(t), c))
    bc = pl.BlockSpec((tile, 16, 128), lambda t, c: (order(t), 0, 0))
    blk = pl.BlockSpec((tile, 256), lambda t, c: (order(t), 0))
    diag = pl.BlockSpec((tile // 16, 256), lambda t, c: (order(t), 0))
    return pl.pallas_call(
        functools.partial(bwd_kernel, flip=flip),
        grid=(blocks, chunks),
        in_specs=[row, row, row, pl.BlockSpec((16, width), lambda t, c: (0, c)), bc, bc, blk,
            pl.BlockSpec((tile * 16, width), lambda t, c: (order(t), c)),
            pl.BlockSpec((16, width), lambda t, c: (prev(t), c))],
        out_specs=[row, row, diag, diag, pl.BlockSpec((chunks, 16, width), lambda t, c: (0, 0, 0))],
        out_shape=[jax.ShapeDtypeStruct((length, lanes), F32), jax.ShapeDtypeStruct((length, lanes), F32),
            jax.ShapeDtypeStruct((length // 16, 256), F32), jax.ShapeDtypeStruct((length // 16, 256), F32),
            jax.ShapeDtypeStruct((chunks, 16, width), F32)],
        scratch_shapes=[pltpu.VMEM((chunks, 16, width), F32), pltpu.VMEM((256, width), BF), pltpu.VMEM((256, width), BF)],
        compiler_params=pltpu.CompilerParams(vmem_limit_bytes=48 * 2**20, dimension_semantics=("arbitrary", "arbitrary")),
        name="bwd_scan",
    )(steps, u, gy, rates2, bb, cb, bblk, states, states)

def blockdiag(rows):
    length = rows.shape[0]
    eye = (jnp.arange(length)[:, None] % 16) == (jnp.arange(256)[None, :] // 16)
    return jnp.where(eye, jnp.tile(rows, (1, 16)), 0).astype(BF)

def lanes_of(rows):
    return jnp.broadcast_to(rows[:, :, None], rows.shape + (128,))


MESH = pl.DeviceIdType.MESH
VMEM = pl.BlockSpec(memory_space=pltpu.VMEM)
HBM = pl.BlockSpec(memory_space=pl.ANY)
DMA = pltpu.SemaphoreType.DMA


def send(src, dst, out_sem, in_sem, to):
    return pltpu.make_async_remote_copy(
        src_ref=src, dst_ref=dst, send_sem=out_sem, recv_sem=in_sem, device_id=to, device_id_type=MESH)


def greet(devices):
    bar = pltpu.get_barrier_semaphore()
    for to in devices:
        pl.semaphore_signal(bar, inc=1, device_id=to, device_id_type=MESH)
    pl.semaphore_wait(bar, len(devices))


def column_sum_kernel(ns, p_ref, o_ref, land, s1, r1, s2, r2):
    d, q = lax.axis_index("dp"), lax.axis_index("seq")
    others = [lax.rem(q + k, ns) for k in range(1, ns)]
    greet([(d, t) for t in others])
    for k, t in enumerate(others):
        send(p_ref.at[t], land.at[q], s1.at[k], r1.at[q], (d, t)).start()
    total = p_ref[q]
    for k, t in enumerate(others):
        send(p_ref.at[t], land.at[t], s1.at[k], r1.at[t], (d, t)).wait_recv()
        total = total + land[t]
    o_ref[q] = total.astype(o_ref.dtype)
    for k, t in enumerate(others):
        send(o_ref.at[q], o_ref.at[q], s2.at[k], r2.at[q], (d, t)).start()
    for k, t in enumerate(others):
        send(o_ref.at[t], o_ref.at[t], s2.at[k], r2.at[t], (d, t)).wait_recv()
    for k, t in enumerate(others):
        send(p_ref.at[t], land.at[q], s1.at[k], r1.at[q], (d, t)).wait_send()
        send(o_ref.at[q], o_ref.at[q], s2.at[k], r2.at[q], (d, t)).wait_send()


def column_sum(partial, ns, out_dtype, cid):
    rows, lanes = partial.shape
    block = (ns, rows // ns, lanes)
    out = pl.pallas_call(
        functools.partial(column_sum_kernel, ns),
        out_shape=jax.ShapeDtypeStruct(block, out_dtype),
        in_specs=[VMEM], out_specs=VMEM,
        scratch_shapes=[pltpu.VMEM(block, partial.dtype), DMA((ns,)), DMA((ns,)), DMA((ns,)), DMA((ns,))],
        compiler_params=pltpu.CompilerParams(
            collective_id=cid, has_side_effects=True, vmem_limit_bytes=32 * 2**20),
        name="column_sum",
    )(partial.reshape(block))
    return out.reshape(rows, lanes)


def mod_gather_kernel(nd, ns, g_ref, o_ref, land, s1, r1, s2, r2):
    d, q = lax.axis_index("dp"), lax.axis_index("seq")
    others = [lax.rem(q + k, ns) for k in range(1, ns)]
    peers = [lax.rem(d + k, nd) for k in range(1, nd)]
    greet([(d, t) for t in others] + [(e, q) for e in peers])
    for k, t in enumerate(others):
        send(g_ref, land.at[q], s1.at[k], r1.at[q], (d, t)).start()
    total = g_ref[...]
    for k, t in enumerate(others):
        send(g_ref, land.at[t], s1.at[k], r1.at[t], (d, t)).wait_recv()
        total = total + land[t]
    o_ref[d] = total
    for k, e in enumerate(peers):
        send(o_ref.at[d], o_ref.at[d], s2.at[k], r2.at[d], (e, q)).start()
    for k, e in enumerate(peers):
        send(o_ref.at[e], o_ref.at[e], s2.at[k], r2.at[e], (e, q)).wait_recv()
    for k, t in enumerate(others):
        send(g_ref, land.at[q], s1.at[k], r1.at[q], (d, t)).wait_send()
    for k, e in enumerate(peers):
        send(o_ref.at[d], o_ref.at[d], s2.at[k], r2.at[d], (e, q)).wait_send()


def mod_gather(g, nd, ns, cid):
    rows, lanes = g.shape
    return pl.pallas_call(
        functools.partial(mod_gather_kernel, nd, ns),
        out_shape=jax.ShapeDtypeStruct((nd, rows, lanes), F32),
        in_specs=[VMEM], out_specs=VMEM,
        scratch_shapes=[pltpu.VMEM((ns, rows, lanes), F32), DMA((ns,)), DMA((ns,)), DMA((nd,)), DMA((nd,))],
        compiler_params=pltpu.CompilerParams(
            collective_id=cid, has_side_effects=True, vmem_limit_bytes=32 * 2**20),
        name="mod_gather",
    )(g)


def home_kernel(nd, ns, nsub, g_ref, sm_ref, gm_ref, f_ref, so_ref, out_ref,
                pair, plane, spair, splane, ssum, up, down,
                sa, ra, sb, rb, sc, rc, ta, ra2, tb, rb2, tc, rc2, su, ru, sd, rd):
    d, q = lax.axis_index("dp"), lax.axis_index("seq")
    nc = nd // 2
    chip, core = d // 2, lax.rem(d, 2)
    mate = chip * 2 + 1 - core
    chips = [lax.rem(chip + k, nc) for k in range(1, nc)]
    others = [lax.rem(q + k, ns) for k in range(1, ns)]
    spread = nd // ns
    final_to = (spread * q + d // ns, lax.rem(d, ns))
    mine = d * ns + q
    final_from = (lax.rem(mine, nd), mine // nd)
    stays = jnp.logical_and(final_to[0] == d, final_to[1] == q)
    bar = pltpu.get_barrier_semaphore()
    friends = [(mate, q)] + [(c * 2 + core, q) for c in chips] + [(d, t) for t in others]
    for to in friends:
        pl.semaphore_signal(bar, inc=1, device_id=to, device_id_type=MESH)
    @pl.when(jnp.logical_not(stays))
    def _():
        pl.semaphore_signal(bar, inc=1, device_id=final_from, device_id_type=MESH)
        pl.semaphore_wait(bar, len(friends) + 1)
    @pl.when(stays)
    def _():
        pl.semaphore_wait(bar, len(friends))

    def first(c):
        return send(g_ref.at[c * 2 + 1 - core], pair.at[c], sa.at[c], ra.at[c], (mate, q))

    def first_small(c):
        return send(sm_ref.at[c * 2 + 1 - core], spair.at[c], ta.at[c], ra2.at[c], (mate, q))

    order = chips + [chip]
    for c in order:
        first(c).start()
        first_small(c).start()

    def rise(t, s, src):
        return send(src, up.at[t, s], su.at[t, s], ru.at[t, s], (d, q + 1))

    def sink(t, s, src):
        return send(src, down.at[t, s], sd.at[t, s], rd.at[t, s], (d, q - 1))

    def added(land, t, s):
        land[t, s] = (land[t, s].astype(F32) + gm_ref[t, s].astype(F32)).astype(BF)

    def step_up(t, s):
        @pl.when(q < t)
        def _():
            @pl.when(q == 0)
            def _():
                rise(t, s, gm_ref.at[t, s]).start()
            @pl.when(q > 0)
            def _():
                rise(t, s, up.at[t, s]).wait_recv()
                added(up, t, s)
                rise(t, s, up.at[t, s]).start()

    def step_down(t, s):
        @pl.when(q > t)
        def _():
            @pl.when(q == ns - 1)
            def _():
                sink(t, s, gm_ref.at[t, s]).start()
            @pl.when(q < ns - 1)
            def _():
                sink(t, s, down.at[t, s]).wait_recv()
                added(down, t, s)
                sink(t, s, down.at[t, s]).start()

    steps = [(k, s) for k in range(ns - 1) for s in range(nsub)]
    middle = len(steps) * 2 // 3

    def walk(some):
        for k, s in some:
            step_up(ns - 1 - k, s)
            step_down(k, s)

    def second(c, src):
        return send(pair.at[c], plane.at[src], sb.at[c], rb.at[src], (c * 2 + core, q))

    def second_small(c, src):
        return send(spair.at[c], splane.at[src], tb.at[c], rb2.at[src], (c * 2 + core, q))

    walk(steps[:1])
    for c in order:
        first(c).wait_recv()
        @pl.loop(0, ns)
        def _(t):
            pair[c, t] = (pair[c, t].astype(F32) + g_ref[c * 2 + core, t].astype(F32)).astype(BF)
        first_small(c).wait_recv()
        spair[c] = spair[c] + sm_ref[c * 2 + core]
        if c is not chip:
            second(c, chip).start()
            second_small(c, chip).start()
    walk(steps[1:middle])

    for c in chips:
        second(c, c).wait_recv()
        second_small(c, c).wait_recv()
    @pl.loop(0, ns)
    def _(t):
        total = pair[chip, t].astype(F32)
        for c in chips:
            total = total + plane[c, t].astype(F32)
        pair[chip, t] = total.astype(BF)
    small = spair[chip]
    for c in chips:
        small = small + splane[c]
    ssum[...] = small

    def third(t, src):
        return send(pair.at[chip, t], f_ref.at[src], sc.at[t], rc.at[src], (d, t))

    last = send(ssum, so_ref, tc, rc2, final_to)
    @pl.when(stays)
    def _():
        so_ref[...] = ssum[...]
    @pl.when(jnp.logical_not(stays))
    def _():
        last.start()
    for t in others:
        third(t, q).start()
    f_ref[q] = pair[chip, q]
    walk(steps[middle:])

    for s in range(nsub):
        total = gm_ref[q, s].astype(F32)
        out_ref[s] = total
        @pl.when(q > 0)
        def _():
            rise(q, s, gm_ref.at[q, s]).wait_recv()
            out_ref[s] += up[q, s].astype(F32)
        @pl.when(q < ns - 1)
        def _():
            sink(q, s, gm_ref.at[q, s]).wait_recv()
            out_ref[s] += down[q, s].astype(F32)
    for t in others:
        third(t, t).wait_recv()
    @pl.when(jnp.logical_not(stays))
    def _():
        last.wait_recv()
        last.wait_send()
    for c in order:
        first(c).wait_send()
        first_small(c).wait_send()
    for c in chips:
        second(c, chip).wait_send()
        second_small(c, chip).wait_send()
    for t in others:
        third(t, q).wait_send()
    for k, s in steps:
        t = ns - 1 - k
        @pl.when(q < t)
        def _():
            rise(t, s, gm_ref.at[t, s]).wait_send()
        @pl.when(q > k)
        def _():
            sink(k, s, gm_ref.at[k, s]).wait_send()


def home(g, small, gm, nd, ns, cid):
    rows, cols = g.shape[2:]
    nc, nsub = nd // 2, 4
    length, width = gm.shape
    part = length // ns // nsub
    v = small.shape[1:]
    gm = gm.reshape(ns, nsub, part, width)
    f, so, out = pl.pallas_call(
        functools.partial(home_kernel, nd, ns, nsub),
        out_shape=[
            jax.ShapeDtypeStruct((ns, rows, cols), BF),
            jax.ShapeDtypeStruct(v, F32),
            jax.ShapeDtypeStruct((nsub, part, width), F32),
        ],
        in_specs=[VMEM] * 3, out_specs=[VMEM] * 3,
        scratch_shapes=[
            pltpu.VMEM((nc, ns, rows, cols), BF), pltpu.VMEM((nc, ns, rows, cols), BF),
            pltpu.VMEM((nc,) + v, F32), pltpu.VMEM((nc,) + v, F32), pltpu.VMEM(v, F32),
            pltpu.VMEM((ns, nsub, part, width), BF), pltpu.VMEM((ns, nsub, part, width), BF),
            DMA((nc,)), DMA((nc,)), DMA((nc,)), DMA((nc,)), DMA((ns,)), DMA((ns,)),
            DMA((nc,)), DMA((nc,)), DMA((nc,)), DMA((nc,)), DMA(()), DMA(()),
            DMA((ns, nsub)), DMA((ns, nsub)), DMA((ns, nsub)), DMA((ns, nsub)),
        ],
        compiler_params=pltpu.CompilerParams(
            collective_id=cid, has_side_effects=True, vmem_limit_bytes=56 * 2**20),
        name="home",
    )(g, small, gm)
    return f, so, out.reshape(length // ns, width)


def start_kernel(nd, ns, nsub, hid, win, wout, pack, mask, emb, modw, modb,
                 hid_o, wx_o, pack_o, mask_o, mod_o,
                 eland, prod, rowp, land1, land2,
                 su, ru, sd, rd, swz, rw, swp, swm, spz, rp, spp, spm, sk, rk, se, re, s1, r1, s2, r2, own):
    d, q = lax.axis_index("dp"), lax.axis_index("seq")
    nc = nd // 2
    chip, core = d // 2, lax.rem(d, 2)
    mate = (chip * 2 + 1 - core, q)
    chips = [lax.rem(chip + k, nc) for k in range(1, nc)]
    others = [lax.rem(q + k, ns) for k in range(1, ns)]
    peers = [lax.rem(d + k, nd) for k in range(1, nd)]
    spread = nd // ns
    me = d * ns + q
    part = wout.shape[1] // ns
    greet([(d, t) for t in others] + [(e, q) for e in peers])

    def column(ref, at):
        return ref.at[:, pl.ds(pl.multiple_of(at * part, 128), part)]

    def pieces(t):
        return (column(win, t), column(win, ns + t), column(wout, t))

    def across(k, t, idx):
        return [
            send(src, wx_o.at[idx, :, j * part:(j + 1) * part], swz.at[k, j], rw.at[idx, j], (d, t))
            for j, src in enumerate(pieces(t))
        ]

    for k, t in enumerate(others):
        for copy in across(k, t, me):
            copy.start()
    keep = [pltpu.make_async_copy(src, wx_o.at[me, :, j * part:(j + 1) * part], own.at[j])
            for j, src in enumerate(pieces(q))]
    keep.append(pltpu.make_async_copy(hid, hid_o.at[q], own.at[3]))
    for copy in keep:
        copy.start()

    plane = d // spread
    slot = lax.rem(d, spread) * ns + q
    pack_z = send(pack, pack_o.at[slot], spz, rp.at[slot], (d, plane))
    pack_own = pltpu.make_async_copy(pack, pack_o.at[slot], own.at[4])

    @pl.when(plane == q)
    def _():
        pack_own.start()

    @pl.when(plane != q)
    def _():
        pack_z.start()

    def masks(k, t, src):
        return send(mask_o.at[src], mask_o.at[src], sk.at[k], rk.at[src], (d, t))

    def embeds(k, e, src):
        return send(eland.at[src], eland.at[src], se.at[k], re.at[src], (e, q))

    mask_o[q] = mask[...]
    eland[d] = emb[...]
    for k, e in enumerate(peers):
        embeds(k, e, d).start()
    for k, t in enumerate(others):
        masks(k, t, q).start()

    def rise(k, s):
        t = jnp.maximum(q - k, 0)
        src = hid.at[s] if k == 0 else hid_o.at[t, s]
        return send(src, hid_o.at[t, s], su.at[k, s], ru.at[k, s], (d, q + 1))

    def sink(k, s):
        t = jnp.minimum(q + k, ns - 1)
        src = hid.at[s] if k == 0 else hid_o.at[t, s]
        return send(src, hid_o.at[t, s], sd.at[k, s], rd.at[k, s], (d, q - 1))

    def hop(k, s):
        @pl.when(q >= k)
        def _():
            if k:
                rise(k - 1, s).wait_recv()
            if k < ns - 1:
                @pl.when(q + 1 < ns)
                def _():
                    rise(k, s).start()

        @pl.when(q + k < ns)
        def _():
            if k:
                sink(k - 1, s).wait_recv()
            if k < ns - 1:
                @pl.when(q >= 1)
                def _():
                    sink(k, s).start()

    for s in range(nsub):
        hop(0, s)

    def piece(ref, idx):
        return ref.at[idx]

    def plane_w(c, idx, t):
        return send(wx_o.at[idx], wx_o.at[idx], swp.at[c, t], rwp_of(idx), (c * 2 + core, q))

    def rwp_of(idx):
        return rw.at[idx, 3]

    def mate_w(c, idx, t):
        return send(wx_o.at[idx], wx_o.at[idx], swm.at[c, t], rwp_of(idx), mate)

    def spread_w(t):
        idx = d * ns + t
        for c in chips:
            plane_w(c, idx, t).start()
        mate_w(chip, idx, t).start()

    for copy in keep[:3]:
        copy.wait()
    spread_w(q)

    for k, e in enumerate(peers):
        embeds(k, e, e).wait_recv()
    rows = modw.shape[0]
    here = lax.broadcasted_iota(jnp.int32, (FREQ, rows), 0)
    pick = here - lax.broadcasted_iota(jnp.int32, (FREQ, rows), 1)
    count = FREQ // (nd * ns)
    keep_col = lax.broadcasted_iota(jnp.int32, (FREQ, rows), 1) < count
    pick = jnp.where(jnp.logical_and(pick == me * count, keep_col), 1.0, 0.0).astype(BF)
    mine = jnp.dot(eland[...].reshape(nd * 16, FREQ), pick, preferred_element_type=F32).astype(BF)
    prod[...] = jnp.dot(mine, modw[...], preferred_element_type=F32)

    lines = prod.shape[1] // 128
    @pl.loop(0, nd)
    def _(e):
        rowp[e] = modb[...]
        for j in range(lines):
            rowp[e, j:j + 1, :] += prod[pl.ds(pl.multiple_of(e * 16, 16), 1), j * 128:(j + 1) * 128]

    def to_item(k, e, src):
        return send(rowp.at[e], land1.at[src], s1.at[k], r1.at[src], (e, q))

    for k, e in enumerate(peers):
        to_item(k, e, d).start()

    for k, t in enumerate(others):
        for copy in across(k, t, d * ns + t):
            copy.wait_recv()
        spread_w(t)

    def plane_p(c, i, t):
        return send(pack_o.at[i], pack_o.at[i], spp.at[c, t], rp.at[i], (c * 2 + core, q))

    def mate_p(c, i, t):
        return send(pack_o.at[i], pack_o.at[i], spm.at[c, t], rp.at[i], mate)

    base = lax.rem(d, spread) * ns

    @pl.when(plane == q)
    def _():
        pack_own.wait()
        for t in others:
            send(pack, pack_o.at[base + t], spz, rp.at[base + t], (d, plane)).wait_recv()
        for t in range(ns):
            for c in chips:
                plane_p(c, base + t, t).start()
            mate_p(chip, base + t, t).start()

    total = rowp[d]
    for k, e in enumerate(peers):
        to_item(k, e, e).wait_recv()
        total = total + land1[e]
    land2[q] = total

    def to_column(k, t, src):
        return send(land2.at[src], land2.at[src], s2.at[k], r2.at[src], (d, t))

    for k, t in enumerate(others):
        to_column(k, t, q).start()

    def relay_w(c, t):
        idx = (c * 2 + core) * ns + t
        plane_w(c, idx, t).wait_recv()
        mate_w(c, idx, t).start()

    def holds(c):
        return (c * 2 + core) // spread == q

    def relay_p(c):
        first = lax.rem(c * 2 + core, spread) * ns
        @pl.when(holds(c))
        def _():
            for t in range(ns):
                plane_p(c, first + t, t).wait_recv()
                mate_p(c, first + t, t).start()

    hops = [(k, s) for k in range(1, ns) for s in range(nsub)]
    relays = [(c, t) for t in [q] + others for c in chips]
    at = 0
    for i, (k, s) in enumerate(hops):
        upto = len(relays) * (i + 1) // len(hops)
        hop(k, s)
        for c, t in relays[at:upto]:
            relay_w(c, t)
        at = upto
    for c in chips:
        relay_p(c)
    for k, t in enumerate(others):
        to_column(k, t, t).wait_recv()
    total = land2[0]
    for t in range(1, ns):
        total = total + land2[t]
    mod_o[...] = total

    twin = 1 - core
    for c in range(nc):
        for t in range(ns):
            idx = (c * 2 + twin) * ns + t
            mate_w(c, idx, t).wait_recv()
        first = lax.rem(c * 2 + twin, spread) * ns
        @pl.when((c * 2 + twin) // spread == q)
        def _():
            for t in range(ns):
                mate_p(c, first + t, t).wait_recv()
    for k, t in enumerate(others):
        masks(k, t, t).wait_recv()
    keep[3].wait()

    for k, t in enumerate(others):
        for copy in across(k, t, me):
            copy.wait_send()
        masks(k, t, q).wait_send()
        to_column(k, t, q).wait_send()
    for k, e in enumerate(peers):
        embeds(k, e, d).wait_send()
        to_item(k, e, d).wait_send()

    @pl.when(plane != q)
    def _():
        pack_z.wait_send()

    @pl.when(plane == q)
    def _():
        for t in range(ns):
            for c in chips:
                plane_p(c, base + t, t).wait_send()
            mate_p(chip, base + t, t).wait_send()

    for t in range(ns):
        for c in chips:
            plane_w(c, d * ns + t, t).wait_send()
            mate_w(c, (c * 2 + core) * ns + t, t).wait_send()
        mate_w(chip, d * ns + t, t).wait_send()
    for c in chips:
        first = lax.rem(c * 2 + core, spread) * ns
        @pl.when(holds(c))
        def _():
            for t in range(ns):
                mate_p(c, first + t, t).wait_send()
    for k in range(ns - 1):
        for s in range(nsub):
            @pl.when(jnp.logical_and(q >= k, q + 1 < ns))
            def _():
                rise(k, s).wait_send()
            @pl.when(jnp.logical_and(q + k < ns, q >= 1))
            def _():
                sink(k, s).wait_send()


def start(hidden, mask, win, wout, pack, embedded, modw, modb, nd, ns, cid):
    nsub = 4
    length, width = hidden.shape
    rows, inner = wout.shape
    nc = nd // 2
    hidden = hidden.reshape(nsub, length // nsub, width)
    lines = modb.shape
    return pl.pallas_call(
        functools.partial(start_kernel, nd, ns, nsub),
        out_shape=[
            jax.ShapeDtypeStruct((ns,) + hidden.shape, BF),
            jax.ShapeDtypeStruct((nd * ns, rows, 3 * inner // ns), BF),
            jax.ShapeDtypeStruct((nd,) + pack.shape, BF),
            jax.ShapeDtypeStruct((ns,) + mask.shape, BF),
            jax.ShapeDtypeStruct(lines, F32),
        ],
        in_specs=[HBM, HBM, HBM, HBM, VMEM, VMEM, VMEM, VMEM],
        out_specs=[HBM, HBM, HBM, VMEM, VMEM],
        scratch_shapes=[
            pltpu.VMEM((nd,) + embedded.shape, BF), pltpu.VMEM((nd * 16, modw.shape[1]), F32),
            pltpu.VMEM((nd,) + lines, F32), pltpu.VMEM((nd,) + lines, F32), pltpu.VMEM((ns,) + lines, F32),
            DMA((ns - 1, nsub)), DMA((ns - 1, nsub)), DMA((ns - 1, nsub)), DMA((ns - 1, nsub)),
            DMA((ns, 3)), DMA((nd * ns, 4)), DMA((nc, ns)), DMA((nc, ns)),
            DMA(()), DMA((nd,)), DMA((nc, ns)), DMA((nc, ns)),
            DMA((ns,)), DMA((ns,)), DMA((nd,)), DMA((nd,)),
            DMA((nd,)), DMA((nd,)), DMA((ns,)), DMA((ns,)), DMA((5,)),
        ],
        compiler_params=pltpu.CompilerParams(
            collective_id=cid, has_side_effects=True, vmem_limit_bytes=40 * 2**20),
        name="start",
    )(hidden, win, wout, pack, mask, embedded, modw, modb)


def frequency_embed(timestep):
    half_width = FREQ // 2
    counter = jnp.arange(half_width, dtype=F32)
    frequency = jnp.exp(counter * (-math.log(10000.0) / half_width))
    angles = timestep.astype(F32)[:, None] * frequency[None, :]
    return jnp.concatenate([jnp.cos(angles), jnp.sin(angles)], axis=1)


def dot(a, b):
    return jnp.dot(a, b, preferred_element_type=F32)


def dot_nt(a, b):
    return lax.dot_general(a, b, (((1,), (1,)), ((), ())), preferred_element_type=F32)


def dot_tn(a, b):
    return lax.dot_general(a, b, (((0,), (0,)), ((), ())), preferred_element_type=F32)


def body(
    hidden,
    pad_mask,
    timestep,
    input_weight,
    select_weight,
    step_weight,
    output_weight,
    decay_forward,
    decay_reverse,
    filter_weight,
    filter_bias,
    step_bias,
    modulation_weight,
    modulation_bias,
    cotangent,
):
    ns, nd = lax.axis_size("seq"), lax.axis_size("dp")
    q, d = lax.axis_index("seq"), lax.axis_index("dp")
    every = ("dp", "seq")
    local_len, width = hidden.shape[1:]
    length = local_len * ns
    inner = output_weight.shape[0]
    part = inner // ns
    rank = step_weight.shape[0]
    state = decay_forward.shape[1]
    taps = filter_weight.shape[0]
    rows_in = input_weight.shape[0]
    lanes = select_weight.shape[1]

    units = part // nd
    embedded = jax.nn.silu(frequency_embed(timestep)).astype(BF)
    fil = jnp.concatenate([filter_weight, filter_bias[None], step_bias[None]])
    fil = jnp.pad(fil, ((0, 16 - fil.shape[0]), (0, lanes - units)))
    mid = jnp.concatenate([step_weight.T, decay_forward, decay_reverse], axis=1)
    pack = jnp.concatenate([select_weight, mid, fil])
    mask = jnp.pad(pad_mask[0].astype(BF).reshape(-1, 128), ((0, 16 - local_len // 128), (0, 0)))
    shard = (-modulation_weight.shape[0] % 16, 0)
    modb = jnp.zeros((-(-3 * width // 1024) * 1024,), F32)
    modb = lax.dynamic_update_slice(modb, modulation_bias.astype(F32), ((d * ns + q) * modulation_bias.shape[0],))
    row_pad = ((0, -rows_in % 16), (0, 0))
    hid, wx, pack, mask, modulation = start(
        hidden[0], mask, jnp.pad(input_weight, row_pad), jnp.pad(output_weight.T, row_pad), pack,
        jnp.pad(embedded, ((0, 15), (0, 0))),
        jnp.pad(modulation_weight, ((0, shard[0]), (0, 0))), modb.reshape(-1, 128), nd, ns, 4)
    hid = hid.reshape(length, width)
    wx = wx[:, :rows_in].reshape(width, 3 * part)
    win, wout = wx[:, : 2 * part], wx[:, 2 * part :]
    mask = mask[:, : local_len // 128].reshape(length, 1).astype(F32)
    select_q = pack[:, :units].reshape(part, lanes)
    mid = pack[:, units : 2 * units].reshape(part, lanes)
    step_q = mid[:, :rank].T
    log_f, log_r = mid[:, rank : rank + state], mid[:, rank + state :]
    fil = pack[:, 2 * units :, :units].transpose(1, 0, 2).reshape(16, part).astype(F32)
    filt32, fbias, sbias = fil[:taps].T, fil[taps][None], fil[taps + 1][None]
    modulation = modulation.reshape(1, -1)[:, : 3 * width]
    shifts = modulation[:, :width]
    scales = modulation[:, width : 2 * width]
    gate_scale = modulation[:, 2 * width :]

    def norm(x):
        x = x.astype(F32)
        centered = x - jnp.mean(x, axis=1, keepdims=True)
        inverse = lax.rsqrt(jnp.mean(centered * centered, axis=1, keepdims=True) + EPS)
        return centered * inverse, inverse

    modded = (norm(hid)[0] * (1.0 + scales) + shifts).astype(BF)
    projected = dot(modded, win)
    inner_part = projected[:, :part].astype(BF).astype(F32) * mask
    gate_branch = projected[:, part:]
    padded = jnp.pad(inner_part, ((taps - 1, 0), (0, 0)))
    filtered = fbias
    for k in range(taps):
        filtered = filtered + filt32[:, k][None, :] * padded[k : k + length]
    sigma_filter = jax.nn.sigmoid(filtered)
    active = (filtered * sigma_filter).astype(BF)
    active32 = active.astype(F32)
    selected = column_sum(dot(active, select_q), ns, BF, 0)
    cot, selected = lax.optimization_barrier((cotangent[0], selected))
    cot = lax.all_gather(cot, "seq", axis=0, tiled=True)
    low_rank = selected[:, :rank].astype(BF)
    b_rows = selected[:, rank : rank + state].astype(F32)
    c_rows = selected[:, rank + state :].astype(F32)
    pre_steps = dot(low_rank, step_q) + sbias
    steps = jax.nn.softplus(pre_steps)
    rates_f = -jnp.exp(log_f.astype(F32)).T
    rates_r = -jnp.exp(log_r.astype(F32)).T
    drive = steps * active32
    bb, cb = lanes_of(b_rows), lanes_of(c_rows)
    bblk, cblk = blockdiag(b_rows), blockdiag(c_rows)
    mixed_f, states_f = fwd_scan(steps, drive, rates_f * LOG2E, bb, cblk, False)
    mixed_r, states_r = fwd_scan(steps, drive, rates_r * LOG2E, bb, cblk, True)
    merged = mixed_f + mixed_r
    sigma_gate = jax.nn.sigmoid(gate_branch)
    silu_gate = gate_branch * sigma_gate
    gated = (merged * silu_gate).astype(BF)
    branch = lax.psum_scatter(dot_nt(gated, wout), "seq", scatter_dimension=0, tiled=True)

    mask_here = pad_mask[0].astype(F32)[:, None]
    cot_here = cotangent[0].astype(F32)
    block_out = (hidden[0].astype(F32) + gate_scale * mask_here * branch).astype(BF)
    grad_gate = jnp.sum(mask_here * cot_here * branch, axis=0)

    grad_branch = (cot.astype(F32) * gate_scale * mask).astype(BF)
    grad_gated = dot(grad_branch, wout)
    grad_merged = grad_gated * silu_gate
    grad_gate_branch = grad_gated * merged * sigma_gate * (1.0 + gate_branch * (1.0 - sigma_gate))
    dlog_f, adjb_f, bg_f, cg_f, rg_f = bwd_scan(
        steps, drive, grad_merged, rates_f * LOG2E, bb, cb, bblk, states_f, False)
    dlog_r, adjb_r, bg_r, cg_r, rg_r = bwd_scan(
        steps, drive, grad_merged, rates_r * LOG2E, bb, cb, bblk, states_r, True)
    adjb = adjb_f + adjb_r
    grad_steps = (dlog_f + dlog_r) * (1.0 / LOG2E) + active32 * adjb
    grad_b = (bg_f + bg_r).reshape(length, state)
    grad_c = (cg_f + cg_r).reshape(length, state)
    grad_decay_f = rg_f.transpose(1, 0, 2).reshape(state, part) * rates_f
    grad_decay_r = rg_r.transpose(1, 0, 2).reshape(state, part) * rates_r
    grad_pre = grad_steps * jax.nn.sigmoid(pre_steps)
    grad_step_bias = jnp.sum(grad_pre, axis=0)
    grad_pre_low = grad_pre.astype(BF)
    grad_step_t = dot_tn(grad_pre_low, low_rank)
    grad_low_rank = dot_nt(grad_pre_low, step_q)
    grad_selected = column_sum(jnp.concatenate([grad_low_rank, grad_b, grad_c], axis=1), ns, BF, 1)
    grad_select = dot_tn(active, grad_selected)
    grad_active = steps * adjb + dot_nt(grad_selected, select_q)
    grad_filtered = grad_active * sigma_filter * (1.0 + filtered * (1.0 - sigma_filter))
    extended = jnp.pad(grad_filtered, ((0, taps - 1), (0, 0)))
    grad_inner = jnp.zeros_like(grad_filtered)
    filter_rows = []
    for k in range(taps):
        lead = taps - 1 - k
        grad_inner = grad_inner + filt32[:, k][None, :] * extended[lead : lead + length]
        filter_rows.append(jnp.sum(grad_filtered * padded[k : k + length], axis=0))
    grad_filter_bias = jnp.sum(grad_filtered, axis=0)
    grad_projected = jnp.concatenate([grad_inner * mask, grad_gate_branch], axis=1).astype(BF)
    fil = jnp.stack(filter_rows + [grad_filter_bias, grad_step_bias])
    fil = fil.reshape(-1, nd, units).transpose(1, 0, 2)
    fil = jnp.pad(fil, ((0, 0), (0, 16 - fil.shape[1]), (0, lanes - units)))
    mid = jnp.concatenate([grad_step_t, grad_decay_f.T, grad_decay_r.T], axis=1)
    small = jnp.concatenate([grad_select.reshape(nd, units, lanes), mid.reshape(nd, units, lanes), fil], axis=1)
    grads = jnp.concatenate([dot_tn(modded, grad_projected), dot_tn(grad_branch, gated)], axis=1)
    grads = grads.astype(BF).reshape(nd, ns, rows_in, 3 * part)
    grads = jnp.pad(grads, ((0, 0), (0, 0), (0, -rows_in % 16), (0, 0)))
    grads, small, grad_modded = home(grads, small, dot_nt(grad_projected, win).astype(BF), nd, ns, 2)
    grads = grads[:, :rows_in].astype(F32)
    g_in = grads[:, :, : 2 * part].reshape(ns, rows_in, 2, part).transpose(1, 2, 0, 3).reshape(rows_in, 2 * inner)
    g_out = grads[:, :, 2 * part :].transpose(1, 0, 2).reshape(rows_in, inner).T
    gs_select = small[:units]
    mid = small[units : 2 * units]
    gs_step, gs_f, gs_r = mid[:, :rank], mid[:, rank : rank + state], mid[:, rank + state :]
    fil = small[2 * units :, :units]

    normed, inverse = norm(hidden[0])
    grad_shifts = jnp.sum(grad_modded, axis=0)
    grad_scales = jnp.sum(grad_modded * normed, axis=0)
    grad_normed = grad_modded * (1.0 + scales)
    grad_hidden = cot_here + inverse * (
        grad_normed
        - jnp.mean(grad_normed, axis=1, keepdims=True)
        - normed * jnp.mean(grad_normed * normed, axis=1, keepdims=True)
    )

    grad_mod = jnp.concatenate([grad_shifts, grad_scales, grad_gate, embedded[0].astype(F32) / ns])
    grad_mod = jnp.pad(grad_mod, (0, -grad_mod.shape[0] % 1024)).reshape(-1, 128)
    grad_mod = mod_gather(grad_mod, nd, ns, 3).reshape(nd, -1)
    embeds = grad_mod[:, 3 * width : 3 * width + FREQ]
    grad_mod = grad_mod[:, : 3 * width]
    me = d * ns + q
    mine = lax.dynamic_slice_in_dim(embeds, me * modulation_weight.shape[0], modulation_weight.shape[0], 1)
    g_modw = lax.dot_general(mine, grad_mod, (((0,), (0,)), ((), ())), precision=HIGHEST)
    g_modb = lax.dynamic_slice_in_dim(
        jnp.sum(grad_mod, axis=0), me * modulation_bias.shape[0], modulation_bias.shape[0], 0)
    return (
        block_out[None],
        grad_hidden.astype(BF)[None],
        g_in,
        gs_select,
        gs_step.T,
        g_out,
        gs_f,
        gs_r,
        fil[:taps],
        fil[taps],
        fil[taps + 1],
        g_modw,
        g_modb,
    )


def solution(mesh):
    return jax.shard_map(
        body,
        mesh=mesh,
        in_specs=(
            P("dp", "seq", None),
            P("dp", "seq"),
            P("dp"),
            P(("dp", "seq"), None),
            P(("dp", "seq"), None),
            P(None, ("dp", "seq")),
            P(None, ("dp", "seq")),
            P(("dp", "seq"), None),
            P(("dp", "seq"), None),
            P(None, ("dp", "seq")),
            P(("dp", "seq")),
            P(("dp", "seq")),
            P(("dp", "seq"), None),
            P(("dp", "seq")),
            P("dp", "seq", None),
        ),
        out_specs=(
            P("dp", "seq", None),
            P("dp", "seq", None),
            P(("dp", "seq"), None),
            P(("dp", "seq"), None),
            P(None, ("dp", "seq")),
            P(None, ("dp", "seq")),
            P(("dp", "seq"), None),
            P(("dp", "seq"), None),
            P(None, ("dp", "seq")),
            P(("dp", "seq")),
            P(("dp", "seq")),
            P(("dp", "seq"), None),
            P(("dp", "seq")),
        ),
        check_vma=False,
    )
```

```python
import functools
import math

import jax
import jax.numpy as jnp
from jax import lax
from jax.experimental import pallas as pl
from jax.experimental.pallas import tpu as pltpu
from jax.sharding import PartitionSpec as P

FREQ = 256
EPS = 1e-06
HIGHEST = lax.Precision.HIGHEST
LOG2E = 1.4426950408889634
SUB = 16
WF = 384
WB = 768
F32, BF = jnp.float32, jnp.bfloat16
NT = (((1,), (1,)), ((), ()))


def columns_of(rows_t, base):
    turned = pltpu.roll(rows_t, rows_t.shape[1] - base, 1)
    return [jnp.broadcast_to(turned[:, j:j + 1], (rows_t.shape[0], 128)) for j in range(SUB)]


def wide(block, lanes):
    return jnp.concatenate([block] * (lanes // 128), axis=1) if lanes > 128 else block


def states_of(base, at):
    return pl.ds(pl.multiple_of((base + at) * 16, 16), 16)


def fwd_kernel(step_f, step_r, u_f, u_r, rate_f, rate_r, bt_f, bt_r, cblk_f, cblk_r,
               y_f, y_r, s_f, s_r, carry, f0, f1, r0, r1):
    rows, lanes = step_f.shape

    @pl.when(pl.program_id(0) == 0)
    def _():
        carry[...] = jnp.zeros(carry.shape, F32)

    wide_by = min(WF, lanes)
    cuts = [slice(c, c + wide_by) for c in range(0, lanes, wide_by)]

    def walk(states, bases, kept):
        cols = [columns_of(bt[...], base) for bt, base in zip((bt_f, bt_r), bases)]
        out = []
        for cut, pair in zip(cuts, states):
            pair = list(pair)
            rates = rate_f[:, cut], rate_r[:, cut]
            for k in range(SUB):
                for z, (step, u, s, j) in enumerate(((step_f, u_f, s_f, k), (step_r, u_r, s_r, SUB - 1 - k))):
                    at = pl.ds(bases[z] + j, 1)
                    decay = jnp.exp2(step[at, cut] * rates[z])
                    pair[z] = decay * pair[z] + u[at, cut] * wide(cols[z][j], wide_by)
                    low = pair[z].astype(BF)
                    s[states_of(bases[z], j), cut] = low
                    kept[z][j * 16:(j + 1) * 16, cut] = low
            out.append(tuple(pair))
        return tuple(out)

    def mix(base, cblk, kept, y):
        here = pl.ds(base, SUB)
        y[here, :] = jnp.dot(cblk[here, :], kept[...], preferred_element_type=F32)

    def start_of(a, flip):
        a = jnp.maximum(a, 0)
        return pl.multiple_of(rows - SUB - a * SUB if flip else a * SUB, SUB)

    def two(i, states):
        for half, (fk, rk, fp, rp) in enumerate(((f0, r0, f1, r1), (f1, r1, f0, r0))):
            a = 2 * i + half
            mix(start_of(a - 1, False), cblk_f, fp, y_f)
            mix(start_of(a - 1, True), cblk_r, rp, y_r)
            states = walk(states, (start_of(a, False), start_of(a, True)), (fk, rk))
        return states

    states = tuple((carry[0, :, cut], carry[1, :, cut]) for cut in cuts)
    states = lax.fori_loop(0, rows // SUB // 2, two, states)
    mix(rows - SUB, cblk_f, f1, y_f)
    mix(0, cblk_r, r1, y_r)
    for cut, pair in zip(cuts, states):
        carry[0, :, cut], carry[1, :, cut] = pair


def fwd_scan(steps, u, rates_f, rates_r, b_t, cblk, tile=128):
    length, lanes = steps.shape
    blocks = length // tile
    specs = []
    for order in (lambda t: t, lambda t: blocks - 1 - t):
        specs.append((
            pl.BlockSpec((tile, lanes), lambda t, order=order: (order(t), 0)),
            pl.BlockSpec((16, lanes), lambda t: (0, 0)),
            pl.BlockSpec((16, tile), lambda t, order=order: (0, order(t))),
            pl.BlockSpec((tile, 256), lambda t, order=order: (order(t), 0)),
            pl.BlockSpec((tile * 16, lanes), lambda t, order=order: (order(t), 0)),
        ))
    (row_f, rate, bt_f, blk_f, s_f), (row_r, _, bt_r, blk_r, s_r) = specs
    y = jax.ShapeDtypeStruct((length, lanes), F32)
    s = jax.ShapeDtypeStruct((length * 16, lanes), BF)
    kept = pltpu.VMEM((256, lanes), BF)
    return pl.pallas_call(
        fwd_kernel,
        grid=(blocks,),
        in_specs=[row_f, row_r, row_f, row_r, rate, rate, bt_f, bt_r, blk_f, blk_r],
        out_specs=[row_f, row_r, s_f, s_r],
        out_shape=[y, y, s, s],
        scratch_shapes=[pltpu.VMEM((2, 16, lanes), F32), kept, kept, kept, kept],
        compiler_params=pltpu.CompilerParams(vmem_limit_bytes=56 * 2**20, dimension_semantics=("arbitrary",)),
        cost_estimate=pl.CostEstimate(flops=length * lanes * 16 * 16, transcendentals=0, bytes_accessed=length * lanes * 80),
        name="fwd_scan",
    )(steps, steps, u, u, rates_f, rates_r, b_t, b_t, cblk, cblk)


def bwd_kernel(step_f, step_r, u_f, u_r, gy_f, gy_r, rate_f, rate_r, ct_f, ct_r, bblk_f, bblk_r, s_f, s_r, sp_f, sp_r,
               dlog_f, dlog_r, adjb_f, adjb_r, bg_f, bg_r, cg_f, cg_r, rg_f, rg_r, carry,
               af0, af1, ar0, ar1, lf0, lf1, lr0, lr1):
    rows, lanes = step_f.shape
    t = pl.program_id(0)
    last = pl.num_programs(0) - 1

    @pl.when(t == 0)
    def _():
        carry[...] = jnp.zeros(carry.shape, F32)
        rg_f[...] = jnp.zeros(rg_f.shape, F32)
        rg_r[...] = jnp.zeros(rg_r.shape, F32)

    ones = (lax.broadcasted_iota(jnp.int32, (SUB, 256), 0) == lax.broadcasted_iota(jnp.int32, (SUB, 256), 1) // 16)
    onesb = ones.astype(BF)
    zero = jnp.zeros((SUB, 256), F32)

    def start_of(a, down):
        a = jnp.maximum(a, 0)
        return pl.multiple_of(rows - SUB - a * SUB if down else a * SUB, SUB)

    wide_by = min(WB, lanes)
    cuts = [slice(c, c + wide_by) for c in range(0, lanes, wide_by)]

    def walk(states, bases, keep_a, keep_l):
        cols = [columns_of(ct[...], base) for ct, base in zip((ct_f, ct_r), bases)]
        out = []
        for cut, pair in zip(cuts, states):
            pair = list(pair)
            rates = rate_f[:, cut], rate_r[:, cut]
            rg = [rg_f[:, cut], rg_r[:, cut]]
            low_rates = [r.astype(BF) for r in rates]
            some = [[], []]
            for k in range(SUB):
                for z, (step, gy, s, sp, j) in enumerate((
                        (step_f, gy_f, s_f, sp_f, SUB - 1 - k), (step_r, gy_r, s_r, sp_r, k))):
                    at = pl.ds(bases[z] + j, 1)
                    row = step[at, cut]
                    adj = gy[at, cut] * wide(cols[z][j], wide_by) + pair[z]
                    pair[z] = jnp.exp2(row * rates[z]) * adj
                    before = bases[z] + (j + 1 if z else j - 1)
                    if k < SUB - 1:
                        inner = s[pl.ds(pl.multiple_of(before * 16, 16), 16), cut]
                    else:
                        inside = before < rows if z else before >= 0
                        safe = jnp.clip(before, 0, rows - 1)
                        inner = s[pl.ds(pl.multiple_of(safe * 16, 16), 16), cut]
                        outer = jnp.where(t == last, jnp.zeros_like(inner), sp[:, cut])
                        inner = jnp.where(inside, inner, outer)
                    grad = pair[z].astype(BF) * inner
                    keep_a[z][j * 16:(j + 1) * 16, cut] = adj.astype(BF)
                    keep_l[z][j * 16:(j + 1) * 16, cut] = grad * low_rates[z]
                    some[z].append(grad * jnp.broadcast_to(row, (16, wide_by)).astype(BF))
                    if len(some[z]) == 4:
                        rg[z] = rg[z] + ((some[z][0] + some[z][1]) + (some[z][2] + some[z][3])).astype(F32)
                        some[z] = []
            rg_f[:, cut], rg_r[:, cut] = rg
            out.append(tuple(pair))
        return tuple(out)

    def mix(base, a_ref, l_ref, u, gy, bblk, s, dlog, adjb, bg, cg):
        here = pl.ds(base, SUB)
        line = pl.ds(base // SUB, 1)
        a = a_ref[...]
        dlog[here, :] = jnp.dot(onesb, l_ref[...], preferred_element_type=F32)
        adjb[here, :] = jnp.dot(bblk[here, :], a, preferred_element_type=F32)
        bgd = lax.dot_general(u[here, :], a, NT, preferred_element_type=F32)
        block = s[pl.ds(pl.multiple_of(base * 16, 256), 256), :]
        cgd = lax.dot_general(gy[here, :].astype(BF), block, NT, preferred_element_type=F32)
        bg[line, :] = jnp.sum(jnp.where(ones, bgd, zero), axis=0, keepdims=True)
        cg[line, :] = jnp.sum(jnp.where(ones, cgd, zero), axis=0, keepdims=True)

    def mix_f(base, a_ref, l_ref):
        mix(base, a_ref, l_ref, u_f, gy_f, bblk_f, s_f, dlog_f, adjb_f, bg_f, cg_f)

    def mix_r(base, a_ref, l_ref):
        mix(base, a_ref, l_ref, u_r, gy_r, bblk_r, s_r, dlog_r, adjb_r, bg_r, cg_r)

    def two(i, states):
        bufs = ((af0, lf0, ar0, lr0), (af1, lf1, ar1, lr1))
        for half in range(2):
            a = 2 * i + half
            naf, nlf, nar, nlr = bufs[half]
            paf, plf, par, plr = bufs[1 - half]
            mix_f(start_of(a - 1, True), paf, plf)
            mix_r(start_of(a - 1, False), par, plr)
            states = walk(states, (start_of(a, True), start_of(a, False)), (naf, nar), (nlf, nlr))
        return states

    states = tuple((carry[0, :, cut], carry[1, :, cut]) for cut in cuts)
    states = lax.fori_loop(0, rows // SUB // 2, two, states)
    mix_f(0, af1, lf1)
    mix_r(rows - SUB, ar1, lr1)
    for cut, pair in zip(cuts, states):
        carry[0, :, cut], carry[1, :, cut] = pair


def bwd_scan(steps, u, gy, rates_f, rates_r, c_t, bblk, states_f, states_r, tile=128):
    length, lanes = steps.shape
    blocks = length // tile
    down = lambda t: blocks - 1 - t
    up = lambda t: t

    def specs(order, before):
        return (
            pl.BlockSpec((tile, lanes), lambda t: (order(t), 0)),
            pl.BlockSpec((16, lanes), lambda t: (0, 0)),
            pl.BlockSpec((16, tile), lambda t: (0, order(t))),
            pl.BlockSpec((tile, 256), lambda t: (order(t), 0)),
            pl.BlockSpec((tile * 16, lanes), lambda t: (order(t), 0)),
            pl.BlockSpec((16, lanes), lambda t: (before(t), 0)),
            pl.BlockSpec((tile // 16, 256), lambda t: (order(t), 0)),
        )

    row_f, rate, ct_f, blk_f, s_f, sp_f, diag_f = specs(down, lambda t: jnp.maximum((blocks - 1 - t) * tile - 1, 0))
    row_r, _, ct_r, blk_r, s_r, sp_r, diag_r = specs(up, lambda t: jnp.minimum((t + 1) * tile, length - 1))
    y = jax.ShapeDtypeStruct((length, lanes), F32)
    diag = jax.ShapeDtypeStruct((length // 16, 256), F32)
    rg = jax.ShapeDtypeStruct((16, lanes), F32)
    kept = pltpu.VMEM((256, lanes), BF)
    return pl.pallas_call(
        bwd_kernel,
        grid=(blocks,),
        in_specs=[row_f, row_r, row_f, row_r, row_f, row_r, rate, rate, ct_f, ct_r, blk_f, blk_r, s_f, s_r, sp_f, sp_r],
        out_specs=[row_f, row_r, row_f, row_r, diag_f, diag_r, diag_f, diag_r, rate, rate],
        out_shape=[y, y, y, y, diag, diag, diag, diag, rg, rg],
        scratch_shapes=[pltpu.VMEM((2, 16, lanes), F32)] + [kept] * 8,
        compiler_params=pltpu.CompilerParams(vmem_limit_bytes=56 * 2**20, dimension_semantics=("arbitrary",)),
        cost_estimate=pl.CostEstimate(flops=length * lanes * 16 * 48, transcendentals=0, bytes_accessed=length * lanes * 100),
        name="bwd_scan",
    )(steps, steps, u, u, gy, gy, rates_f, rates_r, c_t, c_t, bblk, bblk, states_f, states_r, states_f, states_r)


def blockdiag(rows):
    length = rows.shape[0]
    eye = (jnp.arange(length)[:, None] % 16) == (jnp.arange(256)[None, :] // 16)
    return jnp.where(eye, jnp.tile(rows, (1, 16)), 0).astype(BF)


MESH = pl.DeviceIdType.MESH
VMEM = pl.BlockSpec(memory_space=pltpu.VMEM)
HBM = pl.BlockSpec(memory_space=pl.ANY)
DMA = pltpu.SemaphoreType.DMA


def send(src, dst, out_sem, in_sem, to):
    return pltpu.make_async_remote_copy(
        src_ref=src, dst_ref=dst, send_sem=out_sem, recv_sem=in_sem, device_id=to, device_id_type=MESH)


def greet(devices):
    bar = pltpu.get_barrier_semaphore()
    for to in devices:
        pl.semaphore_signal(bar, inc=1, device_id=to, device_id_type=MESH)
    pl.semaphore_wait(bar, len(devices))


def column_sum_kernel(ns, p_ref, o_ref, land, s1, r1, s2, r2):
    d, q = lax.axis_index("dp"), lax.axis_index("seq")
    others = [lax.rem(q + k, ns) for k in range(1, ns)]
    greet([(d, t) for t in others])
    for k, t in enumerate(others):
        send(p_ref.at[t], land.at[q], s1.at[k], r1.at[q], (d, t)).start()
    total = p_ref[q]
    for k, t in enumerate(others):
        send(p_ref.at[t], land.at[t], s1.at[k], r1.at[t], (d, t)).wait_recv()
        total = total + land[t]
    o_ref[q] = total.astype(o_ref.dtype)
    for k, t in enumerate(others):
        send(o_ref.at[q], o_ref.at[q], s2.at[k], r2.at[q], (d, t)).start()
    for k, t in enumerate(others):
        send(o_ref.at[t], o_ref.at[t], s2.at[k], r2.at[t], (d, t)).wait_recv()
    for k, t in enumerate(others):
        send(p_ref.at[t], land.at[q], s1.at[k], r1.at[q], (d, t)).wait_send()
        send(o_ref.at[q], o_ref.at[q], s2.at[k], r2.at[q], (d, t)).wait_send()


def column_sum(partial, ns, out_dtype, cid):
    rows, lanes = partial.shape
    block = (ns, rows // ns, lanes)
    out = pl.pallas_call(
        functools.partial(column_sum_kernel, ns),
        out_shape=jax.ShapeDtypeStruct(block, out_dtype),
        in_specs=[VMEM], out_specs=VMEM,
        scratch_shapes=[pltpu.VMEM(block, partial.dtype), DMA((ns,)), DMA((ns,)), DMA((ns,)), DMA((ns,))],
        compiler_params=pltpu.CompilerParams(
            collective_id=cid, has_side_effects=True, vmem_limit_bytes=32 * 2**20),
        name="column_sum",
    )(partial.reshape(block))
    return out.reshape(rows, lanes)


def mod_gather_kernel(nd, ns, g_ref, o_ref, land, s1, r1, s2, r2):
    d, q = lax.axis_index("dp"), lax.axis_index("seq")
    others = [lax.rem(q + k, ns) for k in range(1, ns)]
    peers = [lax.rem(d + k, nd) for k in range(1, nd)]
    greet([(d, t) for t in others] + [(e, q) for e in peers])
    for k, t in enumerate(others):
        send(g_ref, land.at[q], s1.at[k], r1.at[q], (d, t)).start()
    total = g_ref[...]
    for k, t in enumerate(others):
        send(g_ref, land.at[t], s1.at[k], r1.at[t], (d, t)).wait_recv()
        total = total + land[t]
    o_ref[d] = total
    for k, e in enumerate(peers):
        send(o_ref.at[d], o_ref.at[d], s2.at[k], r2.at[d], (e, q)).start()
    for k, e in enumerate(peers):
        send(o_ref.at[e], o_ref.at[e], s2.at[k], r2.at[e], (e, q)).wait_recv()
    for k, t in enumerate(others):
        send(g_ref, land.at[q], s1.at[k], r1.at[q], (d, t)).wait_send()
    for k, e in enumerate(peers):
        send(o_ref.at[d], o_ref.at[d], s2.at[k], r2.at[d], (e, q)).wait_send()


def mod_gather(g, nd, ns, cid):
    rows, lanes = g.shape
    return pl.pallas_call(
        functools.partial(mod_gather_kernel, nd, ns),
        out_shape=jax.ShapeDtypeStruct((nd, rows, lanes), F32),
        in_specs=[VMEM], out_specs=VMEM,
        scratch_shapes=[pltpu.VMEM((ns, rows, lanes), F32), DMA((ns,)), DMA((ns,)), DMA((nd,)), DMA((nd,))],
        compiler_params=pltpu.CompilerParams(
            collective_id=cid, has_side_effects=True, vmem_limit_bytes=32 * 2**20),
        name="mod_gather",
    )(g)


def home_kernel(nd, ns, nsub, g_ref, sm_ref, gm_ref, f_ref, so_ref, out_ref,
                pair, plane, spair, splane, ssum, up, down,
                sa, ra, sb, rb, sc, rc, ta, ra2, tb, rb2, tc, rc2, su, ru, sd, rd):
    d, q = lax.axis_index("dp"), lax.axis_index("seq")
    nc = nd // 2
    chip, core = d // 2, lax.rem(d, 2)
    mate = chip * 2 + 1 - core
    chips = [lax.rem(chip + k, nc) for k in range(1, nc)]
    others = [lax.rem(q + k, ns) for k in range(1, ns)]
    spread = nd // ns
    final_to = (spread * q + d // ns, lax.rem(d, ns))
    mine = d * ns + q
    final_from = (lax.rem(mine, nd), mine // nd)
    stays = jnp.logical_and(final_to[0] == d, final_to[1] == q)
    bar = pltpu.get_barrier_semaphore()
    friends = [(mate, q)] + [(c * 2 + core, q) for c in chips] + [(d, t) for t in others]
    for to in friends:
        pl.semaphore_signal(bar, inc=1, device_id=to, device_id_type=MESH)
    @pl.when(jnp.logical_not(stays))
    def _():
        pl.semaphore_signal(bar, inc=1, device_id=final_from, device_id_type=MESH)
        pl.semaphore_wait(bar, len(friends) + 1)
    @pl.when(stays)
    def _():
        pl.semaphore_wait(bar, len(friends))

    def first(c):
        return send(g_ref.at[c * 2 + 1 - core], pair.at[c], sa.at[c], ra.at[c], (mate, q))

    def first_small(c):
        return send(sm_ref.at[c * 2 + 1 - core], spair.at[c], ta.at[c], ra2.at[c], (mate, q))

    order = chips + [chip]
    for c in order:
        first(c).start()
        first_small(c).start()

    def rise(t, s, src):
        return send(src, up.at[t, s], su.at[t, s], ru.at[t, s], (d, q + 1))

    def sink(t, s, src):
        return send(src, down.at[t, s], sd.at[t, s], rd.at[t, s], (d, q - 1))

    def added(land, t, s):
        land[t, s] = (land[t, s].astype(F32) + gm_ref[t, s].astype(F32)).astype(BF)

    def step_up(t, s):
        @pl.when(q < t)
        def _():
            @pl.when(q == 0)
            def _():
                rise(t, s, gm_ref.at[t, s]).start()
            @pl.when(q > 0)
            def _():
                rise(t, s, up.at[t, s]).wait_recv()
                added(up, t, s)
                rise(t, s, up.at[t, s]).start()

    def step_down(t, s):
        @pl.when(q > t)
        def _():
            @pl.when(q == ns - 1)
            def _():
                sink(t, s, gm_ref.at[t, s]).start()
            @pl.when(q < ns - 1)
            def _():
                sink(t, s, down.at[t, s]).wait_recv()
                added(down, t, s)
                sink(t, s, down.at[t, s]).start()

    steps = [(k, s) for k in range(ns - 1) for s in range(nsub)]
    middle = len(steps) * 2 // 3

    def walk(some):
        for k, s in some:
            step_up(ns - 1 - k, s)
            step_down(k, s)

    def second(c, src):
        return send(pair.at[c], plane.at[src], sb.at[c], rb.at[src], (c * 2 + core, q))

    def second_small(c, src):
        return send(spair.at[c], splane.at[src], tb.at[c], rb2.at[src], (c * 2 + core, q))

    walk(steps[:1])
    for c in order:
        first(c).wait_recv()
        @pl.loop(0, ns)
        def _(t):
            pair[c, t] = (pair[c, t].astype(F32) + g_ref[c * 2 + core, t].astype(F32)).astype(BF)
        first_small(c).wait_recv()
        spair[c] = spair[c] + sm_ref[c * 2 + core]
        if c is not chip:
            second(c, chip).start()
            second_small(c, chip).start()
    walk(steps[1:middle])

    for c in chips:
        second(c, c).wait_recv()
        second_small(c, c).wait_recv()
    @pl.loop(0, ns)
    def _(t):
        total = pair[chip, t].astype(F32)
        for c in chips:
            total = total + plane[c, t].astype(F32)
        pair[chip, t] = total.astype(BF)
    small = spair[chip]
    for c in chips:
        small = small + splane[c]
    ssum[...] = small

    def third(t, src):
        return send(pair.at[chip, t], f_ref.at[src], sc.at[t], rc.at[src], (d, t))

    last = send(ssum, so_ref, tc, rc2, final_to)
    @pl.when(stays)
    def _():
        so_ref[...] = ssum[...]
    @pl.when(jnp.logical_not(stays))
    def _():
        last.start()
    for t in others:
        third(t, q).start()
    f_ref[q] = pair[chip, q]
    walk(steps[middle:])

    for s in range(nsub):
        total = gm_ref[q, s].astype(F32)
        out_ref[s] = total
        @pl.when(q > 0)
        def _():
            rise(q, s, gm_ref.at[q, s]).wait_recv()
            out_ref[s] += up[q, s].astype(F32)
        @pl.when(q < ns - 1)
        def _():
            sink(q, s, gm_ref.at[q, s]).wait_recv()
            out_ref[s] += down[q, s].astype(F32)
    for t in others:
        third(t, t).wait_recv()
    @pl.when(jnp.logical_not(stays))
    def _():
        last.wait_recv()
        last.wait_send()
    for c in order:
        first(c).wait_send()
        first_small(c).wait_send()
    for c in chips:
        second(c, chip).wait_send()
        second_small(c, chip).wait_send()
    for t in others:
        third(t, q).wait_send()
    for k, s in steps:
        t = ns - 1 - k
        @pl.when(q < t)
        def _():
            rise(t, s, gm_ref.at[t, s]).wait_send()
        @pl.when(q > k)
        def _():
            sink(k, s, gm_ref.at[k, s]).wait_send()


def home(g, small, gm, nd, ns, cid):
    rows, cols = g.shape[2:]
    nc, nsub = nd // 2, 4
    length, width = gm.shape
    part = length // ns // nsub
    v = small.shape[1:]
    gm = gm.reshape(ns, nsub, part, width)
    f, so, out = pl.pallas_call(
        functools.partial(home_kernel, nd, ns, nsub),
        out_shape=[
            jax.ShapeDtypeStruct((ns, rows, cols), BF),
            jax.ShapeDtypeStruct(v, F32),
            jax.ShapeDtypeStruct((nsub, part, width), F32),
        ],
        in_specs=[VMEM] * 3, out_specs=[VMEM] * 3,
        scratch_shapes=[
            pltpu.VMEM((nc, ns, rows, cols), BF), pltpu.VMEM((nc, ns, rows, cols), BF),
            pltpu.VMEM((nc,) + v, F32), pltpu.VMEM((nc,) + v, F32), pltpu.VMEM(v, F32),
            pltpu.VMEM((ns, nsub, part, width), BF), pltpu.VMEM((ns, nsub, part, width), BF),
            DMA((nc,)), DMA((nc,)), DMA((nc,)), DMA((nc,)), DMA((ns,)), DMA((ns,)),
            DMA((nc,)), DMA((nc,)), DMA((nc,)), DMA((nc,)), DMA(()), DMA(()),
            DMA((ns, nsub)), DMA((ns, nsub)), DMA((ns, nsub)), DMA((ns, nsub)),
        ],
        compiler_params=pltpu.CompilerParams(
            collective_id=cid, has_side_effects=True, vmem_limit_bytes=56 * 2**20),
        name="home",
    )(g, small, gm)
    return f, so, out.reshape(length // ns, width)


def start_kernel(nd, ns, nsub, hid, win, wout, pack, mask, emb, modw, modb,
                 hid_o, wx_o, pack_o, mask_o, mod_o,
                 eland, prod, rowp, land1, land2,
                 su, ru, sd, rd, swz, rw, swp, swm, spz, rp, spp, spm, sk, rk, se, re, s1, r1, s2, r2, own):
    d, q = lax.axis_index("dp"), lax.axis_index("seq")
    nc = nd // 2
    chip, core = d // 2, lax.rem(d, 2)
    mate = (chip * 2 + 1 - core, q)
    chips = [lax.rem(chip + k, nc) for k in range(1, nc)]
    others = [lax.rem(q + k, ns) for k in range(1, ns)]
    peers = [lax.rem(d + k, nd) for k in range(1, nd)]
    spread = nd // ns
    me = d * ns + q
    part = wout.shape[1] // ns
    greet([(d, t) for t in others] + [(e, q) for e in peers])

    def column(ref, at):
        return ref.at[:, pl.ds(pl.multiple_of(at * part, 128), part)]

    def pieces(t):
        return (column(win, t), column(win, ns + t), column(wout, t))

    def across(k, t, idx):
        return [
            send(src, wx_o.at[idx, :, j * part:(j + 1) * part], swz.at[k, j], rw.at[idx, j], (d, t))
            for j, src in enumerate(pieces(t))
        ]

    for k, t in enumerate(others):
        for copy in across(k, t, me):
            copy.start()
    keep = [pltpu.make_async_copy(src, wx_o.at[me, :, j * part:(j + 1) * part], own.at[j])
            for j, src in enumerate(pieces(q))]
    keep.append(pltpu.make_async_copy(hid, hid_o.at[q], own.at[3]))
    for copy in keep:
        copy.start()

    plane = d // spread
    slot = lax.rem(d, spread) * ns + q
    pack_z = send(pack, pack_o.at[slot], spz, rp.at[slot], (d, plane))
    pack_own = pltpu.make_async_copy(pack, pack_o.at[slot], own.at[4])

    @pl.when(plane == q)
    def _():
        pack_own.start()

    @pl.when(plane != q)
    def _():
        pack_z.start()

    def masks(k, t, src):
        return send(mask_o.at[src], mask_o.at[src], sk.at[k], rk.at[src], (d, t))

    def embeds(k, e, src):
        return send(eland.at[src], eland.at[src], se.at[k], re.at[src], (e, q))

    mask_o[q] = mask[...]
    eland[d] = emb[...]
    for k, e in enumerate(peers):
        embeds(k, e, d).start()
    for k, t in enumerate(others):
        masks(k, t, q).start()

    def rise(k, s):
        t = jnp.maximum(q - k, 0)
        src = hid.at[s] if k == 0 else hid_o.at[t, s]
        return send(src, hid_o.at[t, s], su.at[k, s], ru.at[k, s], (d, q + 1))

    def sink(k, s):
        t = jnp.minimum(q + k, ns - 1)
        src = hid.at[s] if k == 0 else hid_o.at[t, s]
        return send(src, hid_o.at[t, s], sd.at[k, s], rd.at[k, s], (d, q - 1))

    def hop(k, s):
        @pl.when(q >= k)
        def _():
            if k:
                rise(k - 1, s).wait_recv()
            if k < ns - 1:
                @pl.when(q + 1 < ns)
                def _():
                    rise(k, s).start()

        @pl.when(q + k < ns)
        def _():
            if k:
                sink(k - 1, s).wait_recv()
            if k < ns - 1:
                @pl.when(q >= 1)
                def _():
                    sink(k, s).start()

    for s in range(nsub):
        hop(0, s)

    def piece(ref, idx):
        return ref.at[idx]

    def plane_w(c, idx, t):
        return send(wx_o.at[idx], wx_o.at[idx], swp.at[c, t], rwp_of(idx), (c * 2 + core, q))

    def rwp_of(idx):
        return rw.at[idx, 3]

    def mate_w(c, idx, t):
        return send(wx_o.at[idx], wx_o.at[idx], swm.at[c, t], rwp_of(idx), mate)

    def spread_w(t):
        idx = d * ns + t
        for c in chips:
            plane_w(c, idx, t).start()
        mate_w(chip, idx, t).start()

    for copy in keep[:3]:
        copy.wait()
    spread_w(q)

    for k, e in enumerate(peers):
        embeds(k, e, e).wait_recv()
    rows = modw.shape[0]
    here = lax.broadcasted_iota(jnp.int32, (FREQ, rows), 0)
    pick = here - lax.broadcasted_iota(jnp.int32, (FREQ, rows), 1)
    count = FREQ // (nd * ns)
    keep_col = lax.broadcasted_iota(jnp.int32, (FREQ, rows), 1) < count
    pick = jnp.where(jnp.logical_and(pick == me * count, keep_col), 1.0, 0.0).astype(BF)
    mine = jnp.dot(eland[...].reshape(nd * 16, FREQ), pick, preferred_element_type=F32).astype(BF)
    prod[...] = jnp.dot(mine, modw[...], preferred_element_type=F32)

    lines = prod.shape[1] // 128
    @pl.loop(0, nd)
    def _(e):
        rowp[e] = modb[...]
        for j in range(lines):
            rowp[e, j:j + 1, :] += prod[pl.ds(pl.multiple_of(e * 16, 16), 1), j * 128:(j + 1) * 128]

    def to_item(k, e, src):
        return send(rowp.at[e], land1.at[src], s1.at[k], r1.at[src], (e, q))

    for k, e in enumerate(peers):
        to_item(k, e, d).start()

    for k, t in enumerate(others):
        for copy in across(k, t, d * ns + t):
            copy.wait_recv()
        spread_w(t)

    def plane_p(c, i, t):
        return send(pack_o.at[i], pack_o.at[i], spp.at[c, t], rp.at[i], (c * 2 + core, q))

    def mate_p(c, i, t):
        return send(pack_o.at[i], pack_o.at[i], spm.at[c, t], rp.at[i], mate)

    base = lax.rem(d, spread) * ns

    @pl.when(plane == q)
    def _():
        pack_own.wait()
        for t in others:
            send(pack, pack_o.at[base + t], spz, rp.at[base + t], (d, plane)).wait_recv()
        for t in range(ns):
            for c in chips:
                plane_p(c, base + t, t).start()
            mate_p(chip, base + t, t).start()

    total = rowp[d]
    for k, e in enumerate(peers):
        to_item(k, e, e).wait_recv()
        total = total + land1[e]
    land2[q] = total

    def to_column(k, t, src):
        return send(land2.at[src], land2.at[src], s2.at[k], r2.at[src], (d, t))

    for k, t in enumerate(others):
        to_column(k, t, q).start()

    def relay_w(c, t):
        idx = (c * 2 + core) * ns + t
        plane_w(c, idx, t).wait_recv()
        mate_w(c, idx, t).start()

    def holds(c):
        return (c * 2 + core) // spread == q

    def relay_p(c):
        first = lax.rem(c * 2 + core, spread) * ns
        @pl.when(holds(c))
        def _():
            for t in range(ns):
                plane_p(c, first + t, t).wait_recv()
                mate_p(c, first + t, t).start()

    hops = [(k, s) for k in range(1, ns) for s in range(nsub)]
    relays = [(c, t) for t in [q] + others for c in chips]
    at = 0
    for i, (k, s) in enumerate(hops):
        upto = len(relays) * (i + 1) // len(hops)
        hop(k, s)
        for c, t in relays[at:upto]:
            relay_w(c, t)
        at = upto
    for c in chips:
        relay_p(c)
    for k, t in enumerate(others):
        to_column(k, t, t).wait_recv()
    total = land2[0]
    for t in range(1, ns):
        total = total + land2[t]
    mod_o[...] = total

    twin = 1 - core
    for c in range(nc):
        for t in range(ns):
            idx = (c * 2 + twin) * ns + t
            mate_w(c, idx, t).wait_recv()
        first = lax.rem(c * 2 + twin, spread) * ns
        @pl.when((c * 2 + twin) // spread == q)
        def _():
            for t in range(ns):
                mate_p(c, first + t, t).wait_recv()
    for k, t in enumerate(others):
        masks(k, t, t).wait_recv()
    keep[3].wait()

    for k, t in enumerate(others):
        for copy in across(k, t, me):
            copy.wait_send()
        masks(k, t, q).wait_send()
        to_column(k, t, q).wait_send()
    for k, e in enumerate(peers):
        embeds(k, e, d).wait_send()
        to_item(k, e, d).wait_send()

    @pl.when(plane != q)
    def _():
        pack_z.wait_send()

    @pl.when(plane == q)
    def _():
        for t in range(ns):
            for c in chips:
                plane_p(c, base + t, t).wait_send()
            mate_p(chip, base + t, t).wait_send()

    for t in range(ns):
        for c in chips:
            plane_w(c, d * ns + t, t).wait_send()
            mate_w(c, (c * 2 + core) * ns + t, t).wait_send()
        mate_w(chip, d * ns + t, t).wait_send()
    for c in chips:
        first = lax.rem(c * 2 + core, spread) * ns
        @pl.when(holds(c))
        def _():
            for t in range(ns):
                mate_p(c, first + t, t).wait_send()
    for k in range(ns - 1):
        for s in range(nsub):
            @pl.when(jnp.logical_and(q >= k, q + 1 < ns))
            def _():
                rise(k, s).wait_send()
            @pl.when(jnp.logical_and(q + k < ns, q >= 1))
            def _():
                sink(k, s).wait_send()


def start(hidden, mask, win, wout, pack, embedded, modw, modb, nd, ns, cid):
    nsub = 4
    length, width = hidden.shape
    rows, inner = wout.shape
    nc = nd // 2
    hidden = hidden.reshape(nsub, length // nsub, width)
    lines = modb.shape
    return pl.pallas_call(
        functools.partial(start_kernel, nd, ns, nsub),
        out_shape=[
            jax.ShapeDtypeStruct((ns,) + hidden.shape, BF),
            jax.ShapeDtypeStruct((nd * ns, rows, 3 * inner // ns), BF),
            jax.ShapeDtypeStruct((nd,) + pack.shape, BF),
            jax.ShapeDtypeStruct((ns,) + mask.shape, BF),
            jax.ShapeDtypeStruct(lines, F32),
        ],
        in_specs=[HBM, HBM, HBM, HBM, VMEM, VMEM, VMEM, VMEM],
        out_specs=[HBM, HBM, HBM, VMEM, VMEM],
        scratch_shapes=[
            pltpu.VMEM((nd,) + embedded.shape, BF), pltpu.VMEM((nd * 16, modw.shape[1]), F32),
            pltpu.VMEM((nd,) + lines, F32), pltpu.VMEM((nd,) + lines, F32), pltpu.VMEM((ns,) + lines, F32),
            DMA((ns - 1, nsub)), DMA((ns - 1, nsub)), DMA((ns - 1, nsub)), DMA((ns - 1, nsub)),
            DMA((ns, 3)), DMA((nd * ns, 4)), DMA((nc, ns)), DMA((nc, ns)),
            DMA(()), DMA((nd,)), DMA((nc, ns)), DMA((nc, ns)),
            DMA((ns,)), DMA((ns,)), DMA((nd,)), DMA((nd,)),
            DMA((nd,)), DMA((nd,)), DMA((ns,)), DMA((ns,)), DMA((5,)),
        ],
        compiler_params=pltpu.CompilerParams(
            collective_id=cid, has_side_effects=True, vmem_limit_bytes=40 * 2**20),
        name="start",
    )(hidden, win, wout, pack, mask, embedded, modw, modb)


def frequency_embed(timestep):
    half_width = FREQ // 2
    counter = jnp.arange(half_width, dtype=F32)
    frequency = jnp.exp(counter * (-math.log(10000.0) / half_width))
    angles = timestep.astype(F32)[:, None] * frequency[None, :]
    return jnp.concatenate([jnp.cos(angles), jnp.sin(angles)], axis=1)


def dot(a, b):
    return jnp.dot(a, b, preferred_element_type=F32)


def dot_nt(a, b):
    return lax.dot_general(a, b, (((1,), (1,)), ((), ())), preferred_element_type=F32)


def dot_tn(a, b):
    return lax.dot_general(a, b, (((0,), (0,)), ((), ())), preferred_element_type=F32)


def body(
    hidden,
    pad_mask,
    timestep,
    input_weight,
    select_weight,
    step_weight,
    output_weight,
    decay_forward,
    decay_reverse,
    filter_weight,
    filter_bias,
    step_bias,
    modulation_weight,
    modulation_bias,
    cotangent,
):
    ns, nd = lax.axis_size("seq"), lax.axis_size("dp")
    q, d = lax.axis_index("seq"), lax.axis_index("dp")
    every = ("dp", "seq")
    local_len, width = hidden.shape[1:]
    length = local_len * ns
    inner = output_weight.shape[0]
    part = inner // ns
    rank = step_weight.shape[0]
    state = decay_forward.shape[1]
    taps = filter_weight.shape[0]
    rows_in = input_weight.shape[0]
    lanes = select_weight.shape[1]

    units = part // nd
    embedded = jax.nn.silu(frequency_embed(timestep)).astype(BF)
    fil = jnp.concatenate([filter_weight, filter_bias[None], step_bias[None]])
    fil = jnp.pad(fil, ((0, 16 - fil.shape[0]), (0, lanes - units)))
    mid = jnp.concatenate([step_weight.T, decay_forward, decay_reverse], axis=1)
    pack = jnp.concatenate([select_weight, mid, fil])
    mask = jnp.pad(pad_mask[0].astype(BF).reshape(-1, 128), ((0, 16 - local_len // 128), (0, 0)))
    shard = (-modulation_weight.shape[0] % 16, 0)
    modb = jnp.zeros((-(-3 * width // 1024) * 1024,), F32)
    modb = lax.dynamic_update_slice(modb, modulation_bias.astype(F32), ((d * ns + q) * modulation_bias.shape[0],))
    row_pad = ((0, -rows_in % 16), (0, 0))
    hid, wx, pack, mask, modulation = start(
        hidden[0], mask, jnp.pad(input_weight, row_pad), jnp.pad(output_weight.T, row_pad), pack,
        jnp.pad(embedded, ((0, 15), (0, 0))),
        jnp.pad(modulation_weight, ((0, shard[0]), (0, 0))), modb.reshape(-1, 128), nd, ns, 4)
    hid = hid.reshape(length, width)
    wx = wx[:, :rows_in].reshape(width, 3 * part)
    win, wout = wx[:, : 2 * part], wx[:, 2 * part :]
    mask = mask[:, : local_len // 128].reshape(length, 1).astype(F32)
    select_q = pack[:, :units].reshape(part, lanes)
    mid = pack[:, units : 2 * units].reshape(part, lanes)
    step_q = mid[:, :rank].T
    log_f, log_r = mid[:, rank : rank + state], mid[:, rank + state :]
    fil = pack[:, 2 * units :, :units].transpose(1, 0, 2).reshape(16, part).astype(F32)
    filt32, fbias, sbias = fil[:taps].T, fil[taps][None], fil[taps + 1][None]
    modulation = modulation.reshape(1, -1)[:, : 3 * width]
    shifts = modulation[:, :width]
    scales = modulation[:, width : 2 * width]
    gate_scale = modulation[:, 2 * width :]

    def norm(x):
        x = x.astype(F32)
        centered = x - jnp.mean(x, axis=1, keepdims=True)
        inverse = lax.rsqrt(jnp.mean(centered * centered, axis=1, keepdims=True) + EPS)
        return centered * inverse, inverse

    modded = (norm(hid)[0] * (1.0 + scales) + shifts).astype(BF)
    projected = dot(modded, win)
    inner_part = projected[:, :part].astype(BF).astype(F32) * mask
    gate_branch = projected[:, part:]
    padded = jnp.pad(inner_part, ((taps - 1, 0), (0, 0)))
    filtered = fbias
    for k in range(taps):
        filtered = filtered + filt32[:, k][None, :] * padded[k : k + length]
    sigma_filter = jax.nn.sigmoid(filtered)
    active = (filtered * sigma_filter).astype(BF)
    active32 = active.astype(F32)
    selected = column_sum(dot(active, select_q), ns, BF, 0)
    cot, selected = lax.optimization_barrier((cotangent[0], selected))
    cot = lax.all_gather(cot, "seq", axis=0, tiled=True)
    low_rank = selected[:, :rank].astype(BF)
    b_rows = selected[:, rank : rank + state].astype(F32)
    c_rows = selected[:, rank + state :].astype(F32)
    pre_steps = dot(low_rank, step_q) + sbias
    steps = jax.nn.softplus(pre_steps)
    rates_f = -jnp.exp(log_f.astype(F32)).T
    rates_r = -jnp.exp(log_r.astype(F32)).T
    drive = steps * active32
    rates_f2, rates_r2 = rates_f * LOG2E, rates_r * LOG2E
    mixed_f, mixed_r, states_f, states_r = fwd_scan(steps, drive, rates_f2, rates_r2, b_rows.T, blockdiag(c_rows))
    merged = mixed_f + mixed_r
    sigma_gate = jax.nn.sigmoid(gate_branch)
    silu_gate = gate_branch * sigma_gate
    gated = (merged * silu_gate).astype(BF)
    branch = lax.psum_scatter(dot_nt(gated, wout), "seq", scatter_dimension=0, tiled=True)

    mask_here = pad_mask[0].astype(F32)[:, None]
    cot_here = cotangent[0].astype(F32)
    block_out = (hidden[0].astype(F32) + gate_scale * mask_here * branch).astype(BF)
    grad_gate = jnp.sum(mask_here * cot_here * branch, axis=0)

    grad_branch = (cot.astype(F32) * gate_scale * mask).astype(BF)
    grad_gated = dot(grad_branch, wout)
    grad_merged = grad_gated * silu_gate
    grad_gate_branch = grad_gated * merged * sigma_gate * (1.0 + gate_branch * (1.0 - sigma_gate))
    dlog_f, dlog_r, adjb_f, adjb_r, bg_f, bg_r, cg_f, cg_r, rg_f, rg_r = bwd_scan(
        steps, drive.astype(BF), grad_merged, rates_f2, rates_r2, c_rows.T, blockdiag(b_rows), states_f, states_r)
    adjb = adjb_f + adjb_r
    grad_steps = (dlog_f + dlog_r) * (1.0 / LOG2E) + active32 * adjb
    grad_b = (bg_f + bg_r).reshape(length, state)
    grad_c = (cg_f + cg_r).reshape(length, state)
    grad_decay_f = rg_f * rates_f
    grad_decay_r = rg_r * rates_r
    grad_pre = grad_steps * jax.nn.sigmoid(pre_steps)
    grad_step_bias = jnp.sum(grad_pre, axis=0)
    grad_pre_low = grad_pre.astype(BF)
    grad_step_t = dot_tn(grad_pre_low, low_rank)
    grad_low_rank = dot_nt(grad_pre_low, step_q)
    grad_selected = column_sum(jnp.concatenate([grad_low_rank, grad_b, grad_c], axis=1), ns, BF, 1)
    grad_select = dot_tn(active, grad_selected)
    grad_active = steps * adjb + dot_nt(grad_selected, select_q)
    grad_filtered = grad_active * sigma_filter * (1.0 + filtered * (1.0 - sigma_filter))
    extended = jnp.pad(grad_filtered, ((0, taps - 1), (0, 0)))
    grad_inner = jnp.zeros_like(grad_filtered)
    filter_rows = []
    for k in range(taps):
        lead = taps - 1 - k
        grad_inner = grad_inner + filt32[:, k][None, :] * extended[lead : lead + length]
        filter_rows.append(jnp.sum(grad_filtered * padded[k : k + length], axis=0))
    grad_filter_bias = jnp.sum(grad_filtered, axis=0)
    grad_projected = jnp.concatenate([grad_inner * mask, grad_gate_branch], axis=1).astype(BF)
    fil = jnp.stack(filter_rows + [grad_filter_bias, grad_step_bias])
    fil = fil.reshape(-1, nd, units).transpose(1, 0, 2)
    fil = jnp.pad(fil, ((0, 0), (0, 16 - fil.shape[1]), (0, lanes - units)))
    mid = jnp.concatenate([grad_step_t, grad_decay_f.T, grad_decay_r.T], axis=1)
    small = jnp.concatenate([grad_select.reshape(nd, units, lanes), mid.reshape(nd, units, lanes), fil], axis=1)
    grads = jnp.concatenate([dot_tn(modded, grad_projected), dot_tn(grad_branch, gated)], axis=1)
    grads = grads.astype(BF).reshape(nd, ns, rows_in, 3 * part)
    grads = jnp.pad(grads, ((0, 0), (0, 0), (0, -rows_in % 16), (0, 0)))
    grads, small, grad_modded = home(grads, small, dot_nt(grad_projected, win).astype(BF), nd, ns, 2)
    grads = grads[:, :rows_in].astype(F32)
    g_in = grads[:, :, : 2 * part].reshape(ns, rows_in, 2, part).transpose(1, 2, 0, 3).reshape(rows_in, 2 * inner)
    g_out = grads[:, :, 2 * part :].transpose(1, 0, 2).reshape(rows_in, inner).T
    gs_select = small[:units]
    mid = small[units : 2 * units]
    gs_step, gs_f, gs_r = mid[:, :rank], mid[:, rank : rank + state], mid[:, rank + state :]
    fil = small[2 * units :, :units]

    normed, inverse = norm(hidden[0])
    grad_shifts = jnp.sum(grad_modded, axis=0)
    grad_scales = jnp.sum(grad_modded * normed, axis=0)
    grad_normed = grad_modded * (1.0 + scales)
    grad_hidden = cot_here + inverse * (
        grad_normed
        - jnp.mean(grad_normed, axis=1, keepdims=True)
        - normed * jnp.mean(grad_normed * normed, axis=1, keepdims=True)
    )

    grad_mod = jnp.concatenate([grad_shifts, grad_scales, grad_gate, embedded[0].astype(F32) / ns])
    grad_mod = jnp.pad(grad_mod, (0, -grad_mod.shape[0] % 1024)).reshape(-1, 128)
    grad_mod = mod_gather(grad_mod, nd, ns, 3).reshape(nd, -1)
    embeds = grad_mod[:, 3 * width : 3 * width + FREQ]
    grad_mod = grad_mod[:, : 3 * width]
    me = d * ns + q
    mine = lax.dynamic_slice_in_dim(embeds, me * modulation_weight.shape[0], modulation_weight.shape[0], 1)
    g_modw = lax.dot_general(mine, grad_mod, (((0,), (0,)), ((), ())), precision=HIGHEST)
    g_modb = lax.dynamic_slice_in_dim(
        jnp.sum(grad_mod, axis=0), me * modulation_bias.shape[0], modulation_bias.shape[0], 0)
    return (
        block_out[None],
        grad_hidden.astype(BF)[None],
        g_in,
        gs_select,
        gs_step.T,
        g_out,
        gs_f,
        gs_r,
        fil[:taps],
        fil[taps],
        fil[taps + 1],
        g_modw,
        g_modb,
    )


def solution(mesh):
    return jax.shard_map(
        body,
        mesh=mesh,
        in_specs=(
            P("dp", "seq", None),
            P("dp", "seq"),
            P("dp"),
            P(("dp", "seq"), None),
            P(("dp", "seq"), None),
            P(None, ("dp", "seq")),
            P(None, ("dp", "seq")),
            P(("dp", "seq"), None),
            P(("dp", "seq"), None),
            P(None, ("dp", "seq")),
            P(("dp", "seq")),
            P(("dp", "seq")),
            P(("dp", "seq"), None),
            P(("dp", "seq")),
            P("dp", "seq", None),
        ),
        out_specs=(
            P("dp", "seq", None),
            P("dp", "seq", None),
            P(("dp", "seq"), None),
            P(("dp", "seq"), None),
            P(None, ("dp", "seq")),
            P(None, ("dp", "seq")),
            P(("dp", "seq"), None),
            P(("dp", "seq"), None),
            P(None, ("dp", "seq")),
            P(("dp", "seq")),
            P(("dp", "seq")),
            P(("dp", "seq"), None),
            P(("dp", "seq")),
        ),
        check_vma=False,
    )
```

```python
import functools
import math

import jax
import jax.numpy as jnp
from jax import lax
from jax.experimental import pallas as pl
from jax.experimental.pallas import tpu as pltpu
from jax.sharding import PartitionSpec as P

FREQ = 256
EPS = 1e-06
HIGHEST = lax.Precision.HIGHEST
LOG2E = 1.4426950408889634
SUB = 16
WF = 384
WB = 768
F32, BF = jnp.float32, jnp.bfloat16
NT = (((1,), (1,)), ((), ()))


def columns_of(rows_t, base):
    turned = pltpu.roll(rows_t, rows_t.shape[1] - base, 1)
    return [jnp.broadcast_to(turned[:, j:j + 1], (rows_t.shape[0], 128)) for j in range(SUB)]


def wide(block, lanes):
    return jnp.concatenate([block] * (lanes // 128), axis=1) if lanes > 128 else block


def states_of(base, at):
    return pl.ds(pl.multiple_of((base + at) * 16, 16), 16)


def fwd_kernel(step_f, step_r, u_f, u_r, rate_f, rate_r, bt_f, bt_r, cblk_f, cblk_r,
               y_f, y_r, s_f, s_r, carry, f0, f1, r0, r1):
    rows, lanes = step_f.shape

    @pl.when(pl.program_id(0) == 0)
    def _():
        carry[...] = jnp.zeros(carry.shape, F32)

    wide_by = min(WF, lanes)
    cuts = [slice(c, c + wide_by) for c in range(0, lanes, wide_by)]

    def walk(states, bases, kept):
        cols = [columns_of(bt[...], base) for bt, base in zip((bt_f, bt_r), bases)]
        out = []
        for cut, pair in zip(cuts, states):
            pair = list(pair)
            rates = rate_f[:, cut], rate_r[:, cut]
            for k in range(SUB):
                for z, (step, u, s, j) in enumerate(((step_f, u_f, s_f, k), (step_r, u_r, s_r, SUB - 1 - k))):
                    at = pl.ds(bases[z] + j, 1)
                    decay = jnp.exp2(step[at, cut] * rates[z])
                    pair[z] = decay * pair[z] + u[at, cut] * wide(cols[z][j], wide_by)
                    low = pair[z].astype(BF)
                    s[states_of(bases[z], j), cut] = low
                    kept[z][j * 16:(j + 1) * 16, cut] = low
            out.append(tuple(pair))
        return tuple(out)

    def mix(base, cblk, kept, y):
        here = pl.ds(base, SUB)
        y[here, :] = jnp.dot(cblk[here, :], kept[...], preferred_element_type=F32)

    def start_of(a, flip):
        a = jnp.maximum(a, 0)
        return pl.multiple_of(rows - SUB - a * SUB if flip else a * SUB, SUB)

    def two(i, states):
        for half, (fk, rk, fp, rp) in enumerate(((f0, r0, f1, r1), (f1, r1, f0, r0))):
            a = 2 * i + half
            mix(start_of(a - 1, False), cblk_f, fp, y_f)
            mix(start_of(a - 1, True), cblk_r, rp, y_r)
            states = walk(states, (start_of(a, False), start_of(a, True)), (fk, rk))
        return states

    states = tuple((carry[0, :, cut], carry[1, :, cut]) for cut in cuts)
    states = lax.fori_loop(0, rows // SUB // 2, two, states)
    mix(rows - SUB, cblk_f, f1, y_f)
    mix(0, cblk_r, r1, y_r)
    for cut, pair in zip(cuts, states):
        carry[0, :, cut], carry[1, :, cut] = pair


def fwd_scan(steps, u, rates_f, rates_r, b_t, cblk, tile=128):
    length, lanes = steps.shape
    blocks = length // tile
    specs = []
    for order in (lambda t: t, lambda t: blocks - 1 - t):
        specs.append((
            pl.BlockSpec((tile, lanes), lambda t, order=order: (order(t), 0)),
            pl.BlockSpec((16, lanes), lambda t: (0, 0)),
            pl.BlockSpec((16, tile), lambda t, order=order: (0, order(t))),
            pl.BlockSpec((tile, 256), lambda t, order=order: (order(t), 0)),
            pl.BlockSpec((tile * 16, lanes), lambda t, order=order: (order(t), 0)),
        ))
    (row_f, rate, bt_f, blk_f, s_f), (row_r, _, bt_r, blk_r, s_r) = specs
    y = jax.ShapeDtypeStruct((length, lanes), F32)
    s = jax.ShapeDtypeStruct((length * 16, lanes), BF)
    kept = pltpu.VMEM((256, lanes), BF)
    return pl.pallas_call(
        fwd_kernel,
        grid=(blocks,),
        in_specs=[row_f, row_r, row_f, row_r, rate, rate, bt_f, bt_r, blk_f, blk_r],
        out_specs=[row_f, row_r, s_f, s_r],
        out_shape=[y, y, s, s],
        scratch_shapes=[pltpu.VMEM((2, 16, lanes), F32), kept, kept, kept, kept],
        compiler_params=pltpu.CompilerParams(vmem_limit_bytes=56 * 2**20, dimension_semantics=("arbitrary",)),
        cost_estimate=pl.CostEstimate(flops=length * lanes * 16 * 16, transcendentals=0, bytes_accessed=length * lanes * 80),
        name="fwd_scan",
    )(steps, steps, u, u, rates_f, rates_r, b_t, b_t, cblk, cblk)


def bwd_kernel(step_f, step_r, u_f, u_r, gy_f, gy_r, rate_f, rate_r, ct_f, ct_r, bblk_f, bblk_r, s_f, s_r, sp_f, sp_r,
               dlog_f, dlog_r, adjb_f, adjb_r, bg_f, bg_r, cg_f, cg_r, rg_f, rg_r, carry,
               af0, af1, ar0, ar1, lf0, lf1, lr0, lr1):
    rows, lanes = step_f.shape
    t = pl.program_id(0)
    last = pl.num_programs(0) - 1

    @pl.when(t == 0)
    def _():
        carry[...] = jnp.zeros(carry.shape, F32)
        rg_f[...] = jnp.zeros(rg_f.shape, F32)
        rg_r[...] = jnp.zeros(rg_r.shape, F32)

    ones = (lax.broadcasted_iota(jnp.int32, (SUB, 256), 0) == lax.broadcasted_iota(jnp.int32, (SUB, 256), 1) // 16)
    onesb = ones.astype(BF)
    zero = jnp.zeros((SUB, 256), F32)

    def start_of(a, down):
        a = jnp.maximum(a, 0)
        return pl.multiple_of(rows - SUB - a * SUB if down else a * SUB, SUB)

    wide_by = min(WB, lanes)
    cuts = [slice(c, c + wide_by) for c in range(0, lanes, wide_by)]

    def walk(states, bases, keep_a, keep_l):
        cols = [columns_of(ct[...], base) for ct, base in zip((ct_f, ct_r), bases)]
        out = []
        for cut, pair in zip(cuts, states):
            pair = list(pair)
            rates = rate_f[:, cut], rate_r[:, cut]
            rg = [rg_f[:, cut], rg_r[:, cut]]
            low_rates = [r.astype(BF) for r in rates]
            some = [[], []]
            for k in range(SUB):
                for z, (step, gy, s, sp, j) in enumerate((
                        (step_f, gy_f, s_f, sp_f, SUB - 1 - k), (step_r, gy_r, s_r, sp_r, k))):
                    at = pl.ds(bases[z] + j, 1)
                    row = step[at, cut]
                    adj = gy[at, cut] * wide(cols[z][j], wide_by) + pair[z]
                    pair[z] = jnp.exp2(row * rates[z]) * adj
                    before = bases[z] + (j + 1 if z else j - 1)
                    if k < SUB - 1:
                        inner = s[pl.ds(pl.multiple_of(before * 16, 16), 16), cut]
                    else:
                        inside = before < rows if z else before >= 0
                        safe = jnp.clip(before, 0, rows - 1)
                        inner = s[pl.ds(pl.multiple_of(safe * 16, 16), 16), cut]
                        outer = jnp.where(t == last, jnp.zeros_like(inner), sp[:, cut])
                        inner = jnp.where(inside, inner, outer)
                    grad = pair[z].astype(BF) * inner
                    keep_a[z][j * 16:(j + 1) * 16, cut] = adj.astype(BF)
                    keep_l[z][j * 16:(j + 1) * 16, cut] = grad * low_rates[z]
                    some[z].append(grad * jnp.broadcast_to(row, (16, wide_by)).astype(BF))
                    if len(some[z]) == 4:
                        rg[z] = rg[z] + ((some[z][0] + some[z][1]) + (some[z][2] + some[z][3])).astype(F32)
                        some[z] = []
            rg_f[:, cut], rg_r[:, cut] = rg
            out.append(tuple(pair))
        return tuple(out)

    def mix(base, a_ref, l_ref, u, gy, bblk, s, dlog, adjb, bg, cg):
        here = pl.ds(base, SUB)
        line = pl.ds(base // SUB, 1)
        a = a_ref[...]
        dlog[here, :] = jnp.dot(onesb, l_ref[...], preferred_element_type=F32)
        adjb[here, :] = jnp.dot(bblk[here, :], a, preferred_element_type=F32)
        bgd = lax.dot_general(u[here, :], a, NT, preferred_element_type=F32)
        block = s[pl.ds(pl.multiple_of(base * 16, 256), 256), :]
        cgd = lax.dot_general(gy[here, :].astype(BF), block, NT, preferred_element_type=F32)
        bg[line, :] = jnp.sum(jnp.where(ones, bgd, zero), axis=0, keepdims=True)
        cg[line, :] = jnp.sum(jnp.where(ones, cgd, zero), axis=0, keepdims=True)

    def mix_f(base, a_ref, l_ref):
        mix(base, a_ref, l_ref, u_f, gy_f, bblk_f, s_f, dlog_f, adjb_f, bg_f, cg_f)

    def mix_r(base, a_ref, l_ref):
        mix(base, a_ref, l_ref, u_r, gy_r, bblk_r, s_r, dlog_r, adjb_r, bg_r, cg_r)

    def two(i, states):
        bufs = ((af0, lf0, ar0, lr0), (af1, lf1, ar1, lr1))
        for half in range(2):
            a = 2 * i + half
            naf, nlf, nar, nlr = bufs[half]
            paf, plf, par, plr = bufs[1 - half]
            mix_f(start_of(a - 1, True), paf, plf)
            mix_r(start_of(a - 1, False), par, plr)
            states = walk(states, (start_of(a, True), start_of(a, False)), (naf, nar), (nlf, nlr))
        return states

    states = tuple((carry[0, :, cut], carry[1, :, cut]) for cut in cuts)
    states = lax.fori_loop(0, rows // SUB // 2, two, states)
    mix_f(0, af1, lf1)
    mix_r(rows - SUB, ar1, lr1)
    for cut, pair in zip(cuts, states):
        carry[0, :, cut], carry[1, :, cut] = pair


def bwd_scan(steps, u, gy, rates_f, rates_r, c_t, bblk, states_f, states_r, tile=128):
    length, lanes = steps.shape
    blocks = length // tile
    down = lambda t: blocks - 1 - t
    up = lambda t: t

    def specs(order, before):
        return (
            pl.BlockSpec((tile, lanes), lambda t: (order(t), 0)),
            pl.BlockSpec((16, lanes), lambda t: (0, 0)),
            pl.BlockSpec((16, tile), lambda t: (0, order(t))),
            pl.BlockSpec((tile, 256), lambda t: (order(t), 0)),
            pl.BlockSpec((tile * 16, lanes), lambda t: (order(t), 0)),
            pl.BlockSpec((16, lanes), lambda t: (before(t), 0)),
            pl.BlockSpec((tile // 16, 256), lambda t: (order(t), 0)),
        )

    row_f, rate, ct_f, blk_f, s_f, sp_f, diag_f = specs(down, lambda t: jnp.maximum((blocks - 1 - t) * tile - 1, 0))
    row_r, _, ct_r, blk_r, s_r, sp_r, diag_r = specs(up, lambda t: jnp.minimum((t + 1) * tile, length - 1))
    y = jax.ShapeDtypeStruct((length, lanes), F32)
    diag = jax.ShapeDtypeStruct((length // 16, 256), F32)
    rg = jax.ShapeDtypeStruct((16, lanes), F32)
    kept = pltpu.VMEM((256, lanes), BF)
    return pl.pallas_call(
        bwd_kernel,
        grid=(blocks,),
        in_specs=[row_f, row_r, row_f, row_r, row_f, row_r, rate, rate, ct_f, ct_r, blk_f, blk_r, s_f, s_r, sp_f, sp_r],
        out_specs=[row_f, row_r, row_f, row_r, diag_f, diag_r, diag_f, diag_r, rate, rate],
        out_shape=[y, y, y, y, diag, diag, diag, diag, rg, rg],
        scratch_shapes=[pltpu.VMEM((2, 16, lanes), F32)] + [kept] * 8,
        compiler_params=pltpu.CompilerParams(vmem_limit_bytes=56 * 2**20, dimension_semantics=("arbitrary",)),
        cost_estimate=pl.CostEstimate(flops=length * lanes * 16 * 48, transcendentals=0, bytes_accessed=length * lanes * 100),
        name="bwd_scan",
    )(steps, steps, u, u, gy, gy, rates_f, rates_r, c_t, c_t, bblk, bblk, states_f, states_r, states_f, states_r)


def blockdiag(rows):
    length = rows.shape[0]
    eye = (jnp.arange(length)[:, None] % 16) == (jnp.arange(256)[None, :] // 16)
    return jnp.where(eye, jnp.tile(rows, (1, 16)), 0).astype(BF)


MESH = pl.DeviceIdType.MESH
VMEM = pl.BlockSpec(memory_space=pltpu.VMEM)
HBM = pl.BlockSpec(memory_space=pl.ANY)
DMA = pltpu.SemaphoreType.DMA


def send(src, dst, out_sem, in_sem, to):
    return pltpu.make_async_remote_copy(
        src_ref=src, dst_ref=dst, send_sem=out_sem, recv_sem=in_sem, device_id=to, device_id_type=MESH)


def greet(devices):
    bar = pltpu.get_barrier_semaphore()
    for to in devices:
        pl.semaphore_signal(bar, inc=1, device_id=to, device_id_type=MESH)
    pl.semaphore_wait(bar, len(devices))


def column_sum_kernel(ns, p_ref, o_ref, land, s1, r1, s2, r2):
    d, q = lax.axis_index("dp"), lax.axis_index("seq")
    others = [lax.rem(q + k, ns) for k in range(1, ns)]
    greet([(d, t) for t in others])
    for k, t in enumerate(others):
        send(p_ref.at[t], land.at[q], s1.at[k], r1.at[q], (d, t)).start()
    total = p_ref[q].astype(F32)
    for k, t in enumerate(others):
        send(p_ref.at[t], land.at[t], s1.at[k], r1.at[t], (d, t)).wait_recv()
        total = total + land[t].astype(F32)
    o_ref[q] = total.astype(o_ref.dtype)
    for k, t in enumerate(others):
        send(o_ref.at[q], o_ref.at[q], s2.at[k], r2.at[q], (d, t)).start()
    for k, t in enumerate(others):
        send(o_ref.at[t], o_ref.at[t], s2.at[k], r2.at[t], (d, t)).wait_recv()
    for k, t in enumerate(others):
        send(p_ref.at[t], land.at[q], s1.at[k], r1.at[q], (d, t)).wait_send()
        send(o_ref.at[q], o_ref.at[q], s2.at[k], r2.at[q], (d, t)).wait_send()


def column_sum(partial, ns, out_dtype, cid):
    rows, lanes = partial.shape
    block = (ns, rows // ns, lanes)
    out = pl.pallas_call(
        functools.partial(column_sum_kernel, ns),
        out_shape=jax.ShapeDtypeStruct(block, out_dtype),
        in_specs=[VMEM], out_specs=VMEM,
        scratch_shapes=[pltpu.VMEM(block, partial.dtype), DMA((ns,)), DMA((ns,)), DMA((ns,)), DMA((ns,))],
        compiler_params=pltpu.CompilerParams(
            collective_id=cid, has_side_effects=True, vmem_limit_bytes=32 * 2**20),
        name="column_sum",
    )(partial.reshape(block))
    return out.reshape(rows, lanes)


def mod_gather_kernel(nd, ns, g_ref, o_ref, land, s1, r1, s2, r2):
    d, q = lax.axis_index("dp"), lax.axis_index("seq")
    others = [lax.rem(q + k, ns) for k in range(1, ns)]
    peers = [lax.rem(d + k, nd) for k in range(1, nd)]
    greet([(d, t) for t in others] + [(e, q) for e in peers])
    for k, t in enumerate(others):
        send(g_ref, land.at[q], s1.at[k], r1.at[q], (d, t)).start()
    total = g_ref[...]
    for k, t in enumerate(others):
        send(g_ref, land.at[t], s1.at[k], r1.at[t], (d, t)).wait_recv()
        total = total + land[t]
    o_ref[d] = total
    for k, e in enumerate(peers):
        send(o_ref.at[d], o_ref.at[d], s2.at[k], r2.at[d], (e, q)).start()
    for k, e in enumerate(peers):
        send(o_ref.at[e], o_ref.at[e], s2.at[k], r2.at[e], (e, q)).wait_recv()
    for k, t in enumerate(others):
        send(g_ref, land.at[q], s1.at[k], r1.at[q], (d, t)).wait_send()
    for k, e in enumerate(peers):
        send(o_ref.at[d], o_ref.at[d], s2.at[k], r2.at[d], (e, q)).wait_send()


def mod_gather(g, nd, ns, cid):
    rows, lanes = g.shape
    return pl.pallas_call(
        functools.partial(mod_gather_kernel, nd, ns),
        out_shape=jax.ShapeDtypeStruct((nd, rows, lanes), F32),
        in_specs=[VMEM], out_specs=VMEM,
        scratch_shapes=[pltpu.VMEM((ns, rows, lanes), F32), DMA((ns,)), DMA((ns,)), DMA((nd,)), DMA((nd,))],
        compiler_params=pltpu.CompilerParams(
            collective_id=cid, has_side_effects=True, vmem_limit_bytes=32 * 2**20),
        name="mod_gather",
    )(g)


def home_kernel(nd, ns, nsub, g_ref, sm_ref, gm_ref, f_ref, so_ref, out_ref,
                pair, plane, spair, splane, ssum, up, down,
                sa, ra, sb, rb, sc, rc, ta, ra2, tb, rb2, tc, rc2, su, ru, sd, rd):
    d, q = lax.axis_index("dp"), lax.axis_index("seq")
    nc = nd // 2
    chip, core = d // 2, lax.rem(d, 2)
    mate = chip * 2 + 1 - core
    chips = [lax.rem(chip + k, nc) for k in range(1, nc)]
    others = [lax.rem(q + k, ns) for k in range(1, ns)]
    spread = nd // ns
    final_to = (spread * q + d // ns, lax.rem(d, ns))
    mine = d * ns + q
    final_from = (lax.rem(mine, nd), mine // nd)
    stays = jnp.logical_and(final_to[0] == d, final_to[1] == q)
    bar = pltpu.get_barrier_semaphore()
    friends = [(mate, q)] + [(c * 2 + core, q) for c in chips] + [(d, t) for t in others]
    for to in friends:
        pl.semaphore_signal(bar, inc=1, device_id=to, device_id_type=MESH)
    @pl.when(jnp.logical_not(stays))
    def _():
        pl.semaphore_signal(bar, inc=1, device_id=final_from, device_id_type=MESH)
        pl.semaphore_wait(bar, len(friends) + 1)
    @pl.when(stays)
    def _():
        pl.semaphore_wait(bar, len(friends))

    def first(c):
        return send(g_ref.at[c * 2 + 1 - core], pair.at[c], sa.at[c], ra.at[c], (mate, q))

    def first_small(c):
        return send(sm_ref.at[c * 2 + 1 - core], spair.at[c], ta.at[c], ra2.at[c], (mate, q))

    order = chips + [chip]
    for c in order:
        first(c).start()
        first_small(c).start()

    def rise(t, s, src):
        return send(src, up.at[t, s], su.at[t, s], ru.at[t, s], (d, q + 1))

    def sink(t, s, src):
        return send(src, down.at[t, s], sd.at[t, s], rd.at[t, s], (d, q - 1))

    def added(land, t, s):
        land[t, s] = (land[t, s].astype(F32) + gm_ref[t, s].astype(F32)).astype(BF)

    def step_up(t, s):
        @pl.when(q < t)
        def _():
            @pl.when(q == 0)
            def _():
                rise(t, s, gm_ref.at[t, s]).start()
            @pl.when(q > 0)
            def _():
                rise(t, s, up.at[t, s]).wait_recv()
                added(up, t, s)
                rise(t, s, up.at[t, s]).start()

    def step_down(t, s):
        @pl.when(q > t)
        def _():
            @pl.when(q == ns - 1)
            def _():
                sink(t, s, gm_ref.at[t, s]).start()
            @pl.when(q < ns - 1)
            def _():
                sink(t, s, down.at[t, s]).wait_recv()
                added(down, t, s)
                sink(t, s, down.at[t, s]).start()

    steps = [(k, s) for k in range(ns - 1) for s in range(nsub)]
    middle = len(steps) * 2 // 3

    def walk(some):
        for k, s in some:
            step_up(ns - 1 - k, s)
            step_down(k, s)

    def second(c, src):
        return send(pair.at[c], plane.at[src], sb.at[c], rb.at[src], (c * 2 + core, q))

    def second_small(c, src):
        return send(spair.at[c], splane.at[src], tb.at[c], rb2.at[src], (c * 2 + core, q))

    walk(steps[:1])
    for c in order:
        first(c).wait_recv()
        @pl.loop(0, ns)
        def _(t):
            pair[c, t] = (pair[c, t].astype(F32) + g_ref[c * 2 + core, t].astype(F32)).astype(BF)
        first_small(c).wait_recv()
        spair[c] = spair[c] + sm_ref[c * 2 + core]
        if c is not chip:
            second(c, chip).start()
            second_small(c, chip).start()
    walk(steps[1:middle])

    for c in chips:
        second(c, c).wait_recv()
        second_small(c, c).wait_recv()
    @pl.loop(0, ns)
    def _(t):
        total = pair[chip, t].astype(F32)
        for c in chips:
            total = total + plane[c, t].astype(F32)
        pair[chip, t] = total.astype(BF)
    small = spair[chip]
    for c in chips:
        small = small + splane[c]
    ssum[...] = small

    def third(t, src):
        return send(pair.at[chip, t], f_ref.at[src], sc.at[t], rc.at[src], (d, t))

    last = send(ssum, so_ref, tc, rc2, final_to)
    @pl.when(stays)
    def _():
        so_ref[...] = ssum[...]
    @pl.when(jnp.logical_not(stays))
    def _():
        last.start()
    for t in others:
        third(t, q).start()
    f_ref[q] = pair[chip, q]
    walk(steps[middle:])

    for s in range(nsub):
        total = gm_ref[q, s].astype(F32)
        out_ref[s] = total
        @pl.when(q > 0)
        def _():
            rise(q, s, gm_ref.at[q, s]).wait_recv()
            out_ref[s] += up[q, s].astype(F32)
        @pl.when(q < ns - 1)
        def _():
            sink(q, s, gm_ref.at[q, s]).wait_recv()
            out_ref[s] += down[q, s].astype(F32)
    for t in others:
        third(t, t).wait_recv()
    @pl.when(jnp.logical_not(stays))
    def _():
        last.wait_recv()
        last.wait_send()
    for c in order:
        first(c).wait_send()
        first_small(c).wait_send()
    for c in chips:
        second(c, chip).wait_send()
        second_small(c, chip).wait_send()
    for t in others:
        third(t, q).wait_send()
    for k, s in steps:
        t = ns - 1 - k
        @pl.when(q < t)
        def _():
            rise(t, s, gm_ref.at[t, s]).wait_send()
        @pl.when(q > k)
        def _():
            sink(k, s, gm_ref.at[k, s]).wait_send()


def home(g, small, gm, nd, ns, cid):
    rows, cols = g.shape[2:]
    nc, nsub = nd // 2, 4
    length, width = gm.shape
    part = length // ns // nsub
    v = small.shape[1:]
    gm = gm.reshape(ns, nsub, part, width)
    f, so, out = pl.pallas_call(
        functools.partial(home_kernel, nd, ns, nsub),
        out_shape=[
            jax.ShapeDtypeStruct((ns, rows, cols), BF),
            jax.ShapeDtypeStruct(v, F32),
            jax.ShapeDtypeStruct((nsub, part, width), F32),
        ],
        in_specs=[VMEM] * 3, out_specs=[VMEM] * 3,
        scratch_shapes=[
            pltpu.VMEM((nc, ns, rows, cols), BF), pltpu.VMEM((nc, ns, rows, cols), BF),
            pltpu.VMEM((nc,) + v, F32), pltpu.VMEM((nc,) + v, F32), pltpu.VMEM(v, F32),
            pltpu.VMEM((ns, nsub, part, width), BF), pltpu.VMEM((ns, nsub, part, width), BF),
            DMA((nc,)), DMA((nc,)), DMA((nc,)), DMA((nc,)), DMA((ns,)), DMA((ns,)),
            DMA((nc,)), DMA((nc,)), DMA((nc,)), DMA((nc,)), DMA(()), DMA(()),
            DMA((ns, nsub)), DMA((ns, nsub)), DMA((ns, nsub)), DMA((ns, nsub)),
        ],
        compiler_params=pltpu.CompilerParams(
            collective_id=cid, has_side_effects=True, vmem_limit_bytes=56 * 2**20),
        name="home",
    )(g, small, gm)
    return f, so, out.reshape(length // ns, width)


def start_kernel(nd, ns, nsub, hid, win, wout, pack, mask, emb, modw, modb,
                 hid_o, wx_o, pack_o, mask_o, mod_o,
                 eland, prod, rowp, land1, land2,
                 su, ru, sd, rd, swz, rw, swp, swm, spz, rp, spp, spm, sk, rk, se, re, s1, r1, s2, r2, own):
    d, q = lax.axis_index("dp"), lax.axis_index("seq")
    nc = nd // 2
    chip, core = d // 2, lax.rem(d, 2)
    mate = (chip * 2 + 1 - core, q)
    chips = [lax.rem(chip + k, nc) for k in range(1, nc)]
    others = [lax.rem(q + k, ns) for k in range(1, ns)]
    peers = [lax.rem(d + k, nd) for k in range(1, nd)]
    spread = nd // ns
    me = d * ns + q
    part = wout.shape[1] // ns
    greet([(d, t) for t in others] + [(e, q) for e in peers])

    def column(ref, at):
        return ref.at[:, pl.ds(pl.multiple_of(at * part, 128), part)]

    def pieces(t):
        return (column(win, t), column(win, ns + t), column(wout, t))

    def across(k, t, idx):
        return [
            send(src, wx_o.at[idx, :, j * part:(j + 1) * part], swz.at[k, j], rw.at[idx, j], (d, t))
            for j, src in enumerate(pieces(t))
        ]

    for k, t in enumerate(others):
        for copy in across(k, t, me):
            copy.start()
    keep = [pltpu.make_async_copy(src, wx_o.at[me, :, j * part:(j + 1) * part], own.at[j])
            for j, src in enumerate(pieces(q))]
    keep.append(pltpu.make_async_copy(hid, hid_o.at[q], own.at[3]))
    for copy in keep:
        copy.start()

    plane = d // spread
    slot = lax.rem(d, spread) * ns + q
    pack_z = send(pack, pack_o.at[slot], spz, rp.at[slot], (d, plane))
    pack_own = pltpu.make_async_copy(pack, pack_o.at[slot], own.at[4])

    @pl.when(plane == q)
    def _():
        pack_own.start()

    @pl.when(plane != q)
    def _():
        pack_z.start()

    def masks(k, t, src):
        return send(mask_o.at[src], mask_o.at[src], sk.at[k], rk.at[src], (d, t))

    def embeds(k, e, src):
        return send(eland.at[src], eland.at[src], se.at[k], re.at[src], (e, q))

    mask_o[q] = mask[...]
    eland[d] = emb[...]
    for k, e in enumerate(peers):
        embeds(k, e, d).start()
    for k, t in enumerate(others):
        masks(k, t, q).start()

    def rise(k, s):
        t = jnp.maximum(q - k, 0)
        src = hid.at[s] if k == 0 else hid_o.at[t, s]
        return send(src, hid_o.at[t, s], su.at[k, s], ru.at[k, s], (d, q + 1))

    def sink(k, s):
        t = jnp.minimum(q + k, ns - 1)
        src = hid.at[s] if k == 0 else hid_o.at[t, s]
        return send(src, hid_o.at[t, s], sd.at[k, s], rd.at[k, s], (d, q - 1))

    def hop(k, s):
        @pl.when(q >= k)
        def _():
            if k:
                rise(k - 1, s).wait_recv()
            if k < ns - 1:
                @pl.when(q + 1 < ns)
                def _():
                    rise(k, s).start()

        @pl.when(q + k < ns)
        def _():
            if k:
                sink(k - 1, s).wait_recv()
            if k < ns - 1:
                @pl.when(q >= 1)
                def _():
                    sink(k, s).start()

    for s in range(nsub):
        hop(0, s)

    def piece(ref, idx):
        return ref.at[idx]

    def plane_w(c, idx, t):
        return send(wx_o.at[idx], wx_o.at[idx], swp.at[c, t], rwp_of(idx), (c * 2 + core, q))

    def rwp_of(idx):
        return rw.at[idx, 3]

    def mate_w(c, idx, t):
        return send(wx_o.at[idx], wx_o.at[idx], swm.at[c, t], rwp_of(idx), mate)

    def spread_w(t):
        idx = d * ns + t
        for c in chips:
            plane_w(c, idx, t).start()
        mate_w(chip, idx, t).start()

    for copy in keep[:3]:
        copy.wait()
    spread_w(q)

    for k, e in enumerate(peers):
        embeds(k, e, e).wait_recv()
    rows = modw.shape[0]
    here = lax.broadcasted_iota(jnp.int32, (FREQ, rows), 0)
    pick = here - lax.broadcasted_iota(jnp.int32, (FREQ, rows), 1)
    count = FREQ // (nd * ns)
    keep_col = lax.broadcasted_iota(jnp.int32, (FREQ, rows), 1) < count
    pick = jnp.where(jnp.logical_and(pick == me * count, keep_col), 1.0, 0.0).astype(BF)
    mine = jnp.dot(eland[...].reshape(nd * 16, FREQ), pick, preferred_element_type=F32).astype(BF)
    prod[...] = jnp.dot(mine, modw[...], preferred_element_type=F32)

    lines = prod.shape[1] // 128
    @pl.loop(0, nd)
    def _(e):
        rowp[e] = modb[...]
        for j in range(lines):
            rowp[e, j:j + 1, :] += prod[pl.ds(pl.multiple_of(e * 16, 16), 1), j * 128:(j + 1) * 128]

    def to_item(k, e, src):
        return send(rowp.at[e], land1.at[src], s1.at[k], r1.at[src], (e, q))

    for k, e in enumerate(peers):
        to_item(k, e, d).start()

    for k, t in enumerate(others):
        for copy in across(k, t, d * ns + t):
            copy.wait_recv()
        spread_w(t)

    def plane_p(c, i, t):
        return send(pack_o.at[i], pack_o.at[i], spp.at[c, t], rp.at[i], (c * 2 + core, q))

    def mate_p(c, i, t):
        return send(pack_o.at[i], pack_o.at[i], spm.at[c, t], rp.at[i], mate)

    base = lax.rem(d, spread) * ns

    @pl.when(plane == q)
    def _():
        pack_own.wait()
        for t in others:
            send(pack, pack_o.at[base + t], spz, rp.at[base + t], (d, plane)).wait_recv()
        for t in range(ns):
            for c in chips:
                plane_p(c, base + t, t).start()
            mate_p(chip, base + t, t).start()

    total = rowp[d]
    for k, e in enumerate(peers):
        to_item(k, e, e).wait_recv()
        total = total + land1[e]
    land2[q] = total

    def to_column(k, t, src):
        return send(land2.at[src], land2.at[src], s2.at[k], r2.at[src], (d, t))

    for k, t in enumerate(others):
        to_column(k, t, q).start()

    def relay_w(c, t):
        idx = (c * 2 + core) * ns + t
        plane_w(c, idx, t).wait_recv()
        mate_w(c, idx, t).start()

    def holds(c):
        return (c * 2 + core) // spread == q

    def relay_p(c):
        first = lax.rem(c * 2 + core, spread) * ns
        @pl.when(holds(c))
        def _():
            for t in range(ns):
                plane_p(c, first + t, t).wait_recv()
                mate_p(c, first + t, t).start()

    hops = [(k, s) for k in range(1, ns) for s in range(nsub)]
    relays = [(c, t) for t in [q] + others for c in chips]
    at = 0
    for i, (k, s) in enumerate(hops):
        upto = len(relays) * (i + 1) // len(hops)
        hop(k, s)
        for c, t in relays[at:upto]:
            relay_w(c, t)
        at = upto
    for c in chips:
        relay_p(c)
    for k, t in enumerate(others):
        to_column(k, t, t).wait_recv()
    total = land2[0]
    for t in range(1, ns):
        total = total + land2[t]
    mod_o[...] = total

    twin = 1 - core
    for c in range(nc):
        for t in range(ns):
            idx = (c * 2 + twin) * ns + t
            mate_w(c, idx, t).wait_recv()
        first = lax.rem(c * 2 + twin, spread) * ns
        @pl.when((c * 2 + twin) // spread == q)
        def _():
            for t in range(ns):
                mate_p(c, first + t, t).wait_recv()
    for k, t in enumerate(others):
        masks(k, t, t).wait_recv()
    keep[3].wait()

    for k, t in enumerate(others):
        for copy in across(k, t, me):
            copy.wait_send()
        masks(k, t, q).wait_send()
        to_column(k, t, q).wait_send()
    for k, e in enumerate(peers):
        embeds(k, e, d).wait_send()
        to_item(k, e, d).wait_send()

    @pl.when(plane != q)
    def _():
        pack_z.wait_send()

    @pl.when(plane == q)
    def _():
        for t in range(ns):
            for c in chips:
                plane_p(c, base + t, t).wait_send()
            mate_p(chip, base + t, t).wait_send()

    for t in range(ns):
        for c in chips:
            plane_w(c, d * ns + t, t).wait_send()
            mate_w(c, (c * 2 + core) * ns + t, t).wait_send()
        mate_w(chip, d * ns + t, t).wait_send()
    for c in chips:
        first = lax.rem(c * 2 + core, spread) * ns
        @pl.when(holds(c))
        def _():
            for t in range(ns):
                mate_p(c, first + t, t).wait_send()
    for k in range(ns - 1):
        for s in range(nsub):
            @pl.when(jnp.logical_and(q >= k, q + 1 < ns))
            def _():
                rise(k, s).wait_send()
            @pl.when(jnp.logical_and(q + k < ns, q >= 1))
            def _():
                sink(k, s).wait_send()


def start(hidden, mask, win, wout, pack, embedded, modw, modb, nd, ns, cid):
    nsub = 4
    length, width = hidden.shape
    rows, inner = wout.shape
    nc = nd // 2
    hidden = hidden.reshape(nsub, length // nsub, width)
    lines = modb.shape
    return pl.pallas_call(
        functools.partial(start_kernel, nd, ns, nsub),
        out_shape=[
            jax.ShapeDtypeStruct((ns,) + hidden.shape, BF),
            jax.ShapeDtypeStruct((nd * ns, rows, 3 * inner // ns), BF),
            jax.ShapeDtypeStruct((nd,) + pack.shape, BF),
            jax.ShapeDtypeStruct((ns,) + mask.shape, BF),
            jax.ShapeDtypeStruct(lines, F32),
        ],
        in_specs=[HBM, HBM, HBM, HBM, VMEM, VMEM, VMEM, VMEM],
        out_specs=[HBM, HBM, HBM, VMEM, VMEM],
        scratch_shapes=[
            pltpu.VMEM((nd,) + embedded.shape, BF), pltpu.VMEM((nd * 16, modw.shape[1]), F32),
            pltpu.VMEM((nd,) + lines, F32), pltpu.VMEM((nd,) + lines, F32), pltpu.VMEM((ns,) + lines, F32),
            DMA((ns - 1, nsub)), DMA((ns - 1, nsub)), DMA((ns - 1, nsub)), DMA((ns - 1, nsub)),
            DMA((ns, 3)), DMA((nd * ns, 4)), DMA((nc, ns)), DMA((nc, ns)),
            DMA(()), DMA((nd,)), DMA((nc, ns)), DMA((nc, ns)),
            DMA((ns,)), DMA((ns,)), DMA((nd,)), DMA((nd,)),
            DMA((nd,)), DMA((nd,)), DMA((ns,)), DMA((ns,)), DMA((5,)),
        ],
        compiler_params=pltpu.CompilerParams(
            collective_id=cid, has_side_effects=True, vmem_limit_bytes=40 * 2**20),
        name="start",
    )(hidden, win, wout, pack, mask, embedded, modw, modb)


def end_kernel(nd, ns, nsub, rows, turned,
               gp_h, md_h, wx_h, early_ref, sm_ref, hid_ref, cot_ref, line_ref,
               gin_o, gout_o, so_ref, gh_o, mod_o,
               gp, md, wx, gm, made, pair, plane, spair, splane, ssum, fro, up, down, own, msg, mland,
               ld, sa, ra, sb, rb, sc, rc, se, re, ta, ra2, tb, rb2, tc, rc2, su, ru, sd, rd, s1, r1, s2, r2):
    d, q = lax.axis_index("dp"), lax.axis_index("seq")
    nc = nd // 2
    chip, core = d // 2, lax.rem(d, 2)
    mate = chip * 2 + 1 - core
    pairs = [(1, 1), (1, 0), (0, 1)] + [(a, b) for b in range(2, nc // 2) for a in (0, 1)]
    chips = [lax.rem(chip + a, 2) + 2 * lax.rem(chip // 2 + b, nc // 2) for a, b in pairs]
    others = [lax.rem(q + k, ns) for k in range(1, ns)]
    peers = [lax.rem(d + k, nd) for k in range(1, nd)]
    spread = nd // ns
    final_to = (spread * q + d // ns, lax.rem(d, ns))
    me = d * ns + q
    final_from = (lax.rem(me, nd), me // nd)
    stays = jnp.logical_and(final_to[0] == d, final_to[1] == q)
    length, cols = gp.shape
    part = cols // 2
    width = wx.shape[0]
    local = length // ns
    sub = local // nsub
    rw = pair.shape[2]
    half = ns * rw

    loads = [pltpu.make_async_copy(src, dst, ld.at[i]) for i, (src, dst) in enumerate(
        ((gp_h, gp), (wx_h.at[:, 0:cols], wx), (md_h, md)))]
    for copy in loads:
        copy.start()

    bar = pltpu.get_barrier_semaphore()
    friends = [(e, q) for e in peers] + [(d, t) for t in others]
    for to in friends:
        pl.semaphore_signal(bar, inc=1, device_id=to, device_id_type=MESH)
    @pl.when(jnp.logical_not(stays))
    def _():
        pl.semaphore_signal(bar, inc=1, device_id=final_from, device_id_type=MESH)

    def tokens(t):
        @pl.loop(0, width // 512)
        def _(j):
            here = pl.ds(pl.multiple_of(j * 512, 512), 512)
            full = lax.dot_general(gp[t * local:(t + 1) * local, :], wx[here, :], NT, preferred_element_type=F32)
            full = full.astype(BF)
            for s in range(nsub):
                gm[t, s, :, here] = full[s * sub:(s + 1) * sub]

    def rise(t, s, src):
        return send(src, up.at[t, s], su.at[t, s], ru.at[t, s], (d, q + 1))

    def sink(t, s, src):
        return send(src, down.at[t, s], sd.at[t, s], rd.at[t, s], (d, q - 1))

    def added(land, t, s):
        land[t, s] = (land[t, s].astype(F32) + gm[t, s].astype(F32)).astype(BF)

    def open_up(t, s):
        @pl.when(jnp.logical_and(q == 0, t > 0))
        def _():
            rise(t, s, gm.at[t, s]).start()

    def open_down(t, s):
        @pl.when(jnp.logical_and(q == ns - 1, t < ns - 1))
        def _():
            sink(t, s, gm.at[t, s]).start()

    def step(k, s):
        t = ns - 1 - k

        @pl.when(jnp.logical_and(q < t, q > 0))
        def _():
            rise(t, s, up.at[t, s]).wait_recv()
            added(up, t, s)
            rise(t, s, up.at[t, s]).start()

        @pl.when(jnp.logical_and(q > k, q < ns - 1))
        def _():
            sink(k, s, down.at[k, s]).wait_recv()
            added(down, k, s)
            sink(k, s, down.at[k, s]).start()

    def far(k):
        for t in sorted({ns - 1 - k, k}, reverse=True):
            tokens(t)
            if k == 0 and t:
                @pl.when(stays)
                def _():
                    pl.semaphore_wait(bar, len(friends))

                @pl.when(jnp.logical_not(stays))
                def _():
                    pl.semaphore_wait(bar, len(friends) + 1)
            for s in range(nsub):
                open_up(t, s)
                open_down(t, s)

    loads[0].wait()
    loads[1].wait()
    far(0)
    steps = [(k, s) for k in range(ns - 1) for s in range(nsub)]

    def first(c):
        return send(made.at[c, 1 - core], pair.at[c], sa.at[c], ra.at[c], (mate, q))

    def first_small(c):
        return send(sm_ref.at[c * 2 + 1 - core], spair.at[c], ta.at[c], ra2.at[c], (mate, q))

    def second(c, src):
        return send(pair.at[c], plane.at[src], sb.at[c], rb.at[src], (c * 2 + core, q))

    def second_small(c, src):
        return send(spair.at[c], splane.at[src], tb.at[c], rb2.at[src], (c * 2 + core, q))

    def block(c):
        at = pl.ds(pl.multiple_of(c * 2 * half, 2 * half), 2 * half)
        tile = part if part % 256 else part // 2
        left = md[at, :] if turned else md[:, at].T

        @pl.loop(0, part // tile)
        def _(j):
            n = pl.ds(pl.multiple_of(j * tile, 128), tile)
            full = jnp.dot(left, gp[:, n], preferred_element_type=F32).astype(BF)
            for h in range(2):
                for t in range(ns):
                    line = (h * ns + t) * rw
                    made[c, h, t, :, n] = full[line:line + rw]

    def ready(t, src):
        return send(early_ref.at[t], fro.at[src, :, part:3 * part], se.at[t], re.at[src], (d, t))

    loads[2].wait()
    order = chips + [chip]

    def give(c):
        block(c)
        first(c).start()
        first_small(c).start()

    give(order[0])
    for k in range(1, ns // 2):
        far(k)
    for t in others:
        ready(t, q).start()
    fro[q, :, part:3 * part] = early_ref[q]
    for i, c in enumerate(order):
        if i + 1 < nc:
            give(order[i + 1])
        first(c).wait_recv()
        @pl.loop(0, ns)
        def _(t):
            pair[c, t] = (pair[c, t].astype(F32) + made[c, core, t].astype(F32)).astype(BF)
        first_small(c).wait_recv()
        spair[c] = spair[c] + sm_ref[c * 2 + core]
        if i < nc - 1:
            second(c, chip).start()
            second_small(c, chip).start()
        for k, s in steps[i:i + 1]:
            step(k, s)
    late = len(steps) * 3 // 4
    for k, s in steps[nc:late]:
        step(k, s)

    for c in chips:
        second(c, c).wait_recv()
        second_small(c, c).wait_recv()
    @pl.loop(0, ns)
    def _(t):
        total = pair[chip, t].astype(F32)
        for c in chips:
            total = total + plane[c, t].astype(F32)
        pair[chip, t] = total.astype(BF)
    small = spair[chip]
    for c in chips:
        small = small + splane[c]
    ssum[...] = small

    def third(t, src):
        return send(pair.at[chip, t], fro.at[src, :, 0:part], sc.at[t], rc.at[src], (d, t))

    last = send(ssum, so_ref, tc, rc2, final_to)
    @pl.when(stays)
    def _():
        so_ref[...] = ssum[...]
    @pl.when(jnp.logical_not(stays))
    def _():
        last.start()
    for t in others:
        third(t, q).start()
    fro[q, :, 0:part] = pair[chip, q]
    for k, s in steps[max(nc, late):]:
        step(k, s)

    msg[...] = jnp.zeros(msg.shape, F32)
    msg[2:4, :] = line_ref[1:3, :]
    scale = 1.0 + line_ref[0:1, :]
    for s in range(nsub):
        own[...] = gm[q, s].astype(F32)

        @pl.when(q > 0)
        def _():
            rise(q, s, gm.at[q, s]).wait_recv()
            own[...] += up[q, s].astype(F32)

        @pl.when(q < ns - 1)
        def _():
            sink(q, s, gm.at[q, s]).wait_recv()
            own[...] += down[q, s].astype(F32)

        @pl.loop(0, sub // 16)
        def _(r):
            here = pl.ds(pl.multiple_of(r * 16, 16), 16)
            grad = own[here, :]
            x = hid_ref[s, here, :].astype(F32)
            x = x - jnp.mean(x, axis=1, keepdims=True)
            inverse = lax.rsqrt(jnp.mean(x * x, axis=1, keepdims=True) + EPS)
            normed = x * inverse
            msg[0:1, :] += jnp.sum(grad, axis=0, keepdims=True)
            msg[1:2, :] += jnp.sum(grad * normed, axis=0, keepdims=True)
            grad = grad * scale
            grad = grad - jnp.mean(grad, axis=1, keepdims=True) - normed * jnp.mean(
                grad * normed, axis=1, keepdims=True)
            gh_o[s, here, :] = (cot_ref[s, here, :].astype(F32) + inverse * grad).astype(BF)

    for k, t in enumerate(others):
        send(msg, mland.at[q], s1.at[k], r1.at[q], (d, t)).start()

    def place(src):
        inner = part * ns
        at = src * part
        for j, out in ((0, gin_o), (1, gin_o), (2, gout_o)):
            to = pl.ds(pl.multiple_of(at + (inner if j == 1 else 0), 128), part)
            out[:, to] = fro[src, 0:rows, j * part:(j + 1) * part].astype(F32)

    place(q)
    total = msg[...]
    for k, t in enumerate(others):
        send(msg, mland.at[t], s1.at[k], r1.at[t], (d, t)).wait_recv()
        total = total + mland[t]
    mod_o[d] = total
    for k, e in enumerate(peers):
        send(mod_o.at[d], mod_o.at[d], s2.at[k], r2.at[d], (e, q)).start()
    for t in others:
        third(t, t).wait_recv()
        ready(t, t).wait_recv()
        place(t)
    for k, e in enumerate(peers):
        send(mod_o.at[e], mod_o.at[e], s2.at[k], r2.at[e], (e, q)).wait_recv()
    @pl.when(jnp.logical_not(stays))
    def _():
        last.wait_recv()
        last.wait_send()

    for c in order:
        first(c).wait_send()
        first_small(c).wait_send()
    for c in chips:
        second(c, chip).wait_send()
        second_small(c, chip).wait_send()
    for k, t in enumerate(others):
        third(t, q).wait_send()
        ready(t, q).wait_send()
        send(msg, mland.at[q], s1.at[k], r1.at[q], (d, t)).wait_send()
    for k, e in enumerate(peers):
        send(mod_o.at[d], mod_o.at[d], s2.at[k], r2.at[d], (e, q)).wait_send()
    for k, s in steps:
        t = ns - 1 - k
        @pl.when(q < t)
        def _():
            rise(t, s, gm.at[t, s]).wait_send()
        @pl.when(q > k)
        def _():
            sink(k, s, gm.at[k, s]).wait_send()


def end(grad_projected, modded, wx, early, small, hidden, cot, line, rows, nd, ns, cid):
    length, cols = grad_projected.shape
    part = cols // 2
    width = wx.shape[0]
    inner = part * ns
    nc, nsub = nd // 2, 4
    local = length // ns
    sub = local // nsub
    rw = rows + -rows % 16
    half = ns * rw
    turned = 2 * half % 128 != 0 or rw != rows
    if turned:
        def turn(a):
            a = a.T.reshape(nd * ns, rows, length)
            return jnp.pad(a, ((0, 0), (0, rw - rows), (0, 0))).reshape(nd * ns * rw, length)
        modded = turn(modded)
    early = jnp.pad(early.reshape(ns, rows, cols), ((0, 0), (0, rw - rows), (0, 0)))
    v = small.shape[1:]
    hidden, cot = hidden.reshape(nsub, sub, width), cot.reshape(nsub, sub, width)
    blocks = pltpu.VMEM((nc, ns, rw, part), BF)
    smalls = pltpu.VMEM((nc,) + v, F32)
    runs = pltpu.VMEM((ns, nsub, sub, width), BF)
    gin, gout, so, gh, mod = pl.pallas_call(
        functools.partial(end_kernel, nd, ns, nsub, rows, turned),
        out_shape=[
            jax.ShapeDtypeStruct((rows, 2 * inner), F32),
            jax.ShapeDtypeStruct((rows, inner), F32),
            jax.ShapeDtypeStruct(v, F32),
            jax.ShapeDtypeStruct((nsub, sub, width), BF),
            jax.ShapeDtypeStruct((nd, 8, width), F32),
        ],
        in_specs=[HBM] * 3 + [VMEM] * 5, out_specs=[VMEM] * 5,
        scratch_shapes=[
            pltpu.VMEM(grad_projected.shape, BF), pltpu.VMEM(modded.shape, BF), pltpu.VMEM((width, cols), BF), runs,
            pltpu.VMEM((nc, 2, ns, rw, part), BF), blocks, blocks,
            smalls, smalls, pltpu.VMEM(v, F32), pltpu.VMEM((ns, rw, cols + part), BF), runs, runs,
            pltpu.VMEM((sub, width), F32), pltpu.VMEM((8, width), F32), pltpu.VMEM((ns, 8, width), F32),
            DMA((3,)),
            DMA((nc,)), DMA((nc,)), DMA((nc,)), DMA((nc,)), DMA((ns,)), DMA((ns,)), DMA((ns,)), DMA((ns,)),
            DMA((nc,)), DMA((nc,)), DMA((nc,)), DMA((nc,)), DMA(()), DMA(()),
            DMA((ns, nsub)), DMA((ns, nsub)), DMA((ns, nsub)), DMA((ns, nsub)),
            DMA((ns,)), DMA((ns,)), DMA((nd,)), DMA((nd,)),
        ],
        compiler_params=pltpu.CompilerParams(
            collective_id=cid, has_side_effects=True, vmem_limit_bytes=60 * 2**20),
        name="end",
    )(grad_projected, modded, wx, early, small, hidden, cot, line)
    return gin, gout, so, gh.reshape(local, width), mod


def frequency_embed(timestep):
    half_width = FREQ // 2
    counter = jnp.arange(half_width, dtype=F32)
    frequency = jnp.exp(counter * (-math.log(10000.0) / half_width))
    angles = timestep.astype(F32)[:, None] * frequency[None, :]
    return jnp.concatenate([jnp.cos(angles), jnp.sin(angles)], axis=1)


def dot(a, b):
    return jnp.dot(a, b, preferred_element_type=F32)


def dot_nt(a, b):
    return lax.dot_general(a, b, (((1,), (1,)), ((), ())), preferred_element_type=F32)


def dot_tn(a, b):
    return lax.dot_general(a, b, (((0,), (0,)), ((), ())), preferred_element_type=F32)


def body(
    hidden,
    pad_mask,
    timestep,
    input_weight,
    select_weight,
    step_weight,
    output_weight,
    decay_forward,
    decay_reverse,
    filter_weight,
    filter_bias,
    step_bias,
    modulation_weight,
    modulation_bias,
    cotangent,
):
    ns, nd = lax.axis_size("seq"), lax.axis_size("dp")
    q, d = lax.axis_index("seq"), lax.axis_index("dp")
    every = ("dp", "seq")
    local_len, width = hidden.shape[1:]
    length = local_len * ns
    inner = output_weight.shape[0]
    part = inner // ns
    rank = step_weight.shape[0]
    state = decay_forward.shape[1]
    taps = filter_weight.shape[0]
    rows_in = input_weight.shape[0]
    lanes = select_weight.shape[1]

    units = part // nd
    embedded = jax.nn.silu(frequency_embed(timestep)).astype(BF)
    fil = jnp.concatenate([filter_weight, filter_bias[None], step_bias[None]])
    fil = jnp.pad(fil, ((0, 16 - fil.shape[0]), (0, lanes - units)))
    mid = jnp.concatenate([step_weight.T, decay_forward, decay_reverse], axis=1)
    pack = jnp.concatenate([select_weight, mid, fil])
    mask = jnp.pad(pad_mask[0].astype(BF).reshape(-1, 128), ((0, 16 - local_len // 128), (0, 0)))
    shard = (-modulation_weight.shape[0] % 16, 0)
    modb = jnp.zeros((-(-3 * width // 1024) * 1024,), F32)
    modb = lax.dynamic_update_slice(modb, modulation_bias.astype(F32), ((d * ns + q) * modulation_bias.shape[0],))
    row_pad = ((0, -rows_in % 16), (0, 0))
    hid, wx, pack, mask, modulation = start(
        hidden[0], mask, jnp.pad(input_weight, row_pad), jnp.pad(output_weight.T, row_pad), pack,
        jnp.pad(embedded, ((0, 15), (0, 0))),
        jnp.pad(modulation_weight, ((0, shard[0]), (0, 0))), modb.reshape(-1, 128), nd, ns, 4)
    hid = hid.reshape(length, width)
    wx = wx[:, :rows_in].reshape(width, 3 * part)
    win, wout = wx[:, : 2 * part], wx[:, 2 * part :]
    mask = mask[:, : local_len // 128].reshape(length, 1).astype(F32)
    select_q = pack[:, :units].reshape(part, lanes)
    mid = pack[:, units : 2 * units].reshape(part, lanes)
    step_q = mid[:, :rank].T
    log_f, log_r = mid[:, rank : rank + state], mid[:, rank + state :]
    fil = pack[:, 2 * units :, :units].transpose(1, 0, 2).reshape(16, part).astype(F32)
    filt32, fbias, sbias = fil[:taps].T, fil[taps][None], fil[taps + 1][None]
    modulation = modulation.reshape(1, -1)[:, : 3 * width]
    shifts = modulation[:, :width]
    scales = modulation[:, width : 2 * width]
    gate_scale = modulation[:, 2 * width :]

    def norm(x):
        x = x.astype(F32)
        centered = x - jnp.mean(x, axis=1, keepdims=True)
        inverse = lax.rsqrt(jnp.mean(centered * centered, axis=1, keepdims=True) + EPS)
        return centered * inverse, inverse

    modded = (norm(hid)[0] * (1.0 + scales) + shifts).astype(BF)
    projected = dot(modded, win)
    inner_part = projected[:, :part].astype(BF).astype(F32) * mask
    gate_branch = projected[:, part:]
    padded = jnp.pad(inner_part, ((taps - 1, 0), (0, 0)))
    filtered = fbias
    for k in range(taps):
        filtered = filtered + filt32[:, k][None, :] * padded[k : k + length]
    sigma_filter = jax.nn.sigmoid(filtered)
    active = (filtered * sigma_filter).astype(BF)
    active32 = active.astype(F32)
    selected = column_sum(dot(active, select_q).astype(BF), ns, BF, 0)
    cot, selected = lax.optimization_barrier((cotangent[0], selected))
    cot = lax.all_gather(cot, "seq", axis=0, tiled=True)
    low_rank = selected[:, :rank].astype(BF)
    b_rows = selected[:, rank : rank + state].astype(F32)
    c_rows = selected[:, rank + state :].astype(F32)
    pre_steps = dot(low_rank, step_q) + sbias
    steps = jax.nn.softplus(pre_steps)
    rates_f = -jnp.exp(log_f.astype(F32)).T
    rates_r = -jnp.exp(log_r.astype(F32)).T
    drive = steps * active32
    rates_f2, rates_r2 = rates_f * LOG2E, rates_r * LOG2E
    mixed_f, mixed_r, states_f, states_r = fwd_scan(steps, drive, rates_f2, rates_r2, b_rows.T, blockdiag(c_rows))
    merged = mixed_f + mixed_r
    sigma_gate = jax.nn.sigmoid(gate_branch)
    silu_gate = gate_branch * sigma_gate
    gated = (merged * silu_gate).astype(BF)
    branch = dot_nt(gated, wout).astype(BF)
    branch, cot = lax.optimization_barrier((branch, cot))
    branch = lax.psum_scatter(branch, "seq", scatter_dimension=0, tiled=True).astype(F32)

    mask_here = pad_mask[0].astype(F32)[:, None]
    cot_here = cotangent[0].astype(F32)
    block_out = (hidden[0].astype(F32) + gate_scale * mask_here * branch).astype(BF)
    grad_gate = jnp.sum(mask_here * cot_here * branch, axis=0)

    grad_branch = (cot.astype(F32) * gate_scale * mask).astype(BF)
    grad_gated = dot(grad_branch, wout)
    grad_merged = grad_gated * silu_gate
    grad_gate_branch = grad_gated * merged * sigma_gate * (1.0 + gate_branch * (1.0 - sigma_gate))
    grad_gate_branch = grad_gate_branch.astype(BF)
    early = jnp.concatenate([dot_tn(modded, grad_gate_branch), dot_tn(grad_branch, gated)], axis=1).astype(BF)
    early = lax.psum_scatter(early, "dp", scatter_dimension=0, tiled=True)
    dlog_f, dlog_r, adjb_f, adjb_r, bg_f, bg_r, cg_f, cg_r, rg_f, rg_r = bwd_scan(
        steps, drive.astype(BF), grad_merged, rates_f2, rates_r2, c_rows.T, blockdiag(b_rows), states_f, states_r)
    adjb = adjb_f + adjb_r
    grad_steps = (dlog_f + dlog_r) * (1.0 / LOG2E) + active32 * adjb
    grad_b = (bg_f + bg_r).reshape(length, state)
    grad_c = (cg_f + cg_r).reshape(length, state)
    grad_decay_f = rg_f * rates_f
    grad_decay_r = rg_r * rates_r
    grad_pre = grad_steps * jax.nn.sigmoid(pre_steps)
    grad_step_bias = jnp.sum(grad_pre, axis=0)
    grad_pre_low = grad_pre.astype(BF)
    grad_step_t = dot_tn(grad_pre_low, low_rank)
    grad_low_rank = dot_nt(grad_pre_low, step_q)
    grad_selected = column_sum(jnp.concatenate([grad_low_rank, grad_b, grad_c], axis=1).astype(BF), ns, BF, 1)
    grad_select = dot_tn(active, grad_selected)
    grad_active = steps * adjb + dot_nt(grad_selected, select_q)
    grad_filtered = grad_active * sigma_filter * (1.0 + filtered * (1.0 - sigma_filter))
    extended = jnp.pad(grad_filtered, ((0, taps - 1), (0, 0)))
    grad_inner = jnp.zeros_like(grad_filtered)
    filter_rows = []
    for k in range(taps):
        lead = taps - 1 - k
        grad_inner = grad_inner + filt32[:, k][None, :] * extended[lead : lead + length]
        filter_rows.append(jnp.sum(grad_filtered * padded[k : k + length], axis=0))
    grad_filter_bias = jnp.sum(grad_filtered, axis=0)
    grad_projected = jnp.concatenate([(grad_inner * mask).astype(BF), grad_gate_branch], axis=1)
    fil = jnp.stack(filter_rows + [grad_filter_bias, grad_step_bias])
    fil = fil.reshape(-1, nd, units).transpose(1, 0, 2)
    fil = jnp.pad(fil, ((0, 0), (0, 16 - fil.shape[1]), (0, lanes - units)))
    mid = jnp.concatenate([grad_step_t, grad_decay_f.T, grad_decay_r.T], axis=1)
    small = jnp.concatenate([grad_select.reshape(nd, units, lanes), mid.reshape(nd, units, lanes), fil], axis=1)
    line = jnp.concatenate([scales, grad_gate[None], jnp.pad(embedded.astype(F32) / ns, ((0, 0), (0, width - FREQ))),
                            jnp.zeros((5, width), F32)])
    g_in, g_out, small, grad_hidden, sums = end(
        grad_projected, modded, wx, early, small, hidden[0], cotangent[0], line, rows_in, nd, ns, 2)
    gs_select = small[:units]
    mid = small[units : 2 * units]
    gs_step, gs_f, gs_r = mid[:, :rank], mid[:, rank : rank + state], mid[:, rank + state :]
    fil = small[2 * units :, :units]

    embeds = sums[:, 3, :FREQ]
    grad_mod = sums[:, :3].reshape(nd, 3 * width)
    me = d * ns + q
    mine = lax.dynamic_slice_in_dim(embeds, me * modulation_weight.shape[0], modulation_weight.shape[0], 1)
    g_modw = lax.dot_general(mine, grad_mod, (((0,), (0,)), ((), ())), precision=HIGHEST)
    g_modb = lax.dynamic_slice_in_dim(
        jnp.sum(grad_mod, axis=0), me * modulation_bias.shape[0], modulation_bias.shape[0], 0)
    return (
        block_out[None],
        grad_hidden[None],
        g_in,
        gs_select,
        gs_step.T,
        g_out.T,
        gs_f,
        gs_r,
        fil[:taps],
        fil[taps],
        fil[taps + 1],
        g_modw,
        g_modb,
    )


def solution(mesh):
    return jax.shard_map(
        body,
        mesh=mesh,
        in_specs=(
            P("dp", "seq", None),
            P("dp", "seq"),
            P("dp"),
            P(("dp", "seq"), None),
            P(("dp", "seq"), None),
            P(None, ("dp", "seq")),
            P(None, ("dp", "seq")),
            P(("dp", "seq"), None),
            P(("dp", "seq"), None),
            P(None, ("dp", "seq")),
            P(("dp", "seq")),
            P(("dp", "seq")),
            P(("dp", "seq"), None),
            P(("dp", "seq")),
            P("dp", "seq", None),
        ),
        out_specs=(
            P("dp", "seq", None),
            P("dp", "seq", None),
            P(("dp", "seq"), None),
            P(("dp", "seq"), None),
            P(None, ("dp", "seq")),
            P(None, ("dp", "seq")),
            P(("dp", "seq"), None),
            P(("dp", "seq"), None),
            P(None, ("dp", "seq")),
            P(("dp", "seq")),
            P(("dp", "seq")),
            P(("dp", "seq"), None),
            P(("dp", "seq")),
        ),
        check_vma=False,
    )
```

```python
import functools
import math

import jax
import jax.numpy as jnp
from jax import lax
from jax.experimental import pallas as pl
from jax.experimental.pallas import tpu as pltpu
from jax.sharding import PartitionSpec as P

FREQ = 256
EPS = 1e-06
HIGHEST = lax.Precision.HIGHEST
LOG2E = 1.4426950408889634
SUB = 16
WF = 384
WB = 768
F32, BF = jnp.float32, jnp.bfloat16
NT = (((1,), (1,)), ((), ()))


def columns_of(rows_t, base):
    turned = pltpu.roll(rows_t, rows_t.shape[1] - base, 1)
    return [jnp.broadcast_to(turned[:, j:j + 1], (rows_t.shape[0], 128)) for j in range(SUB)]


def wide(block, lanes):
    return jnp.concatenate([block] * (lanes // 128), axis=1) if lanes > 128 else block


def states_of(base, at):
    return pl.ds(pl.multiple_of((base + at) * 16, 16), 16)


def fwd_kernel(step_f, step_r, u_f, u_r, rate_f, rate_r, bt_f, bt_r, cblk_f, cblk_r,
               y_f, y_r, s_f, s_r, carry, f0, f1, r0, r1):
    rows, lanes = step_f.shape

    @pl.when(pl.program_id(0) == 0)
    def _():
        carry[...] = jnp.zeros(carry.shape, F32)

    wide_by = min(WF, lanes)
    cuts = [slice(c, c + wide_by) for c in range(0, lanes, wide_by)]

    def walk(states, bases, kept):
        cols = [columns_of(bt[...], base) for bt, base in zip((bt_f, bt_r), bases)]
        out = []
        for cut, pair in zip(cuts, states):
            pair = list(pair)
            rates = rate_f[:, cut], rate_r[:, cut]
            for k in range(SUB):
                for z, (step, u, s, j) in enumerate(((step_f, u_f, s_f, k), (step_r, u_r, s_r, SUB - 1 - k))):
                    at = pl.ds(bases[z] + j, 1)
                    decay = jnp.exp2(step[at, cut] * rates[z])
                    pair[z] = decay * pair[z] + u[at, cut] * wide(cols[z][j], wide_by)
                    low = pair[z].astype(BF)
                    s[states_of(bases[z], j), cut] = low
                    kept[z][j * 16:(j + 1) * 16, cut] = low
            out.append(tuple(pair))
        return tuple(out)

    def mix(base, cblk, kept, y):
        here = pl.ds(base, SUB)
        y[here, :] = jnp.dot(cblk[here, :], kept[...], preferred_element_type=F32)

    def start_of(a, flip):
        a = jnp.maximum(a, 0)
        return pl.multiple_of(rows - SUB - a * SUB if flip else a * SUB, SUB)

    def two(i, states):
        for half, (fk, rk, fp, rp) in enumerate(((f0, r0, f1, r1), (f1, r1, f0, r0))):
            a = 2 * i + half
            mix(start_of(a - 1, False), cblk_f, fp, y_f)
            mix(start_of(a - 1, True), cblk_r, rp, y_r)
            states = walk(states, (start_of(a, False), start_of(a, True)), (fk, rk))
        return states

    states = tuple((carry[0, :, cut], carry[1, :, cut]) for cut in cuts)
    states = lax.fori_loop(0, rows // SUB // 2, two, states)
    mix(rows - SUB, cblk_f, f1, y_f)
    mix(0, cblk_r, r1, y_r)
    for cut, pair in zip(cuts, states):
        carry[0, :, cut], carry[1, :, cut] = pair


def fwd_scan(steps, u, rates_f, rates_r, b_t, cblk, tile=128):
    length, lanes = steps.shape
    blocks = length // tile
    specs = []
    for order in (lambda t: t, lambda t: blocks - 1 - t):
        specs.append((
            pl.BlockSpec((tile, lanes), lambda t, order=order: (order(t), 0)),
            pl.BlockSpec((16, lanes), lambda t: (0, 0)),
            pl.BlockSpec((16, tile), lambda t, order=order: (0, order(t))),
            pl.BlockSpec((tile, 256), lambda t, order=order: (order(t), 0)),
            pl.BlockSpec((tile * 16, lanes), lambda t, order=order: (order(t), 0)),
        ))
    (row_f, rate, bt_f, blk_f, s_f), (row_r, _, bt_r, blk_r, s_r) = specs
    y = jax.ShapeDtypeStruct((length, lanes), F32)
    s = jax.ShapeDtypeStruct((length * 16, lanes), BF)
    kept = pltpu.VMEM((256, lanes), BF)
    return pl.pallas_call(
        fwd_kernel,
        grid=(blocks,),
        in_specs=[row_f, row_r, row_f, row_r, rate, rate, bt_f, bt_r, blk_f, blk_r],
        out_specs=[row_f, row_r, s_f, s_r],
        out_shape=[y, y, s, s],
        scratch_shapes=[pltpu.VMEM((2, 16, lanes), F32), kept, kept, kept, kept],
        compiler_params=pltpu.CompilerParams(vmem_limit_bytes=56 * 2**20, dimension_semantics=("arbitrary",)),
        cost_estimate=pl.CostEstimate(flops=length * lanes * 16 * 3200, transcendentals=0, bytes_accessed=length * lanes * 80),
        name="fwd_scan",
    )(steps, steps, u, u, rates_f, rates_r, b_t, b_t, cblk, cblk)


def bwd_kernel(step_f, step_r, u_f, u_r, gy_f, gy_r, rate_f, rate_r, ct_f, ct_r, bblk_f, bblk_r, s_f, s_r, sp_f, sp_r,
               dlog_f, dlog_r, adjb_f, adjb_r, bg_f, bg_r, cg_f, cg_r, rg_f, rg_r, carry,
               af0, af1, ar0, ar1, lf0, lf1, lr0, lr1):
    rows, lanes = step_f.shape
    t = pl.program_id(0)
    last = pl.num_programs(0) - 1

    @pl.when(t == 0)
    def _():
        carry[...] = jnp.zeros(carry.shape, F32)
        rg_f[...] = jnp.zeros(rg_f.shape, F32)
        rg_r[...] = jnp.zeros(rg_r.shape, F32)

    ones = (lax.broadcasted_iota(jnp.int32, (SUB, 256), 0) == lax.broadcasted_iota(jnp.int32, (SUB, 256), 1) // 16)
    onesb = ones.astype(BF)
    zero = jnp.zeros((SUB, 256), F32)

    def start_of(a, down):
        a = jnp.maximum(a, 0)
        return pl.multiple_of(rows - SUB - a * SUB if down else a * SUB, SUB)

    wide_by = min(WB, lanes)
    cuts = [slice(c, c + wide_by) for c in range(0, lanes, wide_by)]

    def walk(states, bases, keep_a, keep_l):
        cols = [columns_of(ct[...], base) for ct, base in zip((ct_f, ct_r), bases)]
        out = []
        for cut, pair in zip(cuts, states):
            pair = list(pair)
            rates = rate_f[:, cut], rate_r[:, cut]
            rg = [rg_f[:, cut], rg_r[:, cut]]
            low_rates = [r.astype(BF) for r in rates]
            some = [[], []]
            for k in range(SUB):
                for z, (step, gy, s, sp, j) in enumerate((
                        (step_f, gy_f, s_f, sp_f, SUB - 1 - k), (step_r, gy_r, s_r, sp_r, k))):
                    at = pl.ds(bases[z] + j, 1)
                    row = step[at, cut]
                    adj = gy[at, cut] * wide(cols[z][j], wide_by) + pair[z]
                    pair[z] = jnp.exp2(row * rates[z]) * adj
                    before = bases[z] + (j + 1 if z else j - 1)
                    if k < SUB - 1:
                        inner = s[pl.ds(pl.multiple_of(before * 16, 16), 16), cut]
                    else:
                        inside = before < rows if z else before >= 0
                        safe = jnp.clip(before, 0, rows - 1)
                        inner = s[pl.ds(pl.multiple_of(safe * 16, 16), 16), cut]
                        outer = jnp.where(t == last, jnp.zeros_like(inner), sp[:, cut])
                        inner = jnp.where(inside, inner, outer)
                    grad = pair[z].astype(BF) * inner
                    keep_a[z][j * 16:(j + 1) * 16, cut] = adj.astype(BF)
                    keep_l[z][j * 16:(j + 1) * 16, cut] = grad * low_rates[z]
                    some[z].append(grad * jnp.broadcast_to(row, (16, wide_by)).astype(BF))
                    if len(some[z]) == 4:
                        rg[z] = rg[z] + ((some[z][0] + some[z][1]) + (some[z][2] + some[z][3])).astype(F32)
                        some[z] = []
            rg_f[:, cut], rg_r[:, cut] = rg
            out.append(tuple(pair))
        return tuple(out)

    def mix(base, a_ref, l_ref, u, gy, bblk, s, dlog, adjb, bg, cg):
        here = pl.ds(base, SUB)
        line = pl.ds(base // SUB, 1)
        a = a_ref[...]
        dlog[here, :] = jnp.dot(onesb, l_ref[...], preferred_element_type=F32)
        adjb[here, :] = jnp.dot(bblk[here, :], a, preferred_element_type=F32)
        bgd = lax.dot_general(u[here, :], a, NT, preferred_element_type=F32)
        block = s[pl.ds(pl.multiple_of(base * 16, 256), 256), :]
        cgd = lax.dot_general(gy[here, :].astype(BF), block, NT, preferred_element_type=F32)
        bg[line, :] = jnp.sum(jnp.where(ones, bgd, zero), axis=0, keepdims=True)
        cg[line, :] = jnp.sum(jnp.where(ones, cgd, zero), axis=0, keepdims=True)

    def mix_f(base, a_ref, l_ref):
        mix(base, a_ref, l_ref, u_f, gy_f, bblk_f, s_f, dlog_f, adjb_f, bg_f, cg_f)

    def mix_r(base, a_ref, l_ref):
        mix(base, a_ref, l_ref, u_r, gy_r, bblk_r, s_r, dlog_r, adjb_r, bg_r, cg_r)

    def two(i, states):
        bufs = ((af0, lf0, ar0, lr0), (af1, lf1, ar1, lr1))
        for half in range(2):
            a = 2 * i + half
            naf, nlf, nar, nlr = bufs[half]
            paf, plf, par, plr = bufs[1 - half]
            mix_f(start_of(a - 1, True), paf, plf)
            mix_r(start_of(a - 1, False), par, plr)
            states = walk(states, (start_of(a, True), start_of(a, False)), (naf, nar), (nlf, nlr))
        return states

    states = tuple((carry[0, :, cut], carry[1, :, cut]) for cut in cuts)
    states = lax.fori_loop(0, rows // SUB // 2, two, states)
    mix_f(0, af1, lf1)
    mix_r(rows - SUB, ar1, lr1)
    for cut, pair in zip(cuts, states):
        carry[0, :, cut], carry[1, :, cut] = pair


def bwd_scan(steps, u, gy, rates_f, rates_r, c_t, bblk, states_f, states_r, tile=128):
    length, lanes = steps.shape
    blocks = length // tile
    down = lambda t: blocks - 1 - t
    up = lambda t: t

    def specs(order, before):
        return (
            pl.BlockSpec((tile, lanes), lambda t: (order(t), 0)),
            pl.BlockSpec((16, lanes), lambda t: (0, 0)),
            pl.BlockSpec((16, tile), lambda t: (0, order(t))),
            pl.BlockSpec((tile, 256), lambda t: (order(t), 0)),
            pl.BlockSpec((tile * 16, lanes), lambda t: (order(t), 0)),
            pl.BlockSpec((16, lanes), lambda t: (before(t), 0)),
            pl.BlockSpec((tile // 16, 256), lambda t: (order(t), 0)),
        )

    row_f, rate, ct_f, blk_f, s_f, sp_f, diag_f = specs(down, lambda t: jnp.maximum((blocks - 1 - t) * tile - 1, 0))
    row_r, _, ct_r, blk_r, s_r, sp_r, diag_r = specs(up, lambda t: jnp.minimum((t + 1) * tile, length - 1))
    y = jax.ShapeDtypeStruct((length, lanes), F32)
    diag = jax.ShapeDtypeStruct((length // 16, 256), F32)
    rg = jax.ShapeDtypeStruct((16, lanes), F32)
    kept = pltpu.VMEM((256, lanes), BF)
    return pl.pallas_call(
        bwd_kernel,
        grid=(blocks,),
        in_specs=[row_f, row_r, row_f, row_r, row_f, row_r, rate, rate, ct_f, ct_r, blk_f, blk_r, s_f, s_r, sp_f, sp_r],
        out_specs=[row_f, row_r, row_f, row_r, diag_f, diag_r, diag_f, diag_r, rate, rate],
        out_shape=[y, y, y, y, diag, diag, diag, diag, rg, rg],
        scratch_shapes=[pltpu.VMEM((2, 16, lanes), F32)] + [kept] * 8,
        compiler_params=pltpu.CompilerParams(vmem_limit_bytes=56 * 2**20, dimension_semantics=("arbitrary",)),
        cost_estimate=pl.CostEstimate(flops=length * lanes * 16 * 6800, transcendentals=0, bytes_accessed=length * lanes * 100),
        name="bwd_scan",
    )(steps, steps, u, u, gy, gy, rates_f, rates_r, c_t, c_t, bblk, bblk, states_f, states_r, states_f, states_r)


def blockdiag(rows):
    length = rows.shape[0]
    eye = (jnp.arange(length)[:, None] % 16) == (jnp.arange(256)[None, :] // 16)
    return jnp.where(eye, jnp.tile(rows, (1, 16)), 0).astype(BF)


MESH = pl.DeviceIdType.MESH
VMEM = pl.BlockSpec(memory_space=pltpu.VMEM)
HBM = pl.BlockSpec(memory_space=pl.ANY)
DMA = pltpu.SemaphoreType.DMA


def send(src, dst, out_sem, in_sem, to):
    return pltpu.make_async_remote_copy(
        src_ref=src, dst_ref=dst, send_sem=out_sem, recv_sem=in_sem, device_id=to, device_id_type=MESH)


def greet(devices):
    bar = pltpu.get_barrier_semaphore()
    for to in devices:
        pl.semaphore_signal(bar, inc=1, device_id=to, device_id_type=MESH)
    pl.semaphore_wait(bar, len(devices))


def column_sum_kernel(ns, p_ref, o_ref, land, s1, r1, s2, r2):
    d, q = lax.axis_index("dp"), lax.axis_index("seq")
    others = [lax.rem(q + k, ns) for k in range(1, ns)]
    greet([(d, t) for t in others])
    for k, t in enumerate(others):
        send(p_ref.at[t], land.at[q], s1.at[k], r1.at[q], (d, t)).start()
    total = p_ref[q].astype(F32)
    for k, t in enumerate(others):
        send(p_ref.at[t], land.at[t], s1.at[k], r1.at[t], (d, t)).wait_recv()
        total = total + land[t].astype(F32)
    o_ref[q] = total.astype(o_ref.dtype)
    for k, t in enumerate(others):
        send(o_ref.at[q], o_ref.at[q], s2.at[k], r2.at[q], (d, t)).start()
    for k, t in enumerate(others):
        send(o_ref.at[t], o_ref.at[t], s2.at[k], r2.at[t], (d, t)).wait_recv()
    for k, t in enumerate(others):
        send(p_ref.at[t], land.at[q], s1.at[k], r1.at[q], (d, t)).wait_send()
        send(o_ref.at[q], o_ref.at[q], s2.at[k], r2.at[q], (d, t)).wait_send()


def column_sum(partial, ns, out_dtype, cid):
    rows, lanes = partial.shape
    block = (ns, rows // ns, lanes)
    out = pl.pallas_call(
        functools.partial(column_sum_kernel, ns),
        out_shape=jax.ShapeDtypeStruct(block, out_dtype),
        in_specs=[VMEM], out_specs=VMEM,
        scratch_shapes=[pltpu.VMEM(block, partial.dtype), DMA((ns,)), DMA((ns,)), DMA((ns,)), DMA((ns,))],
        compiler_params=pltpu.CompilerParams(
            collective_id=cid, has_side_effects=True, vmem_limit_bytes=32 * 2**20),
        name="column_sum",
    )(partial.reshape(block))
    return out.reshape(rows, lanes)


def mod_gather_kernel(nd, ns, g_ref, o_ref, land, s1, r1, s2, r2):
    d, q = lax.axis_index("dp"), lax.axis_index("seq")
    others = [lax.rem(q + k, ns) for k in range(1, ns)]
    peers = [lax.rem(d + k, nd) for k in range(1, nd)]
    greet([(d, t) for t in others] + [(e, q) for e in peers])
    for k, t in enumerate(others):
        send(g_ref, land.at[q], s1.at[k], r1.at[q], (d, t)).start()
    total = g_ref[...]
    for k, t in enumerate(others):
        send(g_ref, land.at[t], s1.at[k], r1.at[t], (d, t)).wait_recv()
        total = total + land[t]
    o_ref[d] = total
    for k, e in enumerate(peers):
        send(o_ref.at[d], o_ref.at[d], s2.at[k], r2.at[d], (e, q)).start()
    for k, e in enumerate(peers):
        send(o_ref.at[e], o_ref.at[e], s2.at[k], r2.at[e], (e, q)).wait_recv()
    for k, t in enumerate(others):
        send(g_ref, land.at[q], s1.at[k], r1.at[q], (d, t)).wait_send()
    for k, e in enumerate(peers):
        send(o_ref.at[d], o_ref.at[d], s2.at[k], r2.at[d], (e, q)).wait_send()


def mod_gather(g, nd, ns, cid):
    rows, lanes = g.shape
    return pl.pallas_call(
        functools.partial(mod_gather_kernel, nd, ns),
        out_shape=jax.ShapeDtypeStruct((nd, rows, lanes), F32),
        in_specs=[VMEM], out_specs=VMEM,
        scratch_shapes=[pltpu.VMEM((ns, rows, lanes), F32), DMA((ns,)), DMA((ns,)), DMA((nd,)), DMA((nd,))],
        compiler_params=pltpu.CompilerParams(
            collective_id=cid, has_side_effects=True, vmem_limit_bytes=32 * 2**20),
        name="mod_gather",
    )(g)


def home_kernel(nd, ns, nsub, g_ref, sm_ref, gm_ref, f_ref, so_ref, out_ref,
                pair, plane, spair, splane, ssum, up, down,
                sa, ra, sb, rb, sc, rc, ta, ra2, tb, rb2, tc, rc2, su, ru, sd, rd):
    d, q = lax.axis_index("dp"), lax.axis_index("seq")
    nc = nd // 2
    chip, core = d // 2, lax.rem(d, 2)
    mate = chip * 2 + 1 - core
    chips = [lax.rem(chip + k, nc) for k in range(1, nc)]
    others = [lax.rem(q + k, ns) for k in range(1, ns)]
    spread = nd // ns
    final_to = (spread * q + d // ns, lax.rem(d, ns))
    mine = d * ns + q
    final_from = (lax.rem(mine, nd), mine // nd)
    stays = jnp.logical_and(final_to[0] == d, final_to[1] == q)
    bar = pltpu.get_barrier_semaphore()
    friends = [(mate, q)] + [(c * 2 + core, q) for c in chips] + [(d, t) for t in others]
    for to in friends:
        pl.semaphore_signal(bar, inc=1, device_id=to, device_id_type=MESH)
    @pl.when(jnp.logical_not(stays))
    def _():
        pl.semaphore_signal(bar, inc=1, device_id=final_from, device_id_type=MESH)
        pl.semaphore_wait(bar, len(friends) + 1)
    @pl.when(stays)
    def _():
        pl.semaphore_wait(bar, len(friends))

    def first(c):
        return send(g_ref.at[c * 2 + 1 - core], pair.at[c], sa.at[c], ra.at[c], (mate, q))

    def first_small(c):
        return send(sm_ref.at[c * 2 + 1 - core], spair.at[c], ta.at[c], ra2.at[c], (mate, q))

    order = chips + [chip]
    for c in order:
        first(c).start()
        first_small(c).start()

    def rise(t, s, src):
        return send(src, up.at[t, s], su.at[t, s], ru.at[t, s], (d, q + 1))

    def sink(t, s, src):
        return send(src, down.at[t, s], sd.at[t, s], rd.at[t, s], (d, q - 1))

    def added(land, t, s):
        land[t, s] = (land[t, s].astype(F32) + gm_ref[t, s].astype(F32)).astype(BF)

    def step_up(t, s):
        @pl.when(q < t)
        def _():
            @pl.when(q == 0)
            def _():
                rise(t, s, gm_ref.at[t, s]).start()
            @pl.when(q > 0)
            def _():
                rise(t, s, up.at[t, s]).wait_recv()
                added(up, t, s)
                rise(t, s, up.at[t, s]).start()

    def step_down(t, s):
        @pl.when(q > t)
        def _():
            @pl.when(q == ns - 1)
            def _():
                sink(t, s, gm_ref.at[t, s]).start()
            @pl.when(q < ns - 1)
            def _():
                sink(t, s, down.at[t, s]).wait_recv()
                added(down, t, s)
                sink(t, s, down.at[t, s]).start()

    steps = [(k, s) for k in range(ns - 1) for s in range(nsub)]
    middle = len(steps) * 2 // 3

    def walk(some):
        for k, s in some:
            step_up(ns - 1 - k, s)
            step_down(k, s)

    def second(c, src):
        return send(pair.at[c], plane.at[src], sb.at[c], rb.at[src], (c * 2 + core, q))

    def second_small(c, src):
        return send(spair.at[c], splane.at[src], tb.at[c], rb2.at[src], (c * 2 + core, q))

    walk(steps[:1])
    for c in order:
        first(c).wait_recv()
        @pl.loop(0, ns)
        def _(t):
            pair[c, t] = (pair[c, t].astype(F32) + g_ref[c * 2 + core, t].astype(F32)).astype(BF)
        first_small(c).wait_recv()
        spair[c] = spair[c] + sm_ref[c * 2 + core]
        if c is not chip:
            second(c, chip).start()
            second_small(c, chip).start()
    walk(steps[1:middle])

    for c in chips:
        second(c, c).wait_recv()
        second_small(c, c).wait_recv()
    @pl.loop(0, ns)
    def _(t):
        total = pair[chip, t].astype(F32)
        for c in chips:
            total = total + plane[c, t].astype(F32)
        pair[chip, t] = total.astype(BF)
    small = spair[chip]
    for c in chips:
        small = small + splane[c]
    ssum[...] = small

    def third(t, src):
        return send(pair.at[chip, t], f_ref.at[src], sc.at[t], rc.at[src], (d, t))

    last = send(ssum, so_ref, tc, rc2, final_to)
    @pl.when(stays)
    def _():
        so_ref[...] = ssum[...]
    @pl.when(jnp.logical_not(stays))
    def _():
        last.start()
    for t in others:
        third(t, q).start()
    f_ref[q] = pair[chip, q]
    walk(steps[middle:])

    for s in range(nsub):
        total = gm_ref[q, s].astype(F32)
        out_ref[s] = total
        @pl.when(q > 0)
        def _():
            rise(q, s, gm_ref.at[q, s]).wait_recv()
            out_ref[s] += up[q, s].astype(F32)
        @pl.when(q < ns - 1)
        def _():
            sink(q, s, gm_ref.at[q, s]).wait_recv()
            out_ref[s] += down[q, s].astype(F32)
    for t in others:
        third(t, t).wait_recv()
    @pl.when(jnp.logical_not(stays))
    def _():
        last.wait_recv()
        last.wait_send()
    for c in order:
        first(c).wait_send()
        first_small(c).wait_send()
    for c in chips:
        second(c, chip).wait_send()
        second_small(c, chip).wait_send()
    for t in others:
        third(t, q).wait_send()
    for k, s in steps:
        t = ns - 1 - k
        @pl.when(q < t)
        def _():
            rise(t, s, gm_ref.at[t, s]).wait_send()
        @pl.when(q > k)
        def _():
            sink(k, s, gm_ref.at[k, s]).wait_send()


def home(g, small, gm, nd, ns, cid):
    rows, cols = g.shape[2:]
    nc, nsub = nd // 2, 4
    length, width = gm.shape
    part = length // ns // nsub
    v = small.shape[1:]
    gm = gm.reshape(ns, nsub, part, width)
    f, so, out = pl.pallas_call(
        functools.partial(home_kernel, nd, ns, nsub),
        out_shape=[
            jax.ShapeDtypeStruct((ns, rows, cols), BF),
            jax.ShapeDtypeStruct(v, F32),
            jax.ShapeDtypeStruct((nsub, part, width), F32),
        ],
        in_specs=[VMEM] * 3, out_specs=[VMEM] * 3,
        scratch_shapes=[
            pltpu.VMEM((nc, ns, rows, cols), BF), pltpu.VMEM((nc, ns, rows, cols), BF),
            pltpu.VMEM((nc,) + v, F32), pltpu.VMEM((nc,) + v, F32), pltpu.VMEM(v, F32),
            pltpu.VMEM((ns, nsub, part, width), BF), pltpu.VMEM((ns, nsub, part, width), BF),
            DMA((nc,)), DMA((nc,)), DMA((nc,)), DMA((nc,)), DMA((ns,)), DMA((ns,)),
            DMA((nc,)), DMA((nc,)), DMA((nc,)), DMA((nc,)), DMA(()), DMA(()),
            DMA((ns, nsub)), DMA((ns, nsub)), DMA((ns, nsub)), DMA((ns, nsub)),
        ],
        compiler_params=pltpu.CompilerParams(
            collective_id=cid, has_side_effects=True, vmem_limit_bytes=56 * 2**20),
        name="home",
    )(g, small, gm)
    return f, so, out.reshape(length // ns, width)


def start_kernel(nd, ns, nsub, hid, win, wout, pack, mask, emb, modw, modb,
                 hid_o, wx_o, pack_o, mask_o, mod_o,
                 eland, prod, rowp, land1, land2,
                 su, ru, sd, rd, swz, rw, swp, swm, spz, rp, spp, spm, sk, rk, se, re, s1, r1, s2, r2, own):
    d, q = lax.axis_index("dp"), lax.axis_index("seq")
    nc = nd // 2
    chip, core = d // 2, lax.rem(d, 2)
    mate = (chip * 2 + 1 - core, q)
    chips = [lax.rem(chip + k, nc) for k in range(1, nc)]
    others = [lax.rem(q + k, ns) for k in range(1, ns)]
    peers = [lax.rem(d + k, nd) for k in range(1, nd)]
    spread = nd // ns
    me = d * ns + q
    part = wout.shape[1] // ns
    greet([(d, t) for t in others] + [(e, q) for e in peers])

    def column(ref, at):
        return ref.at[:, pl.ds(pl.multiple_of(at * part, 128), part)]

    def pieces(t):
        return (column(win, t), column(win, ns + t), column(wout, t))

    def across(k, t, idx):
        return [
            send(src, wx_o.at[idx, :, j * part:(j + 1) * part], swz.at[k, j], rw.at[idx, j], (d, t))
            for j, src in enumerate(pieces(t))
        ]

    for k, t in enumerate(others):
        for copy in across(k, t, me):
            copy.start()
    keep = [pltpu.make_async_copy(src, wx_o.at[me, :, j * part:(j + 1) * part], own.at[j])
            for j, src in enumerate(pieces(q))]
    keep.append(pltpu.make_async_copy(hid, hid_o.at[q], own.at[3]))
    for copy in keep:
        copy.start()

    plane = d // spread
    slot = lax.rem(d, spread) * ns + q
    pack_z = send(pack, pack_o.at[slot], spz, rp.at[slot], (d, plane))
    pack_own = pltpu.make_async_copy(pack, pack_o.at[slot], own.at[4])

    @pl.when(plane == q)
    def _():
        pack_own.start()

    @pl.when(plane != q)
    def _():
        pack_z.start()

    def masks(k, t, src):
        return send(mask_o.at[src], mask_o.at[src], sk.at[k], rk.at[src], (d, t))

    def embeds(k, e, src):
        return send(eland.at[src], eland.at[src], se.at[k], re.at[src], (e, q))

    mask_o[q] = mask[...]
    eland[d] = emb[...]
    for k, e in enumerate(peers):
        embeds(k, e, d).start()
    for k, t in enumerate(others):
        masks(k, t, q).start()

    def rise(k, s):
        t = jnp.maximum(q - k, 0)
        src = hid.at[s] if k == 0 else hid_o.at[t, s]
        return send(src, hid_o.at[t, s], su.at[k, s], ru.at[k, s], (d, q + 1))

    def sink(k, s):
        t = jnp.minimum(q + k, ns - 1)
        src = hid.at[s] if k == 0 else hid_o.at[t, s]
        return send(src, hid_o.at[t, s], sd.at[k, s], rd.at[k, s], (d, q - 1))

    def hop(k, s):
        @pl.when(q >= k)
        def _():
            if k:
                rise(k - 1, s).wait_recv()
            if k < ns - 1:
                @pl.when(q + 1 < ns)
                def _():
                    rise(k, s).start()

        @pl.when(q + k < ns)
        def _():
            if k:
                sink(k - 1, s).wait_recv()
            if k < ns - 1:
                @pl.when(q >= 1)
                def _():
                    sink(k, s).start()

    for s in range(nsub):
        hop(0, s)

    def piece(ref, idx):
        return ref.at[idx]

    def plane_w(c, idx, t):
        return send(wx_o.at[idx], wx_o.at[idx], swp.at[c, t], rwp_of(idx), (c * 2 + core, q))

    def rwp_of(idx):
        return rw.at[idx, 3]

    def mate_w(c, idx, t):
        return send(wx_o.at[idx], wx_o.at[idx], swm.at[c, t], rwp_of(idx), mate)

    def spread_w(t):
        idx = d * ns + t
        for c in chips:
            plane_w(c, idx, t).start()
        mate_w(chip, idx, t).start()

    for copy in keep[:3]:
        copy.wait()
    spread_w(q)

    for k, e in enumerate(peers):
        embeds(k, e, e).wait_recv()
    rows = modw.shape[0]
    here = lax.broadcasted_iota(jnp.int32, (FREQ, rows), 0)
    pick = here - lax.broadcasted_iota(jnp.int32, (FREQ, rows), 1)
    count = FREQ // (nd * ns)
    keep_col = lax.broadcasted_iota(jnp.int32, (FREQ, rows), 1) < count
    pick = jnp.where(jnp.logical_and(pick == me * count, keep_col), 1.0, 0.0).astype(BF)
    mine = jnp.dot(eland[...].reshape(nd * 16, FREQ), pick, preferred_element_type=F32).astype(BF)
    prod[...] = jnp.dot(mine, modw[...], preferred_element_type=F32)

    lines = prod.shape[1] // 128
    @pl.loop(0, nd)
    def _(e):
        rowp[e] = modb[...]
        for j in range(lines):
            rowp[e, j:j + 1, :] += prod[pl.ds(pl.multiple_of(e * 16, 16), 1), j * 128:(j + 1) * 128]

    def to_item(k, e, src):
        return send(rowp.at[e], land1.at[src], s1.at[k], r1.at[src], (e, q))

    for k, e in enumerate(peers):
        to_item(k, e, d).start()

    for k, t in enumerate(others):
        for copy in across(k, t, d * ns + t):
            copy.wait_recv()
        spread_w(t)

    def plane_p(c, i, t):
        return send(pack_o.at[i], pack_o.at[i], spp.at[c, t], rp.at[i], (c * 2 + core, q))

    def mate_p(c, i, t):
        return send(pack_o.at[i], pack_o.at[i], spm.at[c, t], rp.at[i], mate)

    base = lax.rem(d, spread) * ns

    @pl.when(plane == q)
    def _():
        pack_own.wait()
        for t in others:
            send(pack, pack_o.at[base + t], spz, rp.at[base + t], (d, plane)).wait_recv()
        for t in range(ns):
            for c in chips:
                plane_p(c, base + t, t).start()
            mate_p(chip, base + t, t).start()

    total = rowp[d]
    for k, e in enumerate(peers):
        to_item(k, e, e).wait_recv()
        total = total + land1[e]
    land2[q] = total

    def to_column(k, t, src):
        return send(land2.at[src], land2.at[src], s2.at[k], r2.at[src], (d, t))

    for k, t in enumerate(others):
        to_column(k, t, q).start()

    def relay_w(c, t):
        idx = (c * 2 + core) * ns + t
        plane_w(c, idx, t).wait_recv()
        mate_w(c, idx, t).start()

    def holds(c):
        return (c * 2 + core) // spread == q

    def relay_p(c):
        first = lax.rem(c * 2 + core, spread) * ns
        @pl.when(holds(c))
        def _():
            for t in range(ns):
                plane_p(c, first + t, t).wait_recv()
                mate_p(c, first + t, t).start()

    hops = [(k, s) for k in range(1, ns) for s in range(nsub)]
    relays = [(c, t) for t in [q] + others for c in chips]
    at = 0
    for i, (k, s) in enumerate(hops):
        upto = len(relays) * (i + 1) // len(hops)
        hop(k, s)
        for c, t in relays[at:upto]:
            relay_w(c, t)
        at = upto
    for c in chips:
        relay_p(c)
    for k, t in enumerate(others):
        to_column(k, t, t).wait_recv()
    total = land2[0]
    for t in range(1, ns):
        total = total + land2[t]
    mod_o[...] = total

    twin = 1 - core
    for c in range(nc):
        for t in range(ns):
            idx = (c * 2 + twin) * ns + t
            mate_w(c, idx, t).wait_recv()
        first = lax.rem(c * 2 + twin, spread) * ns
        @pl.when((c * 2 + twin) // spread == q)
        def _():
            for t in range(ns):
                mate_p(c, first + t, t).wait_recv()
    for k, t in enumerate(others):
        masks(k, t, t).wait_recv()
    keep[3].wait()

    for k, t in enumerate(others):
        for copy in across(k, t, me):
            copy.wait_send()
        masks(k, t, q).wait_send()
        to_column(k, t, q).wait_send()
    for k, e in enumerate(peers):
        embeds(k, e, d).wait_send()
        to_item(k, e, d).wait_send()

    @pl.when(plane != q)
    def _():
        pack_z.wait_send()

    @pl.when(plane == q)
    def _():
        for t in range(ns):
            for c in chips:
                plane_p(c, base + t, t).wait_send()
            mate_p(chip, base + t, t).wait_send()

    for t in range(ns):
        for c in chips:
            plane_w(c, d * ns + t, t).wait_send()
            mate_w(c, (c * 2 + core) * ns + t, t).wait_send()
        mate_w(chip, d * ns + t, t).wait_send()
    for c in chips:
        first = lax.rem(c * 2 + core, spread) * ns
        @pl.when(holds(c))
        def _():
            for t in range(ns):
                mate_p(c, first + t, t).wait_send()
    for k in range(ns - 1):
        for s in range(nsub):
            @pl.when(jnp.logical_and(q >= k, q + 1 < ns))
            def _():
                rise(k, s).wait_send()
            @pl.when(jnp.logical_and(q + k < ns, q >= 1))
            def _():
                sink(k, s).wait_send()


def start(hidden, mask, win, wout, pack, embedded, modw, modb, nd, ns, cid):
    nsub = 4
    length, width = hidden.shape
    rows, inner = wout.shape
    nc = nd // 2
    hidden = hidden.reshape(nsub, length // nsub, width)
    lines = modb.shape
    return pl.pallas_call(
        functools.partial(start_kernel, nd, ns, nsub),
        out_shape=[
            jax.ShapeDtypeStruct((ns,) + hidden.shape, BF),
            jax.ShapeDtypeStruct((nd * ns, rows, 3 * inner // ns), BF),
            jax.ShapeDtypeStruct((nd,) + pack.shape, BF),
            jax.ShapeDtypeStruct((ns,) + mask.shape, BF),
            jax.ShapeDtypeStruct(lines, F32),
        ],
        in_specs=[HBM, HBM, HBM, HBM, VMEM, VMEM, VMEM, VMEM],
        out_specs=[HBM, HBM, HBM, VMEM, VMEM],
        scratch_shapes=[
            pltpu.VMEM((nd,) + embedded.shape, BF), pltpu.VMEM((nd * 16, modw.shape[1]), F32),
            pltpu.VMEM((nd,) + lines, F32), pltpu.VMEM((nd,) + lines, F32), pltpu.VMEM((ns,) + lines, F32),
            DMA((ns - 1, nsub)), DMA((ns - 1, nsub)), DMA((ns - 1, nsub)), DMA((ns - 1, nsub)),
            DMA((ns, 3)), DMA((nd * ns, 4)), DMA((nc, ns)), DMA((nc, ns)),
            DMA(()), DMA((nd,)), DMA((nc, ns)), DMA((nc, ns)),
            DMA((ns,)), DMA((ns,)), DMA((nd,)), DMA((nd,)),
            DMA((nd,)), DMA((nd,)), DMA((ns,)), DMA((ns,)), DMA((5,)),
        ],
        compiler_params=pltpu.CompilerParams(
            collective_id=cid, has_side_effects=True, vmem_limit_bytes=40 * 2**20),
        name="start",
    )(hidden, win, wout, pack, mask, embedded, modw, modb)


def end_kernel(nd, ns, nsub, rows, turned,
               gp_h, md_h, wx_h, sm_ref, hid_ref, cot_ref, line_ref, early,
               gin_o, gout_o, so_ref, gh_o, mod_o,
               gp, md, wx, gm, made, pair, plane, spair, splane, ssum, fro, ready, up, down, own, acc, msg, mland,
               ld, sa, ra, sb, rb, sc, rc, se, re, ta, ra2, tb, rb2, tc, rc2, su, ru, sd, rd, s1, r1, s2, r2):
    d, q = lax.axis_index("dp"), lax.axis_index("seq")
    nc = nd // 2
    chip, core = d // 2, lax.rem(d, 2)
    mate = chip * 2 + 1 - core
    pairs = [(1, 1), (1, 0), (0, 1)] + [(a, b) for b in range(2, nc // 2) for a in (0, 1)]
    chips = [lax.rem(chip + a, 2) + 2 * lax.rem(chip // 2 + b, nc // 2) for a, b in pairs]
    others = [lax.rem(q + k, ns) for k in range(1, ns)]
    peers = [lax.rem(d + k, nd) for k in range(1, nd)]
    spread = nd // ns
    final_to = (spread * q + d // ns, lax.rem(d, ns))
    me = d * ns + q
    final_from = (lax.rem(me, nd), me // nd)
    stays = jnp.logical_and(final_to[0] == d, final_to[1] == q)
    length, cols = gp.shape
    part = cols // 2
    width = wx.shape[0]
    local = length // ns
    sub = local // nsub
    rw = pair.shape[2]
    half = ns * rw

    loads = [pltpu.make_async_copy(src, dst, ld.at[i]) for i, (src, dst) in enumerate(
        ((gp_h, gp), (wx_h.at[:, 0:cols], wx), (md_h, md)))]
    for copy in loads:
        copy.start()

    bar = pltpu.get_barrier_semaphore()
    friends = [(e, q) for e in peers] + [(d, t) for t in others]
    for to in friends:
        pl.semaphore_signal(bar, inc=1, device_id=to, device_id_type=MESH)
    @pl.when(jnp.logical_not(stays))
    def _():
        pl.semaphore_signal(bar, inc=1, device_id=final_from, device_id_type=MESH)

    def tokens(t):
        @pl.loop(0, width // 512)
        def _(j):
            here = pl.ds(pl.multiple_of(j * 512, 512), 512)
            full = lax.dot_general(gp[t * local:(t + 1) * local, :], wx[here, :], NT, preferred_element_type=F32)
            full = full.astype(BF)
            for s in range(nsub):
                gm[t, s, :, here] = full[s * sub:(s + 1) * sub]

    def rise(t, s, src):
        return send(src, up.at[t, s], su.at[t, s], ru.at[t, s], (d, q + 1))

    def sink(t, s, src):
        return send(src, down.at[t, s], sd.at[t, s], rd.at[t, s], (d, q - 1))

    def added(land, t, s):
        land[t, s] = (land[t, s].astype(F32) + gm[t, s].astype(F32)).astype(BF)

    def open_up(t, s):
        @pl.when(jnp.logical_and(q == 0, t > 0))
        def _():
            rise(t, s, gm.at[t, s]).start()

    def open_down(t, s):
        @pl.when(jnp.logical_and(q == ns - 1, t < ns - 1))
        def _():
            sink(t, s, gm.at[t, s]).start()

    def step(k, s):
        t = ns - 1 - k

        @pl.when(jnp.logical_and(q < t, q > 0))
        def _():
            rise(t, s, up.at[t, s]).wait_recv()
            added(up, t, s)
            rise(t, s, up.at[t, s]).start()

        @pl.when(jnp.logical_and(q > k, q < ns - 1))
        def _():
            sink(k, s, down.at[k, s]).wait_recv()
            added(down, k, s)
            sink(k, s, down.at[k, s]).start()

    def far(k):
        for t in sorted({ns - 1 - k, k}, reverse=True):
            tokens(t)
            for s in range(nsub):
                open_up(t, s)
                open_down(t, s)

    @pl.when(stays)
    def _():
        pl.semaphore_wait(bar, len(friends))

    @pl.when(jnp.logical_not(stays))
    def _():
        pl.semaphore_wait(bar, len(friends) + 1)

    def whole(t, src):
        return send(early.at[t], ready.at[src], se.at[t], re.at[src], (d, t))

    for t in others:
        whole(t, q).start()
    loads[0].wait()
    loads[1].wait()
    far(0)
    steps = [(k, s) for k in range(ns - 1) for s in range(nsub)]

    def first(c):
        return send(made.at[c, 1 - core], pair.at[c], sa.at[c], ra.at[c], (mate, q))

    def first_small(c):
        return send(sm_ref.at[c * 2 + 1 - core], spair.at[c], ta.at[c], ra2.at[c], (mate, q))

    def second(c, src):
        return send(pair.at[c], plane.at[src], sb.at[c], rb.at[src], (c * 2 + core, q))

    def second_small(c, src):
        return send(spair.at[c], splane.at[src], tb.at[c], rb2.at[src], (c * 2 + core, q))

    def block(c):
        at = pl.ds(pl.multiple_of(c * 2 * half, 2 * half), 2 * half)
        tile = part if part % 256 else part // 2
        left = md[at, :] if turned else md[:, at].T

        @pl.loop(0, part // tile)
        def _(j):
            n = pl.ds(pl.multiple_of(j * tile, 128), tile)
            full = jnp.dot(left, gp[:, n], preferred_element_type=F32).astype(BF)
            for h in range(2):
                for t in range(ns):
                    line = (h * ns + t) * rw
                    made[c, h, t, :, n] = full[line:line + rw]

    loads[2].wait()
    order = chips + [chip]

    def give(c):
        block(c)
        first(c).start()
        first_small(c).start()

    give(order[0])
    for k in range(1, ns // 2):
        far(k)
    for i, c in enumerate(order):
        if i + 1 < nc:
            give(order[i + 1])
        first(c).wait_recv()
        @pl.loop(0, ns)
        def _(t):
            pair[c, t] = (pair[c, t].astype(F32) + made[c, core, t].astype(F32)).astype(BF)
        first_small(c).wait_recv()
        spair[c] = spair[c] + sm_ref[c * 2 + core]
        if i < nc - 1:
            second(c, chip).start()
            second_small(c, chip).start()
        for k, s in steps[i:i + 1]:
            step(k, s)
    late = len(steps) * 3 // 4
    for k, s in steps[nc:late]:
        step(k, s)

    for c in chips:
        second(c, c).wait_recv()
        second_small(c, c).wait_recv()
    @pl.loop(0, ns)
    def _(t):
        total = pair[chip, t].astype(F32)
        for c in chips:
            total = total + plane[c, t].astype(F32)
        pair[chip, t] = total.astype(BF)
    small = spair[chip]
    for c in chips:
        small = small + splane[c]
    ssum[...] = small

    def third(t, src):
        return send(pair.at[chip, t], fro.at[src], sc.at[t], rc.at[src], (d, t))

    last = send(ssum, so_ref, tc, rc2, final_to)
    @pl.when(stays)
    def _():
        so_ref[...] = ssum[...]
    @pl.when(jnp.logical_not(stays))
    def _():
        last.start()
    for t in others:
        third(t, q).start()
    fro[q] = pair[chip, q]
    for k, s in steps[max(nc, late):]:
        step(k, s)

    acc[...] = jnp.zeros(acc.shape, F32)
    acc[2:4, :] = line_ref[1:3, :]
    scale = 1.0 + line_ref[0:1, :]
    for s in range(nsub):
        own[...] = gm[q, s].astype(F32)

        @pl.when(q > 0)
        def _():
            rise(q, s, gm.at[q, s]).wait_recv()
            own[...] += up[q, s].astype(F32)

        @pl.when(q < ns - 1)
        def _():
            sink(q, s, gm.at[q, s]).wait_recv()
            own[...] += down[q, s].astype(F32)

        @pl.loop(0, sub // 16)
        def _(r):
            here = pl.ds(pl.multiple_of(r * 16, 16), 16)
            grad = own[here, :]
            x = hid_ref[s, here, :].astype(F32)
            x = x - jnp.mean(x, axis=1, keepdims=True)
            inverse = lax.rsqrt(jnp.mean(x * x, axis=1, keepdims=True) + EPS)
            normed = x * inverse
            acc[0:1, :] += jnp.sum(grad, axis=0, keepdims=True)
            acc[1:2, :] += jnp.sum(grad * normed, axis=0, keepdims=True)
            grad = grad * scale
            grad = grad - jnp.mean(grad, axis=1, keepdims=True) - normed * jnp.mean(
                grad * normed, axis=1, keepdims=True)
            gh_o[s, here, :] = (cot_ref[s, here, :].astype(F32) + inverse * grad).astype(BF)

    msg[...] = jnp.zeros(msg.shape, F32)
    long = msg.shape[1] // 128
    for i in range(3 * width // 128 + FREQ // 128):
        r, c = divmod(i * 128, width)
        to = (i % long) * 128
        msg[i // long:i // long + 1, to:to + 128] = acc[r:r + 1, c:c + 128]
    for k, t in enumerate(others):
        send(msg, mland.at[q], s1.at[k], r1.at[q], (d, t)).start()

    inner = part * ns

    def place(src, rest):
        at = src * part
        gin_o[:, pl.ds(pl.multiple_of(at, 128), part)] = fro[src, 0:rows, :].astype(F32)
        gin_o[:, pl.ds(pl.multiple_of(inner + at, 128), part)] = rest[0:rows, 0:part].astype(F32)
        gout_o[:, pl.ds(pl.multiple_of(at, 128), part)] = rest[0:rows, part:2 * part].astype(F32)

    place(q, early[q])
    total = msg[...]
    for k, t in enumerate(others):
        send(msg, mland.at[t], s1.at[k], r1.at[t], (d, t)).wait_recv()
        total = total + mland[t]
    mod_o[d] = total
    for k, e in enumerate(peers):
        send(mod_o.at[d], mod_o.at[d], s2.at[k], r2.at[d], (e, q)).start()
    for t in others:
        third(t, t).wait_recv()
        whole(t, t).wait_recv()
        place(t, ready[t])
    for k, e in enumerate(peers):
        send(mod_o.at[e], mod_o.at[e], s2.at[k], r2.at[e], (e, q)).wait_recv()
    @pl.when(jnp.logical_not(stays))
    def _():
        last.wait_recv()
        last.wait_send()

    for c in order:
        first(c).wait_send()
        first_small(c).wait_send()
    for c in chips:
        second(c, chip).wait_send()
        second_small(c, chip).wait_send()
    for k, t in enumerate(others):
        third(t, q).wait_send()
        whole(t, q).wait_send()
        send(msg, mland.at[q], s1.at[k], r1.at[q], (d, t)).wait_send()
    for k, e in enumerate(peers):
        send(mod_o.at[d], mod_o.at[d], s2.at[k], r2.at[d], (e, q)).wait_send()
    for k, s in steps:
        t = ns - 1 - k
        @pl.when(q < t)
        def _():
            rise(t, s, gm.at[t, s]).wait_send()
        @pl.when(q > k)
        def _():
            sink(k, s, gm.at[k, s]).wait_send()


def end(grad_projected, modded, wx, early, small, hidden, cot, line, rows, nd, ns, cid):
    length, cols = grad_projected.shape
    part = cols // 2
    width = wx.shape[0]
    inner = part * ns
    nc, nsub = nd // 2, 4
    local = length // ns
    sub = local // nsub
    rw = rows + -rows % 16
    half = ns * rw
    turned = 2 * half % 128 != 0 or rw != rows
    if turned:
        def turn(a):
            a = a.T.reshape(nd * ns, rows, length)
            return jnp.pad(a, ((0, 0), (0, rw - rows), (0, 0))).reshape(nd * ns * rw, length)
        modded = turn(modded)
    early = jnp.pad(early.reshape(ns, rows, cols), ((0, 0), (0, rw - rows), (0, 0)))
    short = -(-(3 * width + FREQ) // 1024) * 128
    v = small.shape[1:]
    hidden, cot = hidden.reshape(nsub, sub, width), cot.reshape(nsub, sub, width)
    blocks = pltpu.VMEM((nc, ns, rw, part), BF)
    smalls = pltpu.VMEM((nc,) + v, F32)
    runs = pltpu.VMEM((ns, nsub, sub, width), BF)
    gin, gout, so, gh, mod = pl.pallas_call(
        functools.partial(end_kernel, nd, ns, nsub, rows, turned),
        out_shape=[
            jax.ShapeDtypeStruct((rows, 2 * inner), F32),
            jax.ShapeDtypeStruct((rows, inner), F32),
            jax.ShapeDtypeStruct(v, F32),
            jax.ShapeDtypeStruct((nsub, sub, width), BF),
            jax.ShapeDtypeStruct((nd, 8, short), F32),
        ],
        in_specs=[HBM] * 3 + [VMEM] * 5, out_specs=[VMEM] * 5,
        scratch_shapes=[
            pltpu.VMEM(grad_projected.shape, BF), pltpu.VMEM(modded.shape, BF), pltpu.VMEM((width, cols), BF), runs,
            pltpu.VMEM((nc, 2, ns, rw, part), BF), blocks, blocks,
            smalls, smalls, pltpu.VMEM(v, F32), pltpu.VMEM((ns, rw, part), BF), pltpu.VMEM((ns, rw, cols), BF), runs, runs,
            pltpu.VMEM((sub, width), F32), pltpu.VMEM((8, width), F32), pltpu.VMEM((8, short), F32),
            pltpu.VMEM((ns, 8, short), F32),
            DMA((3,)),
            DMA((nc,)), DMA((nc,)), DMA((nc,)), DMA((nc,)), DMA((ns,)), DMA((ns,)), DMA((ns,)), DMA((ns,)),
            DMA((nc,)), DMA((nc,)), DMA((nc,)), DMA((nc,)), DMA(()), DMA(()),
            DMA((ns, nsub)), DMA((ns, nsub)), DMA((ns, nsub)), DMA((ns, nsub)),
            DMA((ns,)), DMA((ns,)), DMA((nd,)), DMA((nd,)),
        ],
        compiler_params=pltpu.CompilerParams(
            collective_id=cid, has_side_effects=True, vmem_limit_bytes=60 * 2**20),
        name="end",
    )(grad_projected, modded, wx, small, hidden, cot, line, early)
    return gin, gout, so, gh.reshape(local, width), mod


def frequency_embed(timestep):
    half_width = FREQ // 2
    counter = jnp.arange(half_width, dtype=F32)
    frequency = jnp.exp(counter * (-math.log(10000.0) / half_width))
    angles = timestep.astype(F32)[:, None] * frequency[None, :]
    return jnp.concatenate([jnp.cos(angles), jnp.sin(angles)], axis=1)


def dot(a, b):
    return jnp.dot(a, b, preferred_element_type=F32)


def dot_nt(a, b):
    return lax.dot_general(a, b, (((1,), (1,)), ((), ())), preferred_element_type=F32)


def dot_tn(a, b):
    return lax.dot_general(a, b, (((0,), (0,)), ((), ())), preferred_element_type=F32)


def body(
    hidden,
    pad_mask,
    timestep,
    input_weight,
    select_weight,
    step_weight,
    output_weight,
    decay_forward,
    decay_reverse,
    filter_weight,
    filter_bias,
    step_bias,
    modulation_weight,
    modulation_bias,
    cotangent,
):
    ns, nd = lax.axis_size("seq"), lax.axis_size("dp")
    q, d = lax.axis_index("seq"), lax.axis_index("dp")
    every = ("dp", "seq")
    local_len, width = hidden.shape[1:]
    length = local_len * ns
    inner = output_weight.shape[0]
    part = inner // ns
    rank = step_weight.shape[0]
    state = decay_forward.shape[1]
    taps = filter_weight.shape[0]
    rows_in = input_weight.shape[0]
    lanes = select_weight.shape[1]

    units = part // nd
    embedded = jax.nn.silu(frequency_embed(timestep)).astype(BF)
    fil = jnp.concatenate([filter_weight, filter_bias[None], step_bias[None]])
    fil = jnp.pad(fil, ((0, 16 - fil.shape[0]), (0, lanes - units)))
    mid = jnp.concatenate([step_weight.T, decay_forward, decay_reverse], axis=1)
    pack = jnp.concatenate([select_weight, mid, fil])
    mask = jnp.pad(pad_mask[0].astype(BF).reshape(-1, 128), ((0, 16 - local_len // 128), (0, 0)))
    shard = (-modulation_weight.shape[0] % 16, 0)
    modb = jnp.zeros((-(-3 * width // 1024) * 1024,), F32)
    modb = lax.dynamic_update_slice(modb, modulation_bias.astype(F32), ((d * ns + q) * modulation_bias.shape[0],))
    row_pad = ((0, -rows_in % 16), (0, 0))
    hid, wx, pack, mask, modulation = start(
        hidden[0], mask, jnp.pad(input_weight, row_pad), jnp.pad(output_weight.T, row_pad), pack,
        jnp.pad(embedded, ((0, 15), (0, 0))),
        jnp.pad(modulation_weight, ((0, shard[0]), (0, 0))), modb.reshape(-1, 128), nd, ns, 4)
    hid = hid.reshape(length, width)
    wx = wx[:, :rows_in].reshape(width, 3 * part)
    win, wout = wx[:, : 2 * part], wx[:, 2 * part :]
    mask = mask[:, : local_len // 128].reshape(length, 1).astype(F32)
    select_q = pack[:, :units].reshape(part, lanes)
    mid = pack[:, units : 2 * units].reshape(part, lanes)
    step_q = mid[:, :rank].T
    log_f, log_r = mid[:, rank : rank + state], mid[:, rank + state :]
    fil = pack[:, 2 * units :, :units].transpose(1, 0, 2).reshape(16, part).astype(F32)
    filt32, fbias, sbias = fil[:taps].T, fil[taps][None], fil[taps + 1][None]
    modulation = modulation.reshape(1, -1)[:, : 3 * width]
    shifts = modulation[:, :width]
    scales = modulation[:, width : 2 * width]
    gate_scale = modulation[:, 2 * width :]

    def norm(x):
        x = x.astype(F32)
        centered = x - jnp.mean(x, axis=1, keepdims=True)
        inverse = lax.rsqrt(jnp.mean(centered * centered, axis=1, keepdims=True) + EPS)
        return centered * inverse, inverse

    modded = (norm(hid)[0] * (1.0 + scales) + shifts).astype(BF)
    projected = dot(modded, win)
    inner_part = projected[:, :part].astype(BF).astype(F32) * mask
    gate_branch = projected[:, part:]
    padded = jnp.pad(inner_part, ((taps - 1, 0), (0, 0)))
    filtered = fbias
    for k in range(taps):
        filtered = filtered + filt32[:, k][None, :] * padded[k : k + length]
    sigma_filter = jax.nn.sigmoid(filtered)
    active = (filtered * sigma_filter).astype(BF)
    active32 = active.astype(F32)
    selected = column_sum(dot(active, select_q).astype(BF), ns, BF, 0)
    cot, selected = lax.optimization_barrier((cotangent[0], selected))
    cot = lax.all_gather(cot, "seq", axis=0, tiled=True)
    low_rank = selected[:, :rank].astype(BF)
    b_rows = selected[:, rank : rank + state].astype(F32)
    c_rows = selected[:, rank + state :].astype(F32)
    pre_steps = dot(low_rank, step_q) + sbias
    steps = jax.nn.softplus(pre_steps)
    rates_f = -jnp.exp(log_f.astype(F32)).T
    rates_r = -jnp.exp(log_r.astype(F32)).T
    drive = steps * active32
    rates_f2, rates_r2 = rates_f * LOG2E, rates_r * LOG2E
    mixed_f, mixed_r, states_f, states_r = fwd_scan(steps, drive, rates_f2, rates_r2, b_rows.T, blockdiag(c_rows))
    merged = mixed_f + mixed_r
    sigma_gate = jax.nn.sigmoid(gate_branch)
    silu_gate = gate_branch * sigma_gate
    gated = (merged * silu_gate).astype(BF)
    branch = dot_nt(gated, wout).astype(BF)
    branch, cot = lax.optimization_barrier((branch, cot))
    branch = lax.psum_scatter(branch, "seq", scatter_dimension=0, tiled=True).astype(F32)

    mask_here = pad_mask[0].astype(F32)[:, None]
    cot_here = cotangent[0].astype(F32)
    block_out = (hidden[0].astype(F32) + gate_scale * mask_here * branch).astype(BF)
    grad_gate = jnp.sum(mask_here * cot_here * branch, axis=0)

    grad_branch = (cot.astype(F32) * gate_scale * mask).astype(BF)
    grad_gated = dot(grad_branch, wout)
    grad_merged = grad_gated * silu_gate
    grad_gate_branch = grad_gated * merged * sigma_gate * (1.0 + gate_branch * (1.0 - sigma_gate))
    grad_gate_branch = grad_gate_branch.astype(BF)
    early = jnp.concatenate([dot_tn(modded, grad_gate_branch), dot_tn(grad_branch, gated)], axis=1).astype(BF)
    early = lax.psum_scatter(early, "dp", scatter_dimension=0, tiled=True)
    dlog_f, dlog_r, adjb_f, adjb_r, bg_f, bg_r, cg_f, cg_r, rg_f, rg_r = bwd_scan(
        steps, drive.astype(BF), grad_merged, rates_f2, rates_r2, c_rows.T, blockdiag(b_rows), states_f, states_r)
    adjb = adjb_f + adjb_r
    grad_steps = (dlog_f + dlog_r) * (1.0 / LOG2E) + active32 * adjb
    grad_b = (bg_f + bg_r).reshape(length, state)
    grad_c = (cg_f + cg_r).reshape(length, state)
    grad_decay_f = rg_f * rates_f
    grad_decay_r = rg_r * rates_r
    grad_pre = grad_steps * jax.nn.sigmoid(pre_steps)
    grad_step_bias = jnp.sum(grad_pre, axis=0)
    grad_pre_low = grad_pre.astype(BF)
    grad_step_t = dot_tn(grad_pre_low, low_rank)
    grad_low_rank = dot_nt(grad_pre_low, step_q)
    grad_selected = column_sum(jnp.concatenate([grad_low_rank, grad_b, grad_c], axis=1).astype(BF), ns, BF, 1)
    grad_select = dot_tn(active, grad_selected)
    grad_active = steps * adjb + dot_nt(grad_selected, select_q)
    grad_filtered = grad_active * sigma_filter * (1.0 + filtered * (1.0 - sigma_filter))
    extended = jnp.pad(grad_filtered, ((0, taps - 1), (0, 0)))
    grad_inner = jnp.zeros_like(grad_filtered)
    filter_rows = []
    for k in range(taps):
        lead = taps - 1 - k
        grad_inner = grad_inner + filt32[:, k][None, :] * extended[lead : lead + length]
        filter_rows.append(jnp.sum(grad_filtered * padded[k : k + length], axis=0))
    grad_filter_bias = jnp.sum(grad_filtered, axis=0)
    grad_projected = jnp.concatenate([(grad_inner * mask).astype(BF), grad_gate_branch], axis=1)
    fil = jnp.stack(filter_rows + [grad_filter_bias, grad_step_bias])
    fil = fil.reshape(-1, nd, units).transpose(1, 0, 2)
    fil = jnp.pad(fil, ((0, 0), (0, 16 - fil.shape[1]), (0, lanes - units)))
    mid = jnp.concatenate([grad_step_t, grad_decay_f.T, grad_decay_r.T], axis=1)
    small = jnp.concatenate([grad_select.reshape(nd, units, lanes), mid.reshape(nd, units, lanes), fil], axis=1)
    line = jnp.concatenate([scales, grad_gate[None], jnp.pad(embedded.astype(F32) / ns, ((0, 0), (0, width - FREQ))),
                            jnp.zeros((5, width), F32)])
    g_in, g_out, small, grad_hidden, sums = end(
        grad_projected, modded, wx, early, small, hidden[0], cotangent[0], line, rows_in, nd, ns, 2)
    gs_select = small[:units]
    mid = small[units : 2 * units]
    gs_step, gs_f, gs_r = mid[:, :rank], mid[:, rank : rank + state], mid[:, rank + state :]
    fil = small[2 * units :, :units]

    sums = sums.reshape(nd, -1)
    embeds = sums[:, 3 * width : 3 * width + FREQ]
    grad_mod = sums[:, : 3 * width]
    me = d * ns + q
    mine = lax.dynamic_slice_in_dim(embeds, me * modulation_weight.shape[0], modulation_weight.shape[0], 1)
    g_modw = lax.dot_general(mine, grad_mod, (((0,), (0,)), ((), ())), precision=HIGHEST)
    g_modb = lax.dynamic_slice_in_dim(
        jnp.sum(grad_mod, axis=0), me * modulation_bias.shape[0], modulation_bias.shape[0], 0)
    return (
        block_out[None],
        grad_hidden[None],
        g_in,
        gs_select,
        gs_step.T,
        g_out.T,
        gs_f,
        gs_r,
        fil[:taps],
        fil[taps],
        fil[taps + 1],
        g_modw,
        g_modb,
    )


def solution(mesh):
    return jax.shard_map(
        body,
        mesh=mesh,
        in_specs=(
            P("dp", "seq", None),
            P("dp", "seq"),
            P("dp"),
            P(("dp", "seq"), None),
            P(("dp", "seq"), None),
            P(None, ("dp", "seq")),
            P(None, ("dp", "seq")),
            P(("dp", "seq"), None),
            P(("dp", "seq"), None),
            P(None, ("dp", "seq")),
            P(("dp", "seq")),
            P(("dp", "seq")),
            P(("dp", "seq"), None),
            P(("dp", "seq")),
            P("dp", "seq", None),
        ),
        out_specs=(
            P("dp", "seq", None),
            P("dp", "seq", None),
            P(("dp", "seq"), None),
            P(("dp", "seq"), None),
            P(None, ("dp", "seq")),
            P(None, ("dp", "seq")),
            P(("dp", "seq"), None),
            P(("dp", "seq"), None),
            P(None, ("dp", "seq")),
            P(("dp", "seq")),
            P(("dp", "seq")),
            P(("dp", "seq"), None),
            P(("dp", "seq")),
        ),
        check_vma=False,
    )
```

```python
import functools
import math

import jax
import jax.numpy as jnp
from jax import lax
from jax.experimental import pallas as pl
from jax.experimental.layout import Layout, with_layout_constraint
from jax.experimental.pallas import tpu as pltpu
from jax.sharding import PartitionSpec as P

FREQ = 256
EPS = 1e-06
HIGHEST = lax.Precision.HIGHEST
LOG2E = 1.4426950408889634
SUB = 16
WF = 384
WB = 768
F32, BF = jnp.float32, jnp.bfloat16
NT = (((1,), (1,)), ((), ()))


def columns_of(rows_t, base):
    turned = pltpu.roll(rows_t, rows_t.shape[1] - base, 1)
    return [jnp.broadcast_to(turned[:, j:j + 1], (rows_t.shape[0], 128)) for j in range(SUB)]


def wide(block, lanes):
    return jnp.concatenate([block] * (lanes // 128), axis=1) if lanes > 128 else block


def states_of(base, at):
    return pl.ds(pl.multiple_of((base + at) * 16, 16), 16)


def fwd_kernel(step_f, step_r, u_f, u_r, rate_f, rate_r, bt_f, bt_r, cblk_f, cblk_r,
               y_f, y_r, s_f, s_r, carry, f0, f1, r0, r1):
    rows, lanes = step_f.shape

    @pl.when(pl.program_id(0) == 0)
    def _():
        carry[...] = jnp.zeros(carry.shape, F32)

    wide_by = min(WF, lanes)
    cuts = [slice(c, c + wide_by) for c in range(0, lanes, wide_by)]

    def walk(states, bases, kept):
        cols = [columns_of(bt[...], base) for bt, base in zip((bt_f, bt_r), bases)]
        out = []
        for cut, pair in zip(cuts, states):
            pair = list(pair)
            rates = rate_f[:, cut], rate_r[:, cut]
            for k in range(SUB):
                for z, (step, u, s, j) in enumerate(((step_f, u_f, s_f, k), (step_r, u_r, s_r, SUB - 1 - k))):
                    at = pl.ds(bases[z] + j, 1)
                    decay = jnp.exp2(step[at, cut] * rates[z])
                    pair[z] = decay * pair[z] + u[at, cut] * wide(cols[z][j], wide_by)
                    low = pair[z].astype(BF)
                    s[states_of(bases[z], j), cut] = low
                    kept[z][j * 16:(j + 1) * 16, cut] = low
            out.append(tuple(pair))
        return tuple(out)

    def mix(base, cblk, kept, y):
        here = pl.ds(base, SUB)
        y[here, :] = jnp.dot(cblk[here, :], kept[...], preferred_element_type=F32)

    def start_of(a, flip):
        a = jnp.maximum(a, 0)
        return pl.multiple_of(rows - SUB - a * SUB if flip else a * SUB, SUB)

    def two(i, states):
        for half, (fk, rk, fp, rp) in enumerate(((f0, r0, f1, r1), (f1, r1, f0, r0))):
            a = 2 * i + half
            mix(start_of(a - 1, False), cblk_f, fp, y_f)
            mix(start_of(a - 1, True), cblk_r, rp, y_r)
            states = walk(states, (start_of(a, False), start_of(a, True)), (fk, rk))
        return states

    states = tuple((carry[0, :, cut], carry[1, :, cut]) for cut in cuts)
    states = lax.fori_loop(0, rows // SUB // 2, two, states)
    mix(rows - SUB, cblk_f, f1, y_f)
    mix(0, cblk_r, r1, y_r)
    for cut, pair in zip(cuts, states):
        carry[0, :, cut], carry[1, :, cut] = pair


def fwd_scan(steps, u, rates_f, rates_r, b_t, cblk, tile=128):
    length, lanes = steps.shape
    blocks = length // tile
    specs = []
    for order in (lambda t: t, lambda t: blocks - 1 - t):
        specs.append((
            pl.BlockSpec((tile, lanes), lambda t, order=order: (order(t), 0)),
            pl.BlockSpec((16, lanes), lambda t: (0, 0)),
            pl.BlockSpec((16, tile), lambda t, order=order: (0, order(t))),
            pl.BlockSpec((tile, 256), lambda t, order=order: (order(t), 0)),
            pl.BlockSpec((tile * 16, lanes), lambda t, order=order: (order(t), 0)),
        ))
    (row_f, rate, bt_f, blk_f, s_f), (row_r, _, bt_r, blk_r, s_r) = specs
    y = jax.ShapeDtypeStruct((length, lanes), F32)
    s = jax.ShapeDtypeStruct((length * 16, lanes), BF)
    kept = pltpu.VMEM((256, lanes), BF)
    return pl.pallas_call(
        fwd_kernel,
        grid=(blocks,),
        in_specs=[row_f, row_r, row_f, row_r, rate, rate, bt_f, bt_r, blk_f, blk_r],
        out_specs=[row_f, row_r, s_f, s_r],
        out_shape=[y, y, s, s],
        scratch_shapes=[pltpu.VMEM((2, 16, lanes), F32), kept, kept, kept, kept],
        compiler_params=pltpu.CompilerParams(vmem_limit_bytes=56 * 2**20, dimension_semantics=("arbitrary",)),
        cost_estimate=pl.CostEstimate(flops=length * lanes * 16 * 3200, transcendentals=0, bytes_accessed=length * lanes * 80),
        name="fwd_scan",
    )(steps, steps, u, u, rates_f, rates_r, b_t, b_t, cblk, cblk)


def bwd_kernel(step_f, step_r, u_f, u_r, gy_f, gy_r, rate_f, rate_r, ct_f, ct_r, bblk_f, bblk_r, s_f, s_r, sp_f, sp_r,
               dlog_f, dlog_r, adjb_f, adjb_r, bg_f, bg_r, cg_f, cg_r, rg_f, rg_r, carry,
               af0, af1, ar0, ar1, lf0, lf1, lr0, lr1):
    rows, lanes = step_f.shape
    t = pl.program_id(0)
    last = pl.num_programs(0) - 1

    @pl.when(t == 0)
    def _():
        carry[...] = jnp.zeros(carry.shape, F32)
        rg_f[...] = jnp.zeros(rg_f.shape, F32)
        rg_r[...] = jnp.zeros(rg_r.shape, F32)

    ones = (lax.broadcasted_iota(jnp.int32, (SUB, 256), 0) == lax.broadcasted_iota(jnp.int32, (SUB, 256), 1) // 16)
    onesb = ones.astype(BF)
    zero = jnp.zeros((SUB, 256), F32)

    def start_of(a, down):
        a = jnp.maximum(a, 0)
        return pl.multiple_of(rows - SUB - a * SUB if down else a * SUB, SUB)

    wide_by = min(WB, lanes)
    cuts = [slice(c, c + wide_by) for c in range(0, lanes, wide_by)]

    def walk(states, bases, keep_a, keep_l):
        cols = [columns_of(ct[...], base) for ct, base in zip((ct_f, ct_r), bases)]
        out = []
        for cut, pair in zip(cuts, states):
            pair = list(pair)
            rates = rate_f[:, cut], rate_r[:, cut]
            rg = [rg_f[:, cut], rg_r[:, cut]]
            low_rates = [r.astype(BF) for r in rates]
            some = [[], []]
            for k in range(SUB):
                for z, (step, gy, s, sp, j) in enumerate((
                        (step_f, gy_f, s_f, sp_f, SUB - 1 - k), (step_r, gy_r, s_r, sp_r, k))):
                    at = pl.ds(bases[z] + j, 1)
                    row = step[at, cut]
                    adj = gy[at, cut] * wide(cols[z][j], wide_by) + pair[z]
                    pair[z] = jnp.exp2(row * rates[z]) * adj
                    before = bases[z] + (j + 1 if z else j - 1)
                    if k < SUB - 1:
                        inner = s[pl.ds(pl.multiple_of(before * 16, 16), 16), cut]
                    else:
                        inside = before < rows if z else before >= 0
                        safe = jnp.clip(before, 0, rows - 1)
                        inner = s[pl.ds(pl.multiple_of(safe * 16, 16), 16), cut]
                        outer = jnp.where(t == last, jnp.zeros_like(inner), sp[:, cut])
                        inner = jnp.where(inside, inner, outer)
                    grad = pair[z].astype(BF) * inner
                    keep_a[z][j * 16:(j + 1) * 16, cut] = adj.astype(BF)
                    keep_l[z][j * 16:(j + 1) * 16, cut] = grad * low_rates[z]
                    some[z].append(grad * jnp.broadcast_to(row, (16, wide_by)).astype(BF))
                    if len(some[z]) == 4:
                        rg[z] = rg[z] + ((some[z][0] + some[z][1]) + (some[z][2] + some[z][3])).astype(F32)
                        some[z] = []
            rg_f[:, cut], rg_r[:, cut] = rg
            out.append(tuple(pair))
        return tuple(out)

    def mix(base, a_ref, l_ref, u, gy, bblk, s, dlog, adjb, bg, cg):
        here = pl.ds(base, SUB)
        line = pl.ds(base // SUB, 1)
        a = a_ref[...]
        dlog[here, :] = jnp.dot(onesb, l_ref[...], preferred_element_type=F32)
        adjb[here, :] = jnp.dot(bblk[here, :], a, preferred_element_type=F32)
        bgd = lax.dot_general(u[here, :], a, NT, preferred_element_type=F32)
        block = s[pl.ds(pl.multiple_of(base * 16, 256), 256), :]
        cgd = lax.dot_general(gy[here, :].astype(BF), block, NT, preferred_element_type=F32)
        bg[line, :] = jnp.sum(jnp.where(ones, bgd, zero), axis=0, keepdims=True)
        cg[line, :] = jnp.sum(jnp.where(ones, cgd, zero), axis=0, keepdims=True)

    def mix_f(base, a_ref, l_ref):
        mix(base, a_ref, l_ref, u_f, gy_f, bblk_f, s_f, dlog_f, adjb_f, bg_f, cg_f)

    def mix_r(base, a_ref, l_ref):
        mix(base, a_ref, l_ref, u_r, gy_r, bblk_r, s_r, dlog_r, adjb_r, bg_r, cg_r)

    def two(i, states):
        bufs = ((af0, lf0, ar0, lr0), (af1, lf1, ar1, lr1))
        for half in range(2):
            a = 2 * i + half
            naf, nlf, nar, nlr = bufs[half]
            paf, plf, par, plr = bufs[1 - half]
            mix_f(start_of(a - 1, True), paf, plf)
            mix_r(start_of(a - 1, False), par, plr)
            states = walk(states, (start_of(a, True), start_of(a, False)), (naf, nar), (nlf, nlr))
        return states

    states = tuple((carry[0, :, cut], carry[1, :, cut]) for cut in cuts)
    states = lax.fori_loop(0, rows // SUB // 2, two, states)
    mix_f(0, af1, lf1)
    mix_r(rows - SUB, ar1, lr1)
    for cut, pair in zip(cuts, states):
        carry[0, :, cut], carry[1, :, cut] = pair


def bwd_scan(steps, u, gy, rates_f, rates_r, c_t, bblk, states_f, states_r, tile=128):
    length, lanes = steps.shape
    blocks = length // tile
    down = lambda t: blocks - 1 - t
    up = lambda t: t

    def specs(order, before):
        return (
            pl.BlockSpec((tile, lanes), lambda t: (order(t), 0)),
            pl.BlockSpec((16, lanes), lambda t: (0, 0)),
            pl.BlockSpec((16, tile), lambda t: (0, order(t))),
            pl.BlockSpec((tile, 256), lambda t: (order(t), 0)),
            pl.BlockSpec((tile * 16, lanes), lambda t: (order(t), 0)),
            pl.BlockSpec((16, lanes), lambda t: (before(t), 0)),
            pl.BlockSpec((tile // 16, 256), lambda t: (order(t), 0)),
        )

    row_f, rate, ct_f, blk_f, s_f, sp_f, diag_f = specs(down, lambda t: jnp.maximum((blocks - 1 - t) * tile - 1, 0))
    row_r, _, ct_r, blk_r, s_r, sp_r, diag_r = specs(up, lambda t: jnp.minimum((t + 1) * tile, length - 1))
    y = jax.ShapeDtypeStruct((length, lanes), F32)
    diag = jax.ShapeDtypeStruct((length // 16, 256), F32)
    rg = jax.ShapeDtypeStruct((16, lanes), F32)
    kept = pltpu.VMEM((256, lanes), BF)
    return pl.pallas_call(
        bwd_kernel,
        grid=(blocks,),
        in_specs=[row_f, row_r, row_f, row_r, row_f, row_r, rate, rate, ct_f, ct_r, blk_f, blk_r, s_f, s_r, sp_f, sp_r],
        out_specs=[row_f, row_r, row_f, row_r, diag_f, diag_r, diag_f, diag_r, rate, rate],
        out_shape=[y, y, y, y, diag, diag, diag, diag, rg, rg],
        scratch_shapes=[pltpu.VMEM((2, 16, lanes), F32)] + [kept] * 8,
        compiler_params=pltpu.CompilerParams(vmem_limit_bytes=56 * 2**20, dimension_semantics=("arbitrary",)),
        cost_estimate=pl.CostEstimate(flops=length * lanes * 16 * 6800, transcendentals=0, bytes_accessed=length * lanes * 100),
        name="bwd_scan",
    )(steps, steps, u, u, gy, gy, rates_f, rates_r, c_t, c_t, bblk, bblk, states_f, states_r, states_f, states_r)


def blockdiag(rows):
    length = rows.shape[0]
    eye = (jnp.arange(length)[:, None] % 16) == (jnp.arange(256)[None, :] // 16)
    return jnp.where(eye, jnp.tile(rows, (1, 16)), 0).astype(BF)


MESH = pl.DeviceIdType.MESH
VMEM = pl.BlockSpec(memory_space=pltpu.VMEM)
HBM = pl.BlockSpec(memory_space=pl.ANY)
DMA = pltpu.SemaphoreType.DMA


def send(src, dst, out_sem, in_sem, to):
    return pltpu.make_async_remote_copy(
        src_ref=src, dst_ref=dst, send_sem=out_sem, recv_sem=in_sem, device_id=to, device_id_type=MESH)


def greet(devices):
    bar = pltpu.get_barrier_semaphore()
    for to in devices:
        pl.semaphore_signal(bar, inc=1, device_id=to, device_id_type=MESH)
    pl.semaphore_wait(bar, len(devices))


def column_sum_kernel(ns, p_ref, o_ref, land, s1, r1, s2, r2):
    d, q = lax.axis_index("dp"), lax.axis_index("seq")
    others = [lax.rem(q + k, ns) for k in range(1, ns)]
    greet([(d, t) for t in others])
    for k, t in enumerate(others):
        send(p_ref.at[t], land.at[q], s1.at[k], r1.at[q], (d, t)).start()
    total = p_ref[q].astype(F32)
    for k, t in enumerate(others):
        send(p_ref.at[t], land.at[t], s1.at[k], r1.at[t], (d, t)).wait_recv()
        total = total + land[t].astype(F32)
    o_ref[q] = total.astype(o_ref.dtype)
    for k, t in enumerate(others):
        send(o_ref.at[q], o_ref.at[q], s2.at[k], r2.at[q], (d, t)).start()
    for k, t in enumerate(others):
        send(o_ref.at[t], o_ref.at[t], s2.at[k], r2.at[t], (d, t)).wait_recv()
    for k, t in enumerate(others):
        send(p_ref.at[t], land.at[q], s1.at[k], r1.at[q], (d, t)).wait_send()
        send(o_ref.at[q], o_ref.at[q], s2.at[k], r2.at[q], (d, t)).wait_send()


def column_sum(partial, ns, out_dtype, cid):
    rows, lanes = partial.shape
    block = (ns, rows // ns, lanes)
    out = pl.pallas_call(
        functools.partial(column_sum_kernel, ns),
        out_shape=jax.ShapeDtypeStruct(block, out_dtype),
        in_specs=[VMEM], out_specs=VMEM,
        scratch_shapes=[pltpu.VMEM(block, partial.dtype), DMA((ns,)), DMA((ns,)), DMA((ns,)), DMA((ns,))],
        compiler_params=pltpu.CompilerParams(
            collective_id=cid, has_side_effects=True, vmem_limit_bytes=32 * 2**20),
        name="column_sum",
    )(partial.reshape(block))
    return out.reshape(rows, lanes)


def mod_gather_kernel(nd, ns, g_ref, o_ref, land, s1, r1, s2, r2):
    d, q = lax.axis_index("dp"), lax.axis_index("seq")
    others = [lax.rem(q + k, ns) for k in range(1, ns)]
    peers = [lax.rem(d + k, nd) for k in range(1, nd)]
    greet([(d, t) for t in others] + [(e, q) for e in peers])
    for k, t in enumerate(others):
        send(g_ref, land.at[q], s1.at[k], r1.at[q], (d, t)).start()
    total = g_ref[...]
    for k, t in enumerate(others):
        send(g_ref, land.at[t], s1.at[k], r1.at[t], (d, t)).wait_recv()
        total = total + land[t]
    o_ref[d] = total
    for k, e in enumerate(peers):
        send(o_ref.at[d], o_ref.at[d], s2.at[k], r2.at[d], (e, q)).start()
    for k, e in enumerate(peers):
        send(o_ref.at[e], o_ref.at[e], s2.at[k], r2.at[e], (e, q)).wait_recv()
    for k, t in enumerate(others):
        send(g_ref, land.at[q], s1.at[k], r1.at[q], (d, t)).wait_send()
    for k, e in enumerate(peers):
        send(o_ref.at[d], o_ref.at[d], s2.at[k], r2.at[d], (e, q)).wait_send()


def mod_gather(g, nd, ns, cid):
    rows, lanes = g.shape
    return pl.pallas_call(
        functools.partial(mod_gather_kernel, nd, ns),
        out_shape=jax.ShapeDtypeStruct((nd, rows, lanes), F32),
        in_specs=[VMEM], out_specs=VMEM,
        scratch_shapes=[pltpu.VMEM((ns, rows, lanes), F32), DMA((ns,)), DMA((ns,)), DMA((nd,)), DMA((nd,))],
        compiler_params=pltpu.CompilerParams(
            collective_id=cid, has_side_effects=True, vmem_limit_bytes=32 * 2**20),
        name="mod_gather",
    )(g)


def home_kernel(nd, ns, nsub, g_ref, sm_ref, gm_ref, f_ref, so_ref, out_ref,
                pair, plane, spair, splane, ssum, up, down,
                sa, ra, sb, rb, sc, rc, ta, ra2, tb, rb2, tc, rc2, su, ru, sd, rd):
    d, q = lax.axis_index("dp"), lax.axis_index("seq")
    nc = nd // 2
    chip, core = d // 2, lax.rem(d, 2)
    mate = chip * 2 + 1 - core
    chips = [lax.rem(chip + k, nc) for k in range(1, nc)]
    others = [lax.rem(q + k, ns) for k in range(1, ns)]
    spread = nd // ns
    final_to = (spread * q + d // ns, lax.rem(d, ns))
    mine = d * ns + q
    final_from = (lax.rem(mine, nd), mine // nd)
    stays = jnp.logical_and(final_to[0] == d, final_to[1] == q)
    bar = pltpu.get_barrier_semaphore()
    friends = [(mate, q)] + [(c * 2 + core, q) for c in chips] + [(d, t) for t in others]
    for to in friends:
        pl.semaphore_signal(bar, inc=1, device_id=to, device_id_type=MESH)
    @pl.when(jnp.logical_not(stays))
    def _():
        pl.semaphore_signal(bar, inc=1, device_id=final_from, device_id_type=MESH)
        pl.semaphore_wait(bar, len(friends) + 1)
    @pl.when(stays)
    def _():
        pl.semaphore_wait(bar, len(friends))

    def first(c):
        return send(g_ref.at[c * 2 + 1 - core], pair.at[c], sa.at[c], ra.at[c], (mate, q))

    def first_small(c):
        return send(sm_ref.at[c * 2 + 1 - core], spair.at[c], ta.at[c], ra2.at[c], (mate, q))

    order = chips + [chip]
    for c in order:
        first(c).start()
        first_small(c).start()

    def rise(t, s, src):
        return send(src, up.at[t, s], su.at[t, s], ru.at[t, s], (d, q + 1))

    def sink(t, s, src):
        return send(src, down.at[t, s], sd.at[t, s], rd.at[t, s], (d, q - 1))

    def added(land, t, s):
        land[t, s] = (land[t, s].astype(F32) + gm_ref[t, s].astype(F32)).astype(BF)

    def step_up(t, s):
        @pl.when(q < t)
        def _():
            @pl.when(q == 0)
            def _():
                rise(t, s, gm_ref.at[t, s]).start()
            @pl.when(q > 0)
            def _():
                rise(t, s, up.at[t, s]).wait_recv()
                added(up, t, s)
                rise(t, s, up.at[t, s]).start()

    def step_down(t, s):
        @pl.when(q > t)
        def _():
            @pl.when(q == ns - 1)
            def _():
                sink(t, s, gm_ref.at[t, s]).start()
            @pl.when(q < ns - 1)
            def _():
                sink(t, s, down.at[t, s]).wait_recv()
                added(down, t, s)
                sink(t, s, down.at[t, s]).start()

    steps = [(k, s) for k in range(ns - 1) for s in range(nsub)]
    middle = len(steps) * 2 // 3

    def walk(some):
        for k, s in some:
            step_up(ns - 1 - k, s)
            step_down(k, s)

    def second(c, src):
        return send(pair.at[c], plane.at[src], sb.at[c], rb.at[src], (c * 2 + core, q))

    def second_small(c, src):
        return send(spair.at[c], splane.at[src], tb.at[c], rb2.at[src], (c * 2 + core, q))

    walk(steps[:1])
    for c in order:
        first(c).wait_recv()
        @pl.loop(0, ns)
        def _(t):
            pair[c, t] = (pair[c, t].astype(F32) + g_ref[c * 2 + core, t].astype(F32)).astype(BF)
        first_small(c).wait_recv()
        spair[c] = spair[c] + sm_ref[c * 2 + core]
        if c is not chip:
            second(c, chip).start()
            second_small(c, chip).start()
    walk(steps[1:middle])

    for c in chips:
        second(c, c).wait_recv()
        second_small(c, c).wait_recv()
    @pl.loop(0, ns)
    def _(t):
        total = pair[chip, t].astype(F32)
        for c in chips:
            total = total + plane[c, t].astype(F32)
        pair[chip, t] = total.astype(BF)
    small = spair[chip]
    for c in chips:
        small = small + splane[c]
    ssum[...] = small

    def third(t, src):
        return send(pair.at[chip, t], f_ref.at[src], sc.at[t], rc.at[src], (d, t))

    last = send(ssum, so_ref, tc, rc2, final_to)
    @pl.when(stays)
    def _():
        so_ref[...] = ssum[...]
    @pl.when(jnp.logical_not(stays))
    def _():
        last.start()
    for t in others:
        third(t, q).start()
    f_ref[q] = pair[chip, q]
    walk(steps[middle:])

    for s in range(nsub):
        total = gm_ref[q, s].astype(F32)
        out_ref[s] = total
        @pl.when(q > 0)
        def _():
            rise(q, s, gm_ref.at[q, s]).wait_recv()
            out_ref[s] += up[q, s].astype(F32)
        @pl.when(q < ns - 1)
        def _():
            sink(q, s, gm_ref.at[q, s]).wait_recv()
            out_ref[s] += down[q, s].astype(F32)
    for t in others:
        third(t, t).wait_recv()
    @pl.when(jnp.logical_not(stays))
    def _():
        last.wait_recv()
        last.wait_send()
    for c in order:
        first(c).wait_send()
        first_small(c).wait_send()
    for c in chips:
        second(c, chip).wait_send()
        second_small(c, chip).wait_send()
    for t in others:
        third(t, q).wait_send()
    for k, s in steps:
        t = ns - 1 - k
        @pl.when(q < t)
        def _():
            rise(t, s, gm_ref.at[t, s]).wait_send()
        @pl.when(q > k)
        def _():
            sink(k, s, gm_ref.at[k, s]).wait_send()


def home(g, small, gm, nd, ns, cid):
    rows, cols = g.shape[2:]
    nc, nsub = nd // 2, 4
    length, width = gm.shape
    part = length // ns // nsub
    v = small.shape[1:]
    gm = gm.reshape(ns, nsub, part, width)
    f, so, out = pl.pallas_call(
        functools.partial(home_kernel, nd, ns, nsub),
        out_shape=[
            jax.ShapeDtypeStruct((ns, rows, cols), BF),
            jax.ShapeDtypeStruct(v, F32),
            jax.ShapeDtypeStruct((nsub, part, width), F32),
        ],
        in_specs=[VMEM] * 3, out_specs=[VMEM] * 3,
        scratch_shapes=[
            pltpu.VMEM((nc, ns, rows, cols), BF), pltpu.VMEM((nc, ns, rows, cols), BF),
            pltpu.VMEM((nc,) + v, F32), pltpu.VMEM((nc,) + v, F32), pltpu.VMEM(v, F32),
            pltpu.VMEM((ns, nsub, part, width), BF), pltpu.VMEM((ns, nsub, part, width), BF),
            DMA((nc,)), DMA((nc,)), DMA((nc,)), DMA((nc,)), DMA((ns,)), DMA((ns,)),
            DMA((nc,)), DMA((nc,)), DMA((nc,)), DMA((nc,)), DMA(()), DMA(()),
            DMA((ns, nsub)), DMA((ns, nsub)), DMA((ns, nsub)), DMA((ns, nsub)),
        ],
        compiler_params=pltpu.CompilerParams(
            collective_id=cid, has_side_effects=True, vmem_limit_bytes=56 * 2**20),
        name="home",
    )(g, small, gm)
    return f, so, out.reshape(length // ns, width)


def start_kernel(nd, ns, nsub, fused, hid, win, wout, pack, mask, emb, modw, modb,
                 md_o, inner_o, gate_o, wx_o, select_o, mid_o, fil_o, mask_o, mod_o,
                 hv, wv, mv, iv, gv, pack_v, eland, prod, rowp, land1, land2,
                 su, ru, sd, rd, swz, rwx, swp, swm, spz, rp, spp, spm, sk, rk, se, re, s1, r1, s2, r2, own, out):
    d, q = lax.axis_index("dp"), lax.axis_index("seq")
    nc = nd // 2
    chip, core = d // 2, lax.rem(d, 2)
    mate = (chip * 2 + 1 - core, q)
    chips = [lax.rem(chip + k, nc) for k in range(1, nc)]
    others = [lax.rem(q + k, ns) for k in range(1, ns)]
    peers = [lax.rem(d + k, nd) for k in range(1, nd)]
    spread = nd // ns
    me = d * ns + q
    part = wout.shape[1] // ns
    rw = wout.shape[0]
    units = part // nd
    greet([(d, t) for t in others] + [(e, q) for e in peers])

    def column(ref, at):
        return ref.at[:, pl.ds(pl.multiple_of(at * part, 128), part)]

    def wrows(idx):
        return wv.at[pl.ds(pl.multiple_of(idx * rw, 16), rw), :]

    def pieces(t):
        return (column(win, t), column(win, ns + t), column(wout, t))

    def across(k, t, idx):
        return [
            send(src, wrows(idx).at[:, j * part:(j + 1) * part], swz.at[k, j], rwx.at[idx, j], (d, t))
            for j, src in enumerate(pieces(t))
        ]

    keep = [pltpu.make_async_copy(src, wrows(me).at[:, j * part:(j + 1) * part], own.at[j])
            for j, src in enumerate(pieces(q))]
    keep.append(pltpu.make_async_copy(hid, hv.at[q], own.at[3]))
    for copy in keep:
        copy.start()

    plane = d // spread
    slot = lax.rem(d, spread) * ns + q
    pack_z = send(pack, pack_v.at[slot], spz, rp.at[slot], (d, plane))
    pack_vwn = pltpu.make_async_copy(pack, pack_v.at[slot], own.at[4])

    @pl.when(plane == q)
    def _():
        pack_vwn.start()

    @pl.when(plane != q)
    def _():
        pack_z.start()

    def masks(k, t, src):
        return send(mask_o.at[src], mask_o.at[src], sk.at[k], rk.at[src], (d, t))

    def embeds(k, e, src):
        return send(eland.at[src], eland.at[src], se.at[k], re.at[src], (e, q))

    mask_o[q] = mask[...]
    eland[d] = emb[...]
    for k, e in enumerate(peers):
        embeds(k, e, d).start()
    for k, t in enumerate(others):
        masks(k, t, q).start()

    for k, t in enumerate(others):
        for copy in across(k, t, me)[:2]:
            copy.start()

    def rise(k, s):
        t = jnp.maximum(q - k, 0)
        src = hid.at[s] if k == 0 else hv.at[t, s]
        return send(src, hv.at[t, s], su.at[k, s], ru.at[k, s], (d, q + 1))

    def sink(k, s):
        t = jnp.minimum(q + k, ns - 1)
        src = hid.at[s] if k == 0 else hv.at[t, s]
        return send(src, hv.at[t, s], sd.at[k, s], rd.at[k, s], (d, q - 1))

    def hop(k, s):
        @pl.when(q >= k)
        def _():
            if k:
                rise(k - 1, s).wait_recv()
            if k < ns - 1:
                @pl.when(q + 1 < ns)
                def _():
                    rise(k, s).start()

        @pl.when(q + k < ns)
        def _():
            if k:
                sink(k - 1, s).wait_recv()
            if k < ns - 1:
                @pl.when(q >= 1)
                def _():
                    sink(k, s).start()

    for s in range(nsub):
        hop(0, s)
    for k, t in enumerate(others):
        across(k, t, me)[2].start()

    def cols_of(idx, kind):
        return wrows(idx).at[:, 2 * part * kind:2 * part + part * kind]

    def plane_w(c, idx, t, kind):
        return send(cols_of(idx, kind), cols_of(idx, kind), swp.at[kind, c, t], rwx.at[idx, 3 + kind], (c * 2 + core, q))

    def mate_w(c, idx, t, kind):
        return send(cols_of(idx, kind), cols_of(idx, kind), swm.at[kind, c, t], rwx.at[idx, 3 + kind], mate)

    def spread_w(t, kind):
        idx = d * ns + t
        for c in chips:
            plane_w(c, idx, t, kind).start()
        mate_w(chip, idx, t, kind).start()

    for copy in keep[:3]:
        copy.wait()
    spread_w(q, 0)

    for k, e in enumerate(peers):
        embeds(k, e, e).wait_recv()
    rows = modw.shape[0]
    here = lax.broadcasted_iota(jnp.int32, (FREQ, rows), 0)
    pick = here - lax.broadcasted_iota(jnp.int32, (FREQ, rows), 1)
    count = FREQ // (nd * ns)
    keep_col = lax.broadcasted_iota(jnp.int32, (FREQ, rows), 1) < count
    pick = jnp.where(jnp.logical_and(pick == me * count, keep_col), 1.0, 0.0).astype(BF)
    mine = jnp.dot(eland[...].reshape(nd * 16, FREQ), pick, preferred_element_type=F32).astype(BF)
    prod[...] = jnp.dot(mine, modw[...], preferred_element_type=F32)

    lines = prod.shape[1] // 128
    @pl.loop(0, nd)
    def _(e):
        rowp[e] = modb[...]
        for j in range(lines):
            rowp[e, j:j + 1, :] += prod[pl.ds(pl.multiple_of(e * 16, 16), 1), j * 128:(j + 1) * 128]

    def to_item(k, e, src):
        return send(rowp.at[e], land1.at[src], s1.at[k], r1.at[src], (e, q))

    for k, e in enumerate(peers):
        to_item(k, e, d).start()

    for k, t in enumerate(others):
        for copy in across(k, t, d * ns + t)[:2]:
            copy.wait_recv()
        spread_w(t, 0)

    def plane_p(c, i, t):
        return send(pack_v.at[i], pack_v.at[i], spp.at[c, t], rp.at[i], (c * 2 + core, q))

    def mate_p(c, i, t):
        return send(pack_v.at[i], pack_v.at[i], spm.at[c, t], rp.at[i], mate)

    base = lax.rem(d, spread) * ns

    @pl.when(plane == q)
    def _():
        pack_vwn.wait()
        for t in others:
            send(pack, pack_v.at[base + t], spz, rp.at[base + t], (d, plane)).wait_recv()
        for t in range(ns):
            for c in chips:
                plane_p(c, base + t, t).start()
            mate_p(chip, base + t, t).start()

    total = rowp[d]
    for k, e in enumerate(peers):
        to_item(k, e, e).wait_recv()
        total = total + land1[e]
    land2[q] = total

    def to_column(k, t, src):
        return send(land2.at[src], land2.at[src], s2.at[k], r2.at[src], (d, t))

    for k, t in enumerate(others):
        to_column(k, t, q).start()

    def relay_w(c, t, kind):
        idx = (c * 2 + core) * ns + t
        plane_w(c, idx, t, kind).wait_recv()
        mate_w(c, idx, t, kind).start()

    def holds(c):
        return (c * 2 + core) // spread == q

    def relay_p(c):
        first = lax.rem(c * 2 + core, spread) * ns
        @pl.when(holds(c))
        def _():
            for t in range(ns):
                plane_p(c, first + t, t).wait_recv()
                mate_p(c, first + t, t).start()

    def own_copies(t):
        return [pltpu.make_async_copy(src.at[t], dst.at[t], out.at[t, i]) for i, (src, dst) in enumerate(
            ((mv, md_o), (iv, inner_o), (gv, gate_o)) if fused else ((hv, md_o),))]

    local = hv.shape[1] * hv.shape[2]
    width = hv.shape[3]

    def project(t):
        if fused:
            shift, scale = mod_o[0:1, 0:width], 1.0 + mod_o[0:1, width:2 * width]
            for s in range(nsub):
                @pl.loop(0, local // nsub // 16)
                def _(r):
                    x = hv[t, s, pl.ds(pl.multiple_of(r * 16, 16), 16), :].astype(F32)
                    x = x - jnp.mean(x, axis=1, keepdims=True)
                    x = x * lax.rsqrt(jnp.mean(x * x, axis=1, keepdims=True) + EPS)
                    to = pl.multiple_of(s * (local // nsub) + r * 16, 16)
                    mv[t, pl.ds(to, 16), :] = (x * scale + shift).astype(BF)
            tile = part if part % 256 else part // 2

            @pl.loop(0, part // tile)
            def _(j):
                for target, base in ((iv, 0), (gv, part)):
                    n = pl.ds(pl.multiple_of(base + j * tile, 128), tile)
                    full = jnp.dot(mv[t], wv[:, n], preferred_element_type=F32)
                    target[t, :, pl.ds(pl.multiple_of(j * tile, 128), tile)] = full.astype(target.dtype)
        for copy in own_copies(t):
            copy.start()

    relays = [(c, t) for t in [q] + others for c in chips]
    at = 0
    for s in range(nsub):
        hop(1, s)
        upto = len(relays) * (s + 1) // (2 * nsub)
        for c, t in relays[at:upto]:
            relay_w(c, t, 0)
        at = upto
    spread_w(q, 1)
    for k, t in enumerate(others):
        across(k, t, d * ns + t)[2].wait_recv()
        spread_w(t, 1)
    for c, t in relays[at:]:
        relay_w(c, t, 0)
    for c in chips:
        relay_p(c)

    for k, t in enumerate(others):
        to_column(k, t, t).wait_recv()
    total = land2[0]
    for t in range(1, ns):
        total = total + land2[t]
    mod_o[...] = jnp.zeros(mod_o.shape, F32)
    for i in range(mod_o.shape[1] // 128):
        mod_o[0:1, i * 128:(i + 1) * 128] = total[i:i + 1, :]

    twin = 1 - core
    for c in range(nc):
        for t in range(ns):
            idx = (c * 2 + twin) * ns + t
            mate_w(c, idx, t, 0).wait_recv()
    keep[3].wait()

    def project_at(t):
        @pl.when(jnp.logical_and(t >= 0, t < ns))
        def _():
            project(jnp.clip(t, 0, ns - 1))

    for k in range(2, ns):
        for s in range(nsub):
            hop(k, s)
            if k == 2 and s == 0:
                project(q)
            if s == nsub - 3:
                project_at(q - k + 1)
            if s == nsub - 2:
                project_at(q + k - 1)

    for c, t in relays:
        relay_w(c, t, 1)
    for c in range(nc):
        for t in range(ns):
            idx = (c * 2 + twin) * ns + t
            mate_w(c, idx, t, 1).wait_recv()
    wx_copy = pltpu.make_async_copy(wv, wx_o, own.at[5])
    wx_copy.start()

    for c in range(nc):
        first = lax.rem(c * 2 + twin, spread) * ns
        @pl.when((c * 2 + twin) // spread == q)
        def _():
            for t in range(ns):
                mate_p(c, first + t, t).wait_recv()
    for j in range(nd):
        here = slice(j * units, (j + 1) * units)
        select_o[here, :] = pack_v[j, 0:units, :]
        mid_o[here, :] = pack_v[j, units:2 * units, :]
        fil_o[:, here] = pack_v[j, 2 * units:2 * units + 16, 0:units].astype(F32)

    project_at(q - ns + 1)
    project_at(q + ns - 1)

    for k, t in enumerate(others):
        masks(k, t, t).wait_recv()
    wx_copy.wait()
    for t in range(ns):
        for copy in own_copies(t):
            copy.wait()

    for k, t in enumerate(others):
        for copy in across(k, t, me):
            copy.wait_send()
        masks(k, t, q).wait_send()
        to_column(k, t, q).wait_send()
    for k, e in enumerate(peers):
        embeds(k, e, d).wait_send()
        to_item(k, e, d).wait_send()

    @pl.when(plane != q)
    def _():
        pack_z.wait_send()

    @pl.when(plane == q)
    def _():
        for t in range(ns):
            for c in chips:
                plane_p(c, base + t, t).wait_send()
            mate_p(chip, base + t, t).wait_send()

    for kind in range(2):
        for t in range(ns):
            for c in chips:
                plane_w(c, d * ns + t, t, kind).wait_send()
                mate_w(c, (c * 2 + core) * ns + t, t, kind).wait_send()
            mate_w(chip, d * ns + t, t, kind).wait_send()
    for c in chips:
        first = lax.rem(c * 2 + core, spread) * ns
        @pl.when(holds(c))
        def _():
            for t in range(ns):
                mate_p(c, first + t, t).wait_send()
    for k in range(ns - 1):
        for s in range(nsub):
            @pl.when(jnp.logical_and(q >= k, q + 1 < ns))
            def _():
                rise(k, s).wait_send()
            @pl.when(jnp.logical_and(q + k < ns, q >= 1))
            def _():
                sink(k, s).wait_send()


def start(hidden, mask, win, wout, pack, embedded, modw, modb, fused, nd, ns, cid):
    nsub = 4
    length, width = hidden.shape
    rows, inner = wout.shape
    part = inner // ns
    nc = nd // 2
    hidden = hidden.reshape(nsub, length // nsub, width)
    lines = modb.shape
    runs = (ns,) + (hidden.shape if not fused else (length, width))
    return pl.pallas_call(
        functools.partial(start_kernel, nd, ns, nsub, fused),
        out_shape=[
            jax.ShapeDtypeStruct(runs, BF),
            jax.ShapeDtypeStruct((ns, length, part), BF),
            jax.ShapeDtypeStruct((ns, length, part), F32),
            jax.ShapeDtypeStruct((nd * ns * rows, 3 * part), BF),
            jax.ShapeDtypeStruct((part, 128), BF),
            jax.ShapeDtypeStruct((part, 128), BF),
            jax.ShapeDtypeStruct((16, part), F32),
            jax.ShapeDtypeStruct((ns,) + mask.shape, BF),
            jax.ShapeDtypeStruct((8, modw.shape[1]), F32),
        ],
        in_specs=[HBM, HBM, HBM, HBM, VMEM, VMEM, VMEM, VMEM],
        out_specs=[HBM, HBM, HBM, HBM, VMEM, VMEM, VMEM, VMEM, VMEM],
        scratch_shapes=[
            pltpu.VMEM((ns,) + hidden.shape, BF), pltpu.VMEM((nd * ns * rows, 3 * part), BF),
            pltpu.VMEM((ns, length, width), BF), pltpu.VMEM((ns, length, part), BF), pltpu.VMEM((ns, length, part), F32),
            pltpu.VMEM((nd,) + pack.shape, BF),
            pltpu.VMEM((nd,) + embedded.shape, BF), pltpu.VMEM((nd * 16, modw.shape[1]), F32),
            pltpu.VMEM((nd,) + lines, F32), pltpu.VMEM((nd,) + lines, F32), pltpu.VMEM((ns,) + lines, F32),
            DMA((ns - 1, nsub)), DMA((ns - 1, nsub)), DMA((ns - 1, nsub)), DMA((ns - 1, nsub)),
            DMA((ns, 3)), DMA((nd * ns, 5)), DMA((2, nc, ns)), DMA((2, nc, ns)),
            DMA(()), DMA((nd,)), DMA((nc, ns)), DMA((nc, ns)),
            DMA((ns,)), DMA((ns,)), DMA((nd,)), DMA((nd,)),
            DMA((nd,)), DMA((nd,)), DMA((ns,)), DMA((ns,)), DMA((6,)), DMA((ns, 3)),
        ],
        compiler_params=pltpu.CompilerParams(
            collective_id=cid, has_side_effects=True, vmem_limit_bytes=56 * 2**20),
        name="start",
    )(hidden, win, wout, pack, mask, embedded, modw, modb)


def end_kernel(nd, ns, nsub, rows, turned,
               gp_h, md_h, wx_h, sm_ref, hid_ref, cot_ref, line_ref, early,
               gin_o, gout_o, so_ref, gh_o, mod_o,
               gp, md, wx, gm, made, pair, plane, spair, splane, ssum, fro, ready, up, down, own, acc, msg, mland,
               ld, sa, ra, sb, rb, sc, rc, se, re, ta, ra2, tb, rb2, tc, rc2, su, ru, sd, rd, s1, r1, s2, r2):
    d, q = lax.axis_index("dp"), lax.axis_index("seq")
    nc = nd // 2
    chip, core = d // 2, lax.rem(d, 2)
    mate = chip * 2 + 1 - core
    pairs = [(1, 1), (1, 0), (0, 1)] + [(a, b) for b in range(2, nc // 2) for a in (0, 1)]
    chips = [lax.rem(chip + a, 2) + 2 * lax.rem(chip // 2 + b, nc // 2) for a, b in pairs]
    others = [lax.rem(q + k, ns) for k in range(1, ns)]
    peers = [lax.rem(d + k, nd) for k in range(1, nd)]
    spread = nd // ns
    final_to = (spread * q + d // ns, lax.rem(d, ns))
    me = d * ns + q
    final_from = (lax.rem(me, nd), me // nd)
    stays = jnp.logical_and(final_to[0] == d, final_to[1] == q)
    length, cols = gp.shape
    part = cols // 2
    width = wx.shape[0]
    local = length // ns
    sub = local // nsub
    rw = pair.shape[2]
    half = ns * rw

    loads = [pltpu.make_async_copy(src, dst, ld.at[i]) for i, (src, dst) in enumerate(
        ((gp_h, gp), (wx_h.at[:, 0:cols], wx), (md_h, md)))]
    for copy in loads:
        copy.start()

    bar = pltpu.get_barrier_semaphore()
    friends = [(e, q) for e in peers] + [(d, t) for t in others]
    for to in friends:
        pl.semaphore_signal(bar, inc=1, device_id=to, device_id_type=MESH)
    @pl.when(jnp.logical_not(stays))
    def _():
        pl.semaphore_signal(bar, inc=1, device_id=final_from, device_id_type=MESH)

    def tokens(t):
        @pl.loop(0, width // 512)
        def _(j):
            here = pl.ds(pl.multiple_of(j * 512, 512), 512)
            full = lax.dot_general(gp[t * local:(t + 1) * local, :], wx[here, :], NT, preferred_element_type=F32)
            full = full.astype(BF)
            for s in range(nsub):
                gm[t, s, :, here] = full[s * sub:(s + 1) * sub]

    def rise(t, s, src):
        return send(src, up.at[t, s], su.at[t, s], ru.at[t, s], (d, q + 1))

    def sink(t, s, src):
        return send(src, down.at[t, s], sd.at[t, s], rd.at[t, s], (d, q - 1))

    def added(land, t, s):
        land[t, s] = (land[t, s].astype(F32) + gm[t, s].astype(F32)).astype(BF)

    def open_up(t, s):
        @pl.when(jnp.logical_and(q == 0, t > 0))
        def _():
            rise(t, s, gm.at[t, s]).start()

    def open_down(t, s):
        @pl.when(jnp.logical_and(q == ns - 1, t < ns - 1))
        def _():
            sink(t, s, gm.at[t, s]).start()

    def step(k, s):
        t = ns - 1 - k

        @pl.when(jnp.logical_and(q < t, q > 0))
        def _():
            rise(t, s, up.at[t, s]).wait_recv()
            added(up, t, s)
            rise(t, s, up.at[t, s]).start()

        @pl.when(jnp.logical_and(q > k, q < ns - 1))
        def _():
            sink(k, s, down.at[k, s]).wait_recv()
            added(down, k, s)
            sink(k, s, down.at[k, s]).start()

    def far(k):
        for t in sorted({ns - 1 - k, k}, reverse=True):
            tokens(t)
            for s in range(nsub):
                open_up(t, s)
                open_down(t, s)

    @pl.when(stays)
    def _():
        pl.semaphore_wait(bar, len(friends))

    @pl.when(jnp.logical_not(stays))
    def _():
        pl.semaphore_wait(bar, len(friends) + 1)

    def whole(t, src):
        return send(early.at[t], ready.at[src], se.at[t], re.at[src], (d, t))

    for t in others:
        whole(t, q).start()
    loads[0].wait()
    loads[1].wait()
    far(0)
    steps = [(k, s) for k in range(ns - 1) for s in range(nsub)]

    def first(c):
        return send(made.at[c, 1 - core], pair.at[c], sa.at[c], ra.at[c], (mate, q))

    def first_small(c):
        return send(sm_ref.at[c * 2 + 1 - core], spair.at[c], ta.at[c], ra2.at[c], (mate, q))

    def second(c, src):
        return send(pair.at[c], plane.at[src], sb.at[c], rb.at[src], (c * 2 + core, q))

    def second_small(c, src):
        return send(spair.at[c], splane.at[src], tb.at[c], rb2.at[src], (c * 2 + core, q))

    def block(c):
        at = pl.ds(pl.multiple_of(c * 2 * half, 2 * half), 2 * half)
        tile = part if part % 256 else part // 2
        left = md[at, :] if turned else md[:, at].T

        @pl.loop(0, part // tile)
        def _(j):
            n = pl.ds(pl.multiple_of(j * tile, 128), tile)
            full = jnp.dot(left, gp[:, n], preferred_element_type=F32).astype(BF)
            for h in range(2):
                for t in range(ns):
                    line = (h * ns + t) * rw
                    made[c, h, t, :, n] = full[line:line + rw]

    loads[2].wait()
    order = chips + [chip]

    def give(c):
        block(c)
        first(c).start()
        first_small(c).start()

    give(order[0])
    for k in range(1, ns // 2):
        far(k)
    for i, c in enumerate(order):
        if i + 1 < nc:
            give(order[i + 1])
        first(c).wait_recv()
        @pl.loop(0, ns)
        def _(t):
            pair[c, t] = (pair[c, t].astype(F32) + made[c, core, t].astype(F32)).astype(BF)
        first_small(c).wait_recv()
        spair[c] = spair[c] + sm_ref[c * 2 + core]
        if i < nc - 1:
            second(c, chip).start()
            second_small(c, chip).start()
        for k, s in steps[i:i + 1]:
            step(k, s)
    late = len(steps) * 3 // 4
    for k, s in steps[nc:late]:
        step(k, s)

    for c in chips:
        second(c, c).wait_recv()
        second_small(c, c).wait_recv()
    @pl.loop(0, ns)
    def _(t):
        total = pair[chip, t].astype(F32)
        for c in chips:
            total = total + plane[c, t].astype(F32)
        pair[chip, t] = total.astype(BF)
    small = spair[chip]
    for c in chips:
        small = small + splane[c]
    ssum[...] = small

    def third(t, src):
        return send(pair.at[chip, t], fro.at[src], sc.at[t], rc.at[src], (d, t))

    last = send(ssum, so_ref, tc, rc2, final_to)
    @pl.when(stays)
    def _():
        so_ref[...] = ssum[...]
    @pl.when(jnp.logical_not(stays))
    def _():
        last.start()
    for t in others:
        third(t, q).start()
    fro[q] = pair[chip, q]
    for k, s in steps[max(nc, late):]:
        step(k, s)

    acc[...] = jnp.zeros(acc.shape, F32)
    acc[2:4, :] = line_ref[1:3, :]
    scale = 1.0 + line_ref[0:1, :]
    for s in range(nsub):
        own[...] = gm[q, s].astype(F32)

        @pl.when(q > 0)
        def _():
            rise(q, s, gm.at[q, s]).wait_recv()
            own[...] += up[q, s].astype(F32)

        @pl.when(q < ns - 1)
        def _():
            sink(q, s, gm.at[q, s]).wait_recv()
            own[...] += down[q, s].astype(F32)

        @pl.loop(0, sub // 16)
        def _(r):
            here = pl.ds(pl.multiple_of(r * 16, 16), 16)
            grad = own[here, :]
            x = hid_ref[s, here, :].astype(F32)
            x = x - jnp.mean(x, axis=1, keepdims=True)
            inverse = lax.rsqrt(jnp.mean(x * x, axis=1, keepdims=True) + EPS)
            normed = x * inverse
            acc[0:1, :] += jnp.sum(grad, axis=0, keepdims=True)
            acc[1:2, :] += jnp.sum(grad * normed, axis=0, keepdims=True)
            grad = grad * scale
            grad = grad - jnp.mean(grad, axis=1, keepdims=True) - normed * jnp.mean(
                grad * normed, axis=1, keepdims=True)
            gh_o[s, here, :] = (cot_ref[s, here, :].astype(F32) + inverse * grad).astype(BF)

    msg[...] = jnp.zeros(msg.shape, F32)
    long = msg.shape[1] // 128
    for i in range(3 * width // 128 + FREQ // 128):
        r, c = divmod(i * 128, width)
        to = (i % long) * 128
        msg[i // long:i // long + 1, to:to + 128] = acc[r:r + 1, c:c + 128]
    for k, t in enumerate(others):
        send(msg, mland.at[q], s1.at[k], r1.at[q], (d, t)).start()

    inner = part * ns

    def place(src, rest):
        at = src * part
        gin_o[:, pl.ds(pl.multiple_of(at, 128), part)] = fro[src, 0:rows, :].astype(F32)
        gin_o[:, pl.ds(pl.multiple_of(inner + at, 128), part)] = rest[0:rows, 0:part].astype(F32)
        gout_o[:, pl.ds(pl.multiple_of(at, 128), part)] = rest[0:rows, part:2 * part].astype(F32)

    place(q, early[q])
    total = msg[...]
    for k, t in enumerate(others):
        send(msg, mland.at[t], s1.at[k], r1.at[t], (d, t)).wait_recv()
        total = total + mland[t]
    mod_o[d] = total
    for k, e in enumerate(peers):
        send(mod_o.at[d], mod_o.at[d], s2.at[k], r2.at[d], (e, q)).start()
    for t in others:
        third(t, t).wait_recv()
        whole(t, t).wait_recv()
        place(t, ready[t])
    for k, e in enumerate(peers):
        send(mod_o.at[e], mod_o.at[e], s2.at[k], r2.at[e], (e, q)).wait_recv()
    @pl.when(jnp.logical_not(stays))
    def _():
        last.wait_recv()
        last.wait_send()

    for c in order:
        first(c).wait_send()
        first_small(c).wait_send()
    for c in chips:
        second(c, chip).wait_send()
        second_small(c, chip).wait_send()
    for k, t in enumerate(others):
        third(t, q).wait_send()
        whole(t, q).wait_send()
        send(msg, mland.at[q], s1.at[k], r1.at[q], (d, t)).wait_send()
    for k, e in enumerate(peers):
        send(mod_o.at[d], mod_o.at[d], s2.at[k], r2.at[d], (e, q)).wait_send()
    for k, s in steps:
        t = ns - 1 - k
        @pl.when(q < t)
        def _():
            rise(t, s, gm.at[t, s]).wait_send()
        @pl.when(q > k)
        def _():
            sink(k, s, gm.at[k, s]).wait_send()


def end(grad_projected, modded, wx, early, small, hidden, cot, line, rows, nd, ns, cid):
    length, cols = grad_projected.shape
    part = cols // 2
    width = wx.shape[0]
    inner = part * ns
    nc, nsub = nd // 2, 4
    local = length // ns
    sub = local // nsub
    rw = rows + -rows % 16
    half = ns * rw
    turned = 2 * half % 128 != 0 or rw != rows
    if turned:
        def turn(a):
            a = a.T.reshape(nd * ns, rows, length)
            return jnp.pad(a, ((0, 0), (0, rw - rows), (0, 0))).reshape(nd * ns * rw, length)
        modded = turn(modded)
    early = jnp.pad(early.reshape(ns, rows, cols), ((0, 0), (0, rw - rows), (0, 0)))
    short = -(-(3 * width + FREQ) // 1024) * 128
    v = small.shape[1:]
    hidden, cot = hidden.reshape(nsub, sub, width), cot.reshape(nsub, sub, width)
    blocks = pltpu.VMEM((nc, ns, rw, part), BF)
    smalls = pltpu.VMEM((nc,) + v, F32)
    runs = pltpu.VMEM((ns, nsub, sub, width), BF)
    gin, gout, so, gh, mod = pl.pallas_call(
        functools.partial(end_kernel, nd, ns, nsub, rows, turned),
        out_shape=[
            jax.ShapeDtypeStruct((rows, 2 * inner), F32),
            jax.ShapeDtypeStruct((rows, inner), F32),
            jax.ShapeDtypeStruct(v, F32),
            jax.ShapeDtypeStruct((nsub, sub, width), BF),
            jax.ShapeDtypeStruct((nd, 8, short), F32),
        ],
        in_specs=[HBM] * 3 + [VMEM] * 5, out_specs=[VMEM] * 5,
        scratch_shapes=[
            pltpu.VMEM(grad_projected.shape, BF), pltpu.VMEM(modded.shape, BF), pltpu.VMEM((width, cols), BF), runs,
            pltpu.VMEM((nc, 2, ns, rw, part), BF), blocks, blocks,
            smalls, smalls, pltpu.VMEM(v, F32), pltpu.VMEM((ns, rw, part), BF), pltpu.VMEM((ns, rw, cols), BF), runs, runs,
            pltpu.VMEM((sub, width), F32), pltpu.VMEM((8, width), F32), pltpu.VMEM((8, short), F32),
            pltpu.VMEM((ns, 8, short), F32),
            DMA((3,)),
            DMA((nc,)), DMA((nc,)), DMA((nc,)), DMA((nc,)), DMA((ns,)), DMA((ns,)), DMA((ns,)), DMA((ns,)),
            DMA((nc,)), DMA((nc,)), DMA((nc,)), DMA((nc,)), DMA(()), DMA(()),
            DMA((ns, nsub)), DMA((ns, nsub)), DMA((ns, nsub)), DMA((ns, nsub)),
            DMA((ns,)), DMA((ns,)), DMA((nd,)), DMA((nd,)),
        ],
        compiler_params=pltpu.CompilerParams(
            collective_id=cid, has_side_effects=True, vmem_limit_bytes=60 * 2**20),
        name="end",
    )(grad_projected, modded, wx, small, hidden, cot, line, early)
    return gin, gout, so, gh.reshape(local, width), mod


def frequency_embed(timestep):
    half_width = FREQ // 2
    counter = jnp.arange(half_width, dtype=F32)
    frequency = jnp.exp(counter * (-math.log(10000.0) / half_width))
    angles = timestep.astype(F32)[:, None] * frequency[None, :]
    return jnp.concatenate([jnp.cos(angles), jnp.sin(angles)], axis=1)


def dot(a, b):
    return jnp.dot(a, b, preferred_element_type=F32)


def dot_nt(a, b):
    return lax.dot_general(a, b, (((1,), (1,)), ((), ())), preferred_element_type=F32)


def dot_tn(a, b):
    return lax.dot_general(a, b, (((0,), (0,)), ((), ())), preferred_element_type=F32)


def body(
    hidden,
    pad_mask,
    timestep,
    input_weight,
    select_weight,
    step_weight,
    output_weight,
    decay_forward,
    decay_reverse,
    filter_weight,
    filter_bias,
    step_bias,
    modulation_weight,
    modulation_bias,
    cotangent,
):
    ns, nd = lax.axis_size("seq"), lax.axis_size("dp")
    q, d = lax.axis_index("seq"), lax.axis_index("dp")
    every = ("dp", "seq")
    local_len, width = hidden.shape[1:]
    length = local_len * ns
    inner = output_weight.shape[0]
    part = inner // ns
    rank = step_weight.shape[0]
    state = decay_forward.shape[1]
    taps = filter_weight.shape[0]
    rows_in = input_weight.shape[0]
    lanes = select_weight.shape[1]

    units = part // nd
    embedded = jax.nn.silu(frequency_embed(timestep)).astype(BF)
    fil = jnp.concatenate([filter_weight, filter_bias[None], step_bias[None]])
    fil = jnp.pad(fil, ((0, 16 - fil.shape[0]), (0, lanes - units)))
    mid = jnp.concatenate([step_weight.T, decay_forward, decay_reverse], axis=1)
    pack = jnp.concatenate([select_weight, mid, fil])
    mask = jnp.pad(pad_mask[0].astype(BF).reshape(-1, 128), ((0, 16 - local_len // 128), (0, 0)))
    shard = (-modulation_weight.shape[0] % 16, 0)
    modb = jnp.zeros((-(-3 * width // 1024) * 1024,), F32)
    modb = lax.dynamic_update_slice(modb, modulation_bias.astype(F32), ((d * ns + q) * modulation_bias.shape[0],))
    row_pad = ((0, -rows_in % 16), (0, 0))
    fused = rows_in % 16 == 0
    modded, inner_part, gate_branch, wx, select_q, mid, fil, mask, modulation = start(
        hidden[0], mask, jnp.pad(input_weight, row_pad), jnp.pad(output_weight.T, row_pad), pack,
        jnp.pad(embedded, ((0, 15), (0, 0))),
        jnp.pad(modulation_weight, ((0, shard[0]), (0, 0))), modb.reshape(-1, 128), fused, nd, ns, 4)
    wx = wx.reshape(nd * ns, -1, 3 * part)[:, :rows_in].reshape(width, 3 * part)
    win, wout = wx[:, : 2 * part], wx[:, 2 * part :]
    mask = mask[:, : local_len // 128].reshape(length, 1).astype(F32)
    step_q = mid[:, :rank].T
    log_f, log_r = mid[:, rank : rank + state], mid[:, rank + state :]
    filt32, fbias, sbias = fil[:taps].T, fil[taps][None], fil[taps + 1][None]
    modulation = modulation[:1]
    shifts = modulation[:, :width]
    scales = modulation[:, width : 2 * width]
    gate_scale = modulation[:, 2 * width :]

    def norm(x):
        x = x.astype(F32)
        centered = x - jnp.mean(x, axis=1, keepdims=True)
        inverse = lax.rsqrt(jnp.mean(centered * centered, axis=1, keepdims=True) + EPS)
        return centered * inverse, inverse

    if fused:
        modded = modded.reshape(length, width)
        inner_part, gate_branch = inner_part.reshape(length, part), gate_branch.reshape(length, part)
    else:
        modded = (norm(modded.reshape(length, width))[0] * (1.0 + scales) + shifts).astype(BF)
        projected = dot(modded, win)
        inner_part, gate_branch = projected[:, :part].astype(BF), projected[:, part:]
    inner_part = inner_part.astype(F32) * mask
    padded = jnp.pad(inner_part, ((taps - 1, 0), (0, 0)))
    filtered = fbias
    for k in range(taps):
        filtered = filtered + filt32[:, k][None, :] * padded[k : k + length]
    sigma_filter = jax.nn.sigmoid(filtered)
    active = (filtered * sigma_filter).astype(BF)
    active32 = active.astype(F32)
    selected = column_sum(dot(active, select_q).astype(BF), ns, BF, 0)
    cot, selected = lax.optimization_barrier((cotangent[0], selected))
    cot = lax.all_gather(cot, "seq", axis=0, tiled=True)
    low_rank = selected[:, :rank].astype(BF)
    b_rows = selected[:, rank : rank + state].astype(F32)
    c_rows = selected[:, rank + state :].astype(F32)
    pre_steps = dot(low_rank, step_q) + sbias
    steps = jax.nn.softplus(pre_steps)
    rates_f = -jnp.exp(log_f.astype(F32)).T
    rates_r = -jnp.exp(log_r.astype(F32)).T
    drive = steps * active32
    rates_f2, rates_r2 = rates_f * LOG2E, rates_r * LOG2E
    mixed_f, mixed_r, states_f, states_r = fwd_scan(steps, drive, rates_f2, rates_r2, b_rows.T, blockdiag(c_rows))
    merged = mixed_f + mixed_r
    sigma_gate = jax.nn.sigmoid(gate_branch)
    silu_gate = gate_branch * sigma_gate
    gated = (merged * silu_gate).astype(BF)
    branch = dot_nt(gated, wout).astype(BF)
    branch, cot = lax.optimization_barrier((branch, cot))
    branch = lax.psum_scatter(branch, "seq", scatter_dimension=0, tiled=True).astype(F32)

    mask_here = pad_mask[0].astype(F32)[:, None]
    cot_here = cotangent[0].astype(F32)
    block_out = (hidden[0].astype(F32) + gate_scale * mask_here * branch).astype(BF)
    grad_gate = jnp.sum(mask_here * cot_here * branch, axis=0)

    grad_branch = (cot.astype(F32) * gate_scale * mask).astype(BF)
    grad_gated = dot(grad_branch, wout)
    grad_merged = grad_gated * silu_gate
    grad_gate_branch = grad_gated * merged * sigma_gate * (1.0 + gate_branch * (1.0 - sigma_gate))
    grad_gate_branch = grad_gate_branch.astype(BF)
    rows_first = Layout((0, 1))
    early = jnp.concatenate([
        with_layout_constraint(dot_tn(modded, grad_gate_branch).astype(BF), rows_first),
        with_layout_constraint(dot_tn(grad_branch, gated).astype(BF), rows_first)], axis=1)
    early = lax.psum_scatter(early, "dp", scatter_dimension=0, tiled=True)
    dlog_f, dlog_r, adjb_f, adjb_r, bg_f, bg_r, cg_f, cg_r, rg_f, rg_r = bwd_scan(
        steps, drive.astype(BF), grad_merged, rates_f2, rates_r2, c_rows.T, blockdiag(b_rows), states_f, states_r)
    adjb = adjb_f + adjb_r
    grad_steps = (dlog_f + dlog_r) * (1.0 / LOG2E) + active32 * adjb
    grad_b = (bg_f + bg_r).reshape(length, state)
    grad_c = (cg_f + cg_r).reshape(length, state)
    grad_decay_f = rg_f * rates_f
    grad_decay_r = rg_r * rates_r
    grad_pre = grad_steps * jax.nn.sigmoid(pre_steps)
    grad_step_bias = jnp.sum(grad_pre, axis=0)
    grad_pre_low = grad_pre.astype(BF)
    grad_step_t = dot_tn(grad_pre_low, low_rank)
    grad_low_rank = dot_nt(grad_pre_low, step_q)
    grad_selected = column_sum(jnp.concatenate([grad_low_rank, grad_b, grad_c], axis=1).astype(BF), ns, BF, 1)
    grad_select = dot_tn(active, grad_selected)
    grad_active = steps * adjb + dot_nt(grad_selected, select_q)
    grad_filtered = grad_active * sigma_filter * (1.0 + filtered * (1.0 - sigma_filter))
    extended = jnp.pad(grad_filtered, ((0, taps - 1), (0, 0)))
    grad_inner = jnp.zeros_like(grad_filtered)
    filter_rows = []
    for k in range(taps):
        lead = taps - 1 - k
        grad_inner = grad_inner + filt32[:, k][None, :] * extended[lead : lead + length]
        filter_rows.append(jnp.sum(grad_filtered * padded[k : k + length], axis=0))
    grad_filter_bias = jnp.sum(grad_filtered, axis=0)
    grad_projected = jnp.concatenate([(grad_inner * mask).astype(BF), grad_gate_branch], axis=1)
    fil = jnp.stack(filter_rows + [grad_filter_bias, grad_step_bias])
    fil = fil.reshape(-1, nd, units).transpose(1, 0, 2)
    fil = jnp.pad(fil, ((0, 0), (0, 16 - fil.shape[1]), (0, lanes - units)))
    mid = jnp.concatenate([grad_step_t, grad_decay_f.T, grad_decay_r.T], axis=1)
    small = jnp.concatenate([grad_select.reshape(nd, units, lanes), mid.reshape(nd, units, lanes), fil], axis=1)
    line = jnp.concatenate([scales, grad_gate[None], jnp.pad(embedded.astype(F32) / ns, ((0, 0), (0, width - FREQ))),
                            jnp.zeros((5, width), F32)])
    g_in, g_out, small, grad_hidden, sums = end(
        grad_projected, modded, wx, early, small, hidden[0], cotangent[0], line, rows_in, nd, ns, 2)
    gs_select = small[:units]
    mid = small[units : 2 * units]
    gs_step, gs_f, gs_r = mid[:, :rank], mid[:, rank : rank + state], mid[:, rank + state :]
    fil = small[2 * units :, :units]

    sums = sums.reshape(nd, -1)
    embeds = sums[:, 3 * width : 3 * width + FREQ]
    grad_mod = sums[:, : 3 * width]
    me = d * ns + q
    mine = lax.dynamic_slice_in_dim(embeds, me * modulation_weight.shape[0], modulation_weight.shape[0], 1)
    g_modw = lax.dot_general(mine, grad_mod, (((0,), (0,)), ((), ())), precision=HIGHEST)
    g_modb = lax.dynamic_slice_in_dim(
        jnp.sum(grad_mod, axis=0), me * modulation_bias.shape[0], modulation_bias.shape[0], 0)
    return (
        block_out[None],
        grad_hidden[None],
        g_in,
        gs_select,
        gs_step.T,
        g_out.T,
        gs_f,
        gs_r,
        fil[:taps],
        fil[taps],
        fil[taps + 1],
        g_modw,
        g_modb,
    )


def solution(mesh):
    return jax.shard_map(
        body,
        mesh=mesh,
        in_specs=(
            P("dp", "seq", None),
            P("dp", "seq"),
            P("dp"),
            P(("dp", "seq"), None),
            P(("dp", "seq"), None),
            P(None, ("dp", "seq")),
            P(None, ("dp", "seq")),
            P(("dp", "seq"), None),
            P(("dp", "seq"), None),
            P(None, ("dp", "seq")),
            P(("dp", "seq")),
            P(("dp", "seq")),
            P(("dp", "seq"), None),
            P(("dp", "seq")),
            P("dp", "seq", None),
        ),
        out_specs=(
            P("dp", "seq", None),
            P("dp", "seq", None),
            P(("dp", "seq"), None),
            P(("dp", "seq"), None),
            P(None, ("dp", "seq")),
            P(None, ("dp", "seq")),
            P(("dp", "seq"), None),
            P(("dp", "seq"), None),
            P(None, ("dp", "seq")),
            P(("dp", "seq")),
            P(("dp", "seq")),
            P(("dp", "seq"), None),
            P(("dp", "seq")),
        ),
        check_vma=False,
    )
```

```python
import functools
import math

import jax
import jax.numpy as jnp
from jax import lax
from jax.experimental import pallas as pl
from jax.experimental.layout import Layout, with_layout_constraint
from jax.experimental.pallas import tpu as pltpu
from jax.sharding import PartitionSpec as P

FREQ = 256
EPS = 1e-06
HIGHEST = lax.Precision.HIGHEST
LOG2E = 1.4426950408889634
SUB = 16
WF = 384
WB = 768
F32, BF = jnp.float32, jnp.bfloat16
NT = (((1,), (1,)), ((), ()))


def columns_of(rows_t, base):
    turned = pltpu.roll(rows_t, rows_t.shape[1] - base, 1)
    return [jnp.broadcast_to(turned[:, j:j + 1], (rows_t.shape[0], 128)) for j in range(SUB)]


def wide(block, lanes):
    return jnp.concatenate([block] * (lanes // 128), axis=1) if lanes > 128 else block


def states_of(base, at):
    return pl.ds(pl.multiple_of((base + at) * 16, 16), 16)


def fwd_kernel(step_f, step_r, u_f, u_r, rate_f, rate_r, bt_f, bt_r, cblk_f, cblk_r,
               y_f, y_r, s_f, s_r, carry, f0, f1, r0, r1):
    rows, lanes = step_f.shape

    @pl.when(pl.program_id(0) == 0)
    def _():
        carry[...] = jnp.zeros(carry.shape, F32)

    wide_by = min(WF, lanes)
    cuts = [slice(c, c + wide_by) for c in range(0, lanes, wide_by)]

    def walk(states, bases, kept):
        cols = [columns_of(bt[...], base) for bt, base in zip((bt_f, bt_r), bases)]
        out = []
        for cut, pair in zip(cuts, states):
            pair = list(pair)
            rates = rate_f[:, cut], rate_r[:, cut]
            for k in range(SUB):
                for z, (step, u, s, j) in enumerate(((step_f, u_f, s_f, k), (step_r, u_r, s_r, SUB - 1 - k))):
                    at = pl.ds(bases[z] + j, 1)
                    decay = jnp.exp2(step[at, cut] * rates[z])
                    pair[z] = decay * pair[z] + u[at, cut] * wide(cols[z][j], wide_by)
                    low = pair[z].astype(BF)
                    s[states_of(bases[z], j), cut] = low
                    kept[z][j * 16:(j + 1) * 16, cut] = low
            out.append(tuple(pair))
        return tuple(out)

    def mix(base, cblk, kept, y):
        here = pl.ds(base, SUB)
        y[here, :] = jnp.dot(cblk[here, :], kept[...], preferred_element_type=F32)

    def start_of(a, flip):
        a = jnp.maximum(a, 0)
        return pl.multiple_of(rows - SUB - a * SUB if flip else a * SUB, SUB)

    def two(i, states):
        for half, (fk, rk, fp, rp) in enumerate(((f0, r0, f1, r1), (f1, r1, f0, r0))):
            a = 2 * i + half
            mix(start_of(a - 1, False), cblk_f, fp, y_f)
            mix(start_of(a - 1, True), cblk_r, rp, y_r)
            states = walk(states, (start_of(a, False), start_of(a, True)), (fk, rk))
        return states

    states = tuple((carry[0, :, cut], carry[1, :, cut]) for cut in cuts)
    states = lax.fori_loop(0, rows // SUB // 2, two, states)
    mix(rows - SUB, cblk_f, f1, y_f)
    mix(0, cblk_r, r1, y_r)
    for cut, pair in zip(cuts, states):
        carry[0, :, cut], carry[1, :, cut] = pair


def fwd_scan(steps, u, rates_f, rates_r, b_t, cblk, tile=128):
    length, lanes = steps.shape
    blocks = length // tile
    specs = []
    for order in (lambda t: t, lambda t: blocks - 1 - t):
        specs.append((
            pl.BlockSpec((tile, lanes), lambda t, order=order: (order(t), 0)),
            pl.BlockSpec((16, lanes), lambda t: (0, 0)),
            pl.BlockSpec((16, tile), lambda t, order=order: (0, order(t))),
            pl.BlockSpec((tile, 256), lambda t, order=order: (order(t), 0)),
            pl.BlockSpec((tile * 16, lanes), lambda t, order=order: (order(t), 0)),
        ))
    (row_f, rate, bt_f, blk_f, s_f), (row_r, _, bt_r, blk_r, s_r) = specs
    y = jax.ShapeDtypeStruct((length, lanes), F32)
    s = jax.ShapeDtypeStruct((length * 16, lanes), BF)
    kept = pltpu.VMEM((256, lanes), BF)
    return pl.pallas_call(
        fwd_kernel,
        grid=(blocks,),
        in_specs=[row_f, row_r, row_f, row_r, rate, rate, bt_f, bt_r, blk_f, blk_r],
        out_specs=[row_f, row_r, s_f, s_r],
        out_shape=[y, y, s, s],
        scratch_shapes=[pltpu.VMEM((2, 16, lanes), F32), kept, kept, kept, kept],
        compiler_params=pltpu.CompilerParams(vmem_limit_bytes=56 * 2**20, dimension_semantics=("arbitrary",)),
        cost_estimate=pl.CostEstimate(flops=length * lanes * 16 * 3200, transcendentals=0, bytes_accessed=length * lanes * 80),
        name="fwd_scan",
    )(steps, steps, u, u, rates_f, rates_r, b_t, b_t, cblk, cblk)


def bwd_kernel(step_f, step_r, u_f, u_r, gy_f, gy_r, rate_f, rate_r, ct_f, ct_r, bblk_f, bblk_r, s_f, s_r, sp_f, sp_r,
               dlog_f, dlog_r, adjb_f, adjb_r, bg_f, bg_r, cg_f, cg_r, rg_f, rg_r, carry,
               af0, af1, ar0, ar1, lf0, lf1, lr0, lr1):
    rows, lanes = step_f.shape
    t = pl.program_id(0)
    last = pl.num_programs(0) - 1

    @pl.when(t == 0)
    def _():
        carry[...] = jnp.zeros(carry.shape, F32)
        rg_f[...] = jnp.zeros(rg_f.shape, F32)
        rg_r[...] = jnp.zeros(rg_r.shape, F32)

    ones = (lax.broadcasted_iota(jnp.int32, (SUB, 256), 0) == lax.broadcasted_iota(jnp.int32, (SUB, 256), 1) // 16)
    onesb = ones.astype(BF)
    zero = jnp.zeros((SUB, 256), F32)

    def start_of(a, down):
        a = jnp.maximum(a, 0)
        return pl.multiple_of(rows - SUB - a * SUB if down else a * SUB, SUB)

    wide_by = min(WB, lanes)
    cuts = [slice(c, c + wide_by) for c in range(0, lanes, wide_by)]

    def walk(states, bases, keep_a, keep_l):
        cols = [columns_of(ct[...], base) for ct, base in zip((ct_f, ct_r), bases)]
        out = []
        for cut, pair in zip(cuts, states):
            pair = list(pair)
            rates = rate_f[:, cut], rate_r[:, cut]
            rg = [rg_f[:, cut], rg_r[:, cut]]
            low_rates = [r.astype(BF) for r in rates]
            some = [[], []]
            for k in range(SUB):
                for z, (step, gy, s, sp, j) in enumerate((
                        (step_f, gy_f, s_f, sp_f, SUB - 1 - k), (step_r, gy_r, s_r, sp_r, k))):
                    at = pl.ds(bases[z] + j, 1)
                    row = step[at, cut]
                    adj = gy[at, cut] * wide(cols[z][j], wide_by) + pair[z]
                    pair[z] = jnp.exp2(row * rates[z]) * adj
                    before = bases[z] + (j + 1 if z else j - 1)
                    if k < SUB - 1:
                        inner = s[pl.ds(pl.multiple_of(before * 16, 16), 16), cut]
                    else:
                        inside = before < rows if z else before >= 0
                        safe = jnp.clip(before, 0, rows - 1)
                        inner = s[pl.ds(pl.multiple_of(safe * 16, 16), 16), cut]
                        outer = jnp.where(t == last, jnp.zeros_like(inner), sp[:, cut])
                        inner = jnp.where(inside, inner, outer)
                    grad = pair[z].astype(BF) * inner
                    keep_a[z][j * 16:(j + 1) * 16, cut] = adj.astype(BF)
                    keep_l[z][j * 16:(j + 1) * 16, cut] = grad * low_rates[z]
                    some[z].append(grad * jnp.broadcast_to(row, (16, wide_by)).astype(BF))
                    if len(some[z]) == 4:
                        rg[z] = rg[z] + ((some[z][0] + some[z][1]) + (some[z][2] + some[z][3])).astype(F32)
                        some[z] = []
            rg_f[:, cut], rg_r[:, cut] = rg
            out.append(tuple(pair))
        return tuple(out)

    mix_by = 256 if lanes % 256 == 0 else 128

    def mix(base, a_ref, l_ref, u, gy, bblk, s, dlog, adjb, bg, cg):
        here = pl.ds(base, SUB)
        line = pl.ds(base // SUB, 1)
        group = pl.ds(pl.multiple_of(base * 16, 256), 256)
        bgd = cgd = zero
        for c in range(0, lanes, mix_by):
            cut = slice(c, c + mix_by)
            dlog[here, cut] = jnp.dot(onesb, l_ref[:, cut], preferred_element_type=F32)
            a = a_ref[:, cut]
            adjb[here, cut] = jnp.dot(bblk[here, :], a, preferred_element_type=F32)
            bgd = bgd + lax.dot_general(u[here, cut], a, NT, preferred_element_type=F32)
            cgd = cgd + lax.dot_general(gy[here, cut].astype(BF), s[group, cut], NT, preferred_element_type=F32)
        bg[line, :] = jnp.sum(jnp.where(ones, bgd, zero), axis=0, keepdims=True)
        cg[line, :] = jnp.sum(jnp.where(ones, cgd, zero), axis=0, keepdims=True)

    def mix_f(base, a_ref, l_ref):
        mix(base, a_ref, l_ref, u_f, gy_f, bblk_f, s_f, dlog_f, adjb_f, bg_f, cg_f)

    def mix_r(base, a_ref, l_ref):
        mix(base, a_ref, l_ref, u_r, gy_r, bblk_r, s_r, dlog_r, adjb_r, bg_r, cg_r)

    def two(i, states):
        bufs = ((af0, lf0, ar0, lr0), (af1, lf1, ar1, lr1))
        for half in range(2):
            a = 2 * i + half
            naf, nlf, nar, nlr = bufs[half]
            paf, plf, par, plr = bufs[1 - half]
            mix_f(start_of(a - 1, True), paf, plf)
            mix_r(start_of(a - 1, False), par, plr)
            states = walk(states, (start_of(a, True), start_of(a, False)), (naf, nar), (nlf, nlr))
        return states

    states = tuple((carry[0, :, cut], carry[1, :, cut]) for cut in cuts)
    states = lax.fori_loop(0, rows // SUB // 2, two, states)
    mix_f(0, af1, lf1)
    mix_r(rows - SUB, ar1, lr1)
    for cut, pair in zip(cuts, states):
        carry[0, :, cut], carry[1, :, cut] = pair


def bwd_scan(steps, u, gy, rates_f, rates_r, c_t, bblk, states_f, states_r, tile=128):
    length, lanes = steps.shape
    blocks = length // tile
    down = lambda t: blocks - 1 - t
    up = lambda t: t

    def specs(order, before):
        return (
            pl.BlockSpec((tile, lanes), lambda t: (order(t), 0)),
            pl.BlockSpec((16, lanes), lambda t: (0, 0)),
            pl.BlockSpec((16, tile), lambda t: (0, order(t))),
            pl.BlockSpec((tile, 256), lambda t: (order(t), 0)),
            pl.BlockSpec((tile * 16, lanes), lambda t: (order(t), 0)),
            pl.BlockSpec((16, lanes), lambda t: (before(t), 0)),
            pl.BlockSpec((tile // 16, 256), lambda t: (order(t), 0)),
        )

    row_f, rate, ct_f, blk_f, s_f, sp_f, diag_f = specs(down, lambda t: jnp.maximum((blocks - 1 - t) * tile - 1, 0))
    row_r, _, ct_r, blk_r, s_r, sp_r, diag_r = specs(up, lambda t: jnp.minimum((t + 1) * tile, length - 1))
    y = jax.ShapeDtypeStruct((length, lanes), F32)
    diag = jax.ShapeDtypeStruct((length // 16, 256), F32)
    rg = jax.ShapeDtypeStruct((16, lanes), F32)
    kept = pltpu.VMEM((256, lanes), BF)
    return pl.pallas_call(
        bwd_kernel,
        grid=(blocks,),
        in_specs=[row_f, row_r, row_f, row_r, row_f, row_r, rate, rate, ct_f, ct_r, blk_f, blk_r, s_f, s_r, sp_f, sp_r],
        out_specs=[row_f, row_r, row_f, row_r, diag_f, diag_r, diag_f, diag_r, rate, rate],
        out_shape=[y, y, y, y, diag, diag, diag, diag, rg, rg],
        scratch_shapes=[pltpu.VMEM((2, 16, lanes), F32)] + [kept] * 8,
        compiler_params=pltpu.CompilerParams(vmem_limit_bytes=56 * 2**20, dimension_semantics=("arbitrary",)),
        cost_estimate=pl.CostEstimate(flops=length * lanes * 16 * 6800, transcendentals=0, bytes_accessed=length * lanes * 100),
        name="bwd_scan",
    )(steps, steps, u, u, gy, gy, rates_f, rates_r, c_t, c_t, bblk, bblk, states_f, states_r, states_f, states_r)


def blockdiag(rows):
    length = rows.shape[0]
    eye = (jnp.arange(length)[:, None] % 16) == (jnp.arange(256)[None, :] // 16)
    return jnp.where(eye, jnp.tile(rows, (1, 16)), 0).astype(BF)


MESH = pl.DeviceIdType.MESH
VMEM = pl.BlockSpec(memory_space=pltpu.VMEM)
HBM = pl.BlockSpec(memory_space=pl.ANY)
DMA = pltpu.SemaphoreType.DMA


def send(src, dst, out_sem, in_sem, to):
    return pltpu.make_async_remote_copy(
        src_ref=src, dst_ref=dst, send_sem=out_sem, recv_sem=in_sem, device_id=to, device_id_type=MESH)


def greet(devices):
    bar = pltpu.get_barrier_semaphore()
    for to in devices:
        pl.semaphore_signal(bar, inc=1, device_id=to, device_id_type=MESH)
    pl.semaphore_wait(bar, len(devices))


def column_sum_kernel(ns, p_ref, o_ref, land, s1, r1, s2, r2):
    d, q = lax.axis_index("dp"), lax.axis_index("seq")
    others = [lax.rem(q + k, ns) for k in range(1, ns)]
    greet([(d, t) for t in others])
    for k, t in enumerate(others):
        send(p_ref.at[t], land.at[q], s1.at[k], r1.at[q], (d, t)).start()
    total = p_ref[q].astype(F32)
    for k, t in enumerate(others):
        send(p_ref.at[t], land.at[t], s1.at[k], r1.at[t], (d, t)).wait_recv()
        total = total + land[t].astype(F32)
    o_ref[q] = total.astype(o_ref.dtype)
    for k, t in enumerate(others):
        send(o_ref.at[q], o_ref.at[q], s2.at[k], r2.at[q], (d, t)).start()
    for k, t in enumerate(others):
        send(o_ref.at[t], o_ref.at[t], s2.at[k], r2.at[t], (d, t)).wait_recv()
    for k, t in enumerate(others):
        send(p_ref.at[t], land.at[q], s1.at[k], r1.at[q], (d, t)).wait_send()
        send(o_ref.at[q], o_ref.at[q], s2.at[k], r2.at[q], (d, t)).wait_send()


def column_sum(partial, ns, out_dtype, cid):
    rows, lanes = partial.shape
    block = (ns, rows // ns, lanes)
    out = pl.pallas_call(
        functools.partial(column_sum_kernel, ns),
        out_shape=jax.ShapeDtypeStruct(block, out_dtype),
        in_specs=[VMEM], out_specs=VMEM,
        scratch_shapes=[pltpu.VMEM(block, partial.dtype), DMA((ns,)), DMA((ns,)), DMA((ns,)), DMA((ns,))],
        compiler_params=pltpu.CompilerParams(
            collective_id=cid, has_side_effects=True, vmem_limit_bytes=32 * 2**20),
        name="column_sum",
    )(partial.reshape(block))
    return out.reshape(rows, lanes)


def mod_gather_kernel(nd, ns, g_ref, o_ref, land, s1, r1, s2, r2):
    d, q = lax.axis_index("dp"), lax.axis_index("seq")
    others = [lax.rem(q + k, ns) for k in range(1, ns)]
    peers = [lax.rem(d + k, nd) for k in range(1, nd)]
    greet([(d, t) for t in others] + [(e, q) for e in peers])
    for k, t in enumerate(others):
        send(g_ref, land.at[q], s1.at[k], r1.at[q], (d, t)).start()
    total = g_ref[...]
    for k, t in enumerate(others):
        send(g_ref, land.at[t], s1.at[k], r1.at[t], (d, t)).wait_recv()
        total = total + land[t]
    o_ref[d] = total
    for k, e in enumerate(peers):
        send(o_ref.at[d], o_ref.at[d], s2.at[k], r2.at[d], (e, q)).start()
    for k, e in enumerate(peers):
        send(o_ref.at[e], o_ref.at[e], s2.at[k], r2.at[e], (e, q)).wait_recv()
    for k, t in enumerate(others):
        send(g_ref, land.at[q], s1.at[k], r1.at[q], (d, t)).wait_send()
    for k, e in enumerate(peers):
        send(o_ref.at[d], o_ref.at[d], s2.at[k], r2.at[d], (e, q)).wait_send()


def mod_gather(g, nd, ns, cid):
    rows, lanes = g.shape
    return pl.pallas_call(
        functools.partial(mod_gather_kernel, nd, ns),
        out_shape=jax.ShapeDtypeStruct((nd, rows, lanes), F32),
        in_specs=[VMEM], out_specs=VMEM,
        scratch_shapes=[pltpu.VMEM((ns, rows, lanes), F32), DMA((ns,)), DMA((ns,)), DMA((nd,)), DMA((nd,))],
        compiler_params=pltpu.CompilerParams(
            collective_id=cid, has_side_effects=True, vmem_limit_bytes=32 * 2**20),
        name="mod_gather",
    )(g)


def home_kernel(nd, ns, nsub, g_ref, sm_ref, gm_ref, f_ref, so_ref, out_ref,
                pair, plane, spair, splane, ssum, up, down,
                sa, ra, sb, rb, sc, rc, ta, ra2, tb, rb2, tc, rc2, su, ru, sd, rd):
    d, q = lax.axis_index("dp"), lax.axis_index("seq")
    nc = nd // 2
    chip, core = d // 2, lax.rem(d, 2)
    mate = chip * 2 + 1 - core
    chips = [lax.rem(chip + k, nc) for k in range(1, nc)]
    others = [lax.rem(q + k, ns) for k in range(1, ns)]
    spread = nd // ns
    final_to = (spread * q + d // ns, lax.rem(d, ns))
    mine = d * ns + q
    final_from = (lax.rem(mine, nd), mine // nd)
    stays = jnp.logical_and(final_to[0] == d, final_to[1] == q)
    bar = pltpu.get_barrier_semaphore()
    friends = [(mate, q)] + [(c * 2 + core, q) for c in chips] + [(d, t) for t in others]
    for to in friends:
        pl.semaphore_signal(bar, inc=1, device_id=to, device_id_type=MESH)
    @pl.when(jnp.logical_not(stays))
    def _():
        pl.semaphore_signal(bar, inc=1, device_id=final_from, device_id_type=MESH)
        pl.semaphore_wait(bar, len(friends) + 1)
    @pl.when(stays)
    def _():
        pl.semaphore_wait(bar, len(friends))

    def first(c):
        return send(g_ref.at[c * 2 + 1 - core], pair.at[c], sa.at[c], ra.at[c], (mate, q))

    def first_small(c):
        return send(sm_ref.at[c * 2 + 1 - core], spair.at[c], ta.at[c], ra2.at[c], (mate, q))

    order = chips + [chip]
    for c in order:
        first(c).start()
        first_small(c).start()

    def rise(t, s, src):
        return send(src, up.at[t, s], su.at[t, s], ru.at[t, s], (d, q + 1))

    def sink(t, s, src):
        return send(src, down.at[t, s], sd.at[t, s], rd.at[t, s], (d, q - 1))

    def added(land, t, s):
        land[t, s] = (land[t, s].astype(F32) + gm_ref[t, s].astype(F32)).astype(BF)

    def step_up(t, s):
        @pl.when(q < t)
        def _():
            @pl.when(q == 0)
            def _():
                rise(t, s, gm_ref.at[t, s]).start()
            @pl.when(q > 0)
            def _():
                rise(t, s, up.at[t, s]).wait_recv()
                added(up, t, s)
                rise(t, s, up.at[t, s]).start()

    def step_down(t, s):
        @pl.when(q > t)
        def _():
            @pl.when(q == ns - 1)
            def _():
                sink(t, s, gm_ref.at[t, s]).start()
            @pl.when(q < ns - 1)
            def _():
                sink(t, s, down.at[t, s]).wait_recv()
                added(down, t, s)
                sink(t, s, down.at[t, s]).start()

    steps = [(k, s) for k in range(ns - 1) for s in range(nsub)]
    middle = len(steps) * 2 // 3

    def walk(some):
        for k, s in some:
            step_up(ns - 1 - k, s)
            step_down(k, s)

    def second(c, src):
        return send(pair.at[c], plane.at[src], sb.at[c], rb.at[src], (c * 2 + core, q))

    def second_small(c, src):
        return send(spair.at[c], splane.at[src], tb.at[c], rb2.at[src], (c * 2 + core, q))

    walk(steps[:1])
    for c in order:
        first(c).wait_recv()
        @pl.loop(0, ns)
        def _(t):
            pair[c, t] = (pair[c, t].astype(F32) + g_ref[c * 2 + core, t].astype(F32)).astype(BF)
        first_small(c).wait_recv()
        spair[c] = spair[c] + sm_ref[c * 2 + core]
        if c is not chip:
            second(c, chip).start()
            second_small(c, chip).start()
    walk(steps[1:middle])

    for c in chips:
        second(c, c).wait_recv()
        second_small(c, c).wait_recv()
    @pl.loop(0, ns)
    def _(t):
        total = pair[chip, t].astype(F32)
        for c in chips:
            total = total + plane[c, t].astype(F32)
        pair[chip, t] = total.astype(BF)
    small = spair[chip]
    for c in chips:
        small = small + splane[c]
    ssum[...] = small

    def third(t, src):
        return send(pair.at[chip, t], f_ref.at[src], sc.at[t], rc.at[src], (d, t))

    last = send(ssum, so_ref, tc, rc2, final_to)
    @pl.when(stays)
    def _():
        so_ref[...] = ssum[...]
    @pl.when(jnp.logical_not(stays))
    def _():
        last.start()
    for t in others:
        third(t, q).start()
    f_ref[q] = pair[chip, q]
    walk(steps[middle:])

    for s in range(nsub):
        total = gm_ref[q, s].astype(F32)
        out_ref[s] = total
        @pl.when(q > 0)
        def _():
            rise(q, s, gm_ref.at[q, s]).wait_recv()
            out_ref[s] += up[q, s].astype(F32)
        @pl.when(q < ns - 1)
        def _():
            sink(q, s, gm_ref.at[q, s]).wait_recv()
            out_ref[s] += down[q, s].astype(F32)
    for t in others:
        third(t, t).wait_recv()
    @pl.when(jnp.logical_not(stays))
    def _():
        last.wait_recv()
        last.wait_send()
    for c in order:
        first(c).wait_send()
        first_small(c).wait_send()
    for c in chips:
        second(c, chip).wait_send()
        second_small(c, chip).wait_send()
    for t in others:
        third(t, q).wait_send()
    for k, s in steps:
        t = ns - 1 - k
        @pl.when(q < t)
        def _():
            rise(t, s, gm_ref.at[t, s]).wait_send()
        @pl.when(q > k)
        def _():
            sink(k, s, gm_ref.at[k, s]).wait_send()


def home(g, small, gm, nd, ns, cid):
    rows, cols = g.shape[2:]
    nc, nsub = nd // 2, 4
    length, width = gm.shape
    part = length // ns // nsub
    v = small.shape[1:]
    gm = gm.reshape(ns, nsub, part, width)
    f, so, out = pl.pallas_call(
        functools.partial(home_kernel, nd, ns, nsub),
        out_shape=[
            jax.ShapeDtypeStruct((ns, rows, cols), BF),
            jax.ShapeDtypeStruct(v, F32),
            jax.ShapeDtypeStruct((nsub, part, width), F32),
        ],
        in_specs=[VMEM] * 3, out_specs=[VMEM] * 3,
        scratch_shapes=[
            pltpu.VMEM((nc, ns, rows, cols), BF), pltpu.VMEM((nc, ns, rows, cols), BF),
            pltpu.VMEM((nc,) + v, F32), pltpu.VMEM((nc,) + v, F32), pltpu.VMEM(v, F32),
            pltpu.VMEM((ns, nsub, part, width), BF), pltpu.VMEM((ns, nsub, part, width), BF),
            DMA((nc,)), DMA((nc,)), DMA((nc,)), DMA((nc,)), DMA((ns,)), DMA((ns,)),
            DMA((nc,)), DMA((nc,)), DMA((nc,)), DMA((nc,)), DMA(()), DMA(()),
            DMA((ns, nsub)), DMA((ns, nsub)), DMA((ns, nsub)), DMA((ns, nsub)),
        ],
        compiler_params=pltpu.CompilerParams(
            collective_id=cid, has_side_effects=True, vmem_limit_bytes=56 * 2**20),
        name="home",
    )(g, small, gm)
    return f, so, out.reshape(length // ns, width)


def start_kernel(nd, ns, nsub, fused, hid, win, wout, mask, emb, modw, modb, select, step, dec_f, dec_r, taps, fbias, sbias,
                 md_o, inner_o, gate_o, wx_o, select_o, step_o, rate_o, fil_o, mask_o, mod_o,
                 hv, wv, mv, iv, gv, pack, modw_v, pack_v, eland, prod, rowp, land1, land2,
                 su, ru, sd, rd, swz, rwx, swp, swm, spz, rp, spp, spm, sk, rk, se, re, s1, r1, s2, r2, own, out):
    d, q = lax.axis_index("dp"), lax.axis_index("seq")
    nc = nd // 2
    chip, core = d // 2, lax.rem(d, 2)
    mate = (chip * 2 + 1 - core, q)
    chips = [lax.rem(chip + k, nc) for k in range(1, nc)]
    others = [lax.rem(q + k, ns) for k in range(1, ns)]
    peers = [lax.rem(d + k, nd) for k in range(1, nd)]
    spread = nd // ns
    me = d * ns + q
    part = wout.shape[1] // ns
    rw = wout.shape[0]
    units = part // nd
    rank, states = step.shape[0], dec_f.shape[0]
    above = units + -units % 16
    taps_at = above + rank + 2 * states

    pack[...] = jnp.zeros(pack.shape, BF)
    pack[0:units, :] = select[...]
    pack[above:above + rank, 0:units] = step[...]
    pack[above + rank:above + rank + states, 0:units] = dec_f[...]
    pack[above + rank + states:taps_at, 0:units] = dec_r[...]
    pack[taps_at:taps_at + 16, 0:units] = jnp.concatenate(
        [taps[...].astype(F32), fbias[...].astype(F32), sbias[...].astype(F32),
         jnp.zeros((14 - taps.shape[0], units), F32)]).astype(BF)
    modw_v[...] = jnp.zeros(modw_v.shape, BF)
    modw_v[0:modw.shape[0], :] = modw[...]
    greet([(d, t) for t in others] + [(e, q) for e in peers])

    def column(ref, at):
        return ref.at[:, pl.ds(pl.multiple_of(at * part, 128), part)]

    def wrows(idx):
        return wv.at[pl.ds(pl.multiple_of(idx * rw, 16), rw), :]

    def pieces(t):
        return (column(win, t), column(win, ns + t), column(wout, t))

    def across(k, t, idx):
        return [
            send(src, wrows(idx).at[:, j * part:(j + 1) * part], swz.at[k, j], rwx.at[idx, j], (d, t))
            for j, src in enumerate(pieces(t))
        ]

    keep = [pltpu.make_async_copy(src, wrows(me).at[:, j * part:(j + 1) * part], own.at[j])
            for j, src in enumerate(pieces(q))]
    keep.append(pltpu.make_async_copy(hid, hv.at[q], own.at[3]))
    for copy in keep:
        copy.start()

    plane = d // spread
    slot = lax.rem(d, spread) * ns + q
    pack_z = send(pack, pack_v.at[slot], spz, rp.at[slot], (d, plane))
    pack_vwn = pltpu.make_async_copy(pack, pack_v.at[slot], own.at[4])

    @pl.when(plane == q)
    def _():
        pack_vwn.start()

    @pl.when(plane != q)
    def _():
        pack_z.start()

    def masks(k, t, src):
        return send(mask_o.at[src], mask_o.at[src], sk.at[k], rk.at[src], (d, t))

    def embeds(k, e, src):
        return send(eland.at[src], eland.at[src], se.at[k], re.at[src], (e, q))

    mask_o[q] = jnp.zeros(mask_o.shape[1:], BF)
    mask_o[q, 0:mask.shape[0], :] = mask[...].astype(F32).astype(BF)
    eland[d] = jnp.zeros(eland.shape[1:], BF)
    eland[d, 0:1, :] = emb[...]
    for k, e in enumerate(peers):
        embeds(k, e, d).start()
    for k, t in enumerate(others):
        masks(k, t, q).start()

    for k, t in enumerate(others):
        for copy in across(k, t, me)[:2]:
            copy.start()

    def rise(k, s):
        t = jnp.maximum(q - k, 0)
        src = hid.at[s] if k == 0 else hv.at[t, s]
        return send(src, hv.at[t, s], su.at[k, s], ru.at[k, s], (d, q + 1))

    def sink(k, s):
        t = jnp.minimum(q + k, ns - 1)
        src = hid.at[s] if k == 0 else hv.at[t, s]
        return send(src, hv.at[t, s], sd.at[k, s], rd.at[k, s], (d, q - 1))

    def hop(k, s):
        @pl.when(q >= k)
        def _():
            if k:
                rise(k - 1, s).wait_recv()
            if k < ns - 1:
                @pl.when(q + 1 < ns)
                def _():
                    rise(k, s).start()

        @pl.when(q + k < ns)
        def _():
            if k:
                sink(k - 1, s).wait_recv()
            if k < ns - 1:
                @pl.when(q >= 1)
                def _():
                    sink(k, s).start()

    for s in range(nsub):
        hop(0, s)
    for k, t in enumerate(others):
        across(k, t, me)[2].start()

    def cols_of(idx, kind):
        return wrows(idx).at[:, 2 * part * kind:2 * part + part * kind]

    def plane_w(c, idx, t, kind):
        return send(cols_of(idx, kind), cols_of(idx, kind), swp.at[kind, c, t], rwx.at[idx, 3 + kind], (c * 2 + core, q))

    def mate_w(c, idx, t, kind):
        return send(cols_of(idx, kind), cols_of(idx, kind), swm.at[kind, c, t], rwx.at[idx, 3 + kind], mate)

    def spread_w(t, kind):
        idx = d * ns + t
        for c in chips:
            plane_w(c, idx, t, kind).start()
        mate_w(chip, idx, t, kind).start()

    for copy in keep[:3]:
        copy.wait()
    spread_w(q, 0)

    for k, e in enumerate(peers):
        embeds(k, e, e).wait_recv()
    rows = modw_v.shape[0]
    here = lax.broadcasted_iota(jnp.int32, (FREQ, rows), 0)
    pick = here - lax.broadcasted_iota(jnp.int32, (FREQ, rows), 1)
    count = FREQ // (nd * ns)
    keep_col = lax.broadcasted_iota(jnp.int32, (FREQ, rows), 1) < count
    pick = jnp.where(jnp.logical_and(pick == me * count, keep_col), 1.0, 0.0).astype(BF)
    mine = jnp.dot(eland[...].reshape(nd * 16, FREQ), pick, preferred_element_type=F32).astype(BF)
    prod[...] = jnp.dot(mine, modw_v[...], preferred_element_type=F32)

    lines = prod.shape[1] // 128
    @pl.loop(0, nd)
    def _(e):
        rowp[e] = modb[...]
        for j in range(lines):
            rowp[e, j:j + 1, :] += prod[pl.ds(pl.multiple_of(e * 16, 16), 1), j * 128:(j + 1) * 128]

    def to_item(k, e, src):
        return send(rowp.at[e], land1.at[src], s1.at[k], r1.at[src], (e, q))

    for k, e in enumerate(peers):
        to_item(k, e, d).start()

    for k, t in enumerate(others):
        for copy in across(k, t, d * ns + t)[:2]:
            copy.wait_recv()
        spread_w(t, 0)

    def plane_p(c, i, t):
        return send(pack_v.at[i], pack_v.at[i], spp.at[c, t], rp.at[i], (c * 2 + core, q))

    def mate_p(c, i, t):
        return send(pack_v.at[i], pack_v.at[i], spm.at[c, t], rp.at[i], mate)

    base = lax.rem(d, spread) * ns

    @pl.when(plane == q)
    def _():
        pack_vwn.wait()
        for t in others:
            send(pack, pack_v.at[base + t], spz, rp.at[base + t], (d, plane)).wait_recv()
        for t in range(ns):
            for c in chips:
                plane_p(c, base + t, t).start()
            mate_p(chip, base + t, t).start()

    total = rowp[d]
    for k, e in enumerate(peers):
        to_item(k, e, e).wait_recv()
        total = total + land1[e]
    land2[q] = total

    def to_column(k, t, src):
        return send(land2.at[src], land2.at[src], s2.at[k], r2.at[src], (d, t))

    for k, t in enumerate(others):
        to_column(k, t, q).start()

    def relay_w(c, t, kind):
        idx = (c * 2 + core) * ns + t
        plane_w(c, idx, t, kind).wait_recv()
        mate_w(c, idx, t, kind).start()

    def holds(c):
        return (c * 2 + core) // spread == q

    def relay_p(c):
        first = lax.rem(c * 2 + core, spread) * ns
        @pl.when(holds(c))
        def _():
            for t in range(ns):
                plane_p(c, first + t, t).wait_recv()
                mate_p(c, first + t, t).start()

    def own_copies(t):
        return [pltpu.make_async_copy(src.at[t], dst.at[t], out.at[t, i]) for i, (src, dst) in enumerate(
            ((mv, md_o), (iv, inner_o), (gv, gate_o)) if fused else ((hv, md_o),))]

    local = hv.shape[1] * hv.shape[2]
    width = hv.shape[3]

    def project(t):
        if fused:
            shift, scale = mod_o[0:1, 0:width], 1.0 + mod_o[0:1, width:2 * width]
            for s in range(nsub):
                @pl.loop(0, local // nsub // 16)
                def _(r):
                    x = hv[t, s, pl.ds(pl.multiple_of(r * 16, 16), 16), :].astype(F32)
                    x = x - jnp.mean(x, axis=1, keepdims=True)
                    x = x * lax.rsqrt(jnp.mean(x * x, axis=1, keepdims=True) + EPS)
                    to = pl.multiple_of(s * (local // nsub) + r * 16, 16)
                    mv[t, pl.ds(to, 16), :] = (x * scale + shift).astype(BF)
            tile = part if part % 256 else part // 2

            @pl.loop(0, part // tile)
            def _(j):
                for target, base in ((iv, 0), (gv, part)):
                    n = pl.ds(pl.multiple_of(base + j * tile, 128), tile)
                    full = jnp.dot(mv[t], wv[:, n], preferred_element_type=F32)
                    target[t, :, pl.ds(pl.multiple_of(j * tile, 128), tile)] = full.astype(target.dtype)
        for copy in own_copies(t):
            copy.start()

    relays = [(c, t) for t in [q] + others for c in chips]
    at = 0
    for s in range(nsub):
        hop(1, s)
        upto = len(relays) * (s + 1) // (2 * nsub)
        for c, t in relays[at:upto]:
            relay_w(c, t, 0)
        at = upto
    spread_w(q, 1)
    for k, t in enumerate(others):
        across(k, t, d * ns + t)[2].wait_recv()
        spread_w(t, 1)
    for c, t in relays[at:]:
        relay_w(c, t, 0)
    for c in chips:
        relay_p(c)

    for k, t in enumerate(others):
        to_column(k, t, t).wait_recv()
    total = land2[0]
    for t in range(1, ns):
        total = total + land2[t]
    mod_o[...] = jnp.zeros(mod_o.shape, F32)
    for i in range(mod_o.shape[1] // 128):
        mod_o[0:1, i * 128:(i + 1) * 128] = total[i:i + 1, :]

    twin = 1 - core
    for c in range(nc):
        for t in range(ns):
            idx = (c * 2 + twin) * ns + t
            mate_w(c, idx, t, 0).wait_recv()
    keep[3].wait()

    def project_at(t):
        @pl.when(jnp.logical_and(t >= 0, t < ns))
        def _():
            project(jnp.clip(t, 0, ns - 1))

    for k in range(2, ns):
        for s in range(nsub):
            hop(k, s)
            if k == 2 and s == 0:
                project(q)
            if s == nsub - 3:
                project_at(q - k + 1)
            if s == nsub - 2:
                project_at(q + k - 1)

    for c, t in relays:
        relay_w(c, t, 1)
    for c in range(nc):
        for t in range(ns):
            idx = (c * 2 + twin) * ns + t
            mate_w(c, idx, t, 1).wait_recv()
    wx_copy = pltpu.make_async_copy(wv, wx_o, own.at[5])
    wx_copy.start()

    for c in range(nc):
        first = lax.rem(c * 2 + twin, spread) * ns
        @pl.when((c * 2 + twin) // spread == q)
        def _():
            for t in range(ns):
                mate_p(c, first + t, t).wait_recv()
    for j in range(nd):
        here = slice(j * units, (j + 1) * units)
        select_o[here, :] = pack_v[j, 0:units, :]
        step_o[:, here] = pack_v[j, above:above + rank, 0:units]
        rate_o[0:2 * states, here] = -jnp.exp(pack_v[j, above + rank:taps_at, 0:units].astype(F32))
        fil_o[:, here] = pack_v[j, taps_at:taps_at + 16, 0:units].astype(F32)
    rate_o[2 * states:4 * states, :] = rate_o[0:2 * states, :] * LOG2E

    project_at(q - ns + 1)
    project_at(q + ns - 1)

    for k, t in enumerate(others):
        masks(k, t, t).wait_recv()
    wx_copy.wait()
    for t in range(ns):
        for copy in own_copies(t):
            copy.wait()

    for k, t in enumerate(others):
        for copy in across(k, t, me):
            copy.wait_send()
        masks(k, t, q).wait_send()
        to_column(k, t, q).wait_send()
    for k, e in enumerate(peers):
        embeds(k, e, d).wait_send()
        to_item(k, e, d).wait_send()

    @pl.when(plane != q)
    def _():
        pack_z.wait_send()

    @pl.when(plane == q)
    def _():
        for t in range(ns):
            for c in chips:
                plane_p(c, base + t, t).wait_send()
            mate_p(chip, base + t, t).wait_send()

    for kind in range(2):
        for t in range(ns):
            for c in chips:
                plane_w(c, d * ns + t, t, kind).wait_send()
                mate_w(c, (c * 2 + core) * ns + t, t, kind).wait_send()
            mate_w(chip, d * ns + t, t, kind).wait_send()
    for c in chips:
        first = lax.rem(c * 2 + core, spread) * ns
        @pl.when(holds(c))
        def _():
            for t in range(ns):
                mate_p(c, first + t, t).wait_send()
    for k in range(ns - 1):
        for s in range(nsub):
            @pl.when(jnp.logical_and(q >= k, q + 1 < ns))
            def _():
                rise(k, s).wait_send()
            @pl.when(jnp.logical_and(q + k < ns, q >= 1))
            def _():
                sink(k, s).wait_send()


def start(hidden, mask, win, wout, embedded, modw, modb, small, fused, nd, ns, cid):
    nsub = 4
    length, width = hidden.shape
    rows, inner = wout.shape
    part = inner // ns
    nc = nd // 2
    hidden = hidden.reshape(nsub, length // nsub, width)
    lines = modb.shape
    rank, units, states = small[1].shape[0], part // nd, small[2].shape[0]
    pack = (units + -units % 16 + rank + 2 * states + 16, 128)
    held = modw.shape[0] + -modw.shape[0] % 16
    runs = (ns,) + (hidden.shape if not fused else (length, width))
    return pl.pallas_call(
        functools.partial(start_kernel, nd, ns, nsub, fused),
        out_shape=[
            jax.ShapeDtypeStruct(runs, BF),
            jax.ShapeDtypeStruct((ns, length, part), BF),
            jax.ShapeDtypeStruct((ns, length, part), F32),
            jax.ShapeDtypeStruct((nd * ns * rows, 3 * part), BF),
            jax.ShapeDtypeStruct((part, 128), BF),
            jax.ShapeDtypeStruct((rank, part), BF),
            jax.ShapeDtypeStruct((4 * states, part), F32),
            jax.ShapeDtypeStruct((16, part), F32),
            jax.ShapeDtypeStruct((ns, 16, 128), BF),
            jax.ShapeDtypeStruct((8, modw.shape[1]), F32),
        ],
        in_specs=[HBM, HBM, HBM] + [VMEM] * 11,
        out_specs=[HBM] * 4 + [VMEM] * 6,
        scratch_shapes=[
            pltpu.VMEM((ns,) + hidden.shape, BF), pltpu.VMEM((nd * ns * rows, 3 * part), BF),
            pltpu.VMEM((ns, length, width), BF), pltpu.VMEM((ns, length, part), BF), pltpu.VMEM((ns, length, part), F32),
            pltpu.VMEM(pack, BF), pltpu.VMEM((held, modw.shape[1]), BF), pltpu.VMEM((nd,) + pack, BF),
            pltpu.VMEM((nd, 16, FREQ), BF), pltpu.VMEM((nd * 16, modw.shape[1]), F32),
            pltpu.VMEM((nd,) + lines, F32), pltpu.VMEM((nd,) + lines, F32), pltpu.VMEM((ns,) + lines, F32),
            DMA((ns - 1, nsub)), DMA((ns - 1, nsub)), DMA((ns - 1, nsub)), DMA((ns - 1, nsub)),
            DMA((ns, 3)), DMA((nd * ns, 5)), DMA((2, nc, ns)), DMA((2, nc, ns)),
            DMA(()), DMA((nd,)), DMA((nc, ns)), DMA((nc, ns)),
            DMA((ns,)), DMA((ns,)), DMA((nd,)), DMA((nd,)),
            DMA((nd,)), DMA((nd,)), DMA((ns,)), DMA((ns,)), DMA((6,)), DMA((ns, 3)),
        ],
        compiler_params=pltpu.CompilerParams(
            collective_id=cid, has_side_effects=True, vmem_limit_bytes=56 * 2**20),
        name="start",
    )(hidden, win, wout, mask, embedded, modw, modb, *small)


def end_kernel(nd, ns, nsub, rows, turned,
               gp_h, md_h, wx_h, gsel, gstep, gdf, gdr, gfil, hid_ref, cot_ref, line_ref, early,
               gin_o, gout_o, sel_o, step_o, df_o, dr_o, taps_o, fb_o, sb_o, gh_o, mod_o,
               gp, md, wx, sm_ref, so_ref, gm, made, pair, plane, spair, splane, ssum, fro, ready, up, down, own, acc, msg, mland,
               ld, sa, ra, sb, rb, sc, rc, se, re, ta, ra2, tb, rb2, tc, rc2, su, ru, sd, rd, s1, r1, s2, r2):
    d, q = lax.axis_index("dp"), lax.axis_index("seq")
    nc = nd // 2
    chip, core = d // 2, lax.rem(d, 2)
    mate = chip * 2 + 1 - core
    pairs = [(1, 1), (1, 0), (0, 1)] + [(a, b) for b in range(2, nc // 2) for a in (0, 1)]
    chips = [lax.rem(chip + a, 2) + 2 * lax.rem(chip // 2 + b, nc // 2) for a, b in pairs]
    others = [lax.rem(q + k, ns) for k in range(1, ns)]
    peers = [lax.rem(d + k, nd) for k in range(1, nd)]
    spread = nd // ns
    final_to = (spread * q + d // ns, lax.rem(d, ns))
    me = d * ns + q
    final_from = (lax.rem(me, nd), me // nd)
    stays = jnp.logical_and(final_to[0] == d, final_to[1] == q)
    length, cols = gp.shape
    part = cols // 2
    width = wx.shape[0]
    local = length // ns
    sub = local // nsub
    rw = pair.shape[2]
    half = ns * rw

    loads = [pltpu.make_async_copy(src, dst, ld.at[i]) for i, (src, dst) in enumerate(
        ((gp_h, gp), (wx_h.at[:, 0:cols], wx), (md_h, md)))]
    for copy in loads:
        copy.start()

    units = part // nd
    rank, states, taps = gstep.shape[0], gdf.shape[0], taps_o.shape[0]
    above = units + -units % 16
    taps_at = above + rank + 2 * states
    bar = pltpu.get_barrier_semaphore()
    friends = [(e, q) for e in peers] + [(d, t) for t in others]
    for to in friends:
        pl.semaphore_signal(bar, inc=1, device_id=to, device_id_type=MESH)
    @pl.when(jnp.logical_not(stays))
    def _():
        pl.semaphore_signal(bar, inc=1, device_id=final_from, device_id_type=MESH)

    def tokens(t):
        @pl.loop(0, width // 512)
        def _(j):
            here = pl.ds(pl.multiple_of(j * 512, 512), 512)
            full = lax.dot_general(gp[t * local:(t + 1) * local, :], wx[here, :], NT, preferred_element_type=F32)
            full = full.astype(BF)
            for s in range(nsub):
                gm[t, s, :, here] = full[s * sub:(s + 1) * sub]

    def rise(t, s, src):
        return send(src, up.at[t, s], su.at[t, s], ru.at[t, s], (d, q + 1))

    def sink(t, s, src):
        return send(src, down.at[t, s], sd.at[t, s], rd.at[t, s], (d, q - 1))

    def added(land, t, s):
        land[t, s] = (land[t, s].astype(F32) + gm[t, s].astype(F32)).astype(BF)

    def open_up(t, s):
        @pl.when(jnp.logical_and(q == 0, t > 0))
        def _():
            rise(t, s, gm.at[t, s]).start()

    def open_down(t, s):
        @pl.when(jnp.logical_and(q == ns - 1, t < ns - 1))
        def _():
            sink(t, s, gm.at[t, s]).start()

    def step(k, s):
        t = ns - 1 - k

        @pl.when(jnp.logical_and(q < t, q > 0))
        def _():
            rise(t, s, up.at[t, s]).wait_recv()
            added(up, t, s)
            rise(t, s, up.at[t, s]).start()

        @pl.when(jnp.logical_and(q > k, q < ns - 1))
        def _():
            sink(k, s, down.at[k, s]).wait_recv()
            added(down, k, s)
            sink(k, s, down.at[k, s]).start()

    def far(k):
        for t in sorted({ns - 1 - k, k}, reverse=True):
            tokens(t)
            for s in range(nsub):
                open_up(t, s)
                open_down(t, s)

    @pl.when(stays)
    def _():
        pl.semaphore_wait(bar, len(friends))

    @pl.when(jnp.logical_not(stays))
    def _():
        pl.semaphore_wait(bar, len(friends) + 1)

    def whole(t, src):
        return send(early.at[t], ready.at[src], se.at[t], re.at[src], (d, t))

    for t in others:
        whole(t, q).start()
    loads[0].wait()
    loads[1].wait()
    far(0)
    steps = [(k, s) for k in range(ns - 1) for s in range(nsub)]

    def first(c):
        return send(made.at[c, 1 - core], pair.at[c], sa.at[c], ra.at[c], (mate, q))

    def first_small(c):
        return send(sm_ref.at[c * 2 + 1 - core], spair.at[c], ta.at[c], ra2.at[c], (mate, q))

    def second(c, src):
        return send(pair.at[c], plane.at[src], sb.at[c], rb.at[src], (c * 2 + core, q))

    def second_small(c, src):
        return send(spair.at[c], splane.at[src], tb.at[c], rb2.at[src], (c * 2 + core, q))

    def block(c):
        at = pl.ds(pl.multiple_of(c * 2 * half, 2 * half), 2 * half)
        tile = part if part % 256 else part // 2
        left = md[at, :] if turned else md[:, at].T

        @pl.loop(0, part // tile)
        def _(j):
            n = pl.ds(pl.multiple_of(j * tile, 128), tile)
            full = jnp.dot(left, gp[:, n], preferred_element_type=F32).astype(BF)
            for h in range(2):
                for t in range(ns):
                    line = (h * ns + t) * rw
                    made[c, h, t, :, n] = full[line:line + rw]

    sm_ref[...] = jnp.zeros(sm_ref.shape, F32)
    for j in range(nd):
        here = slice(j * units, (j + 1) * units)
        sm_ref[j, 0:units, :] = gsel[here, :]
        sm_ref[j, above:above + rank, 0:units] = gstep[:, here]
        sm_ref[j, above + rank:above + rank + states, 0:units] = gdf[:, here]
        sm_ref[j, above + rank + states:taps_at, 0:units] = gdr[:, here]
        sm_ref[j, taps_at:taps_at + 8, 0:units] = gfil[:, here]

    loads[2].wait()
    order = chips + [chip]

    def give(c):
        block(c)
        first(c).start()
        first_small(c).start()

    give(order[0])
    for k in range(1, ns // 2):
        far(k)
    for i, c in enumerate(order):
        if i + 1 < nc:
            give(order[i + 1])
        first(c).wait_recv()
        @pl.loop(0, ns)
        def _(t):
            pair[c, t] = (pair[c, t].astype(F32) + made[c, core, t].astype(F32)).astype(BF)
        first_small(c).wait_recv()
        spair[c] = spair[c] + sm_ref[c * 2 + core]
        if i < nc - 1:
            second(c, chip).start()
            second_small(c, chip).start()
        for k, s in steps[i:i + 1]:
            step(k, s)
    late = len(steps) * 3 // 4
    for k, s in steps[nc:late]:
        step(k, s)

    for c in chips:
        second(c, c).wait_recv()
        second_small(c, c).wait_recv()
    @pl.loop(0, ns)
    def _(t):
        total = pair[chip, t].astype(F32)
        for c in chips:
            total = total + plane[c, t].astype(F32)
        pair[chip, t] = total.astype(BF)
    small = spair[chip]
    for c in chips:
        small = small + splane[c]
    ssum[...] = small

    def third(t, src):
        return send(pair.at[chip, t], fro.at[src], sc.at[t], rc.at[src], (d, t))

    last = send(ssum, so_ref, tc, rc2, final_to)
    @pl.when(stays)
    def _():
        so_ref[...] = ssum[...]
    @pl.when(jnp.logical_not(stays))
    def _():
        last.start()
    for t in others:
        third(t, q).start()
    fro[q] = pair[chip, q]
    for k, s in steps[max(nc, late):]:
        step(k, s)

    acc[...] = jnp.zeros(acc.shape, F32)
    acc[2:4, :] = line_ref[1:3, :]
    scale = 1.0 + line_ref[0:1, :]
    for s in range(nsub):
        own[...] = gm[q, s].astype(F32)

        @pl.when(q > 0)
        def _():
            rise(q, s, gm.at[q, s]).wait_recv()
            own[...] += up[q, s].astype(F32)

        @pl.when(q < ns - 1)
        def _():
            sink(q, s, gm.at[q, s]).wait_recv()
            own[...] += down[q, s].astype(F32)

        @pl.loop(0, sub // 16)
        def _(r):
            here = pl.ds(pl.multiple_of(r * 16, 16), 16)
            grad = own[here, :]
            x = hid_ref[s, here, :].astype(F32)
            x = x - jnp.mean(x, axis=1, keepdims=True)
            inverse = lax.rsqrt(jnp.mean(x * x, axis=1, keepdims=True) + EPS)
            normed = x * inverse
            acc[0:1, :] += jnp.sum(grad, axis=0, keepdims=True)
            acc[1:2, :] += jnp.sum(grad * normed, axis=0, keepdims=True)
            grad = grad * scale
            grad = grad - jnp.mean(grad, axis=1, keepdims=True) - normed * jnp.mean(
                grad * normed, axis=1, keepdims=True)
            gh_o[s, here, :] = (cot_ref[s, here, :].astype(F32) + inverse * grad).astype(BF)

    msg[...] = jnp.zeros(msg.shape, F32)
    long = msg.shape[1] // 128
    for i in range(3 * width // 128 + FREQ // 128):
        r, c = divmod(i * 128, width)
        to = (i % long) * 128
        msg[i // long:i // long + 1, to:to + 128] = acc[r:r + 1, c:c + 128]
    for k, t in enumerate(others):
        send(msg, mland.at[q], s1.at[k], r1.at[q], (d, t)).start()

    inner = part * ns

    def place(src, rest):
        at = src * part
        gin_o[:, pl.ds(pl.multiple_of(at, 128), part)] = fro[src, 0:rows, :].astype(F32)
        gin_o[:, pl.ds(pl.multiple_of(inner + at, 128), part)] = rest[0:rows, 0:part].astype(F32)
        gout_o[:, pl.ds(pl.multiple_of(at, 128), part)] = rest[0:rows, part:2 * part].astype(F32)

    place(q, early[q])
    total = msg[...]
    for k, t in enumerate(others):
        send(msg, mland.at[t], s1.at[k], r1.at[t], (d, t)).wait_recv()
        total = total + mland[t]
    mod_o[d] = total
    for k, e in enumerate(peers):
        send(mod_o.at[d], mod_o.at[d], s2.at[k], r2.at[d], (e, q)).start()
    for t in others:
        third(t, t).wait_recv()
        whole(t, t).wait_recv()
        place(t, ready[t])
    for k, e in enumerate(peers):
        send(mod_o.at[e], mod_o.at[e], s2.at[k], r2.at[e], (e, q)).wait_recv()
    @pl.when(jnp.logical_not(stays))
    def _():
        last.wait_recv()
        last.wait_send()

    sel_o[...] = so_ref[0:units, :]
    step_o[...] = so_ref[above:above + rank, 0:units]
    df_o[...] = so_ref[above + rank:above + rank + states, 0:units]
    dr_o[...] = so_ref[above + rank + states:taps_at, 0:units]
    taps_o[...] = so_ref[taps_at:taps_at + taps, 0:units]
    fb_o[...] = so_ref[taps_at + taps:taps_at + taps + 1, 0:units]
    sb_o[...] = so_ref[taps_at + taps + 1:taps_at + taps + 2, 0:units]
    for c in order:
        first(c).wait_send()
        first_small(c).wait_send()
    for c in chips:
        second(c, chip).wait_send()
        second_small(c, chip).wait_send()
    for k, t in enumerate(others):
        third(t, q).wait_send()
        whole(t, q).wait_send()
        send(msg, mland.at[q], s1.at[k], r1.at[q], (d, t)).wait_send()
    for k, e in enumerate(peers):
        send(mod_o.at[d], mod_o.at[d], s2.at[k], r2.at[d], (e, q)).wait_send()
    for k, s in steps:
        t = ns - 1 - k
        @pl.when(q < t)
        def _():
            rise(t, s, gm.at[t, s]).wait_send()
        @pl.when(q > k)
        def _():
            sink(k, s, gm.at[k, s]).wait_send()


def end(grad_projected, modded, wx, early, small, taps, hidden, cot, line, rows, nd, ns, cid):
    length, cols = grad_projected.shape
    part = cols // 2
    width = wx.shape[0]
    inner = part * ns
    nc, nsub = nd // 2, 4
    local = length // ns
    sub = local // nsub
    rw = rows + -rows % 16
    half = ns * rw
    turned = 2 * half % 128 != 0 or rw != rows
    if turned:
        def turn(a):
            a = a.T.reshape(nd * ns, rows, length)
            return jnp.pad(a, ((0, 0), (0, rw - rows), (0, 0))).reshape(nd * ns * rw, length)
        modded = turn(modded)
    early = jnp.pad(early.reshape(ns, rows, cols), ((0, 0), (0, rw - rows), (0, 0)))
    short = -(-(3 * width + FREQ) // 1024) * 128
    units, rank, states = part // nd, small[1].shape[0], small[2].shape[0]
    v = (units + -units % 16 + rank + 2 * states + 16, 128)
    hidden, cot = hidden.reshape(nsub, sub, width), cot.reshape(nsub, sub, width)
    blocks = pltpu.VMEM((nc, ns, rw, part), BF)
    smalls = pltpu.VMEM((nc,) + v, F32)
    runs = pltpu.VMEM((ns, nsub, sub, width), BF)
    gin, gout, *own, gh, mod = pl.pallas_call(
        functools.partial(end_kernel, nd, ns, nsub, rows, turned),
        out_shape=[
            jax.ShapeDtypeStruct((rows, 2 * inner), F32),
            jax.ShapeDtypeStruct((rows, inner), F32),
            jax.ShapeDtypeStruct((units, 128), F32),
            jax.ShapeDtypeStruct((rank, units), F32),
            jax.ShapeDtypeStruct((states, units), F32),
            jax.ShapeDtypeStruct((states, units), F32),
            jax.ShapeDtypeStruct((taps, units), F32),
            jax.ShapeDtypeStruct((1, units), F32),
            jax.ShapeDtypeStruct((1, units), F32),
            jax.ShapeDtypeStruct((nsub, sub, width), BF),
            jax.ShapeDtypeStruct((nd, 8, short), F32),
        ],
        in_specs=[HBM] * 3 + [VMEM] * 9, out_specs=[VMEM] * 11,
        scratch_shapes=[
            pltpu.VMEM(grad_projected.shape, BF), pltpu.VMEM(modded.shape, BF), pltpu.VMEM((width, cols), BF),
            pltpu.VMEM((nd,) + v, F32), pltpu.VMEM(v, F32), runs,
            pltpu.VMEM((nc, 2, ns, rw, part), BF), blocks, blocks,
            smalls, smalls, pltpu.VMEM(v, F32), pltpu.VMEM((ns, rw, part), BF), pltpu.VMEM((ns, rw, cols), BF), runs, runs,
            pltpu.VMEM((sub, width), F32), pltpu.VMEM((8, width), F32), pltpu.VMEM((8, short), F32),
            pltpu.VMEM((ns, 8, short), F32),
            DMA((3,)),
            DMA((nc,)), DMA((nc,)), DMA((nc,)), DMA((nc,)), DMA((ns,)), DMA((ns,)), DMA((ns,)), DMA((ns,)),
            DMA((nc,)), DMA((nc,)), DMA((nc,)), DMA((nc,)), DMA(()), DMA(()),
            DMA((ns, nsub)), DMA((ns, nsub)), DMA((ns, nsub)), DMA((ns, nsub)),
            DMA((ns,)), DMA((ns,)), DMA((nd,)), DMA((nd,)),
        ],
        compiler_params=pltpu.CompilerParams(
            collective_id=cid, has_side_effects=True, vmem_limit_bytes=60 * 2**20),
        name="end",
    )(grad_projected, modded, wx, *small, hidden, cot, line, early)
    return gin, gout, own, gh.reshape(local, width), mod


def frequency_embed(timestep):
    half_width = FREQ // 2
    counter = jnp.arange(half_width, dtype=F32)
    frequency = jnp.exp(counter * (-math.log(10000.0) / half_width))
    angles = timestep.astype(F32)[:, None] * frequency[None, :]
    return jnp.concatenate([jnp.cos(angles), jnp.sin(angles)], axis=1)


def dot(a, b):
    return jnp.dot(a, b, preferred_element_type=F32)


def dot_nt(a, b):
    return lax.dot_general(a, b, (((1,), (1,)), ((), ())), preferred_element_type=F32)


def dot_tn(a, b):
    return lax.dot_general(a, b, (((0,), (0,)), ((), ())), preferred_element_type=F32)


def body(
    hidden,
    pad_mask,
    timestep,
    input_weight,
    select_weight,
    step_weight,
    output_weight,
    decay_forward,
    decay_reverse,
    filter_weight,
    filter_bias,
    step_bias,
    modulation_weight,
    modulation_bias,
    cotangent,
):
    ns, nd = lax.axis_size("seq"), lax.axis_size("dp")
    q, d = lax.axis_index("seq"), lax.axis_index("dp")
    every = ("dp", "seq")
    local_len, width = hidden.shape[1:]
    length = local_len * ns
    inner = output_weight.shape[0]
    part = inner // ns
    rank = step_weight.shape[0]
    state = decay_forward.shape[1]
    taps = filter_weight.shape[0]
    rows_in = input_weight.shape[0]
    lanes = select_weight.shape[1]

    units = part // nd
    embedded = jax.nn.silu(frequency_embed(timestep)).astype(BF)
    modb = jnp.zeros((-(-3 * width // 1024) * 1024,), F32)
    modb = lax.dynamic_update_slice(modb, modulation_bias.astype(F32), ((d * ns + q) * modulation_bias.shape[0],))
    row_pad = ((0, -rows_in % 16), (0, 0))
    fused = rows_in % 16 == 0
    modded, inner_part, gate_branch, wx, select_q, step_q, rates, fil, mask, modulation = start(
        hidden[0], pad_mask.reshape(-1, 128), jnp.pad(input_weight, row_pad), jnp.pad(output_weight.T, row_pad),
        embedded, modulation_weight, modb.reshape(-1, 128),
        (select_weight, step_weight, decay_forward.T, decay_reverse.T, filter_weight, filter_bias[None], step_bias[None]),
        fused, nd, ns, 4)
    wx = wx.reshape(nd * ns, -1, 3 * part)[:, :rows_in].reshape(width, 3 * part)
    win, wout = wx[:, : 2 * part], wx[:, 2 * part :]
    mask = mask[:, : local_len // 128].reshape(length, 1).astype(F32)
    rates_f, rates_r, rates_f2, rates_r2 = [rates[k * state : (k + 1) * state] for k in range(4)]
    modulation = modulation[:1]
    shifts = modulation[:, :width]
    scales = modulation[:, width : 2 * width]
    gate_scale = modulation[:, 2 * width :]

    def norm(x):
        x = x.astype(F32)
        centered = x - jnp.mean(x, axis=1, keepdims=True)
        inverse = lax.rsqrt(jnp.mean(centered * centered, axis=1, keepdims=True) + EPS)
        return centered * inverse, inverse

    if fused:
        modded = modded.reshape(length, width)
        inner_part, gate_branch = inner_part.reshape(length, part), gate_branch.reshape(length, part)
    else:
        modded = (norm(modded.reshape(length, width))[0] * (1.0 + scales) + shifts).astype(BF)
        projected = dot(modded, win)
        inner_part, gate_branch = projected[:, :part].astype(BF), projected[:, part:]
    inner_part = inner_part.astype(F32) * mask
    padded = jnp.pad(inner_part, ((taps - 1, 0), (0, 0)))
    filtered = fil[taps][None]
    for k in range(taps):
        filtered = filtered + fil[k][None] * padded[k : k + length]
    sigma_filter = jax.nn.sigmoid(filtered)
    active = (filtered * sigma_filter).astype(BF)
    active32 = active.astype(F32)
    selected = column_sum(dot(active, select_q).astype(BF), ns, BF, 0)
    cot, selected = lax.optimization_barrier((cotangent[0], selected))
    cot = lax.all_gather(cot, "seq", axis=0, tiled=True)
    low_rank = selected[:, :rank].astype(BF)
    b_rows = selected[:, rank : rank + state].astype(F32)
    c_rows = selected[:, rank + state :].astype(F32)
    pre_steps = dot(low_rank, step_q) + fil[taps + 1][None]
    steps = jax.nn.softplus(pre_steps)
    drive = steps * active32
    mixed_f, mixed_r, states_f, states_r = fwd_scan(steps, drive, rates_f2, rates_r2, b_rows.T, blockdiag(c_rows))
    merged = mixed_f + mixed_r
    sigma_gate = jax.nn.sigmoid(gate_branch)
    silu_gate = gate_branch * sigma_gate
    gated = (merged * silu_gate).astype(BF)
    branch = dot_nt(gated, wout).astype(BF)
    branch, cot = lax.optimization_barrier((branch, cot))
    branch = lax.psum_scatter(branch, "seq", scatter_dimension=0, tiled=True).astype(F32)

    mask_here = pad_mask[0].astype(F32)[:, None]
    cot_here = cotangent[0].astype(F32)
    block_out = (hidden[0].astype(F32) + gate_scale * mask_here * branch).astype(BF)
    grad_gate = jnp.sum(mask_here * cot_here * branch, axis=0)

    grad_branch = lax.optimization_barrier((cot.astype(F32) * gate_scale * mask).astype(BF))
    grad_gated = dot(grad_branch, wout)
    grad_merged = grad_gated * silu_gate
    grad_gate_branch = grad_gated * merged * sigma_gate * (1.0 + gate_branch * (1.0 - sigma_gate))
    grad_gate_branch = grad_gate_branch.astype(BF)
    rows_first = Layout((0, 1))
    early = jnp.concatenate([
        with_layout_constraint(dot_tn(modded, grad_gate_branch).astype(BF), rows_first),
        with_layout_constraint(dot_tn(grad_branch, gated).astype(BF), rows_first)], axis=1)
    early = lax.psum_scatter(early, "dp", scatter_dimension=0, tiled=True)
    dlog_f, dlog_r, adjb_f, adjb_r, bg_f, bg_r, cg_f, cg_r, rg_f, rg_r = bwd_scan(
        steps, drive.astype(BF), grad_merged, rates_f2, rates_r2, c_rows.T, blockdiag(b_rows), states_f, states_r)
    adjb = adjb_f + adjb_r
    grad_steps = (dlog_f + dlog_r) * (1.0 / LOG2E) + active32 * adjb
    grad_b = (bg_f + bg_r).reshape(length, state)
    grad_c = (cg_f + cg_r).reshape(length, state)
    grad_decay_f = rg_f * rates_f
    grad_decay_r = rg_r * rates_r
    grad_pre = grad_steps * jax.nn.sigmoid(pre_steps)
    grad_step_bias = jnp.sum(grad_pre, axis=0)
    grad_pre_low = grad_pre.astype(BF)
    grad_step = dot_tn(low_rank, grad_pre_low)
    grad_low_rank = dot_nt(grad_pre_low, step_q)
    grad_selected = column_sum(jnp.concatenate([grad_low_rank, grad_b, grad_c], axis=1).astype(BF), ns, BF, 1)
    grad_select = dot_tn(active, grad_selected)
    grad_active = steps * adjb + dot_nt(grad_selected, select_q)
    grad_filtered = grad_active * sigma_filter * (1.0 + filtered * (1.0 - sigma_filter))
    extended = jnp.pad(grad_filtered, ((0, taps - 1), (0, 0)))
    grad_inner = jnp.zeros_like(grad_filtered)
    filter_rows = []
    for k in range(taps):
        lead = taps - 1 - k
        grad_inner = grad_inner + fil[k][None] * extended[lead : lead + length]
        filter_rows.append(jnp.sum(grad_filtered * padded[k : k + length], axis=0))
    grad_filter_bias = jnp.sum(grad_filtered, axis=0)
    grad_projected = jnp.concatenate([(grad_inner * mask).astype(BF), grad_gate_branch], axis=1)
    grad_fil = jnp.stack(filter_rows + [grad_filter_bias, grad_step_bias])
    grad_fil = jnp.pad(grad_fil, ((0, 8 - grad_fil.shape[0]), (0, 0)))
    line = jnp.concatenate([scales, grad_gate[None], jnp.pad(embedded.astype(F32) / ns, ((0, 0), (0, width - FREQ))),
                            jnp.zeros((5, width), F32)])
    g_in, g_out, own, grad_hidden, sums = end(
        grad_projected, modded, wx, early, (grad_select, grad_step, grad_decay_f, grad_decay_r, grad_fil), taps, hidden[0], cotangent[0], line, rows_in, nd, ns, 2)
    gs_select, gs_step, gs_f, gs_r, gs_taps, gs_fbias, gs_sbias = own
    sums = sums.reshape(nd, -1)
    embeds = sums[:, 3 * width : 3 * width + FREQ]
    grad_mod = sums[:, : 3 * width]
    me = d * ns + q
    mine = lax.dynamic_slice_in_dim(embeds, me * modulation_weight.shape[0], modulation_weight.shape[0], 1)
    g_modw = lax.dot_general(mine, grad_mod, (((0,), (0,)), ((), ())), precision=HIGHEST)
    g_modb = lax.dynamic_slice_in_dim(
        jnp.sum(grad_mod, axis=0), me * modulation_bias.shape[0], modulation_bias.shape[0], 0)
    return (
        block_out[None],
        grad_hidden[None],
        g_in,
        gs_select,
        gs_step,
        g_out.T,
        gs_f.T,
        gs_r.T,
        gs_taps,
        gs_fbias[0],
        gs_sbias[0],
        g_modw,
        g_modb,
    )


def solution(mesh):
    return jax.shard_map(
        body,
        mesh=mesh,
        in_specs=(
            P("dp", "seq", None),
            P("dp", "seq"),
            P("dp"),
            P(("dp", "seq"), None),
            P(("dp", "seq"), None),
            P(None, ("dp", "seq")),
            P(None, ("dp", "seq")),
            P(("dp", "seq"), None),
            P(("dp", "seq"), None),
            P(None, ("dp", "seq")),
            P(("dp", "seq")),
            P(("dp", "seq")),
            P(("dp", "seq"), None),
            P(("dp", "seq")),
            P("dp", "seq", None),
        ),
        out_specs=(
            P("dp", "seq", None),
            P("dp", "seq", None),
            P(("dp", "seq"), None),
            P(("dp", "seq"), None),
            P(None, ("dp", "seq")),
            P(None, ("dp", "seq")),
            P(("dp", "seq"), None),
            P(("dp", "seq"), None),
            P(None, ("dp", "seq")),
            P(("dp", "seq")),
            P(("dp", "seq")),
            P(("dp", "seq"), None),
            P(("dp", "seq")),
        ),
        check_vma=False,
    )
```

```python
import functools
import math

import jax
import jax.numpy as jnp
from jax import lax
from jax.experimental import pallas as pl
from jax.experimental.layout import Layout, with_layout_constraint
from jax.experimental.pallas import tpu as pltpu
from jax.sharding import PartitionSpec as P

FREQ = 256
EPS = 1e-06
HIGHEST = lax.Precision.HIGHEST
LOG2E = 1.4426950408889634
SUB = 16
WF = 384
WB = 768
F32, BF = jnp.float32, jnp.bfloat16
NT = (((1,), (1,)), ((), ()))


def columns_of(rows_t, base):
    turned = pltpu.roll(rows_t, rows_t.shape[1] - base, 1)
    return [jnp.broadcast_to(turned[:, j:j + 1], (rows_t.shape[0], 128)) for j in range(SUB)]


def wide(block, lanes):
    return jnp.concatenate([block] * (lanes // 128), axis=1) if lanes > 128 else block


def states_of(base, at):
    return pl.ds(pl.multiple_of((base + at) * 16, 16), 16)


def fwd_kernel(step_f, step_r, u_f, u_r, rate_f, rate_r, bt_f, bt_r, cblk_f, cblk_r,
               y_f, y_r, s_f, s_r, carry, f0, f1, r0, r1):
    rows, lanes = step_f.shape

    @pl.when(pl.program_id(0) == 0)
    def _():
        carry[...] = jnp.zeros(carry.shape, F32)

    wide_by = min(WF, lanes)
    cuts = [slice(c, c + wide_by) for c in range(0, lanes, wide_by)]

    def walk(states, bases, kept):
        cols = [columns_of(bt[...], base) for bt, base in zip((bt_f, bt_r), bases)]
        out = []
        for cut, pair in zip(cuts, states):
            pair = list(pair)
            rates = rate_f[:, cut], rate_r[:, cut]
            for k in range(SUB):
                for z, (step, u, s, j) in enumerate(((step_f, u_f, s_f, k), (step_r, u_r, s_r, SUB - 1 - k))):
                    at = pl.ds(bases[z] + j, 1)
                    decay = jnp.exp2(step[at, cut] * rates[z])
                    pair[z] = decay * pair[z] + u[at, cut] * wide(cols[z][j], wide_by)
                    low = pair[z].astype(BF)
                    s[states_of(bases[z], j), cut] = low
                    kept[z][j * 16:(j + 1) * 16, cut] = low
            out.append(tuple(pair))
        return tuple(out)

    def mix(base, cblk, kept, y):
        here = pl.ds(base, SUB)
        y[here, :] = jnp.dot(cblk[here, :], kept[...], preferred_element_type=F32)

    def start_of(a, flip):
        a = jnp.maximum(a, 0)
        return pl.multiple_of(rows - SUB - a * SUB if flip else a * SUB, SUB)

    def two(i, states):
        for half, (fk, rk, fp, rp) in enumerate(((f0, r0, f1, r1), (f1, r1, f0, r0))):
            a = 2 * i + half
            mix(start_of(a - 1, False), cblk_f, fp, y_f)
            mix(start_of(a - 1, True), cblk_r, rp, y_r)
            states = walk(states, (start_of(a, False), start_of(a, True)), (fk, rk))
        return states

    states = tuple((carry[0, :, cut], carry[1, :, cut]) for cut in cuts)
    states = lax.fori_loop(0, rows // SUB // 2, two, states)
    mix(rows - SUB, cblk_f, f1, y_f)
    mix(0, cblk_r, r1, y_r)
    for cut, pair in zip(cuts, states):
        carry[0, :, cut], carry[1, :, cut] = pair


def fwd_scan(steps, u, rates_f, rates_r, b_t, cblk, tile=128):
    length, lanes = steps.shape
    blocks = length // tile
    specs = []
    for order in (lambda t: t, lambda t: blocks - 1 - t):
        specs.append((
            pl.BlockSpec((tile, lanes), lambda t, order=order: (order(t), 0)),
            pl.BlockSpec((16, lanes), lambda t: (0, 0)),
            pl.BlockSpec((16, tile), lambda t, order=order: (0, order(t))),
            pl.BlockSpec((tile, 256), lambda t, order=order: (order(t), 0)),
            pl.BlockSpec((tile * 16, lanes), lambda t, order=order: (order(t), 0)),
        ))
    (row_f, rate, bt_f, blk_f, s_f), (row_r, _, bt_r, blk_r, s_r) = specs
    y = jax.ShapeDtypeStruct((length, lanes), F32)
    s = jax.ShapeDtypeStruct((length * 16, lanes), BF)
    kept = pltpu.VMEM((256, lanes), BF)
    return pl.pallas_call(
        fwd_kernel,
        grid=(blocks,),
        in_specs=[row_f, row_r, row_f, row_r, rate, rate, bt_f, bt_r, blk_f, blk_r],
        out_specs=[row_f, row_r, s_f, s_r],
        out_shape=[y, y, s, s],
        scratch_shapes=[pltpu.VMEM((2, 16, lanes), F32), kept, kept, kept, kept],
        compiler_params=pltpu.CompilerParams(vmem_limit_bytes=56 * 2**20, dimension_semantics=("arbitrary",)),
        cost_estimate=pl.CostEstimate(flops=length * lanes * 16 * 3200, transcendentals=0, bytes_accessed=length * lanes * 80),
        name="fwd_scan",
    )(steps, steps, u, u, rates_f, rates_r, b_t, b_t, cblk, cblk)


def bwd_kernel(step_f, step_r, u_f, u_r, gy_f, gy_r, rate_f, rate_r, ct_f, ct_r, bblk_f, bblk_r, s_f, s_r, sp_f, sp_r,
               dlog_f, dlog_r, adjb_f, adjb_r, bg_f, bg_r, cg_f, cg_r, rg_f, rg_r, carry,
               af0, af1, ar0, ar1, lf0, lf1, lr0, lr1):
    rows, lanes = step_f.shape
    t = pl.program_id(0)
    last = pl.num_programs(0) - 1

    @pl.when(t == 0)
    def _():
        carry[...] = jnp.zeros(carry.shape, F32)
        rg_f[...] = jnp.zeros(rg_f.shape, F32)
        rg_r[...] = jnp.zeros(rg_r.shape, F32)

    ones = (lax.broadcasted_iota(jnp.int32, (SUB, 256), 0) == lax.broadcasted_iota(jnp.int32, (SUB, 256), 1) // 16)
    onesb = ones.astype(BF)
    zero = jnp.zeros((SUB, 256), F32)

    def start_of(a, down):
        a = jnp.maximum(a, 0)
        return pl.multiple_of(rows - SUB - a * SUB if down else a * SUB, SUB)

    wide_by = min(WB, lanes)
    cuts = [slice(c, c + wide_by) for c in range(0, lanes, wide_by)]

    def walk(states, bases, keep_a, keep_l):
        cols = [columns_of(ct[...], base) for ct, base in zip((ct_f, ct_r), bases)]
        out = []
        for cut, pair in zip(cuts, states):
            pair = list(pair)
            rates = rate_f[:, cut], rate_r[:, cut]
            rg = [rg_f[:, cut], rg_r[:, cut]]
            low_rates = [r.astype(BF) for r in rates]
            some = [[], []]
            for k in range(SUB):
                for z, (step, gy, s, sp, j) in enumerate((
                        (step_f, gy_f, s_f, sp_f, SUB - 1 - k), (step_r, gy_r, s_r, sp_r, k))):
                    at = pl.ds(bases[z] + j, 1)
                    row = step[at, cut]
                    adj = gy[at, cut] * wide(cols[z][j], wide_by) + pair[z]
                    pair[z] = jnp.exp2(row * rates[z]) * adj
                    before = bases[z] + (j + 1 if z else j - 1)
                    if k < SUB - 1:
                        inner = s[pl.ds(pl.multiple_of(before * 16, 16), 16), cut]
                    else:
                        inside = before < rows if z else before >= 0
                        safe = jnp.clip(before, 0, rows - 1)
                        inner = s[pl.ds(pl.multiple_of(safe * 16, 16), 16), cut]
                        outer = jnp.where(t == last, jnp.zeros_like(inner), sp[:, cut])
                        inner = jnp.where(inside, inner, outer)
                    grad = pair[z].astype(BF) * inner
                    keep_a[z][j * 16:(j + 1) * 16, cut] = adj.astype(BF)
                    keep_l[z][j * 16:(j + 1) * 16, cut] = grad * low_rates[z]
                    some[z].append(grad * jnp.broadcast_to(row, (16, wide_by)).astype(BF))
                    if len(some[z]) == 4:
                        rg[z] = rg[z] + ((some[z][0] + some[z][1]) + (some[z][2] + some[z][3])).astype(F32)
                        some[z] = []
            rg_f[:, cut], rg_r[:, cut] = rg
            out.append(tuple(pair))
        return tuple(out)

    mix_by = 256 if lanes % 256 == 0 else 128

    def mix(base, a_ref, l_ref, u, gy, bblk, s, dlog, adjb, bg, cg):
        here = pl.ds(base, SUB)
        line = pl.ds(base // SUB, 1)
        group = pl.ds(pl.multiple_of(base * 16, 256), 256)
        bgd = cgd = zero
        for c in range(0, lanes, mix_by):
            cut = slice(c, c + mix_by)
            dlog[here, cut] = jnp.dot(onesb, l_ref[:, cut], preferred_element_type=F32)
            a = a_ref[:, cut]
            adjb[here, cut] = jnp.dot(bblk[here, :], a, preferred_element_type=F32)
            bgd = bgd + lax.dot_general(u[here, cut], a, NT, preferred_element_type=F32)
            cgd = cgd + lax.dot_general(gy[here, cut].astype(BF), s[group, cut], NT, preferred_element_type=F32)
        bg[line, :] = jnp.sum(jnp.where(ones, bgd, zero), axis=0, keepdims=True)
        cg[line, :] = jnp.sum(jnp.where(ones, cgd, zero), axis=0, keepdims=True)

    def mix_f(base, a_ref, l_ref):
        mix(base, a_ref, l_ref, u_f, gy_f, bblk_f, s_f, dlog_f, adjb_f, bg_f, cg_f)

    def mix_r(base, a_ref, l_ref):
        mix(base, a_ref, l_ref, u_r, gy_r, bblk_r, s_r, dlog_r, adjb_r, bg_r, cg_r)

    def two(i, states):
        bufs = ((af0, lf0, ar0, lr0), (af1, lf1, ar1, lr1))
        for half in range(2):
            a = 2 * i + half
            naf, nlf, nar, nlr = bufs[half]
            paf, plf, par, plr = bufs[1 - half]
            mix_f(start_of(a - 1, True), paf, plf)
            mix_r(start_of(a - 1, False), par, plr)
            states = walk(states, (start_of(a, True), start_of(a, False)), (naf, nar), (nlf, nlr))
        return states

    states = tuple((carry[0, :, cut], carry[1, :, cut]) for cut in cuts)
    states = lax.fori_loop(0, rows // SUB // 2, two, states)
    mix_f(0, af1, lf1)
    mix_r(rows - SUB, ar1, lr1)
    for cut, pair in zip(cuts, states):
        carry[0, :, cut], carry[1, :, cut] = pair


def bwd_scan(steps, u, gy, rates_f, rates_r, c_t, bblk, states_f, states_r, tile=128):
    length, lanes = steps.shape
    blocks = length // tile
    down = lambda t: blocks - 1 - t
    up = lambda t: t

    def specs(order, before):
        return (
            pl.BlockSpec((tile, lanes), lambda t: (order(t), 0)),
            pl.BlockSpec((16, lanes), lambda t: (0, 0)),
            pl.BlockSpec((16, tile), lambda t: (0, order(t))),
            pl.BlockSpec((tile, 256), lambda t: (order(t), 0)),
            pl.BlockSpec((tile * 16, lanes), lambda t: (order(t), 0)),
            pl.BlockSpec((16, lanes), lambda t: (before(t), 0)),
            pl.BlockSpec((tile // 16, 256), lambda t: (order(t), 0)),
        )

    row_f, rate, ct_f, blk_f, s_f, sp_f, diag_f = specs(down, lambda t: jnp.maximum((blocks - 1 - t) * tile - 1, 0))
    row_r, _, ct_r, blk_r, s_r, sp_r, diag_r = specs(up, lambda t: jnp.minimum((t + 1) * tile, length - 1))
    y = jax.ShapeDtypeStruct((length, lanes), F32)
    diag = jax.ShapeDtypeStruct((length // 16, 256), F32)
    rg = jax.ShapeDtypeStruct((16, lanes), F32)
    kept = pltpu.VMEM((256, lanes), BF)
    return pl.pallas_call(
        bwd_kernel,
        grid=(blocks,),
        in_specs=[row_f, row_r, row_f, row_r, row_f, row_r, rate, rate, ct_f, ct_r, blk_f, blk_r, s_f, s_r, sp_f, sp_r],
        out_specs=[row_f, row_r, row_f, row_r, diag_f, diag_r, diag_f, diag_r, rate, rate],
        out_shape=[y, y, y, y, diag, diag, diag, diag, rg, rg],
        scratch_shapes=[pltpu.VMEM((2, 16, lanes), F32)] + [kept] * 8,
        compiler_params=pltpu.CompilerParams(vmem_limit_bytes=56 * 2**20, dimension_semantics=("arbitrary",)),
        cost_estimate=pl.CostEstimate(flops=length * lanes * 16 * 6800, transcendentals=0, bytes_accessed=length * lanes * 100),
        name="bwd_scan",
    )(steps, steps, u, u, gy, gy, rates_f, rates_r, c_t, c_t, bblk, bblk, states_f, states_r, states_f, states_r)


def blockdiag(rows):
    length = rows.shape[0]
    eye = (jnp.arange(length)[:, None] % 16) == (jnp.arange(256)[None, :] // 16)
    return jnp.where(eye, jnp.tile(rows, (1, 16)), 0).astype(BF)


MESH = pl.DeviceIdType.MESH
VMEM = pl.BlockSpec(memory_space=pltpu.VMEM)
HBM = pl.BlockSpec(memory_space=pl.ANY)
DMA = pltpu.SemaphoreType.DMA


def send(src, dst, out_sem, in_sem, to):
    return pltpu.make_async_remote_copy(
        src_ref=src, dst_ref=dst, send_sem=out_sem, recv_sem=in_sem, device_id=to, device_id_type=MESH)


def greet(devices):
    bar = pltpu.get_barrier_semaphore()
    for to in devices:
        pl.semaphore_signal(bar, inc=1, device_id=to, device_id_type=MESH)
    pl.semaphore_wait(bar, len(devices))


def column_sum_kernel(ns, p_ref, o_ref, land, s1, r1, s2, r2):
    d, q = lax.axis_index("dp"), lax.axis_index("seq")
    others = [lax.rem(q + k, ns) for k in range(1, ns)]
    greet([(d, t) for t in others])
    for k, t in enumerate(others):
        send(p_ref.at[t], land.at[q], s1.at[k], r1.at[q], (d, t)).start()
    total = p_ref[q].astype(F32)
    for k, t in enumerate(others):
        send(p_ref.at[t], land.at[t], s1.at[k], r1.at[t], (d, t)).wait_recv()
        total = total + land[t].astype(F32)
    o_ref[q] = total.astype(o_ref.dtype)
    for k, t in enumerate(others):
        send(o_ref.at[q], o_ref.at[q], s2.at[k], r2.at[q], (d, t)).start()
    for k, t in enumerate(others):
        send(o_ref.at[t], o_ref.at[t], s2.at[k], r2.at[t], (d, t)).wait_recv()
    for k, t in enumerate(others):
        send(p_ref.at[t], land.at[q], s1.at[k], r1.at[q], (d, t)).wait_send()
        send(o_ref.at[q], o_ref.at[q], s2.at[k], r2.at[q], (d, t)).wait_send()


def column_sum(partial, ns, out_dtype, cid):
    rows, lanes = partial.shape
    block = (ns, rows // ns, lanes)
    out = pl.pallas_call(
        functools.partial(column_sum_kernel, ns),
        out_shape=jax.ShapeDtypeStruct(block, out_dtype),
        in_specs=[VMEM], out_specs=VMEM,
        scratch_shapes=[pltpu.VMEM(block, partial.dtype), DMA((ns,)), DMA((ns,)), DMA((ns,)), DMA((ns,))],
        compiler_params=pltpu.CompilerParams(
            collective_id=cid, has_side_effects=True, vmem_limit_bytes=32 * 2**20),
        name="column_sum",
    )(partial.reshape(block))
    return out.reshape(rows, lanes)


def mod_gather_kernel(nd, ns, g_ref, o_ref, land, s1, r1, s2, r2):
    d, q = lax.axis_index("dp"), lax.axis_index("seq")
    others = [lax.rem(q + k, ns) for k in range(1, ns)]
    peers = [lax.rem(d + k, nd) for k in range(1, nd)]
    greet([(d, t) for t in others] + [(e, q) for e in peers])
    for k, t in enumerate(others):
        send(g_ref, land.at[q], s1.at[k], r1.at[q], (d, t)).start()
    total = g_ref[...]
    for k, t in enumerate(others):
        send(g_ref, land.at[t], s1.at[k], r1.at[t], (d, t)).wait_recv()
        total = total + land[t]
    o_ref[d] = total
    for k, e in enumerate(peers):
        send(o_ref.at[d], o_ref.at[d], s2.at[k], r2.at[d], (e, q)).start()
    for k, e in enumerate(peers):
        send(o_ref.at[e], o_ref.at[e], s2.at[k], r2.at[e], (e, q)).wait_recv()
    for k, t in enumerate(others):
        send(g_ref, land.at[q], s1.at[k], r1.at[q], (d, t)).wait_send()
    for k, e in enumerate(peers):
        send(o_ref.at[d], o_ref.at[d], s2.at[k], r2.at[d], (e, q)).wait_send()


def mod_gather(g, nd, ns, cid):
    rows, lanes = g.shape
    return pl.pallas_call(
        functools.partial(mod_gather_kernel, nd, ns),
        out_shape=jax.ShapeDtypeStruct((nd, rows, lanes), F32),
        in_specs=[VMEM], out_specs=VMEM,
        scratch_shapes=[pltpu.VMEM((ns, rows, lanes), F32), DMA((ns,)), DMA((ns,)), DMA((nd,)), DMA((nd,))],
        compiler_params=pltpu.CompilerParams(
            collective_id=cid, has_side_effects=True, vmem_limit_bytes=32 * 2**20),
        name="mod_gather",
    )(g)


def home_kernel(nd, ns, nsub, g_ref, sm_ref, gm_ref, f_ref, so_ref, out_ref,
                pair, plane, spair, splane, ssum, up, down,
                sa, ra, sb, rb, sc, rc, ta, ra2, tb, rb2, tc, rc2, su, ru, sd, rd):
    d, q = lax.axis_index("dp"), lax.axis_index("seq")
    nc = nd // 2
    chip, core = d // 2, lax.rem(d, 2)
    mate = chip * 2 + 1 - core
    chips = [lax.rem(chip + k, nc) for k in range(1, nc)]
    others = [lax.rem(q + k, ns) for k in range(1, ns)]
    spread = nd // ns
    final_to = (spread * q + d // ns, lax.rem(d, ns))
    mine = d * ns + q
    final_from = (lax.rem(mine, nd), mine // nd)
    stays = jnp.logical_and(final_to[0] == d, final_to[1] == q)
    bar = pltpu.get_barrier_semaphore()
    friends = [(mate, q)] + [(c * 2 + core, q) for c in chips] + [(d, t) for t in others]
    for to in friends:
        pl.semaphore_signal(bar, inc=1, device_id=to, device_id_type=MESH)
    @pl.when(jnp.logical_not(stays))
    def _():
        pl.semaphore_signal(bar, inc=1, device_id=final_from, device_id_type=MESH)
        pl.semaphore_wait(bar, len(friends) + 1)
    @pl.when(stays)
    def _():
        pl.semaphore_wait(bar, len(friends))

    def first(c):
        return send(g_ref.at[c * 2 + 1 - core], pair.at[c], sa.at[c], ra.at[c], (mate, q))

    def first_small(c):
        return send(sm_ref.at[c * 2 + 1 - core], spair.at[c], ta.at[c], ra2.at[c], (mate, q))

    order = chips + [chip]
    for c in order:
        first(c).start()
        first_small(c).start()

    def rise(t, s, src):
        return send(src, up.at[t, s], su.at[t, s], ru.at[t, s], (d, q + 1))

    def sink(t, s, src):
        return send(src, down.at[t, s], sd.at[t, s], rd.at[t, s], (d, q - 1))

    def added(land, t, s):
        land[t, s] = (land[t, s].astype(F32) + gm_ref[t, s].astype(F32)).astype(BF)

    def step_up(t, s):
        @pl.when(q < t)
        def _():
            @pl.when(q == 0)
            def _():
                rise(t, s, gm_ref.at[t, s]).start()
            @pl.when(q > 0)
            def _():
                rise(t, s, up.at[t, s]).wait_recv()
                added(up, t, s)
                rise(t, s, up.at[t, s]).start()

    def step_down(t, s):
        @pl.when(q > t)
        def _():
            @pl.when(q == ns - 1)
            def _():
                sink(t, s, gm_ref.at[t, s]).start()
            @pl.when(q < ns - 1)
            def _():
                sink(t, s, down.at[t, s]).wait_recv()
                added(down, t, s)
                sink(t, s, down.at[t, s]).start()

    steps = [(k, s) for k in range(ns - 1) for s in range(nsub)]
    middle = len(steps) * 2 // 3

    def walk(some):
        for k, s in some:
            step_up(ns - 1 - k, s)
            step_down(k, s)

    def second(c, src):
        return send(pair.at[c], plane.at[src], sb.at[c], rb.at[src], (c * 2 + core, q))

    def second_small(c, src):
        return send(spair.at[c], splane.at[src], tb.at[c], rb2.at[src], (c * 2 + core, q))

    walk(steps[:1])
    for c in order:
        first(c).wait_recv()
        @pl.loop(0, ns)
        def _(t):
            pair[c, t] = (pair[c, t].astype(F32) + g_ref[c * 2 + core, t].astype(F32)).astype(BF)
        first_small(c).wait_recv()
        spair[c] = spair[c] + sm_ref[c * 2 + core]
        if c is not chip:
            second(c, chip).start()
            second_small(c, chip).start()
    walk(steps[1:middle])

    for c in chips:
        second(c, c).wait_recv()
        second_small(c, c).wait_recv()
    @pl.loop(0, ns)
    def _(t):
        total = pair[chip, t].astype(F32)
        for c in chips:
            total = total + plane[c, t].astype(F32)
        pair[chip, t] = total.astype(BF)
    small = spair[chip]
    for c in chips:
        small = small + splane[c]
    ssum[...] = small

    def third(t, src):
        return send(pair.at[chip, t], f_ref.at[src], sc.at[t], rc.at[src], (d, t))

    last = send(ssum, so_ref, tc, rc2, final_to)
    @pl.when(stays)
    def _():
        so_ref[...] = ssum[...]
    @pl.when(jnp.logical_not(stays))
    def _():
        last.start()
    for t in others:
        third(t, q).start()
    f_ref[q] = pair[chip, q]
    walk(steps[middle:])

    for s in range(nsub):
        total = gm_ref[q, s].astype(F32)
        out_ref[s] = total
        @pl.when(q > 0)
        def _():
            rise(q, s, gm_ref.at[q, s]).wait_recv()
            out_ref[s] += up[q, s].astype(F32)
        @pl.when(q < ns - 1)
        def _():
            sink(q, s, gm_ref.at[q, s]).wait_recv()
            out_ref[s] += down[q, s].astype(F32)
    for t in others:
        third(t, t).wait_recv()
    @pl.when(jnp.logical_not(stays))
    def _():
        last.wait_recv()
        last.wait_send()
    for c in order:
        first(c).wait_send()
        first_small(c).wait_send()
    for c in chips:
        second(c, chip).wait_send()
        second_small(c, chip).wait_send()
    for t in others:
        third(t, q).wait_send()
    for k, s in steps:
        t = ns - 1 - k
        @pl.when(q < t)
        def _():
            rise(t, s, gm_ref.at[t, s]).wait_send()
        @pl.when(q > k)
        def _():
            sink(k, s, gm_ref.at[k, s]).wait_send()


def home(g, small, gm, nd, ns, cid):
    rows, cols = g.shape[2:]
    nc, nsub = nd // 2, 4
    length, width = gm.shape
    part = length // ns // nsub
    v = small.shape[1:]
    gm = gm.reshape(ns, nsub, part, width)
    f, so, out = pl.pallas_call(
        functools.partial(home_kernel, nd, ns, nsub),
        out_shape=[
            jax.ShapeDtypeStruct((ns, rows, cols), BF),
            jax.ShapeDtypeStruct(v, F32),
            jax.ShapeDtypeStruct((nsub, part, width), F32),
        ],
        in_specs=[VMEM] * 3, out_specs=[VMEM] * 3,
        scratch_shapes=[
            pltpu.VMEM((nc, ns, rows, cols), BF), pltpu.VMEM((nc, ns, rows, cols), BF),
            pltpu.VMEM((nc,) + v, F32), pltpu.VMEM((nc,) + v, F32), pltpu.VMEM(v, F32),
            pltpu.VMEM((ns, nsub, part, width), BF), pltpu.VMEM((ns, nsub, part, width), BF),
            DMA((nc,)), DMA((nc,)), DMA((nc,)), DMA((nc,)), DMA((ns,)), DMA((ns,)),
            DMA((nc,)), DMA((nc,)), DMA((nc,)), DMA((nc,)), DMA(()), DMA(()),
            DMA((ns, nsub)), DMA((ns, nsub)), DMA((ns, nsub)), DMA((ns, nsub)),
        ],
        compiler_params=pltpu.CompilerParams(
            collective_id=cid, has_side_effects=True, vmem_limit_bytes=56 * 2**20),
        name="home",
    )(g, small, gm)
    return f, so, out.reshape(length // ns, width)


def start_kernel(nd, ns, nsub, fused, hid, win, wout, mask, emb, modw, modb, select, step, dec_f, dec_r, taps, fbias, sbias,
                 md_o, nm_o, inner_o, gate_o, wx_o, select_o, step_o, rate_o, fil_o, mask_o, mod_o,
                 hv, wv, mv, nv, iv, gv, pack, modw_v, pack_v, eland, prod, rowp, land1, land2,
                 su, ru, sd, rd, swz, rwx, swp, swm, spz, rp, spp, spm, sk, rk, se, re, s1, r1, s2, r2, own, out):
    d, q = lax.axis_index("dp"), lax.axis_index("seq")
    nc = nd // 2
    chip, core = d // 2, lax.rem(d, 2)
    mate = (chip * 2 + 1 - core, q)
    chips = [lax.rem(chip + k, nc) for k in range(1, nc)]
    others = [lax.rem(q + k, ns) for k in range(1, ns)]
    peers = [lax.rem(d + k, nd) for k in range(1, nd)]
    spread = nd // ns
    me = d * ns + q
    part = wout.shape[1] // ns
    rw = wout.shape[0]
    units = part // nd
    rank, states = step.shape[0], dec_f.shape[0]
    above = units + -units % 16
    taps_at = above + rank + 2 * states

    pack[...] = jnp.zeros(pack.shape, BF)
    pack[0:units, :] = select[...]
    pack[above:above + rank, 0:units] = step[...]
    pack[above + rank:above + rank + states, 0:units] = dec_f[...]
    pack[above + rank + states:taps_at, 0:units] = dec_r[...]
    pack[taps_at:taps_at + 16, 0:units] = jnp.concatenate(
        [taps[...].astype(F32), fbias[...].astype(F32), sbias[...].astype(F32),
         jnp.zeros((14 - taps.shape[0], units), F32)]).astype(BF)
    modw_v[...] = jnp.zeros(modw_v.shape, BF)
    modw_v[0:modw.shape[0], :] = modw[...]
    greet([(d, t) for t in others] + [(e, q) for e in peers])

    def column(ref, at):
        return ref.at[:, pl.ds(pl.multiple_of(at * part, 128), part)]

    def wrows(idx):
        return wv.at[pl.ds(pl.multiple_of(idx * rw, 16), rw), :]

    def pieces(t):
        return (column(win, t), column(win, ns + t), column(wout, t))

    def across(k, t, idx):
        return [
            send(src, wrows(idx).at[:, j * part:(j + 1) * part], swz.at[k, j], rwx.at[idx, j], (d, t))
            for j, src in enumerate(pieces(t))
        ]

    keep = [pltpu.make_async_copy(src, wrows(me).at[:, j * part:(j + 1) * part], own.at[j])
            for j, src in enumerate(pieces(q))]
    keep.append(pltpu.make_async_copy(hid, hv.at[q], own.at[3]))
    for copy in keep:
        copy.start()

    plane = d // spread
    slot = lax.rem(d, spread) * ns + q
    pack_z = send(pack, pack_v.at[slot], spz, rp.at[slot], (d, plane))
    pack_vwn = pltpu.make_async_copy(pack, pack_v.at[slot], own.at[4])

    @pl.when(plane == q)
    def _():
        pack_vwn.start()

    @pl.when(plane != q)
    def _():
        pack_z.start()

    def masks(k, t, src):
        return send(mask_o.at[src], mask_o.at[src], sk.at[k], rk.at[src], (d, t))

    def embeds(k, e, src):
        return send(eland.at[src], eland.at[src], se.at[k], re.at[src], (e, q))

    mask_o[q] = jnp.zeros(mask_o.shape[1:], BF)
    mask_o[q, 0:mask.shape[0], :] = mask[...].astype(F32).astype(BF)
    eland[d] = jnp.zeros(eland.shape[1:], BF)
    eland[d, 0:1, :] = emb[...]
    for k, e in enumerate(peers):
        embeds(k, e, d).start()
    for k, t in enumerate(others):
        masks(k, t, q).start()

    for k, t in enumerate(others):
        for copy in across(k, t, me)[:2]:
            copy.start()

    def rise(k, s):
        t = jnp.maximum(q - k, 0)
        src = hid.at[s] if k == 0 else hv.at[t, s]
        return send(src, hv.at[t, s], su.at[k, s], ru.at[k, s], (d, q + 1))

    def sink(k, s):
        t = jnp.minimum(q + k, ns - 1)
        src = hid.at[s] if k == 0 else hv.at[t, s]
        return send(src, hv.at[t, s], sd.at[k, s], rd.at[k, s], (d, q - 1))

    def hop(k, s):
        @pl.when(q >= k)
        def _():
            if k:
                rise(k - 1, s).wait_recv()
            if k < ns - 1:
                @pl.when(q + 1 < ns)
                def _():
                    rise(k, s).start()

        @pl.when(q + k < ns)
        def _():
            if k:
                sink(k - 1, s).wait_recv()
            if k < ns - 1:
                @pl.when(q >= 1)
                def _():
                    sink(k, s).start()

    for s in range(nsub):
        hop(0, s)
    for k, t in enumerate(others):
        across(k, t, me)[2].start()

    def cols_of(idx, kind):
        return wrows(idx).at[:, 2 * part * kind:2 * part + part * kind]

    def plane_w(c, idx, t, kind):
        return send(cols_of(idx, kind), cols_of(idx, kind), swp.at[kind, c, t], rwx.at[idx, 3 + kind], (c * 2 + core, q))

    def mate_w(c, idx, t, kind):
        return send(cols_of(idx, kind), cols_of(idx, kind), swm.at[kind, c, t], rwx.at[idx, 3 + kind], mate)

    def spread_w(t, kind):
        idx = d * ns + t
        for c in chips:
            plane_w(c, idx, t, kind).start()
        mate_w(chip, idx, t, kind).start()

    for copy in keep[:3]:
        copy.wait()
    spread_w(q, 0)

    for k, e in enumerate(peers):
        embeds(k, e, e).wait_recv()
    rows = modw_v.shape[0]
    here = lax.broadcasted_iota(jnp.int32, (FREQ, rows), 0)
    pick = here - lax.broadcasted_iota(jnp.int32, (FREQ, rows), 1)
    count = FREQ // (nd * ns)
    keep_col = lax.broadcasted_iota(jnp.int32, (FREQ, rows), 1) < count
    pick = jnp.where(jnp.logical_and(pick == me * count, keep_col), 1.0, 0.0).astype(BF)
    mine = jnp.dot(eland[...].reshape(nd * 16, FREQ), pick, preferred_element_type=F32).astype(BF)
    prod[...] = jnp.dot(mine, modw_v[...], preferred_element_type=F32)

    lines = prod.shape[1] // 128
    @pl.loop(0, nd)
    def _(e):
        rowp[e] = modb[...]
        for j in range(lines):
            rowp[e, j:j + 1, :] += prod[pl.ds(pl.multiple_of(e * 16, 16), 1), j * 128:(j + 1) * 128]

    def to_item(k, e, src):
        return send(rowp.at[e], land1.at[src], s1.at[k], r1.at[src], (e, q))

    for k, e in enumerate(peers):
        to_item(k, e, d).start()

    for k, t in enumerate(others):
        for copy in across(k, t, d * ns + t)[:2]:
            copy.wait_recv()
        spread_w(t, 0)

    def plane_p(c, i, t):
        return send(pack_v.at[i], pack_v.at[i], spp.at[c, t], rp.at[i], (c * 2 + core, q))

    def mate_p(c, i, t):
        return send(pack_v.at[i], pack_v.at[i], spm.at[c, t], rp.at[i], mate)

    base = lax.rem(d, spread) * ns

    @pl.when(plane == q)
    def _():
        pack_vwn.wait()
        for t in others:
            send(pack, pack_v.at[base + t], spz, rp.at[base + t], (d, plane)).wait_recv()
        for t in range(ns):
            for c in chips:
                plane_p(c, base + t, t).start()
            mate_p(chip, base + t, t).start()

    total = rowp[d]
    for k, e in enumerate(peers):
        to_item(k, e, e).wait_recv()
        total = total + land1[e]
    land2[q] = total

    def to_column(k, t, src):
        return send(land2.at[src], land2.at[src], s2.at[k], r2.at[src], (d, t))

    for k, t in enumerate(others):
        to_column(k, t, q).start()

    def relay_w(c, t, kind):
        idx = (c * 2 + core) * ns + t
        plane_w(c, idx, t, kind).wait_recv()
        mate_w(c, idx, t, kind).start()

    def holds(c):
        return (c * 2 + core) // spread == q

    def relay_p(c):
        first = lax.rem(c * 2 + core, spread) * ns
        @pl.when(holds(c))
        def _():
            for t in range(ns):
                plane_p(c, first + t, t).wait_recv()
                mate_p(c, first + t, t).start()

    def own_copies(t):
        return [pltpu.make_async_copy(src.at[t], dst.at[t], out.at[t, i]) for i, (src, dst) in enumerate(
            ((mv, md_o), (iv, inner_o), (gv, gate_o), (nv, nm_o)) if fused else ((hv, md_o),))]

    local = hv.shape[1] * hv.shape[2]
    width = hv.shape[3]

    def project(t):
        if fused:
            shift, scale = mod_o[0:1, 0:width], 1.0 + mod_o[0:1, width:2 * width]
            for s in range(nsub):
                @pl.loop(0, local // nsub // 16)
                def _(r):
                    x = hv[t, s, pl.ds(pl.multiple_of(r * 16, 16), 16), :].astype(F32)
                    x = x - jnp.mean(x, axis=1, keepdims=True)
                    x = x * lax.rsqrt(jnp.mean(x * x, axis=1, keepdims=True) + EPS)
                    to = pl.multiple_of(s * (local // nsub) + r * 16, 16)
                    nv[t, pl.ds(to, 16), :] = x.astype(BF)
                    mv[t, pl.ds(to, 16), :] = (x * scale + shift).astype(BF)
            tile = part if part % 256 else part // 2

            @pl.loop(0, part // tile)
            def _(j):
                for target, base in ((iv, 0), (gv, part)):
                    n = pl.ds(pl.multiple_of(base + j * tile, 128), tile)
                    full = jnp.dot(mv[t], wv[:, n], preferred_element_type=F32)
                    target[t, :, pl.ds(pl.multiple_of(j * tile, 128), tile)] = full.astype(target.dtype)
        for copy in own_copies(t):
            copy.start()

    relays = [(c, t) for t in [q] + others for c in chips]
    at = 0
    for s in range(nsub):
        hop(1, s)
        upto = len(relays) * (s + 1) // (2 * nsub)
        for c, t in relays[at:upto]:
            relay_w(c, t, 0)
        at = upto
    spread_w(q, 1)
    for k, t in enumerate(others):
        across(k, t, d * ns + t)[2].wait_recv()
        spread_w(t, 1)
    for c, t in relays[at:]:
        relay_w(c, t, 0)
    for c in chips:
        relay_p(c)

    for k, t in enumerate(others):
        to_column(k, t, t).wait_recv()
    total = land2[0]
    for t in range(1, ns):
        total = total + land2[t]
    mod_o[...] = jnp.zeros(mod_o.shape, F32)
    for i in range(mod_o.shape[1] // 128):
        mod_o[0:1, i * 128:(i + 1) * 128] = total[i:i + 1, :]

    twin = 1 - core
    for c in range(nc):
        for t in range(ns):
            idx = (c * 2 + twin) * ns + t
            mate_w(c, idx, t, 0).wait_recv()
    keep[3].wait()

    def project_at(t):
        @pl.when(jnp.logical_and(t >= 0, t < ns))
        def _():
            project(jnp.clip(t, 0, ns - 1))

    for k in range(2, ns):
        for s in range(nsub):
            hop(k, s)
            if k == 2 and s == 0:
                project(q)
            if s == nsub - 3:
                project_at(q - k + 1)
            if s == nsub - 2:
                project_at(q + k - 1)

    for c, t in relays:
        relay_w(c, t, 1)
    for c in range(nc):
        for t in range(ns):
            idx = (c * 2 + twin) * ns + t
            mate_w(c, idx, t, 1).wait_recv()
    wx_copy = pltpu.make_async_copy(wv, wx_o, own.at[5])
    wx_copy.start()

    for c in range(nc):
        first = lax.rem(c * 2 + twin, spread) * ns
        @pl.when((c * 2 + twin) // spread == q)
        def _():
            for t in range(ns):
                mate_p(c, first + t, t).wait_recv()
    for j in range(nd):
        here = slice(j * units, (j + 1) * units)
        select_o[here, :] = pack_v[j, 0:units, :]
        step_o[:, here] = pack_v[j, above:above + rank, 0:units]
        rate_o[0:2 * states, here] = -jnp.exp(pack_v[j, above + rank:taps_at, 0:units].astype(F32))
        fil_o[:, here] = pack_v[j, taps_at:taps_at + 16, 0:units].astype(F32)
    rate_o[2 * states:4 * states, :] = rate_o[0:2 * states, :] * LOG2E

    project_at(q - ns + 1)
    project_at(q + ns - 1)

    for k, t in enumerate(others):
        masks(k, t, t).wait_recv()
    wx_copy.wait()
    for t in range(ns):
        for copy in own_copies(t):
            copy.wait()

    for k, t in enumerate(others):
        for copy in across(k, t, me):
            copy.wait_send()
        masks(k, t, q).wait_send()
        to_column(k, t, q).wait_send()
    for k, e in enumerate(peers):
        embeds(k, e, d).wait_send()
        to_item(k, e, d).wait_send()

    @pl.when(plane != q)
    def _():
        pack_z.wait_send()

    @pl.when(plane == q)
    def _():
        for t in range(ns):
            for c in chips:
                plane_p(c, base + t, t).wait_send()
            mate_p(chip, base + t, t).wait_send()

    for kind in range(2):
        for t in range(ns):
            for c in chips:
                plane_w(c, d * ns + t, t, kind).wait_send()
                mate_w(c, (c * 2 + core) * ns + t, t, kind).wait_send()
            mate_w(chip, d * ns + t, t, kind).wait_send()
    for c in chips:
        first = lax.rem(c * 2 + core, spread) * ns
        @pl.when(holds(c))
        def _():
            for t in range(ns):
                mate_p(c, first + t, t).wait_send()
    for k in range(ns - 1):
        for s in range(nsub):
            @pl.when(jnp.logical_and(q >= k, q + 1 < ns))
            def _():
                rise(k, s).wait_send()
            @pl.when(jnp.logical_and(q + k < ns, q >= 1))
            def _():
                sink(k, s).wait_send()


def start(hidden, mask, win, wout, embedded, modw, modb, small, fused, nd, ns, cid):
    nsub = 4
    length, width = hidden.shape
    rows, inner = wout.shape
    part = inner // ns
    nc = nd // 2
    hidden = hidden.reshape(nsub, length // nsub, width)
    lines = modb.shape
    rank, units, states = small[1].shape[0], part // nd, small[2].shape[0]
    pack = (units + -units % 16 + rank + 2 * states + 16, 128)
    held = modw.shape[0] + -modw.shape[0] % 16
    runs = (ns,) + (hidden.shape if not fused else (length, width))
    return pl.pallas_call(
        functools.partial(start_kernel, nd, ns, nsub, fused),
        out_shape=[
            jax.ShapeDtypeStruct(runs, BF),
            jax.ShapeDtypeStruct((ns, length, width), BF),
            jax.ShapeDtypeStruct((ns, length, part), BF),
            jax.ShapeDtypeStruct((ns, length, part), F32),
            jax.ShapeDtypeStruct((nd * ns * rows, 3 * part), BF),
            jax.ShapeDtypeStruct((part, 128), BF),
            jax.ShapeDtypeStruct((rank, part), BF),
            jax.ShapeDtypeStruct((4 * states, part), F32),
            jax.ShapeDtypeStruct((16, part), F32),
            jax.ShapeDtypeStruct((ns, 16, 128), BF),
            jax.ShapeDtypeStruct((8, modw.shape[1]), F32),
        ],
        in_specs=[HBM, HBM, HBM] + [VMEM] * 11,
        out_specs=[HBM] * 5 + [VMEM] * 6,
        scratch_shapes=[
            pltpu.VMEM((ns,) + hidden.shape, BF), pltpu.VMEM((nd * ns * rows, 3 * part), BF),
            pltpu.VMEM((ns, length, width), BF), pltpu.VMEM((ns, length, width), BF), pltpu.VMEM((ns, length, part), BF), pltpu.VMEM((ns, length, part), F32),
            pltpu.VMEM(pack, BF), pltpu.VMEM((held, modw.shape[1]), BF), pltpu.VMEM((nd,) + pack, BF),
            pltpu.VMEM((nd, 16, FREQ), BF), pltpu.VMEM((nd * 16, modw.shape[1]), F32),
            pltpu.VMEM((nd,) + lines, F32), pltpu.VMEM((nd,) + lines, F32), pltpu.VMEM((ns,) + lines, F32),
            DMA((ns - 1, nsub)), DMA((ns - 1, nsub)), DMA((ns - 1, nsub)), DMA((ns - 1, nsub)),
            DMA((ns, 3)), DMA((nd * ns, 5)), DMA((2, nc, ns)), DMA((2, nc, ns)),
            DMA(()), DMA((nd,)), DMA((nc, ns)), DMA((nc, ns)),
            DMA((ns,)), DMA((ns,)), DMA((nd,)), DMA((nd,)),
            DMA((nd,)), DMA((nd,)), DMA((ns,)), DMA((ns,)), DMA((6,)), DMA((ns, 4)),
        ],
        compiler_params=pltpu.CompilerParams(
            collective_id=cid, has_side_effects=True, vmem_limit_bytes=56 * 2**20),
        name="start",
    )(hidden, win, wout, mask, embedded, modw, modb, *small)


def end_kernel(nd, ns, nsub, rows, turned,
               gi_h, gg_h, md_h, nm_h, wx_h, gsel, gstep, gdf, gdr, gfil, hid_ref, cot_ref, line_ref, early,
               gin_o, gout_o, sel_o, step_o, df_o, dr_o, taps_o, fb_o, sb_o, gh_o, mod_o,
               gp, md, nm, wx, sm_ref, so_ref, gm, made, pair, plane, spair, splane, ssum, fro, ready, up, down, own, acc, msg, mland,
               ld, sa, ra, sb, rb, sc, rc, se, re, ta, ra2, tb, rb2, tc, rc2, su, ru, sd, rd, s1, r1, s2, r2):
    d, q = lax.axis_index("dp"), lax.axis_index("seq")
    nc = nd // 2
    chip, core = d // 2, lax.rem(d, 2)
    mate = chip * 2 + 1 - core
    pairs = [(1, 1), (1, 0), (0, 1)] + [(a, b) for b in range(2, nc // 2) for a in (0, 1)]
    chips = [lax.rem(chip + a, 2) + 2 * lax.rem(chip // 2 + b, nc // 2) for a, b in pairs]
    others = [lax.rem(q + k, ns) for k in range(1, ns)]
    peers = [lax.rem(d + k, nd) for k in range(1, nd)]
    spread = nd // ns
    final_to = (spread * q + d // ns, lax.rem(d, ns))
    me = d * ns + q
    final_from = (lax.rem(me, nd), me // nd)
    stays = jnp.logical_and(final_to[0] == d, final_to[1] == q)
    length, cols = gp.shape
    part = cols // 2
    width = wx.shape[0]
    local = length // ns
    sub = local // nsub
    rw = pair.shape[2]
    half = ns * rw

    loads = [pltpu.make_async_copy(src, dst, ld.at[i]) for i, (src, dst) in enumerate(
        ((gi_h, gp.at[:, 0:part]), (gg_h, gp.at[:, part:cols]), (wx_h.at[:, 0:cols], wx), (nm_h, nm), (md_h, md)))]
    for copy in loads:
        copy.start()

    units = part // nd
    rank, states, taps = gstep.shape[0], gdf.shape[0], taps_o.shape[0]
    above = units + -units % 16
    taps_at = above + rank + 2 * states
    bar = pltpu.get_barrier_semaphore()
    friends = [(e, q) for e in peers] + [(d, t) for t in others]
    for to in friends:
        pl.semaphore_signal(bar, inc=1, device_id=to, device_id_type=MESH)
    @pl.when(jnp.logical_not(stays))
    def _():
        pl.semaphore_signal(bar, inc=1, device_id=final_from, device_id_type=MESH)

    def tokens(t):
        @pl.loop(0, width // 512)
        def _(j):
            here = pl.ds(pl.multiple_of(j * 512, 512), 512)
            lines = slice(t * local, (t + 1) * local)
            full = lax.dot_general(gp[lines, :], wx[here, :], NT, preferred_element_type=F32)
            acc[0:1, here] += jnp.sum(full, axis=0, keepdims=True)
            acc[1:2, here] += jnp.sum(full * nm[lines, here].astype(F32), axis=0, keepdims=True)
            full = full.astype(BF)
            for s in range(nsub):
                gm[t, s, :, here] = full[s * sub:(s + 1) * sub]

    def rise(t, s, src):
        return send(src, up.at[t, s], su.at[t, s], ru.at[t, s], (d, q + 1))

    def sink(t, s, src):
        return send(src, down.at[t, s], sd.at[t, s], rd.at[t, s], (d, q - 1))

    def added(land, t, s):
        land[t, s] = (land[t, s].astype(F32) + gm[t, s].astype(F32)).astype(BF)

    def open_up(t, s):
        @pl.when(jnp.logical_and(q == 0, t > 0))
        def _():
            rise(t, s, gm.at[t, s]).start()

    def open_down(t, s):
        @pl.when(jnp.logical_and(q == ns - 1, t < ns - 1))
        def _():
            sink(t, s, gm.at[t, s]).start()

    def step(k, s):
        t = ns - 1 - k

        @pl.when(jnp.logical_and(q < t, q > 0))
        def _():
            rise(t, s, up.at[t, s]).wait_recv()
            added(up, t, s)
            rise(t, s, up.at[t, s]).start()

        @pl.when(jnp.logical_and(q > k, q < ns - 1))
        def _():
            sink(k, s, down.at[k, s]).wait_recv()
            added(down, k, s)
            sink(k, s, down.at[k, s]).start()

    def far(k):
        for t in sorted({ns - 1 - k, k}, reverse=True):
            tokens(t)
            for s in range(nsub):
                open_up(t, s)
                open_down(t, s)

    @pl.when(stays)
    def _():
        pl.semaphore_wait(bar, len(friends))

    @pl.when(jnp.logical_not(stays))
    def _():
        pl.semaphore_wait(bar, len(friends) + 1)

    def whole(t, src):
        return send(early.at[t], ready.at[src], se.at[t], re.at[src], (d, t))

    for t in others:
        whole(t, q).start()
    for copy in loads[:4]:
        copy.wait()
    acc[...] = jnp.zeros(acc.shape, F32)
    acc[2:4, :] = line_ref[1:3, :]
    far(0)
    steps = [(k, s) for k in range(ns - 1) for s in range(nsub)]

    def first(c):
        return send(made.at[c, 1 - core], pair.at[c], sa.at[c], ra.at[c], (mate, q))

    def first_small(c):
        return send(sm_ref.at[c * 2 + 1 - core], spair.at[c], ta.at[c], ra2.at[c], (mate, q))

    def second(c, src):
        return send(pair.at[c], plane.at[src], sb.at[c], rb.at[src], (c * 2 + core, q))

    def second_small(c, src):
        return send(spair.at[c], splane.at[src], tb.at[c], rb2.at[src], (c * 2 + core, q))

    def block(c):
        at = pl.ds(pl.multiple_of(c * 2 * half, 2 * half), 2 * half)
        tile = part if part % 256 else part // 2
        left = md[at, :] if turned else md[:, at].T

        @pl.loop(0, part // tile)
        def _(j):
            n = pl.ds(pl.multiple_of(j * tile, 128), tile)
            full = jnp.dot(left, gp[:, n], preferred_element_type=F32).astype(BF)
            for h in range(2):
                for t in range(ns):
                    line = (h * ns + t) * rw
                    made[c, h, t, :, n] = full[line:line + rw]

    sm_ref[...] = jnp.zeros(sm_ref.shape, F32)
    for j in range(nd):
        here = slice(j * units, (j + 1) * units)
        sm_ref[j, 0:units, :] = gsel[here, :]
        sm_ref[j, above:above + rank, 0:units] = gstep[:, here]
        sm_ref[j, above + rank:above + rank + states, 0:units] = gdf[:, here]
        sm_ref[j, above + rank + states:taps_at, 0:units] = gdr[:, here]
        sm_ref[j, taps_at:taps_at + 8, 0:units] = gfil[:, here]

    loads[4].wait()
    order = chips + [chip]

    def give(c):
        block(c)
        first(c).start()
        first_small(c).start()

    give(order[0])
    for k in range(1, ns // 2):
        far(k)
    msg[...] = jnp.zeros(msg.shape, F32)
    long = msg.shape[1] // 128
    for i in range(3 * width // 128 + FREQ // 128):
        r, c = divmod(i * 128, width)
        to = (i % long) * 128
        msg[i // long:i // long + 1, to:to + 128] = acc[r:r + 1, c:c + 128]
    for k, t in enumerate(others):
        send(msg, mland.at[q], s1.at[k], r1.at[q], (d, t)).start()

    for i, c in enumerate(order):
        if i + 1 < nc:
            give(order[i + 1])
        first(c).wait_recv()
        @pl.loop(0, ns)
        def _(t):
            pair[c, t] = (pair[c, t].astype(F32) + made[c, core, t].astype(F32)).astype(BF)
        first_small(c).wait_recv()
        spair[c] = spair[c] + sm_ref[c * 2 + core]
        if i < nc - 1:
            second(c, chip).start()
            second_small(c, chip).start()
        for k, s in steps[i:i + 1]:
            step(k, s)
    late = len(steps) * 3 // 4
    for k, s in steps[nc:late]:
        step(k, s)

    for c in chips:
        second(c, c).wait_recv()
        second_small(c, c).wait_recv()
    @pl.loop(0, ns)
    def _(t):
        total = pair[chip, t].astype(F32)
        for c in chips:
            total = total + plane[c, t].astype(F32)
        pair[chip, t] = total.astype(BF)
    small = spair[chip]
    for c in chips:
        small = small + splane[c]
    ssum[...] = small

    def third(t, src):
        return send(pair.at[chip, t], fro.at[src], sc.at[t], rc.at[src], (d, t))

    last = send(ssum, so_ref, tc, rc2, final_to)
    @pl.when(stays)
    def _():
        so_ref[...] = ssum[...]
    @pl.when(jnp.logical_not(stays))
    def _():
        last.start()
    for t in others:
        third(t, q).start()
    fro[q] = pair[chip, q]
    for k, s in steps[max(nc, late):]:
        step(k, s)

    total = msg[...]
    for k, t in enumerate(others):
        send(msg, mland.at[t], s1.at[k], r1.at[t], (d, t)).wait_recv()
        total = total + mland[t]
    mod_o[d] = total
    for k, e in enumerate(peers):
        send(mod_o.at[d], mod_o.at[d], s2.at[k], r2.at[d], (e, q)).start()
    scale = 1.0 + line_ref[0:1, :]
    for s in range(nsub):
        own[...] = gm[q, s].astype(F32)

        @pl.when(q > 0)
        def _():
            rise(q, s, gm.at[q, s]).wait_recv()
            own[...] += up[q, s].astype(F32)

        @pl.when(q < ns - 1)
        def _():
            sink(q, s, gm.at[q, s]).wait_recv()
            own[...] += down[q, s].astype(F32)

        @pl.loop(0, sub // 16)
        def _(r):
            here = pl.ds(pl.multiple_of(r * 16, 16), 16)
            grad = own[here, :]
            x = hid_ref[s, here, :].astype(F32)
            x = x - jnp.mean(x, axis=1, keepdims=True)
            inverse = lax.rsqrt(jnp.mean(x * x, axis=1, keepdims=True) + EPS)
            normed = x * inverse
            grad = grad * scale
            grad = grad - jnp.mean(grad, axis=1, keepdims=True) - normed * jnp.mean(
                grad * normed, axis=1, keepdims=True)
            gh_o[s, here, :] = (cot_ref[s, here, :].astype(F32) + inverse * grad).astype(BF)

    inner = part * ns

    def place(src, rest):
        at = src * part
        gin_o[:, pl.ds(pl.multiple_of(at, 128), part)] = fro[src, 0:rows, :].astype(F32)
        gin_o[:, pl.ds(pl.multiple_of(inner + at, 128), part)] = rest[0:rows, 0:part].astype(F32)
        gout_o[:, pl.ds(pl.multiple_of(at, 128), part)] = rest[0:rows, part:2 * part].astype(F32)

    place(q, early[q])
    for t in others:
        third(t, t).wait_recv()
        whole(t, t).wait_recv()
        place(t, ready[t])
    for k, e in enumerate(peers):
        send(mod_o.at[e], mod_o.at[e], s2.at[k], r2.at[e], (e, q)).wait_recv()
    @pl.when(jnp.logical_not(stays))
    def _():
        last.wait_recv()
        last.wait_send()

    sel_o[...] = so_ref[0:units, :]
    step_o[...] = so_ref[above:above + rank, 0:units]
    df_o[...] = so_ref[above + rank:above + rank + states, 0:units]
    dr_o[...] = so_ref[above + rank + states:taps_at, 0:units]
    taps_o[...] = so_ref[taps_at:taps_at + taps, 0:units]
    fb_o[...] = so_ref[taps_at + taps:taps_at + taps + 1, 0:units]
    sb_o[...] = so_ref[taps_at + taps + 1:taps_at + taps + 2, 0:units]
    for c in order:
        first(c).wait_send()
        first_small(c).wait_send()
    for c in chips:
        second(c, chip).wait_send()
        second_small(c, chip).wait_send()
    for k, t in enumerate(others):
        third(t, q).wait_send()
        whole(t, q).wait_send()
        send(msg, mland.at[q], s1.at[k], r1.at[q], (d, t)).wait_send()
    for k, e in enumerate(peers):
        send(mod_o.at[d], mod_o.at[d], s2.at[k], r2.at[d], (e, q)).wait_send()
    for k, s in steps:
        t = ns - 1 - k
        @pl.when(q < t)
        def _():
            rise(t, s, gm.at[t, s]).wait_send()
        @pl.when(q > k)
        def _():
            sink(k, s, gm.at[k, s]).wait_send()


def end(grad_inner, grad_gate, modded, normed, wx, early, small, taps, hidden, cot, line, rows, nd, ns, cid):
    length, part = grad_inner.shape
    cols = 2 * part
    width = wx.shape[0]
    inner = part * ns
    nc, nsub = nd // 2, 4
    local = length // ns
    sub = local // nsub
    rw = rows + -rows % 16
    half = ns * rw
    turned = 2 * half % 128 != 0 or rw != rows
    if turned:
        def turn(a):
            a = a.T.reshape(nd * ns, rows, length)
            return jnp.pad(a, ((0, 0), (0, rw - rows), (0, 0))).reshape(nd * ns * rw, length)
        modded = turn(modded)
    early = jnp.pad(early.reshape(ns, rows, cols), ((0, 0), (0, rw - rows), (0, 0)))
    short = -(-(3 * width + FREQ) // 1024) * 128
    units, rank, states = part // nd, small[1].shape[0], small[2].shape[0]
    v = (units + -units % 16 + rank + 2 * states + 16, 128)
    hidden, cot = hidden.reshape(nsub, sub, width), cot.reshape(nsub, sub, width)
    blocks = pltpu.VMEM((nc, ns, rw, part), BF)
    smalls = pltpu.VMEM((nc,) + v, F32)
    runs = pltpu.VMEM((ns, nsub, sub, width), BF)
    gin, gout, *own, gh, mod = pl.pallas_call(
        functools.partial(end_kernel, nd, ns, nsub, rows, turned),
        out_shape=[
            jax.ShapeDtypeStruct((rows, 2 * inner), F32),
            jax.ShapeDtypeStruct((rows, inner), F32),
            jax.ShapeDtypeStruct((units, 128), F32),
            jax.ShapeDtypeStruct((rank, units), F32),
            jax.ShapeDtypeStruct((states, units), F32),
            jax.ShapeDtypeStruct((states, units), F32),
            jax.ShapeDtypeStruct((taps, units), F32),
            jax.ShapeDtypeStruct((1, units), F32),
            jax.ShapeDtypeStruct((1, units), F32),
            jax.ShapeDtypeStruct((nsub, sub, width), BF),
            jax.ShapeDtypeStruct((nd, 8, short), F32),
        ],
        in_specs=[HBM] * 5 + [VMEM] * 9, out_specs=[VMEM] * 11,
        scratch_shapes=[
            pltpu.VMEM((length, cols), BF), pltpu.VMEM(modded.shape, BF), pltpu.VMEM(normed.shape, BF),
            pltpu.VMEM((width, cols), BF),
            pltpu.VMEM((nd,) + v, F32), pltpu.VMEM(v, F32), runs,
            pltpu.VMEM((nc, 2, ns, rw, part), BF), blocks, blocks,
            smalls, smalls, pltpu.VMEM(v, F32), pltpu.VMEM((ns, rw, part), BF), pltpu.VMEM((ns, rw, cols), BF), runs, runs,
            pltpu.VMEM((sub, width), F32), pltpu.VMEM((8, width), F32), pltpu.VMEM((8, short), F32),
            pltpu.VMEM((ns, 8, short), F32),
            DMA((5,)),
            DMA((nc,)), DMA((nc,)), DMA((nc,)), DMA((nc,)), DMA((ns,)), DMA((ns,)), DMA((ns,)), DMA((ns,)),
            DMA((nc,)), DMA((nc,)), DMA((nc,)), DMA((nc,)), DMA(()), DMA(()),
            DMA((ns, nsub)), DMA((ns, nsub)), DMA((ns, nsub)), DMA((ns, nsub)),
            DMA((ns,)), DMA((ns,)), DMA((nd,)), DMA((nd,)),
        ],
        compiler_params=pltpu.CompilerParams(
            collective_id=cid, has_side_effects=True, vmem_limit_bytes=60 * 2**20),
        name="end",
    )(grad_inner, grad_gate, modded, normed, wx, *small, hidden, cot, line, early)
    return gin, gout, own, gh.reshape(local, width), mod


def frequency_embed(timestep):
    half_width = FREQ // 2
    counter = jnp.arange(half_width, dtype=F32)
    frequency = jnp.exp(counter * (-math.log(10000.0) / half_width))
    angles = timestep.astype(F32)[:, None] * frequency[None, :]
    return jnp.concatenate([jnp.cos(angles), jnp.sin(angles)], axis=1)


def dot(a, b):
    return jnp.dot(a, b, preferred_element_type=F32)


def dot_nt(a, b):
    return lax.dot_general(a, b, (((1,), (1,)), ((), ())), preferred_element_type=F32)


def dot_tn(a, b):
    return lax.dot_general(a, b, (((0,), (0,)), ((), ())), preferred_element_type=F32)


def body(
    hidden,
    pad_mask,
    timestep,
    input_weight,
    select_weight,
    step_weight,
    output_weight,
    decay_forward,
    decay_reverse,
    filter_weight,
    filter_bias,
    step_bias,
    modulation_weight,
    modulation_bias,
    cotangent,
):
    ns, nd = lax.axis_size("seq"), lax.axis_size("dp")
    q, d = lax.axis_index("seq"), lax.axis_index("dp")
    every = ("dp", "seq")
    local_len, width = hidden.shape[1:]
    length = local_len * ns
    inner = output_weight.shape[0]
    part = inner // ns
    rank = step_weight.shape[0]
    state = decay_forward.shape[1]
    taps = filter_weight.shape[0]
    rows_in = input_weight.shape[0]
    lanes = select_weight.shape[1]

    units = part // nd
    embedded = jax.nn.silu(frequency_embed(timestep)).astype(BF)
    modb = jnp.zeros((-(-3 * width // 1024) * 1024,), F32)
    modb = lax.dynamic_update_slice(modb, modulation_bias.astype(F32), ((d * ns + q) * modulation_bias.shape[0],))
    row_pad = ((0, -rows_in % 16), (0, 0))
    fused = rows_in % 16 == 0
    modded, normed, inner_part, gate_branch, wx, select_q, step_q, rates, fil, mask, modulation = start(
        hidden[0], pad_mask.reshape(-1, 128), jnp.pad(input_weight, row_pad), jnp.pad(output_weight.T, row_pad),
        embedded, modulation_weight, modb.reshape(-1, 128),
        (select_weight, step_weight, decay_forward.T, decay_reverse.T, filter_weight, filter_bias[None], step_bias[None]),
        fused, nd, ns, 4)
    wx = wx.reshape(nd * ns, -1, 3 * part)[:, :rows_in].reshape(width, 3 * part)
    win, wout = wx[:, : 2 * part], wx[:, 2 * part :]
    mask = mask[:, : local_len // 128].reshape(length, 1).astype(F32)
    rates_f, rates_r, rates_f2, rates_r2 = [rates[k * state : (k + 1) * state] for k in range(4)]
    modulation = modulation[:1]
    shifts = modulation[:, :width]
    scales = modulation[:, width : 2 * width]
    gate_scale = modulation[:, 2 * width :]

    def norm(x):
        x = x.astype(F32)
        centered = x - jnp.mean(x, axis=1, keepdims=True)
        inverse = lax.rsqrt(jnp.mean(centered * centered, axis=1, keepdims=True) + EPS)
        return centered * inverse, inverse

    if fused:
        modded, normed = modded.reshape(length, width), normed.reshape(length, width)
        inner_part, gate_branch = inner_part.reshape(length, part), gate_branch.reshape(length, part)
    else:
        normed = norm(modded.reshape(length, width))[0]
        modded, normed = (normed * (1.0 + scales) + shifts).astype(BF), normed.astype(BF)
        projected = dot(modded, win)
        inner_part, gate_branch = projected[:, :part].astype(BF), projected[:, part:]
    inner_part = inner_part.astype(F32) * mask
    padded = jnp.pad(inner_part, ((taps - 1, 0), (0, 0)))
    filtered = fil[taps][None]
    for k in range(taps):
        filtered = filtered + fil[k][None] * padded[k : k + length]
    sigma_filter = jax.nn.sigmoid(filtered)
    active = (filtered * sigma_filter).astype(BF)
    active32 = active.astype(F32)
    selected = column_sum(dot(active, select_q).astype(BF), ns, BF, 0)
    cot, selected = lax.optimization_barrier((cotangent[0], selected))
    cot = lax.all_gather(cot, "seq", axis=0, tiled=True)
    low_rank = selected[:, :rank].astype(BF)
    b_rows = selected[:, rank : rank + state].astype(F32)
    c_rows = selected[:, rank + state :].astype(F32)
    pre_steps = dot(low_rank, step_q) + fil[taps + 1][None]
    steps = jax.nn.softplus(pre_steps)
    drive = steps * active32
    mixed_f, mixed_r, states_f, states_r = fwd_scan(steps, drive, rates_f2, rates_r2, b_rows.T, blockdiag(c_rows))
    merged = mixed_f + mixed_r
    sigma_gate = jax.nn.sigmoid(gate_branch)
    silu_gate = gate_branch * sigma_gate
    gated = (merged * silu_gate).astype(BF)
    branch = dot_nt(gated, wout).astype(BF)
    branch, cot = lax.optimization_barrier((branch, cot))
    branch = lax.psum_scatter(branch, "seq", scatter_dimension=0, tiled=True).astype(F32)

    mask_here = pad_mask[0].astype(F32)[:, None]
    cot_here = cotangent[0].astype(F32)
    block_out = (hidden[0].astype(F32) + gate_scale * mask_here * branch).astype(BF)
    grad_gate = jnp.sum(mask_here * cot_here * branch, axis=0)

    grad_branch = lax.optimization_barrier((cot.astype(F32) * gate_scale * mask).astype(BF))
    grad_gated = dot(grad_branch, wout)
    grad_merged = grad_gated * silu_gate
    grad_gate_branch = grad_gated * merged * sigma_gate * (1.0 + gate_branch * (1.0 - sigma_gate))
    grad_gate_branch = grad_gate_branch.astype(BF)
    rows_first = Layout((0, 1))
    early = jnp.concatenate([
        with_layout_constraint(dot_tn(modded, grad_gate_branch).astype(BF), rows_first),
        with_layout_constraint(dot_tn(grad_branch, gated).astype(BF), rows_first)], axis=1)
    early = lax.psum_scatter(early, "dp", scatter_dimension=0, tiled=True)
    dlog_f, dlog_r, adjb_f, adjb_r, bg_f, bg_r, cg_f, cg_r, rg_f, rg_r = bwd_scan(
        steps, drive.astype(BF), grad_merged, rates_f2, rates_r2, c_rows.T, blockdiag(b_rows), states_f, states_r)
    adjb = adjb_f + adjb_r
    grad_steps = (dlog_f + dlog_r) * (1.0 / LOG2E) + active32 * adjb
    grad_b = (bg_f + bg_r).reshape(length, state)
    grad_c = (cg_f + cg_r).reshape(length, state)
    grad_decay_f = rg_f * rates_f
    grad_decay_r = rg_r * rates_r
    grad_pre = grad_steps * jax.nn.sigmoid(pre_steps)
    grad_step_bias = jnp.sum(grad_pre, axis=0)
    grad_pre_low = grad_pre.astype(BF)
    grad_step = dot_tn(low_rank, grad_pre_low)
    grad_low_rank = dot_nt(grad_pre_low, step_q)
    grad_selected = column_sum(jnp.concatenate([grad_low_rank, grad_b, grad_c], axis=1).astype(BF), ns, BF, 1)
    grad_select = dot_tn(active, grad_selected)
    grad_active = steps * adjb + dot_nt(grad_selected, select_q)
    grad_filtered = grad_active * sigma_filter * (1.0 + filtered * (1.0 - sigma_filter))
    extended = jnp.pad(grad_filtered, ((0, taps - 1), (0, 0)))
    grad_inner = jnp.zeros_like(grad_filtered)
    filter_rows = []
    for k in range(taps):
        lead = taps - 1 - k
        grad_inner = grad_inner + fil[k][None] * extended[lead : lead + length]
        filter_rows.append(jnp.sum(grad_filtered * padded[k : k + length], axis=0))
    grad_filter_bias = jnp.sum(grad_filtered, axis=0)
    grad_inner = (grad_inner * mask).astype(BF)
    grad_fil = jnp.stack(filter_rows + [grad_filter_bias, grad_step_bias])
    grad_fil = jnp.pad(grad_fil, ((0, 8 - grad_fil.shape[0]), (0, 0)))
    line = jnp.concatenate([scales, grad_gate[None], jnp.pad(embedded.astype(F32) / ns, ((0, 0), (0, width - FREQ))),
                            jnp.zeros((5, width), F32)])
    g_in, g_out, own, grad_hidden, sums = end(
        grad_inner, grad_gate_branch, modded, normed, wx, early, (grad_select, grad_step, grad_decay_f, grad_decay_r, grad_fil), taps, hidden[0], cotangent[0], line, rows_in, nd, ns, 2)
    gs_select, gs_step, gs_f, gs_r, gs_taps, gs_fbias, gs_sbias = own
    sums = sums.reshape(nd, -1)
    embeds = sums[:, 3 * width : 3 * width + FREQ]
    grad_mod = sums[:, : 3 * width]
    me = d * ns + q
    mine = lax.dynamic_slice_in_dim(embeds, me * modulation_weight.shape[0], modulation_weight.shape[0], 1)
    g_modw = lax.dot_general(mine, grad_mod, (((0,), (0,)), ((), ())), precision=HIGHEST)
    g_modb = lax.dynamic_slice_in_dim(
        jnp.sum(grad_mod, axis=0), me * modulation_bias.shape[0], modulation_bias.shape[0], 0)
    return (
        block_out[None],
        grad_hidden[None],
        g_in,
        gs_select,
        gs_step,
        g_out.T,
        gs_f.T,
        gs_r.T,
        gs_taps,
        gs_fbias[0],
        gs_sbias[0],
        g_modw,
        g_modb,
    )


def solution(mesh):
    return jax.shard_map(
        body,
        mesh=mesh,
        in_specs=(
            P("dp", "seq", None),
            P("dp", "seq"),
            P("dp"),
            P(("dp", "seq"), None),
            P(("dp", "seq"), None),
            P(None, ("dp", "seq")),
            P(None, ("dp", "seq")),
            P(("dp", "seq"), None),
            P(("dp", "seq"), None),
            P(None, ("dp", "seq")),
            P(("dp", "seq")),
            P(("dp", "seq")),
            P(("dp", "seq"), None),
            P(("dp", "seq")),
            P("dp", "seq", None),
        ),
        out_specs=(
            P("dp", "seq", None),
            P("dp", "seq", None),
            P(("dp", "seq"), None),
            P(("dp", "seq"), None),
            P(None, ("dp", "seq")),
            P(None, ("dp", "seq")),
            P(("dp", "seq"), None),
            P(("dp", "seq"), None),
            P(None, ("dp", "seq")),
            P(("dp", "seq")),
            P(("dp", "seq")),
            P(("dp", "seq"), None),
            P(("dp", "seq")),
        ),
        check_vma=False,
    )
```

```python
import functools
import math

import jax
import jax.numpy as jnp
from jax import lax
from jax.experimental import pallas as pl
from jax.experimental.layout import Layout, with_layout_constraint
from jax.experimental.pallas import tpu as pltpu
from jax.sharding import PartitionSpec as P

FREQ = 256
EPS = 1e-06
HIGHEST = lax.Precision.HIGHEST
LOG2E = 1.4426950408889634
SUB = 16
WF = 384
WB = 768
F32, BF = jnp.float32, jnp.bfloat16
NT = (((1,), (1,)), ((), ()))


def columns_of(rows_t, base):
    turned = pltpu.roll(rows_t, rows_t.shape[1] - base, 1)
    return [jnp.broadcast_to(turned[:, j:j + 1], (rows_t.shape[0], 128)) for j in range(SUB)]


def wide(block, lanes):
    return jnp.concatenate([block] * (lanes // 128), axis=1) if lanes > 128 else block


def states_of(base, at):
    return pl.ds(pl.multiple_of((base + at) * 16, 16), 16)


def fwd_kernel(step_f, step_r, u_f, u_r, rate_f, rate_r, bt_f, bt_r, cblk_f, cblk_r,
               y_f, y_r, s_f, s_r, carry, f0, f1, r0, r1):
    rows, lanes = step_f.shape

    @pl.when(pl.program_id(0) == 0)
    def _():
        carry[...] = jnp.zeros(carry.shape, F32)

    wide_by = min(WF, lanes)
    cuts = [slice(c, c + wide_by) for c in range(0, lanes, wide_by)]

    def walk(states, bases, kept):
        cols = [columns_of(bt[...], base) for bt, base in zip((bt_f, bt_r), bases)]
        out = []
        for cut, pair in zip(cuts, states):
            pair = list(pair)
            rates = rate_f[:, cut], rate_r[:, cut]
            for k in range(SUB):
                for z, (step, u, s, j) in enumerate(((step_f, u_f, s_f, k), (step_r, u_r, s_r, SUB - 1 - k))):
                    at = pl.ds(bases[z] + j, 1)
                    decay = jnp.exp2(step[at, cut] * rates[z])
                    pair[z] = decay * pair[z] + u[at, cut] * wide(cols[z][j], wide_by)
                    low = pair[z].astype(BF)
                    s[states_of(bases[z], j), cut] = low
                    kept[z][j * 16:(j + 1) * 16, cut] = low
            out.append(tuple(pair))
        return tuple(out)

    def mix(base, cblk, kept, y):
        here = pl.ds(base, SUB)
        y[here, :] = jnp.dot(cblk[here, :], kept[...], preferred_element_type=F32)

    def start_of(a, flip):
        a = jnp.maximum(a, 0)
        return pl.multiple_of(rows - SUB - a * SUB if flip else a * SUB, SUB)

    def two(i, states):
        for half, (fk, rk, fp, rp) in enumerate(((f0, r0, f1, r1), (f1, r1, f0, r0))):
            a = 2 * i + half
            mix(start_of(a - 1, False), cblk_f, fp, y_f)
            mix(start_of(a - 1, True), cblk_r, rp, y_r)
            states = walk(states, (start_of(a, False), start_of(a, True)), (fk, rk))
        return states

    states = tuple((carry[0, :, cut], carry[1, :, cut]) for cut in cuts)
    states = lax.fori_loop(0, rows // SUB // 2, two, states)
    mix(rows - SUB, cblk_f, f1, y_f)
    mix(0, cblk_r, r1, y_r)
    for cut, pair in zip(cuts, states):
        carry[0, :, cut], carry[1, :, cut] = pair


def fwd_scan(steps, u, rates_f, rates_r, b_t, cblk, tile=128):
    length, lanes = steps.shape
    blocks = length // tile
    specs = []
    for order in (lambda t: t, lambda t: blocks - 1 - t):
        specs.append((
            pl.BlockSpec((tile, lanes), lambda t, order=order: (order(t), 0)),
            pl.BlockSpec((16, lanes), lambda t: (0, 0)),
            pl.BlockSpec((16, tile), lambda t, order=order: (0, order(t))),
            pl.BlockSpec((tile, 256), lambda t, order=order: (order(t), 0)),
            pl.BlockSpec((tile * 16, lanes), lambda t, order=order: (order(t), 0)),
        ))
    (row_f, rate, bt_f, blk_f, s_f), (row_r, _, bt_r, blk_r, s_r) = specs
    y = jax.ShapeDtypeStruct((length, lanes), F32)
    s = jax.ShapeDtypeStruct((length * 16, lanes), BF)
    kept = pltpu.VMEM((256, lanes), BF)
    return pl.pallas_call(
        fwd_kernel,
        grid=(blocks,),
        in_specs=[row_f, row_r, row_f, row_r, rate, rate, bt_f, bt_r, blk_f, blk_r],
        out_specs=[row_f, row_r, s_f, s_r],
        out_shape=[y, y, s, s],
        scratch_shapes=[pltpu.VMEM((2, 16, lanes), F32), kept, kept, kept, kept],
        compiler_params=pltpu.CompilerParams(vmem_limit_bytes=56 * 2**20, dimension_semantics=("arbitrary",)),
        cost_estimate=pl.CostEstimate(flops=length * lanes * 16 * 3200, transcendentals=0, bytes_accessed=length * lanes * 80),
        name="fwd_scan",
    )(steps, steps, u, u, rates_f, rates_r, b_t, b_t, cblk, cblk)


def bwd_kernel(step_f, step_r, u_f, u_r, gy_f, gy_r, rate_f, rate_r, ct_f, ct_r, bblk_f, bblk_r, s_f, s_r, sp_f, sp_r,
               dlog_f, dlog_r, adjb_f, adjb_r, bg_f, bg_r, cg_f, cg_r, rg_f, rg_r, carry,
               af0, af1, ar0, ar1, lf0, lf1, lr0, lr1):
    rows, lanes = step_f.shape
    t = pl.program_id(0)
    last = pl.num_programs(0) - 1

    @pl.when(t == 0)
    def _():
        carry[...] = jnp.zeros(carry.shape, F32)
        rg_f[...] = jnp.zeros(rg_f.shape, F32)
        rg_r[...] = jnp.zeros(rg_r.shape, F32)

    ones = (lax.broadcasted_iota(jnp.int32, (SUB, 256), 0) == lax.broadcasted_iota(jnp.int32, (SUB, 256), 1) // 16)
    onesb = ones.astype(BF)
    zero = jnp.zeros((SUB, 256), F32)

    def start_of(a, down):
        a = jnp.maximum(a, 0)
        return pl.multiple_of(rows - SUB - a * SUB if down else a * SUB, SUB)

    wide_by = min(WB, lanes)
    cuts = [slice(c, c + wide_by) for c in range(0, lanes, wide_by)]

    def walk(states, bases, keep_a, keep_l):
        cols = [columns_of(ct[...], base) for ct, base in zip((ct_f, ct_r), bases)]
        out = []
        for cut, pair in zip(cuts, states):
            pair = list(pair)
            rates = rate_f[:, cut], rate_r[:, cut]
            rg = [rg_f[:, cut], rg_r[:, cut]]
            low_rates = [r.astype(BF) for r in rates]
            some = [[], []]
            for k in range(SUB):
                for z, (step, gy, s, sp, j) in enumerate((
                        (step_f, gy_f, s_f, sp_f, SUB - 1 - k), (step_r, gy_r, s_r, sp_r, k))):
                    at = pl.ds(bases[z] + j, 1)
                    row = step[at, cut]
                    adj = gy[at, cut] * wide(cols[z][j], wide_by) + pair[z]
                    pair[z] = jnp.exp2(row * rates[z]) * adj
                    before = bases[z] + (j + 1 if z else j - 1)
                    if k < SUB - 1:
                        inner = s[pl.ds(pl.multiple_of(before * 16, 16), 16), cut]
                    else:
                        inside = before < rows if z else before >= 0
                        safe = jnp.clip(before, 0, rows - 1)
                        inner = s[pl.ds(pl.multiple_of(safe * 16, 16), 16), cut]
                        outer = jnp.where(t == last, jnp.zeros_like(inner), sp[:, cut])
                        inner = jnp.where(inside, inner, outer)
                    grad = pair[z].astype(BF) * inner
                    keep_a[z][j * 16:(j + 1) * 16, cut] = adj.astype(BF)
                    keep_l[z][j * 16:(j + 1) * 16, cut] = grad * low_rates[z]
                    some[z].append(grad * jnp.broadcast_to(row, (16, wide_by)).astype(BF))
                    if len(some[z]) == 4:
                        rg[z] = rg[z] + ((some[z][0] + some[z][1]) + (some[z][2] + some[z][3])).astype(F32)
                        some[z] = []
            rg_f[:, cut], rg_r[:, cut] = rg
            out.append(tuple(pair))
        return tuple(out)

    mix_by = 256 if lanes % 256 == 0 else 128

    def mix(base, a_ref, l_ref, u, gy, bblk, s, dlog, adjb, bg, cg):
        here = pl.ds(base, SUB)
        line = pl.ds(base // SUB, 1)
        group = pl.ds(pl.multiple_of(base * 16, 256), 256)
        bgd = cgd = zero
        for c in range(0, lanes, mix_by):
            cut = slice(c, c + mix_by)
            dlog[here, cut] = jnp.dot(onesb, l_ref[:, cut], preferred_element_type=F32)
            a = a_ref[:, cut]
            adjb[here, cut] = jnp.dot(bblk[here, :], a, preferred_element_type=F32)
            bgd = bgd + lax.dot_general(u[here, cut].astype(BF), a, NT, preferred_element_type=F32)
            cgd = cgd + lax.dot_general(gy[here, cut].astype(BF), s[group, cut], NT, preferred_element_type=F32)
        bg[line, :] = jnp.sum(jnp.where(ones, bgd, zero), axis=0, keepdims=True)
        cg[line, :] = jnp.sum(jnp.where(ones, cgd, zero), axis=0, keepdims=True)

    def mix_f(base, a_ref, l_ref):
        mix(base, a_ref, l_ref, u_f, gy_f, bblk_f, s_f, dlog_f, adjb_f, bg_f, cg_f)

    def mix_r(base, a_ref, l_ref):
        mix(base, a_ref, l_ref, u_r, gy_r, bblk_r, s_r, dlog_r, adjb_r, bg_r, cg_r)

    def two(i, states):
        bufs = ((af0, lf0, ar0, lr0), (af1, lf1, ar1, lr1))
        for half in range(2):
            a = 2 * i + half
            naf, nlf, nar, nlr = bufs[half]
            paf, plf, par, plr = bufs[1 - half]
            mix_f(start_of(a - 1, True), paf, plf)
            mix_r(start_of(a - 1, False), par, plr)
            states = walk(states, (start_of(a, True), start_of(a, False)), (naf, nar), (nlf, nlr))
        return states

    states = tuple((carry[0, :, cut], carry[1, :, cut]) for cut in cuts)
    states = lax.fori_loop(0, rows // SUB // 2, two, states)
    mix_f(0, af1, lf1)
    mix_r(rows - SUB, ar1, lr1)
    for cut, pair in zip(cuts, states):
        carry[0, :, cut], carry[1, :, cut] = pair


def bwd_scan(steps, u, gy, rates_f, rates_r, c_t, bblk, states_f, states_r, tile=128):
    length, lanes = steps.shape
    blocks = length // tile
    down = lambda t: blocks - 1 - t
    up = lambda t: t

    def specs(order, before):
        return (
            pl.BlockSpec((tile, lanes), lambda t: (order(t), 0)),
            pl.BlockSpec((16, lanes), lambda t: (0, 0)),
            pl.BlockSpec((16, tile), lambda t: (0, order(t))),
            pl.BlockSpec((tile, 256), lambda t: (order(t), 0)),
            pl.BlockSpec((tile * 16, lanes), lambda t: (order(t), 0)),
            pl.BlockSpec((16, lanes), lambda t: (before(t), 0)),
            pl.BlockSpec((tile // 16, 256), lambda t: (order(t), 0)),
        )

    row_f, rate, ct_f, blk_f, s_f, sp_f, diag_f = specs(down, lambda t: jnp.maximum((blocks - 1 - t) * tile - 1, 0))
    row_r, _, ct_r, blk_r, s_r, sp_r, diag_r = specs(up, lambda t: jnp.minimum((t + 1) * tile, length - 1))
    y = jax.ShapeDtypeStruct((length, lanes), F32)
    diag = jax.ShapeDtypeStruct((length // 16, 256), F32)
    rg = jax.ShapeDtypeStruct((16, lanes), F32)
    kept = pltpu.VMEM((256, lanes), BF)
    return pl.pallas_call(
        bwd_kernel,
        grid=(blocks,),
        in_specs=[row_f, row_r, row_f, row_r, row_f, row_r, rate, rate, ct_f, ct_r, blk_f, blk_r, s_f, s_r, sp_f, sp_r],
        out_specs=[row_f, row_r, row_f, row_r, diag_f, diag_r, diag_f, diag_r, rate, rate],
        out_shape=[y, y, y, y, diag, diag, diag, diag, rg, rg],
        scratch_shapes=[pltpu.VMEM((2, 16, lanes), F32)] + [kept] * 8,
        compiler_params=pltpu.CompilerParams(vmem_limit_bytes=56 * 2**20, dimension_semantics=("arbitrary",)),
        cost_estimate=pl.CostEstimate(flops=length * lanes * 16 * 6800, transcendentals=0, bytes_accessed=length * lanes * 100),
        name="bwd_scan",
    )(steps, steps, u, u, gy, gy, rates_f, rates_r, c_t, c_t, bblk, bblk, states_f, states_r, states_f, states_r)


def blockdiag(rows):
    length = rows.shape[0]
    eye = (jnp.arange(length)[:, None] % 16) == (jnp.arange(256)[None, :] // 16)
    return jnp.where(eye, jnp.tile(rows, (1, 16)), 0).astype(BF)


MESH = pl.DeviceIdType.MESH
VMEM = pl.BlockSpec(memory_space=pltpu.VMEM)
HBM = pl.BlockSpec(memory_space=pl.ANY)
DMA = pltpu.SemaphoreType.DMA


def send(src, dst, out_sem, in_sem, to):
    return pltpu.make_async_remote_copy(
        src_ref=src, dst_ref=dst, send_sem=out_sem, recv_sem=in_sem, device_id=to, device_id_type=MESH)


def greet(devices):
    bar = pltpu.get_barrier_semaphore()
    for to in devices:
        pl.semaphore_signal(bar, inc=1, device_id=to, device_id_type=MESH)
    pl.semaphore_wait(bar, len(devices))


def column_sum_kernel(ns, p_ref, o_ref, land, s1, r1, s2, r2):
    d, q = lax.axis_index("dp"), lax.axis_index("seq")
    others = [lax.rem(q + k, ns) for k in range(1, ns)]
    greet([(d, t) for t in others])
    for k, t in enumerate(others):
        send(p_ref.at[t], land.at[q], s1.at[k], r1.at[q], (d, t)).start()
    total = p_ref[q].astype(F32)
    for k, t in enumerate(others):
        send(p_ref.at[t], land.at[t], s1.at[k], r1.at[t], (d, t)).wait_recv()
        total = total + land[t].astype(F32)
    o_ref[q] = total.astype(o_ref.dtype)
    for k, t in enumerate(others):
        send(o_ref.at[q], o_ref.at[q], s2.at[k], r2.at[q], (d, t)).start()
    for k, t in enumerate(others):
        send(o_ref.at[t], o_ref.at[t], s2.at[k], r2.at[t], (d, t)).wait_recv()
    for k, t in enumerate(others):
        send(p_ref.at[t], land.at[q], s1.at[k], r1.at[q], (d, t)).wait_send()
        send(o_ref.at[q], o_ref.at[q], s2.at[k], r2.at[q], (d, t)).wait_send()


def column_sum(partial, ns, out_dtype, cid):
    rows, lanes = partial.shape
    block = (ns, rows // ns, lanes)
    out = pl.pallas_call(
        functools.partial(column_sum_kernel, ns),
        out_shape=jax.ShapeDtypeStruct(block, out_dtype),
        in_specs=[VMEM], out_specs=VMEM,
        scratch_shapes=[pltpu.VMEM(block, partial.dtype), DMA((ns,)), DMA((ns,)), DMA((ns,)), DMA((ns,))],
        compiler_params=pltpu.CompilerParams(
            collective_id=cid, has_side_effects=True, vmem_limit_bytes=32 * 2**20),
        name="column_sum",
    )(partial.reshape(block))
    return out.reshape(rows, lanes)


def column_grads_kernel(ns, pre_ref, step_ref, bf_ref, br_ref, cf_ref, cr_ref, o_ref, state_ref, rows_ref, p_ref, *rest):
    rank = step_ref.shape[0]
    local = p_ref.shape[1]
    groups = local // 16
    rows_ref[...] = jnp.zeros(rows_ref.shape, BF)
    rows_ref[0:rank, :] = step_ref[...]
    for t in range(ns):
        lines = slice(t * groups, (t + 1) * groups)
        b, c = bf_ref[lines, :] + br_ref[lines, :], cf_ref[lines, :] + cr_ref[lines, :]
        for l in range(16):
            here = slice(l * 16, (l + 1) * 16)
            state_ref[pl.ds(l, groups, stride=16), :] = jnp.concatenate(
                [jnp.zeros((groups, rank), F32), b[:, here], c[:, here]], axis=1)
        low = lax.dot_general(pre_ref[t * local:(t + 1) * local, :], rows_ref[...], NT, preferred_element_type=F32)
        p_ref[t] = (low + state_ref[...]).astype(BF)
    column_sum_kernel(ns, p_ref, o_ref, *rest)


def column_grads(pre, step, b_f, b_r, c_f, c_r, ns, cid):
    rows, lanes = pre.shape[0], step.shape[0] + 32
    block = (ns, rows // ns, lanes)
    out = pl.pallas_call(
        functools.partial(column_grads_kernel, ns),
        out_shape=jax.ShapeDtypeStruct(block, BF),
        in_specs=[VMEM] * 6, out_specs=VMEM,
        scratch_shapes=[
            pltpu.VMEM((rows // ns, lanes), F32), pltpu.VMEM((lanes, pre.shape[1]), BF), pltpu.VMEM(block, BF),
            pltpu.VMEM(block, BF), DMA((ns,)), DMA((ns,)), DMA((ns,)), DMA((ns,))],
        compiler_params=pltpu.CompilerParams(
            collective_id=cid, has_side_effects=True, vmem_limit_bytes=32 * 2**20),
        name="column_grads",
    )(pre, step, b_f, b_r, c_f, c_r)
    return out.reshape(rows, lanes)


def start_kernel(nd, ns, nsub, fused, hid, win, wout, mask, emb, modw, modb, select, step, dec_f, dec_r, taps, fbias, sbias,
                 md_o, nm_o, inner_o, gate_o, wx_o, select_o, step_o, rate_o, fil_o, mask_o, mod_o,
                 hv, wv, mv, nv, iv, gv, pack, modw_v, pack_v, eland, prod, rowp, land1, land2,
                 su, ru, sd, rd, swz, rwx, swp, swm, spz, rp, spp, spm, sk, rk, se, re, s1, r1, s2, r2, own, out):
    d, q = lax.axis_index("dp"), lax.axis_index("seq")
    nc = nd // 2
    chip, core = d // 2, lax.rem(d, 2)
    mate = (chip * 2 + 1 - core, q)
    chips = [lax.rem(chip + k, nc) for k in range(1, nc)]
    others = [lax.rem(q + k, ns) for k in range(1, ns)]
    peers = [lax.rem(d + k, nd) for k in range(1, nd)]
    spread = nd // ns
    me = d * ns + q
    part = wout.shape[1] // ns
    rw = wout.shape[0]
    units = part // nd
    rank, states = step.shape[0], dec_f.shape[0]
    above = units + -units % 16
    taps_at = above + rank + 2 * states

    pack[...] = jnp.zeros(pack.shape, BF)
    pack[0:units, :] = select[...]
    pack[above:above + rank, 0:units] = step[...]
    pack[above + rank:above + rank + states, 0:units] = dec_f[...]
    pack[above + rank + states:taps_at, 0:units] = dec_r[...]
    pack[taps_at:taps_at + 16, 0:units] = jnp.concatenate(
        [taps[...].astype(F32), fbias[...].astype(F32), sbias[...].astype(F32),
         jnp.zeros((14 - taps.shape[0], units), F32)]).astype(BF)
    modw_v[...] = jnp.zeros(modw_v.shape, BF)
    modw_v[0:modw.shape[0], :] = modw[...]
    greet([(d, t) for t in others] + [(e, q) for e in peers])

    def column(ref, at):
        return ref.at[:, pl.ds(pl.multiple_of(at * part, 128), part)]

    def wrows(idx):
        return wv.at[pl.ds(pl.multiple_of(idx * rw, 16), rw), :]

    def pieces(t):
        return (column(win, t), column(win, ns + t), column(wout, t))

    def across(k, t, idx):
        return [
            send(src, wrows(idx).at[:, j * part:(j + 1) * part], swz.at[k, j], rwx.at[idx, j], (d, t))
            for j, src in enumerate(pieces(t))
        ]

    keep = [pltpu.make_async_copy(src, wrows(me).at[:, j * part:(j + 1) * part], own.at[j])
            for j, src in enumerate(pieces(q))]
    keep.append(pltpu.make_async_copy(hid, hv.at[q], own.at[3]))
    for copy in keep:
        copy.start()

    plane = d // spread
    slot = lax.rem(d, spread) * ns + q
    pack_z = send(pack, pack_v.at[slot], spz, rp.at[slot], (d, plane))
    pack_vwn = pltpu.make_async_copy(pack, pack_v.at[slot], own.at[4])

    @pl.when(plane == q)
    def _():
        pack_vwn.start()

    @pl.when(plane != q)
    def _():
        pack_z.start()

    def masks(k, t, src):
        return send(mask_o.at[src], mask_o.at[src], sk.at[k], rk.at[src], (d, t))

    def embeds(k, e, src):
        return send(eland.at[src], eland.at[src], se.at[k], re.at[src], (e, q))

    mask_o[q] = jnp.zeros(mask_o.shape[1:], BF)
    mask_o[q, 0:mask.shape[0], :] = mask[...].astype(F32).astype(BF)
    eland[d] = jnp.zeros(eland.shape[1:], BF)
    eland[d, 0:1, :] = emb[...]
    for k, e in enumerate(peers):
        embeds(k, e, d).start()
    for k, t in enumerate(others):
        masks(k, t, q).start()

    for k, t in enumerate(others):
        for copy in across(k, t, me)[:2]:
            copy.start()

    def rise(k, s):
        t = jnp.maximum(q - k, 0)
        src = hid.at[s] if k == 0 else hv.at[t, s]
        return send(src, hv.at[t, s], su.at[k, s], ru.at[k, s], (d, q + 1))

    def sink(k, s):
        t = jnp.minimum(q + k, ns - 1)
        src = hid.at[s] if k == 0 else hv.at[t, s]
        return send(src, hv.at[t, s], sd.at[k, s], rd.at[k, s], (d, q - 1))

    def hop(k, s):
        @pl.when(q >= k)
        def _():
            if k:
                rise(k - 1, s).wait_recv()
            if k < ns - 1:
                @pl.when(q + 1 < ns)
                def _():
                    rise(k, s).start()

        @pl.when(q + k < ns)
        def _():
            if k:
                sink(k - 1, s).wait_recv()
            if k < ns - 1:
                @pl.when(q >= 1)
                def _():
                    sink(k, s).start()

    for s in range(nsub):
        hop(0, s)
    for k, t in enumerate(others):
        across(k, t, me)[2].start()

    def cols_of(idx, kind):
        return wrows(idx).at[:, 2 * part * kind:2 * part + part * kind]

    def plane_w(c, idx, t, kind):
        return send(cols_of(idx, kind), cols_of(idx, kind), swp.at[kind, c, t], rwx.at[idx, 3 + kind], (c * 2 + core, q))

    def mate_w(c, idx, t, kind):
        return send(cols_of(idx, kind), cols_of(idx, kind), swm.at[kind, c, t], rwx.at[idx, 3 + kind], mate)

    def spread_w(t, kind):
        idx = d * ns + t
        for c in chips:
            plane_w(c, idx, t, kind).start()
        mate_w(chip, idx, t, kind).start()

    for copy in keep[:3]:
        copy.wait()
    spread_w(q, 0)

    for k, e in enumerate(peers):
        embeds(k, e, e).wait_recv()
    rows = modw_v.shape[0]
    here = lax.broadcasted_iota(jnp.int32, (FREQ, rows), 0)
    pick = here - lax.broadcasted_iota(jnp.int32, (FREQ, rows), 1)
    count = FREQ // (nd * ns)
    keep_col = lax.broadcasted_iota(jnp.int32, (FREQ, rows), 1) < count
    pick = jnp.where(jnp.logical_and(pick == me * count, keep_col), 1.0, 0.0).astype(BF)
    mine = jnp.dot(eland[...].reshape(nd * 16, FREQ), pick, preferred_element_type=F32).astype(BF)
    prod[...] = jnp.dot(mine, modw_v[...], preferred_element_type=F32)

    lines = prod.shape[1] // 128
    @pl.loop(0, nd)
    def _(e):
        rowp[e] = modb[...]
        for j in range(lines):
            rowp[e, j:j + 1, :] += prod[pl.ds(pl.multiple_of(e * 16, 16), 1), j * 128:(j + 1) * 128]

    def to_item(k, e, src):
        return send(rowp.at[e], land1.at[src], s1.at[k], r1.at[src], (e, q))

    for k, e in enumerate(peers):
        to_item(k, e, d).start()

    for k, t in enumerate(others):
        for copy in across(k, t, d * ns + t)[:2]:
            copy.wait_recv()
        spread_w(t, 0)

    def plane_p(c, i, t):
        return send(pack_v.at[i], pack_v.at[i], spp.at[c, t], rp.at[i], (c * 2 + core, q))

    def mate_p(c, i, t):
        return send(pack_v.at[i], pack_v.at[i], spm.at[c, t], rp.at[i], mate)

    base = lax.rem(d, spread) * ns

    @pl.when(plane == q)
    def _():
        pack_vwn.wait()
        for t in others:
            send(pack, pack_v.at[base + t], spz, rp.at[base + t], (d, plane)).wait_recv()
        for t in range(ns):
            for c in chips:
                plane_p(c, base + t, t).start()
            mate_p(chip, base + t, t).start()

    total = rowp[d]
    for k, e in enumerate(peers):
        to_item(k, e, e).wait_recv()
        total = total + land1[e]
    land2[q] = total

    def to_column(k, t, src):
        return send(land2.at[src], land2.at[src], s2.at[k], r2.at[src], (d, t))

    for k, t in enumerate(others):
        to_column(k, t, q).start()

    def relay_w(c, t, kind):
        idx = (c * 2 + core) * ns + t
        plane_w(c, idx, t, kind).wait_recv()
        mate_w(c, idx, t, kind).start()

    def holds(c):
        return (c * 2 + core) // spread == q

    def relay_p(c):
        first = lax.rem(c * 2 + core, spread) * ns
        @pl.when(holds(c))
        def _():
            for t in range(ns):
                plane_p(c, first + t, t).wait_recv()
                mate_p(c, first + t, t).start()

    def own_copies(t):
        return [pltpu.make_async_copy(src.at[t], dst.at[t], out.at[t, i]) for i, (src, dst) in enumerate(
            ((mv, md_o), (iv, inner_o), (gv, gate_o), (nv, nm_o)) if fused else ((hv, md_o),))]

    local = hv.shape[1] * hv.shape[2]
    width = hv.shape[3]

    def project(t):
        if fused:
            shift, scale = mod_o[0:1, 0:width], 1.0 + mod_o[0:1, width:2 * width]
            for s in range(nsub):
                @pl.loop(0, local // nsub // 16)
                def _(r):
                    x = hv[t, s, pl.ds(pl.multiple_of(r * 16, 16), 16), :].astype(F32)
                    x = x - jnp.mean(x, axis=1, keepdims=True)
                    x = x * lax.rsqrt(jnp.mean(x * x, axis=1, keepdims=True) + EPS)
                    to = pl.multiple_of(s * (local // nsub) + r * 16, 16)
                    nv[t, pl.ds(to, 16), :] = x.astype(BF)
                    mv[t, pl.ds(to, 16), :] = (x * scale + shift).astype(BF)
            tile = part if part % 256 else part // 2

            @pl.loop(0, part // tile)
            def _(j):
                for target, base in ((iv, 0), (gv, part)):
                    n = pl.ds(pl.multiple_of(base + j * tile, 128), tile)
                    full = jnp.dot(mv[t], wv[:, n], preferred_element_type=F32)
                    target[t, :, pl.ds(pl.multiple_of(j * tile, 128), tile)] = full.astype(target.dtype)
        for copy in own_copies(t):
            copy.start()

    relays = [(c, t) for t in [q] + others for c in chips]
    at = 0
    for s in range(nsub):
        hop(1, s)
        upto = len(relays) * (s + 1) // (2 * nsub)
        for c, t in relays[at:upto]:
            relay_w(c, t, 0)
        at = upto
    spread_w(q, 1)
    for k, t in enumerate(others):
        across(k, t, d * ns + t)[2].wait_recv()
        spread_w(t, 1)
    for c, t in relays[at:]:
        relay_w(c, t, 0)
    for c in chips:
        relay_p(c)

    for k, t in enumerate(others):
        to_column(k, t, t).wait_recv()
    total = land2[0]
    for t in range(1, ns):
        total = total + land2[t]
    mod_o[...] = jnp.zeros(mod_o.shape, F32)
    for i in range(mod_o.shape[1] // 128):
        mod_o[0:1, i * 128:(i + 1) * 128] = total[i:i + 1, :]

    twin = 1 - core
    for c in range(nc):
        for t in range(ns):
            idx = (c * 2 + twin) * ns + t
            mate_w(c, idx, t, 0).wait_recv()
    keep[3].wait()

    def project_at(t):
        @pl.when(jnp.logical_and(t >= 0, t < ns))
        def _():
            project(jnp.clip(t, 0, ns - 1))

    for k in range(2, ns):
        for s in range(nsub):
            hop(k, s)
            if k == 2 and s == 0:
                project(q)
            if s == nsub - 3:
                project_at(q - k + 1)
            if s == nsub - 2:
                project_at(q + k - 1)

    for c, t in relays:
        relay_w(c, t, 1)
    for c in range(nc):
        for t in range(ns):
            idx = (c * 2 + twin) * ns + t
            mate_w(c, idx, t, 1).wait_recv()
    wx_copy = pltpu.make_async_copy(wv, wx_o, own.at[5])
    wx_copy.start()

    for c in range(nc):
        first = lax.rem(c * 2 + twin, spread) * ns
        @pl.when((c * 2 + twin) // spread == q)
        def _():
            for t in range(ns):
                mate_p(c, first + t, t).wait_recv()
    for j in range(nd):
        here = slice(j * units, (j + 1) * units)
        select_o[here, :] = pack_v[j, 0:units, :]
        step_o[:, here] = pack_v[j, above:above + rank, 0:units]
        rate_o[0:2 * states, here] = -jnp.exp(pack_v[j, above + rank:taps_at, 0:units].astype(F32))
        fil_o[:, here] = pack_v[j, taps_at:taps_at + 16, 0:units].astype(F32)
    rate_o[2 * states:4 * states, :] = rate_o[0:2 * states, :] * LOG2E

    project_at(q - ns + 1)
    project_at(q + ns - 1)

    for k, t in enumerate(others):
        masks(k, t, t).wait_recv()
    wx_copy.wait()
    for t in range(ns):
        for copy in own_copies(t):
            copy.wait()

    for k, t in enumerate(others):
        for copy in across(k, t, me):
            copy.wait_send()
        masks(k, t, q).wait_send()
        to_column(k, t, q).wait_send()
    for k, e in enumerate(peers):
        embeds(k, e, d).wait_send()
        to_item(k, e, d).wait_send()

    @pl.when(plane != q)
    def _():
        pack_z.wait_send()

    @pl.when(plane == q)
    def _():
        for t in range(ns):
            for c in chips:
                plane_p(c, base + t, t).wait_send()
            mate_p(chip, base + t, t).wait_send()

    for kind in range(2):
        for t in range(ns):
            for c in chips:
                plane_w(c, d * ns + t, t, kind).wait_send()
                mate_w(c, (c * 2 + core) * ns + t, t, kind).wait_send()
            mate_w(chip, d * ns + t, t, kind).wait_send()
    for c in chips:
        first = lax.rem(c * 2 + core, spread) * ns
        @pl.when(holds(c))
        def _():
            for t in range(ns):
                mate_p(c, first + t, t).wait_send()
    for k in range(ns - 1):
        for s in range(nsub):
            @pl.when(jnp.logical_and(q >= k, q + 1 < ns))
            def _():
                rise(k, s).wait_send()
            @pl.when(jnp.logical_and(q + k < ns, q >= 1))
            def _():
                sink(k, s).wait_send()


def start(hidden, mask, win, wout, embedded, modw, modb, small, fused, nd, ns, cid):
    nsub = 4
    length, width = hidden.shape
    rows, inner = wout.shape
    part = inner // ns
    nc = nd // 2
    hidden = hidden.reshape(nsub, length // nsub, width)
    lines = modb.shape
    rank, units, states = small[1].shape[0], part // nd, small[2].shape[0]
    pack = (units + -units % 16 + rank + 2 * states + 16, 128)
    held = modw.shape[0] + -modw.shape[0] % 16
    runs = (ns,) + (hidden.shape if not fused else (length, width))
    return pl.pallas_call(
        functools.partial(start_kernel, nd, ns, nsub, fused),
        out_shape=[
            jax.ShapeDtypeStruct(runs, BF),
            jax.ShapeDtypeStruct((ns, length, width), BF),
            jax.ShapeDtypeStruct((ns, length, part), BF),
            jax.ShapeDtypeStruct((ns, length, part), F32),
            jax.ShapeDtypeStruct((nd * ns * rows, 3 * part), BF),
            jax.ShapeDtypeStruct((part, 128), BF),
            jax.ShapeDtypeStruct((rank, part), BF),
            jax.ShapeDtypeStruct((4 * states, part), F32),
            jax.ShapeDtypeStruct((16, part), F32),
            jax.ShapeDtypeStruct((ns, 16, 128), BF),
            jax.ShapeDtypeStruct((8, modw.shape[1]), F32),
        ],
        in_specs=[HBM, HBM, HBM] + [VMEM] * 11,
        out_specs=[HBM] * 5 + [VMEM] * 6,
        scratch_shapes=[
            pltpu.VMEM((ns,) + hidden.shape, BF), pltpu.VMEM((nd * ns * rows, 3 * part), BF),
            pltpu.VMEM((ns, length, width), BF), pltpu.VMEM((ns, length, width), BF), pltpu.VMEM((ns, length, part), BF), pltpu.VMEM((ns, length, part), F32),
            pltpu.VMEM(pack, BF), pltpu.VMEM((held, modw.shape[1]), BF), pltpu.VMEM((nd,) + pack, BF),
            pltpu.VMEM((nd, 16, FREQ), BF), pltpu.VMEM((nd * 16, modw.shape[1]), F32),
            pltpu.VMEM((nd,) + lines, F32), pltpu.VMEM((nd,) + lines, F32), pltpu.VMEM((ns,) + lines, F32),
            DMA((ns - 1, nsub)), DMA((ns - 1, nsub)), DMA((ns - 1, nsub)), DMA((ns - 1, nsub)),
            DMA((ns, 3)), DMA((nd * ns, 5)), DMA((2, nc, ns)), DMA((2, nc, ns)),
            DMA(()), DMA((nd,)), DMA((nc, ns)), DMA((nc, ns)),
            DMA((ns,)), DMA((ns,)), DMA((nd,)), DMA((nd,)),
            DMA((nd,)), DMA((nd,)), DMA((ns,)), DMA((ns,)), DMA((6,)), DMA((ns, 4)),
        ],
        compiler_params=pltpu.CompilerParams(
            collective_id=cid, has_side_effects=True, vmem_limit_bytes=56 * 2**20),
        name="start",
    )(hidden, win, wout, mask, embedded, modw, modb, *small)


def end_kernel(nd, ns, nsub, rows, turned, nfil,
               gi_h, gg_h, md_h, nm_h, wx_h, gsel, gstep, gdf, gdr, rates, hid_ref, cot_ref, mod_ref, gate_ref, emb_ref, early, *rest):
    gfil = rest[:nfil]
    (gin_o, gout_o, sel_o, step_o, df_o, dr_o, taps_o, fb_o, sb_o, gh_o, mod_o,
               gp, md, nm, wx, sm_ref, so_ref, gm, made, pair, plane, spair, splane, ssum, fro, ready, up, down, own, acc, msg, mland,
               ld, sa, ra, sb, rb, sc, rc, se, re, ta, ra2, tb, rb2, tc, rc2, su, ru, sd, rd, s1, r1, s2, r2) = rest[nfil:]
    d, q = lax.axis_index("dp"), lax.axis_index("seq")
    nc = nd // 2
    chip, core = d // 2, lax.rem(d, 2)
    mate = chip * 2 + 1 - core
    pairs = [(1, 1), (1, 0), (0, 1)] + [(a, b) for b in range(2, nc // 2) for a in (0, 1)]
    chips = [lax.rem(chip + a, 2) + 2 * lax.rem(chip // 2 + b, nc // 2) for a, b in pairs]
    others = [lax.rem(q + k, ns) for k in range(1, ns)]
    peers = [lax.rem(d + k, nd) for k in range(1, nd)]
    spread = nd // ns
    final_to = (spread * q + d // ns, lax.rem(d, ns))
    me = d * ns + q
    final_from = (lax.rem(me, nd), me // nd)
    stays = jnp.logical_and(final_to[0] == d, final_to[1] == q)
    length, cols = gp.shape
    part = cols // 2
    width = wx.shape[0]
    local = length // ns
    sub = local // nsub
    rw = pair.shape[2]
    half = ns * rw

    loads = [pltpu.make_async_copy(src, dst, ld.at[i]) for i, (src, dst) in enumerate(
        ((gi_h, gp.at[:, 0:part]), (gg_h, gp.at[:, part:cols]), (wx_h.at[:, 0:cols], wx), (nm_h, nm), (md_h, md)))]
    for copy in loads:
        copy.start()

    units = part // nd
    rank, states, taps = gstep.shape[0], gdf.shape[0], taps_o.shape[0]
    above = units + -units % 16
    taps_at = above + rank + 2 * states
    bar = pltpu.get_barrier_semaphore()
    friends = [(e, q) for e in peers] + [(d, t) for t in others]
    for to in friends:
        pl.semaphore_signal(bar, inc=1, device_id=to, device_id_type=MESH)
    @pl.when(jnp.logical_not(stays))
    def _():
        pl.semaphore_signal(bar, inc=1, device_id=final_from, device_id_type=MESH)

    def tokens(t):
        @pl.loop(0, width // 512)
        def _(j):
            here = pl.ds(pl.multiple_of(j * 512, 512), 512)
            lines = slice(t * local, (t + 1) * local)
            full = lax.dot_general(gp[lines, :], wx[here, :], NT, preferred_element_type=F32)
            acc[0:1, here] += jnp.sum(full, axis=0, keepdims=True)
            acc[1:2, here] += jnp.sum(full * nm[lines, here].astype(F32), axis=0, keepdims=True)
            full = full.astype(BF)
            for s in range(nsub):
                gm[t, s, :, here] = full[s * sub:(s + 1) * sub]

    def rise(t, s, src):
        return send(src, up.at[t, s], su.at[t, s], ru.at[t, s], (d, q + 1))

    def sink(t, s, src):
        return send(src, down.at[t, s], sd.at[t, s], rd.at[t, s], (d, q - 1))

    def added(land, t, s):
        land[t, s] = (land[t, s].astype(F32) + gm[t, s].astype(F32)).astype(BF)

    def open_up(t, s):
        @pl.when(jnp.logical_and(q == 0, t > 0))
        def _():
            rise(t, s, gm.at[t, s]).start()

    def open_down(t, s):
        @pl.when(jnp.logical_and(q == ns - 1, t < ns - 1))
        def _():
            sink(t, s, gm.at[t, s]).start()

    def step(k, s):
        t = ns - 1 - k

        @pl.when(jnp.logical_and(q < t, q > 0))
        def _():
            rise(t, s, up.at[t, s]).wait_recv()
            added(up, t, s)
            rise(t, s, up.at[t, s]).start()

        @pl.when(jnp.logical_and(q > k, q < ns - 1))
        def _():
            sink(k, s, down.at[k, s]).wait_recv()
            added(down, k, s)
            sink(k, s, down.at[k, s]).start()

    def far(k):
        for t in sorted({ns - 1 - k, k}, reverse=True):
            tokens(t)
            for s in range(nsub):
                open_up(t, s)
                open_down(t, s)

    @pl.when(stays)
    def _():
        pl.semaphore_wait(bar, len(friends))

    @pl.when(jnp.logical_not(stays))
    def _():
        pl.semaphore_wait(bar, len(friends) + 1)

    def whole(t, src):
        return send(early.at[t], ready.at[src], se.at[t], re.at[src], (d, t))

    for t in others:
        whole(t, q).start()
    for copy in loads[:4]:
        copy.wait()
    acc[...] = jnp.zeros(acc.shape, F32)
    acc[2:3, :] = jnp.sum(gate_ref[...], axis=0, keepdims=True)
    acc[3:4, 0:FREQ] = emb_ref[...].astype(F32) * (1.0 / ns)
    far(0)
    steps = [(k, s) for k in range(ns - 1) for s in range(nsub)]

    def first(c):
        return send(made.at[c, 1 - core], pair.at[c], sa.at[c], ra.at[c], (mate, q))

    def first_small(c):
        return send(sm_ref.at[c * 2 + 1 - core], spair.at[c], ta.at[c], ra2.at[c], (mate, q))

    def second(c, src):
        return send(pair.at[c], plane.at[src], sb.at[c], rb.at[src], (c * 2 + core, q))

    def second_small(c, src):
        return send(spair.at[c], splane.at[src], tb.at[c], rb2.at[src], (c * 2 + core, q))

    def block(c):
        at = pl.ds(pl.multiple_of(c * 2 * half, 2 * half), 2 * half)
        tile = part if part % 256 else part // 2
        left = md[at, :] if turned else md[:, at].T

        @pl.loop(0, part // tile)
        def _(j):
            n = pl.ds(pl.multiple_of(j * tile, 128), tile)
            full = jnp.dot(left, gp[:, n], preferred_element_type=F32).astype(BF)
            for h in range(2):
                for t in range(ns):
                    line = (h * ns + t) * rw
                    made[c, h, t, :, n] = full[line:line + rw]

    sm_ref[...] = jnp.zeros(sm_ref.shape, F32)
    for j in range(nd):
        here = slice(j * units, (j + 1) * units)
        sm_ref[j, 0:units, :] = gsel[here, :]
        sm_ref[j, above:above + rank, 0:units] = gstep[:, here]
        sm_ref[j, above + rank:above + rank + states, 0:units] = gdf[:, here] * rates[0:states, here]
        sm_ref[j, above + rank + states:taps_at, 0:units] = gdr[:, here] * rates[states:2 * states, here]
        for i, line in enumerate(gfil):
            sm_ref[j, taps_at + i:taps_at + i + 1, 0:units] = jnp.sum(line[:, here], axis=0, keepdims=True)

    loads[4].wait()
    order = chips + [chip]

    def give(c):
        block(c)
        first(c).start()
        first_small(c).start()

    give(order[0])
    for k in range(1, ns // 2):
        far(k)
    msg[...] = jnp.zeros(msg.shape, F32)
    long = msg.shape[1] // 128
    for i in range(3 * width // 128 + FREQ // 128):
        r, c = divmod(i * 128, width)
        to = (i % long) * 128
        msg[i // long:i // long + 1, to:to + 128] = acc[r:r + 1, c:c + 128]
    for k, t in enumerate(others):
        send(msg, mland.at[q], s1.at[k], r1.at[q], (d, t)).start()

    for i, c in enumerate(order):
        if i + 1 < nc:
            give(order[i + 1])
        first(c).wait_recv()
        @pl.loop(0, ns)
        def _(t):
            pair[c, t] = (pair[c, t].astype(F32) + made[c, core, t].astype(F32)).astype(BF)
        first_small(c).wait_recv()
        spair[c] = spair[c] + sm_ref[c * 2 + core]
        if i < nc - 1:
            second(c, chip).start()
            second_small(c, chip).start()
        for k, s in steps[i:i + 1]:
            step(k, s)
    late = len(steps) * 3 // 4
    for k, s in steps[nc:late]:
        step(k, s)

    for c in chips:
        second(c, c).wait_recv()
        second_small(c, c).wait_recv()
    @pl.loop(0, ns)
    def _(t):
        total = pair[chip, t].astype(F32)
        for c in chips:
            total = total + plane[c, t].astype(F32)
        pair[chip, t] = total.astype(BF)
    small = spair[chip]
    for c in chips:
        small = small + splane[c]
    ssum[...] = small

    def third(t, src):
        return send(pair.at[chip, t], fro.at[src], sc.at[t], rc.at[src], (d, t))

    last = send(ssum, so_ref, tc, rc2, final_to)
    @pl.when(stays)
    def _():
        so_ref[...] = ssum[...]
    @pl.when(jnp.logical_not(stays))
    def _():
        last.start()
    for t in others:
        third(t, q).start()
    fro[q] = pair[chip, q]
    for k, s in steps[max(nc, late):]:
        step(k, s)

    total = msg[...]
    for k, t in enumerate(others):
        send(msg, mland.at[t], s1.at[k], r1.at[t], (d, t)).wait_recv()
        total = total + mland[t]
    mod_o[d] = total
    for k, e in enumerate(peers):
        send(mod_o.at[d], mod_o.at[d], s2.at[k], r2.at[d], (e, q)).start()
    scale = 1.0 + mod_ref[0:1, width:2 * width]
    for s in range(nsub):
        own[...] = gm[q, s].astype(F32)

        @pl.when(q > 0)
        def _():
            rise(q, s, gm.at[q, s]).wait_recv()
            own[...] += up[q, s].astype(F32)

        @pl.when(q < ns - 1)
        def _():
            sink(q, s, gm.at[q, s]).wait_recv()
            own[...] += down[q, s].astype(F32)

        @pl.loop(0, sub // 16)
        def _(r):
            here = pl.ds(pl.multiple_of(r * 16, 16), 16)
            grad = own[here, :]
            x = hid_ref[s, here, :].astype(F32)
            x = x - jnp.mean(x, axis=1, keepdims=True)
            inverse = lax.rsqrt(jnp.mean(x * x, axis=1, keepdims=True) + EPS)
            normed = x * inverse
            grad = grad * scale
            grad = grad - jnp.mean(grad, axis=1, keepdims=True) - normed * jnp.mean(
                grad * normed, axis=1, keepdims=True)
            gh_o[s, here, :] = (cot_ref[s, here, :].astype(F32) + inverse * grad).astype(BF)

    inner = part * ns

    def place(src, rest):
        at = src * part
        gin_o[:, pl.ds(pl.multiple_of(at, 128), part)] = fro[src, 0:rows, :].astype(F32)
        gin_o[:, pl.ds(pl.multiple_of(inner + at, 128), part)] = rest[0:rows, 0:part].astype(F32)
        gout_o[:, pl.ds(pl.multiple_of(at, 128), part)] = rest[0:rows, part:2 * part].astype(F32)

    place(q, early[q])
    for t in others:
        third(t, t).wait_recv()
        whole(t, t).wait_recv()
        place(t, ready[t])
    for k, e in enumerate(peers):
        send(mod_o.at[e], mod_o.at[e], s2.at[k], r2.at[e], (e, q)).wait_recv()
    @pl.when(jnp.logical_not(stays))
    def _():
        last.wait_recv()
        last.wait_send()

    sel_o[...] = so_ref[0:units, :]
    step_o[...] = so_ref[above:above + rank, 0:units]
    df_o[...] = so_ref[above + rank:above + rank + states, 0:units]
    dr_o[...] = so_ref[above + rank + states:taps_at, 0:units]
    taps_o[...] = so_ref[taps_at:taps_at + taps, 0:units]
    fb_o[...] = so_ref[taps_at + taps:taps_at + taps + 1, 0:units]
    sb_o[...] = so_ref[taps_at + taps + 1:taps_at + taps + 2, 0:units]
    for c in order:
        first(c).wait_send()
        first_small(c).wait_send()
    for c in chips:
        second(c, chip).wait_send()
        second_small(c, chip).wait_send()
    for k, t in enumerate(others):
        third(t, q).wait_send()
        whole(t, q).wait_send()
        send(msg, mland.at[q], s1.at[k], r1.at[q], (d, t)).wait_send()
    for k, e in enumerate(peers):
        send(mod_o.at[d], mod_o.at[d], s2.at[k], r2.at[d], (e, q)).wait_send()
    for k, s in steps:
        t = ns - 1 - k
        @pl.when(q < t)
        def _():
            rise(t, s, gm.at[t, s]).wait_send()
        @pl.when(q > k)
        def _():
            sink(k, s, gm.at[k, s]).wait_send()


def end(grad_inner, grad_gate, modded, normed, wx, early, small, fil, hidden, cot, modulation, grad_gate_scale, embedded, rows, nd, ns, cid):
    length, part = grad_inner.shape
    cols = 2 * part
    width = wx.shape[0]
    inner = part * ns
    nc, nsub = nd // 2, 4
    local = length // ns
    sub = local // nsub
    rw = rows + -rows % 16
    half = ns * rw
    turned = 2 * half % 128 != 0 or rw != rows
    if turned:
        def turn(a):
            a = a.T.reshape(nd * ns, rows, length)
            return jnp.pad(a, ((0, 0), (0, rw - rows), (0, 0))).reshape(nd * ns * rw, length)
        modded = turn(modded)
    early = jnp.pad(early.reshape(ns, rows, cols), ((0, 0), (0, rw - rows), (0, 0)))
    short = -(-(3 * width + FREQ) // 1024) * 128
    units, rank, states = part // nd, small[1].shape[0], small[2].shape[0]
    v = (units + -units % 16 + rank + 2 * states + 16, 128)
    hidden, cot = hidden.reshape(nsub, sub, width), cot.reshape(nsub, sub, width)
    blocks = pltpu.VMEM((nc, ns, rw, part), BF)
    smalls = pltpu.VMEM((nc,) + v, F32)
    runs = pltpu.VMEM((ns, nsub, sub, width), BF)
    gin, gout, *own, gh, mod = pl.pallas_call(
        functools.partial(end_kernel, nd, ns, nsub, rows, turned, len(fil)),
        out_shape=[
            jax.ShapeDtypeStruct((rows, 2 * inner), F32),
            jax.ShapeDtypeStruct((rows, inner), F32),
            jax.ShapeDtypeStruct((units, 128), F32),
            jax.ShapeDtypeStruct((rank, units), F32),
            jax.ShapeDtypeStruct((states, units), F32),
            jax.ShapeDtypeStruct((states, units), F32),
            jax.ShapeDtypeStruct((len(fil) - 2, units), F32),
            jax.ShapeDtypeStruct((1, units), F32),
            jax.ShapeDtypeStruct((1, units), F32),
            jax.ShapeDtypeStruct((nsub, sub, width), BF),
            jax.ShapeDtypeStruct((nd, 8, short), F32),
        ],
        in_specs=[HBM] * 5 + [VMEM] * (11 + len(fil)), out_specs=[VMEM] * 11,
        scratch_shapes=[
            pltpu.VMEM((length, cols), BF), pltpu.VMEM(modded.shape, BF), pltpu.VMEM(normed.shape, BF),
            pltpu.VMEM((width, cols), BF),
            pltpu.VMEM((nd,) + v, F32), pltpu.VMEM(v, F32), runs,
            pltpu.VMEM((nc, 2, ns, rw, part), BF), blocks, blocks,
            smalls, smalls, pltpu.VMEM(v, F32), pltpu.VMEM((ns, rw, part), BF), pltpu.VMEM((ns, rw, cols), BF), runs, runs,
            pltpu.VMEM((sub, width), F32), pltpu.VMEM((8, width), F32), pltpu.VMEM((8, short), F32),
            pltpu.VMEM((ns, 8, short), F32),
            DMA((5,)),
            DMA((nc,)), DMA((nc,)), DMA((nc,)), DMA((nc,)), DMA((ns,)), DMA((ns,)), DMA((ns,)), DMA((ns,)),
            DMA((nc,)), DMA((nc,)), DMA((nc,)), DMA((nc,)), DMA(()), DMA(()),
            DMA((ns, nsub)), DMA((ns, nsub)), DMA((ns, nsub)), DMA((ns, nsub)),
            DMA((ns,)), DMA((ns,)), DMA((nd,)), DMA((nd,)),
        ],
        compiler_params=pltpu.CompilerParams(
            collective_id=cid, has_side_effects=True, vmem_limit_bytes=60 * 2**20),
        name="end",
    )(grad_inner, grad_gate, modded, normed, wx, *small, hidden, cot, modulation, grad_gate_scale, embedded, early, *fil)
    return gin, gout, own, gh.reshape(local, width), mod


def frequency_embed(timestep):
    half_width = FREQ // 2
    counter = jnp.arange(half_width, dtype=F32)
    frequency = jnp.exp(counter * (-math.log(10000.0) / half_width))
    angles = timestep.astype(F32)[:, None] * frequency[None, :]
    return jnp.concatenate([jnp.cos(angles), jnp.sin(angles)], axis=1)


def dot(a, b):
    return jnp.dot(a, b, preferred_element_type=F32)


def dot_nt(a, b):
    return lax.dot_general(a, b, (((1,), (1,)), ((), ())), preferred_element_type=F32)


def dot_tn(a, b):
    return lax.dot_general(a, b, (((0,), (0,)), ((), ())), preferred_element_type=F32)


def by_eight(a):
    return jnp.sum(a.reshape(-1, 8, a.shape[1]), axis=0)


def body(
    hidden,
    pad_mask,
    timestep,
    input_weight,
    select_weight,
    step_weight,
    output_weight,
    decay_forward,
    decay_reverse,
    filter_weight,
    filter_bias,
    step_bias,
    modulation_weight,
    modulation_bias,
    cotangent,
):
    ns, nd = lax.axis_size("seq"), lax.axis_size("dp")
    q, d = lax.axis_index("seq"), lax.axis_index("dp")
    every = ("dp", "seq")
    local_len, width = hidden.shape[1:]
    length = local_len * ns
    inner = output_weight.shape[0]
    part = inner // ns
    rank = step_weight.shape[0]
    state = decay_forward.shape[1]
    taps = filter_weight.shape[0]
    rows_in = input_weight.shape[0]
    lanes = select_weight.shape[1]

    units = part // nd
    embedded = jax.nn.silu(frequency_embed(timestep)).astype(BF)
    modb = jnp.zeros((-(-3 * width // 1024) * 1024,), F32)
    modb = lax.dynamic_update_slice(modb, modulation_bias.astype(F32), ((d * ns + q) * modulation_bias.shape[0],))
    row_pad = ((0, -rows_in % 16), (0, 0))
    fused = rows_in % 16 == 0
    modded, normed, inner_part, gate_branch, wx, select_q, step_q, rates, fil, mask, modulation = start(
        hidden[0], pad_mask.reshape(-1, 128), jnp.pad(input_weight, row_pad), jnp.pad(output_weight.T, row_pad),
        embedded, modulation_weight, modb.reshape(-1, 128),
        (select_weight, step_weight, decay_forward.T, decay_reverse.T, filter_weight, filter_bias[None], step_bias[None]),
        fused, nd, ns, 4)
    wx = wx.reshape(nd * ns, -1, 3 * part)[:, :rows_in].reshape(width, 3 * part)
    win, wout = wx[:, : 2 * part], wx[:, 2 * part :]
    mask = mask[:, : local_len // 128].reshape(length, 1).astype(F32)
    rates_f, rates_r, rates_f2, rates_r2 = [rates[k * state : (k + 1) * state] for k in range(4)]
    modulation_rows, modulation = modulation, modulation[:1]
    shifts = modulation[:, :width]
    scales = modulation[:, width : 2 * width]
    gate_scale = modulation[:, 2 * width :]

    def norm(x):
        x = x.astype(F32)
        centered = x - jnp.mean(x, axis=1, keepdims=True)
        inverse = lax.rsqrt(jnp.mean(centered * centered, axis=1, keepdims=True) + EPS)
        return centered * inverse, inverse

    if fused:
        modded, normed = modded.reshape(length, width), normed.reshape(length, width)
        inner_part, gate_branch = inner_part.reshape(length, part), gate_branch.reshape(length, part)
    else:
        normed = norm(modded.reshape(length, width))[0]
        modded, normed = (normed * (1.0 + scales) + shifts).astype(BF), normed.astype(BF)
        projected = dot(modded, win)
        inner_part, gate_branch = projected[:, :part].astype(BF), projected[:, part:]
    inner_part = inner_part.astype(F32) * mask
    padded = jnp.pad(inner_part, ((taps - 1, 0), (0, 0)))
    filtered = fil[taps][None]
    for k in range(taps):
        filtered = filtered + fil[k][None] * padded[k : k + length]
    sigma_filter = jax.nn.sigmoid(filtered)
    active = (filtered * sigma_filter).astype(BF)
    active32 = active.astype(F32)
    selected = column_sum(dot(active, select_q).astype(BF), ns, BF, 0)
    cot, selected = lax.optimization_barrier((cotangent[0], selected))
    cot = lax.all_gather(cot, "seq", axis=0, tiled=True)
    low_rank = selected[:, :rank].astype(BF)
    b_rows = selected[:, rank : rank + state].astype(F32)
    c_rows = selected[:, rank + state :].astype(F32)
    pre_steps = dot(low_rank, step_q) + fil[taps + 1][None]
    steps = jax.nn.softplus(pre_steps)
    drive = steps * active32
    mixed_f, mixed_r, states_f, states_r = fwd_scan(steps, drive, rates_f2, rates_r2, b_rows.T, blockdiag(c_rows))
    merged = mixed_f + mixed_r
    sigma_gate = jax.nn.sigmoid(gate_branch)
    silu_gate = gate_branch * sigma_gate
    gated = (merged * silu_gate).astype(BF)
    branch = dot_nt(gated, wout).astype(BF)
    branch, cot = lax.optimization_barrier((branch, cot))
    branch = lax.psum_scatter(branch, "seq", scatter_dimension=0, tiled=True).astype(F32)

    mask_here = pad_mask[0].astype(F32)[:, None]
    cot_here = cotangent[0].astype(F32)
    block_out = (hidden[0].astype(F32) + gate_scale * mask_here * branch).astype(BF)
    grad_gate = by_eight(mask_here * cot_here * branch)

    grad_branch = lax.optimization_barrier((cot.astype(F32) * gate_scale * mask).astype(BF))
    grad_gated = dot(grad_branch, wout)
    grad_merged = grad_gated * silu_gate
    grad_gate_branch = grad_gated * merged * sigma_gate * (1.0 + gate_branch * (1.0 - sigma_gate))
    grad_gate_branch = grad_gate_branch.astype(BF)
    rows_first = Layout((0, 1))
    early = jnp.concatenate([
        with_layout_constraint(dot_tn(modded, grad_gate_branch).astype(BF), rows_first),
        with_layout_constraint(dot_tn(grad_branch, gated).astype(BF), rows_first)], axis=1)
    early = lax.psum_scatter(early, "dp", scatter_dimension=0, tiled=True)
    dlog_f, dlog_r, adjb_f, adjb_r, bg_f, bg_r, cg_f, cg_r, rg_f, rg_r = bwd_scan(
        steps, drive, grad_merged, rates_f2, rates_r2, c_rows.T, blockdiag(b_rows), states_f, states_r)
    adjb = adjb_f + adjb_r
    grad_steps = (dlog_f + dlog_r) * (1.0 / LOG2E) + active32 * adjb
    grad_pre = grad_steps * -jnp.expm1(-steps)
    grad_step_bias = jnp.sum(grad_pre, axis=0, keepdims=True)
    grad_pre_low = grad_pre.astype(BF)
    grad_step = dot_tn(low_rank, grad_pre_low)
    grad_selected = column_grads(grad_pre_low, step_q, bg_f, bg_r, cg_f, cg_r, ns, 1)
    grad_select = dot_tn(active, grad_selected)
    grad_active = steps * adjb + dot_nt(grad_selected, select_q)
    grad_filtered = grad_active * sigma_filter * (1.0 + filtered * (1.0 - sigma_filter))
    extended = jnp.pad(grad_filtered, ((0, taps - 1), (0, 0)))
    grad_inner = jnp.zeros_like(grad_filtered)
    filter_rows = []
    for k in range(taps):
        lead = taps - 1 - k
        grad_inner = grad_inner + fil[k][None] * extended[lead : lead + length]
        filter_rows.append(by_eight(grad_filtered * padded[k : k + length]))
    grad_filter_bias = by_eight(grad_filtered)
    grad_inner = (grad_inner * mask).astype(BF)
    g_in, g_out, own, grad_hidden, sums = end(
        grad_inner, grad_gate_branch, modded, normed, wx, early, (grad_select, grad_step, rg_f, rg_r, rates),
        filter_rows + [grad_filter_bias, grad_step_bias], hidden[0], cotangent[0], modulation_rows, grad_gate, embedded,
        rows_in, nd, ns, 2)
    gs_select, gs_step, gs_f, gs_r, gs_taps, gs_fbias, gs_sbias = own
    sums = sums.reshape(nd, -1)
    embeds = sums[:, 3 * width : 3 * width + FREQ]
    grad_mod = sums[:, : 3 * width]
    me = d * ns + q
    mine = lax.dynamic_slice_in_dim(embeds, me * modulation_weight.shape[0], modulation_weight.shape[0], 1)
    g_modw = lax.dot_general(mine, grad_mod, (((0,), (0,)), ((), ())), precision=HIGHEST)
    g_modb = lax.dynamic_slice_in_dim(
        jnp.sum(grad_mod, axis=0), me * modulation_bias.shape[0], modulation_bias.shape[0], 0)
    return (
        block_out[None],
        grad_hidden[None],
        g_in,
        gs_select,
        gs_step,
        g_out.T,
        gs_f.T,
        gs_r.T,
        gs_taps,
        gs_fbias[0],
        gs_sbias[0],
        g_modw,
        g_modb,
    )


def solution(mesh):
    return jax.shard_map(
        body,
        mesh=mesh,
        in_specs=(
            P("dp", "seq", None),
            P("dp", "seq"),
            P("dp"),
            P(("dp", "seq"), None),
            P(("dp", "seq"), None),
            P(None, ("dp", "seq")),
            P(None, ("dp", "seq")),
            P(("dp", "seq"), None),
            P(("dp", "seq"), None),
            P(None, ("dp", "seq")),
            P(("dp", "seq")),
            P(("dp", "seq")),
            P(("dp", "seq"), None),
            P(("dp", "seq")),
            P("dp", "seq", None),
        ),
        out_specs=(
            P("dp", "seq", None),
            P("dp", "seq", None),
            P(("dp", "seq"), None),
            P(("dp", "seq"), None),
            P(None, ("dp", "seq")),
            P(None, ("dp", "seq")),
            P(("dp", "seq"), None),
            P(("dp", "seq"), None),
            P(None, ("dp", "seq")),
            P(("dp", "seq")),
            P(("dp", "seq")),
            P(("dp", "seq"), None),
            P(("dp", "seq")),
        ),
        check_vma=False,
    )
```

```python
import functools
import math

import jax
import jax.numpy as jnp
from jax import lax
from jax.experimental import pallas as pl
from jax.experimental.layout import Layout, with_layout_constraint
from jax.experimental.pallas import tpu as pltpu
from jax.sharding import PartitionSpec as P

FREQ = 256
EPS = 1e-06
HIGHEST = lax.Precision.HIGHEST
LOG2E = 1.4426950408889634
SUB = 16
WF = 384
WB = 768
F32, BF = jnp.float32, jnp.bfloat16
NT = (((1,), (1,)), ((), ()))


def columns_of(rows_t, base):
    turned = pltpu.roll(rows_t, rows_t.shape[1] - base, 1)
    return [jnp.broadcast_to(turned[:, j:j + 1], (rows_t.shape[0], 128)) for j in range(SUB)]


def wide(block, lanes):
    return jnp.concatenate([block] * (lanes // 128), axis=1) if lanes > 128 else block


def states_of(base, at):
    return pl.ds(pl.multiple_of((base + at) * 16, 16), 16)


def fwd_kernel(step_f, step_r, u_f, u_r, rate_f, rate_r, bt_f, bt_r, cblk_f, cblk_r,
               y_f, y_r, s_f, s_r, carry, f0, f1, r0, r1):
    rows, lanes = step_f.shape

    @pl.when(pl.program_id(0) == 0)
    def _():
        carry[...] = jnp.zeros(carry.shape, F32)

    wide_by = min(WF, lanes)
    cuts = [slice(c, c + wide_by) for c in range(0, lanes, wide_by)]

    def walk(states, bases, kept):
        cols = [columns_of(bt[...], base) for bt, base in zip((bt_f, bt_r), bases)]
        out = []
        for cut, pair in zip(cuts, states):
            pair = list(pair)
            rates = rate_f[:, cut], rate_r[:, cut]
            for k in range(SUB):
                for z, (step, u, s, j) in enumerate(((step_f, u_f, s_f, k), (step_r, u_r, s_r, SUB - 1 - k))):
                    at = pl.ds(bases[z] + j, 1)
                    decay = jnp.exp2(step[at, cut] * rates[z])
                    pair[z] = decay * pair[z] + u[at, cut] * wide(cols[z][j], wide_by)
                    low = pair[z].astype(BF)
                    s[states_of(bases[z], j), cut] = low
                    kept[z][j * 16:(j + 1) * 16, cut] = low
            out.append(tuple(pair))
        return tuple(out)

    def mix(base, cblk, kept, y):
        here = pl.ds(base, SUB)
        y[here, :] = jnp.dot(cblk[here, :], kept[...], preferred_element_type=F32)

    def start_of(a, flip):
        a = jnp.maximum(a, 0)
        return pl.multiple_of(rows - SUB - a * SUB if flip else a * SUB, SUB)

    def two(i, states):
        for half, (fk, rk, fp, rp) in enumerate(((f0, r0, f1, r1), (f1, r1, f0, r0))):
            a = 2 * i + half
            mix(start_of(a - 1, False), cblk_f, fp, y_f)
            mix(start_of(a - 1, True), cblk_r, rp, y_r)
            states = walk(states, (start_of(a, False), start_of(a, True)), (fk, rk))
        return states

    states = tuple((carry[0, :, cut], carry[1, :, cut]) for cut in cuts)
    states = lax.fori_loop(0, rows // SUB // 2, two, states)
    mix(rows - SUB, cblk_f, f1, y_f)
    mix(0, cblk_r, r1, y_r)
    for cut, pair in zip(cuts, states):
        carry[0, :, cut], carry[1, :, cut] = pair


def fwd_scan(steps, u, rates_f, rates_r, b_t, cblk, tile=128):
    length, lanes = steps.shape
    blocks = length // tile
    specs = []
    for order in (lambda t: t, lambda t: blocks - 1 - t):
        specs.append((
            pl.BlockSpec((tile, lanes), lambda t, order=order: (order(t), 0)),
            pl.BlockSpec((16, lanes), lambda t: (0, 0)),
            pl.BlockSpec((16, tile), lambda t, order=order: (0, order(t))),
            pl.BlockSpec((tile, 256), lambda t, order=order: (order(t), 0)),
            pl.BlockSpec((tile * 16, lanes), lambda t, order=order: (order(t), 0)),
        ))
    (row_f, rate, bt_f, blk_f, s_f), (row_r, _, bt_r, blk_r, s_r) = specs
    y = jax.ShapeDtypeStruct((length, lanes), F32)
    s = jax.ShapeDtypeStruct((length * 16, lanes), BF)
    kept = pltpu.VMEM((256, lanes), BF)
    return pl.pallas_call(
        fwd_kernel,
        grid=(blocks,),
        in_specs=[row_f, row_r, row_f, row_r, rate, rate, bt_f, bt_r, blk_f, blk_r],
        out_specs=[row_f, row_r, s_f, s_r],
        out_shape=[y, y, s, s],
        scratch_shapes=[pltpu.VMEM((2, 16, lanes), F32), kept, kept, kept, kept],
        compiler_params=pltpu.CompilerParams(vmem_limit_bytes=56 * 2**20, dimension_semantics=("arbitrary",)),
        cost_estimate=pl.CostEstimate(flops=length * lanes * 16 * 3200, transcendentals=0, bytes_accessed=length * lanes * 80),
        name="fwd_scan",
    )(steps, steps, u, u, rates_f, rates_r, b_t, b_t, cblk, cblk)


def bwd_kernel(step_f, step_r, u_f, u_r, gy_f, gy_r, rate_f, rate_r, ct_f, ct_r, bblk_f, bblk_r, s_f, s_r, sp_f, sp_r,
               dlog_f, dlog_r, adjb_f, adjb_r, bg_f, bg_r, cg_f, cg_r, rg_f, rg_r, carry,
               af0, af1, ar0, ar1, lf0, lf1, lr0, lr1):
    rows, lanes = step_f.shape
    t = pl.program_id(0)
    last = pl.num_programs(0) - 1

    @pl.when(t == 0)
    def _():
        carry[...] = jnp.zeros(carry.shape, F32)
        rg_f[...] = jnp.zeros(rg_f.shape, F32)
        rg_r[...] = jnp.zeros(rg_r.shape, F32)

    ones = (lax.broadcasted_iota(jnp.int32, (SUB, 256), 0) == lax.broadcasted_iota(jnp.int32, (SUB, 256), 1) // 16)
    onesb = ones.astype(BF)
    zero = jnp.zeros((SUB, 256), F32)

    def start_of(a, down):
        a = jnp.maximum(a, 0)
        return pl.multiple_of(rows - SUB - a * SUB if down else a * SUB, SUB)

    wide_by = min(WB, lanes)
    cuts = [slice(c, c + wide_by) for c in range(0, lanes, wide_by)]

    def walk(states, bases, keep_a, keep_l):
        cols = [columns_of(ct[...], base) for ct, base in zip((ct_f, ct_r), bases)]
        out = []
        for cut, pair in zip(cuts, states):
            pair = list(pair)
            rates = rate_f[:, cut], rate_r[:, cut]
            rg = [rg_f[:, cut], rg_r[:, cut]]
            low_rates = [r.astype(BF) for r in rates]
            some = [[], []]
            for k in range(SUB):
                for z, (step, gy, s, sp, j) in enumerate((
                        (step_f, gy_f, s_f, sp_f, SUB - 1 - k), (step_r, gy_r, s_r, sp_r, k))):
                    at = pl.ds(bases[z] + j, 1)
                    row = step[at, cut]
                    adj = gy[at, cut] * wide(cols[z][j], wide_by) + pair[z]
                    pair[z] = jnp.exp2(row * rates[z]) * adj
                    before = bases[z] + (j + 1 if z else j - 1)
                    if k < SUB - 1:
                        inner = s[pl.ds(pl.multiple_of(before * 16, 16), 16), cut]
                    else:
                        inside = before < rows if z else before >= 0
                        safe = jnp.clip(before, 0, rows - 1)
                        inner = s[pl.ds(pl.multiple_of(safe * 16, 16), 16), cut]
                        outer = jnp.where(t == last, jnp.zeros_like(inner), sp[:, cut])
                        inner = jnp.where(inside, inner, outer)
                    grad = pair[z].astype(BF) * inner
                    keep_a[z][j * 16:(j + 1) * 16, cut] = adj.astype(BF)
                    keep_l[z][j * 16:(j + 1) * 16, cut] = grad * low_rates[z]
                    some[z].append(grad * jnp.broadcast_to(row, (16, wide_by)).astype(BF))
                    if len(some[z]) == 4:
                        rg[z] = rg[z] + ((some[z][0] + some[z][1]) + (some[z][2] + some[z][3])).astype(F32)
                        some[z] = []
            rg_f[:, cut], rg_r[:, cut] = rg
            out.append(tuple(pair))
        return tuple(out)

    mix_by = 256 if lanes % 256 == 0 else 128

    def mix(base, a_ref, l_ref, u, gy, bblk, s, dlog, adjb, bg, cg):
        here = pl.ds(base, SUB)
        line = pl.ds(base // SUB, 1)
        group = pl.ds(pl.multiple_of(base * 16, 256), 256)
        bgd = cgd = zero
        for c in range(0, lanes, mix_by):
            cut = slice(c, c + mix_by)
            dlog[here, cut] = jnp.dot(onesb, l_ref[:, cut], preferred_element_type=F32)
            a = a_ref[:, cut]
            adjb[here, cut] = jnp.dot(bblk[here, :], a, preferred_element_type=F32)
            bgd = bgd + lax.dot_general(u[here, cut].astype(BF), a, NT, preferred_element_type=F32)
            cgd = cgd + lax.dot_general(gy[here, cut].astype(BF), s[group, cut], NT, preferred_element_type=F32)
        bg[line, :] = jnp.sum(jnp.where(ones, bgd, zero), axis=0, keepdims=True)
        cg[line, :] = jnp.sum(jnp.where(ones, cgd, zero), axis=0, keepdims=True)

    def mix_f(base, a_ref, l_ref):
        mix(base, a_ref, l_ref, u_f, gy_f, bblk_f, s_f, dlog_f, adjb_f, bg_f, cg_f)

    def mix_r(base, a_ref, l_ref):
        mix(base, a_ref, l_ref, u_r, gy_r, bblk_r, s_r, dlog_r, adjb_r, bg_r, cg_r)

    def two(i, states):
        bufs = ((af0, lf0, ar0, lr0), (af1, lf1, ar1, lr1))
        for half in range(2):
            a = 2 * i + half
            naf, nlf, nar, nlr = bufs[half]
            paf, plf, par, plr = bufs[1 - half]
            mix_f(start_of(a - 1, True), paf, plf)
            mix_r(start_of(a - 1, False), par, plr)
            states = walk(states, (start_of(a, True), start_of(a, False)), (naf, nar), (nlf, nlr))
        return states

    states = tuple((carry[0, :, cut], carry[1, :, cut]) for cut in cuts)
    states = lax.fori_loop(0, rows // SUB // 2, two, states)
    mix_f(0, af1, lf1)
    mix_r(rows - SUB, ar1, lr1)
    for cut, pair in zip(cuts, states):
        carry[0, :, cut], carry[1, :, cut] = pair


def bwd_scan(steps, u, gy, rates_f, rates_r, c_t, bblk, states_f, states_r, tile=128):
    length, lanes = steps.shape
    blocks = length // tile
    down = lambda t: blocks - 1 - t
    up = lambda t: t

    def specs(order, before):
        return (
            pl.BlockSpec((tile, lanes), lambda t: (order(t), 0)),
            pl.BlockSpec((16, lanes), lambda t: (0, 0)),
            pl.BlockSpec((16, tile), lambda t: (0, order(t))),
            pl.BlockSpec((tile, 256), lambda t: (order(t), 0)),
            pl.BlockSpec((tile * 16, lanes), lambda t: (order(t), 0)),
            pl.BlockSpec((16, lanes), lambda t: (before(t), 0)),
            pl.BlockSpec((tile // 16, 256), lambda t: (order(t), 0)),
        )

    row_f, rate, ct_f, blk_f, s_f, sp_f, diag_f = specs(down, lambda t: jnp.maximum((blocks - 1 - t) * tile - 1, 0))
    row_r, _, ct_r, blk_r, s_r, sp_r, diag_r = specs(up, lambda t: jnp.minimum((t + 1) * tile, length - 1))
    y = jax.ShapeDtypeStruct((length, lanes), F32)
    diag = jax.ShapeDtypeStruct((length // 16, 256), F32)
    rg = jax.ShapeDtypeStruct((16, lanes), F32)
    kept = pltpu.VMEM((256, lanes), BF)
    return pl.pallas_call(
        bwd_kernel,
        grid=(blocks,),
        in_specs=[row_f, row_r, row_f, row_r, row_f, row_r, rate, rate, ct_f, ct_r, blk_f, blk_r, s_f, s_r, sp_f, sp_r],
        out_specs=[row_f, row_r, row_f, row_r, diag_f, diag_r, diag_f, diag_r, rate, rate],
        out_shape=[y, y, y, y, diag, diag, diag, diag, rg, rg],
        scratch_shapes=[pltpu.VMEM((2, 16, lanes), F32)] + [kept] * 8,
        compiler_params=pltpu.CompilerParams(vmem_limit_bytes=56 * 2**20, dimension_semantics=("arbitrary",)),
        cost_estimate=pl.CostEstimate(flops=length * lanes * 16 * 6800, transcendentals=0, bytes_accessed=length * lanes * 100),
        name="bwd_scan",
    )(steps, steps, u, u, gy, gy, rates_f, rates_r, c_t, c_t, bblk, bblk, states_f, states_r, states_f, states_r)


def blockdiag(rows):
    length = rows.shape[0]
    eye = (jnp.arange(length)[:, None] % 16) == (jnp.arange(256)[None, :] // 16)
    return jnp.where(eye, jnp.tile(rows, (1, 16)), 0).astype(BF)


MESH = pl.DeviceIdType.MESH
VMEM = pl.BlockSpec(memory_space=pltpu.VMEM)
HBM = pl.BlockSpec(memory_space=pl.ANY)
DMA = pltpu.SemaphoreType.DMA


def send(src, dst, out_sem, in_sem, to):
    return pltpu.make_async_remote_copy(
        src_ref=src, dst_ref=dst, send_sem=out_sem, recv_sem=in_sem, device_id=to, device_id_type=MESH)


def greet(devices):
    bar = pltpu.get_barrier_semaphore()
    for to in devices:
        pl.semaphore_signal(bar, inc=1, device_id=to, device_id_type=MESH)
    pl.semaphore_wait(bar, len(devices))


def column_sum_kernel(ns, p_ref, o_ref, land, s1, r1, s2, r2):
    d, q = lax.axis_index("dp"), lax.axis_index("seq")
    others = [lax.rem(q + k, ns) for k in range(1, ns)]
    greet([(d, t) for t in others])
    for k, t in enumerate(others):
        send(p_ref.at[t], land.at[q], s1.at[k], r1.at[q], (d, t)).start()
    total = p_ref[q].astype(F32)
    for k, t in enumerate(others):
        send(p_ref.at[t], land.at[t], s1.at[k], r1.at[t], (d, t)).wait_recv()
        total = total + land[t].astype(F32)
    o_ref[q] = total.astype(o_ref.dtype)
    for k, t in enumerate(others):
        send(o_ref.at[q], o_ref.at[q], s2.at[k], r2.at[q], (d, t)).start()
    for k, t in enumerate(others):
        send(o_ref.at[t], o_ref.at[t], s2.at[k], r2.at[t], (d, t)).wait_recv()
    for k, t in enumerate(others):
        send(p_ref.at[t], land.at[q], s1.at[k], r1.at[q], (d, t)).wait_send()
        send(o_ref.at[q], o_ref.at[q], s2.at[k], r2.at[q], (d, t)).wait_send()


def column_sum(partial, ns, out_dtype, cid):
    rows, lanes = partial.shape
    block = (ns, rows // ns, lanes)
    out = pl.pallas_call(
        functools.partial(column_sum_kernel, ns),
        out_shape=jax.ShapeDtypeStruct(block, out_dtype),
        in_specs=[VMEM], out_specs=VMEM,
        scratch_shapes=[pltpu.VMEM(block, partial.dtype), DMA((ns,)), DMA((ns,)), DMA((ns,)), DMA((ns,))],
        compiler_params=pltpu.CompilerParams(
            collective_id=cid, has_side_effects=True, vmem_limit_bytes=32 * 2**20),
        name="column_sum",
    )(partial.reshape(block))
    return out.reshape(rows, lanes)


def column_grads_kernel(ns, pre_ref, step_ref, bf_ref, br_ref, cf_ref, cr_ref, o_ref, state_ref, rows_ref, p_ref, *rest):
    rank = step_ref.shape[0]
    local = p_ref.shape[1]
    groups = local // 16
    rows_ref[...] = jnp.zeros(rows_ref.shape, BF)
    rows_ref[0:rank, :] = step_ref[...]
    for t in range(ns):
        lines = slice(t * groups, (t + 1) * groups)
        b, c = bf_ref[lines, :] + br_ref[lines, :], cf_ref[lines, :] + cr_ref[lines, :]
        for l in range(16):
            here = slice(l * 16, (l + 1) * 16)
            state_ref[pl.ds(l, groups, stride=16), :] = jnp.concatenate(
                [jnp.zeros((groups, rank), F32), b[:, here], c[:, here]], axis=1)
        low = lax.dot_general(pre_ref[t * local:(t + 1) * local, :], rows_ref[...], NT, preferred_element_type=F32)
        p_ref[t] = (low + state_ref[...]).astype(BF)
    column_sum_kernel(ns, p_ref, o_ref, *rest)


def column_grads(pre, step, b_f, b_r, c_f, c_r, ns, cid):
    rows, lanes = pre.shape[0], step.shape[0] + 32
    block = (ns, rows // ns, lanes)
    out = pl.pallas_call(
        functools.partial(column_grads_kernel, ns),
        out_shape=jax.ShapeDtypeStruct(block, BF),
        in_specs=[VMEM] * 6, out_specs=VMEM,
        scratch_shapes=[
            pltpu.VMEM((rows // ns, lanes), F32), pltpu.VMEM((lanes, pre.shape[1]), BF), pltpu.VMEM(block, BF),
            pltpu.VMEM(block, BF), DMA((ns,)), DMA((ns,)), DMA((ns,)), DMA((ns,))],
        compiler_params=pltpu.CompilerParams(
            collective_id=cid, has_side_effects=True, vmem_limit_bytes=32 * 2**20),
        name="column_grads",
    )(pre, step, b_f, b_r, c_f, c_r)
    return out.reshape(rows, lanes)


def start_kernel(nd, ns, nsub, fused, hid, win, wout, mask, emb, modw, modb, select, step, dec_f, dec_r, taps, fbias, sbias,
                 md_o, nm_o, inner_o, gate_o, wx_o, select_o, step_o, rate_o, fil_o, mask_o, mod_o,
                 hv, wv, mv, nv, iv, gv, pack, modw_v, pack_v, eland, prod, rowp, land1, land2,
                 su, ru, sd, rd, swz, rwx, swp, swm, spz, rp, spp, spm, sk, rk, se, re, s1, r1, s2, r2, own, out):
    d, q = lax.axis_index("dp"), lax.axis_index("seq")
    nc = nd // 2
    chip, core = d // 2, lax.rem(d, 2)
    mate = (chip * 2 + 1 - core, q)
    chips = [lax.rem(chip + k, nc) for k in range(1, nc)]
    others = [lax.rem(q + k, ns) for k in range(1, ns)]
    peers = [lax.rem(d + k, nd) for k in range(1, nd)]
    spread = nd // ns
    me = d * ns + q
    part = wout.shape[1] // ns
    rw = wout.shape[0]
    units = part // nd
    rank, states = step.shape[0], dec_f.shape[0]
    above = units + -units % 16
    taps_at = above + rank + 2 * states

    pack[...] = jnp.zeros(pack.shape, BF)
    pack[0:units, :] = select[...]
    pack[above:above + rank, 0:units] = step[...]
    pack[above + rank:above + rank + states, 0:units] = dec_f[...]
    pack[above + rank + states:taps_at, 0:units] = dec_r[...]
    pack[taps_at:taps_at + 16, 0:units] = jnp.concatenate(
        [taps[...].astype(F32), fbias[...].astype(F32), sbias[...].astype(F32),
         jnp.zeros((14 - taps.shape[0], units), F32)]).astype(BF)
    modw_v[...] = jnp.zeros(modw_v.shape, BF)
    modw_v[0:modw.shape[0], :] = modw[...]
    greet([(d, t) for t in others] + [(e, q) for e in peers])

    def column(ref, at):
        return ref.at[:, pl.ds(pl.multiple_of(at * part, 128), part)]

    def wrows(idx):
        return wv.at[pl.ds(pl.multiple_of(idx * rw, 16), rw), :]

    def pieces(t):
        return (column(win, t), column(win, ns + t), column(wout, t))

    def across(k, t, idx):
        return [
            send(src, wrows(idx).at[:, j * part:(j + 1) * part], swz.at[k, j], rwx.at[idx, j], (d, t))
            for j, src in enumerate(pieces(t))
        ]

    keep = [pltpu.make_async_copy(src, wrows(me).at[:, j * part:(j + 1) * part], own.at[j])
            for j, src in enumerate(pieces(q))]
    keep.append(pltpu.make_async_copy(hid, hv.at[q], own.at[3]))
    for copy in keep:
        copy.start()

    plane = d // spread
    slot = lax.rem(d, spread) * ns + q
    pack_z = send(pack, pack_v.at[slot], spz, rp.at[slot], (d, plane))
    pack_vwn = pltpu.make_async_copy(pack, pack_v.at[slot], own.at[4])

    @pl.when(plane == q)
    def _():
        pack_vwn.start()

    @pl.when(plane != q)
    def _():
        pack_z.start()

    def masks(k, t, src):
        return send(mask_o.at[src], mask_o.at[src], sk.at[k], rk.at[src], (d, t))

    def embeds(k, e, src):
        return send(eland.at[src], eland.at[src], se.at[k], re.at[src], (e, q))

    mask_o[q] = jnp.zeros(mask_o.shape[1:], BF)
    mask_o[q, 0:mask.shape[0], :] = mask[...].astype(F32).astype(BF)
    eland[d] = jnp.zeros(eland.shape[1:], BF)
    eland[d, 0:1, :] = emb[...]
    for k, e in enumerate(peers):
        embeds(k, e, d).start()
    for k, t in enumerate(others):
        masks(k, t, q).start()

    for k, t in enumerate(others):
        for copy in across(k, t, me)[:2]:
            copy.start()

    def rise(k, s):
        t = jnp.maximum(q - k, 0)
        src = hid.at[s] if k == 0 else hv.at[t, s]
        return send(src, hv.at[t, s], su.at[k, s], ru.at[k, s], (d, jnp.minimum(q + 1, ns - 1)))

    def sink(k, s):
        t = jnp.minimum(q + k, ns - 1)
        src = hid.at[s] if k == 0 else hv.at[t, s]
        return send(src, hv.at[t, s], sd.at[k, s], rd.at[k, s], (d, jnp.maximum(q - 1, 0)))

    def hop(k, s):
        @pl.when(q >= k)
        def _():
            if k:
                rise(k - 1, s).wait_recv()
            if k < ns - 1:
                @pl.when(q + 1 < ns)
                def _():
                    rise(k, s).start()

        @pl.when(q + k < ns)
        def _():
            if k:
                sink(k - 1, s).wait_recv()
            if k < ns - 1:
                @pl.when(q >= 1)
                def _():
                    sink(k, s).start()

    for s in range(nsub):
        hop(0, s)
    for k, t in enumerate(others):
        across(k, t, me)[2].start()

    def cols_of(idx, kind):
        return wrows(idx).at[:, 2 * part * kind:2 * part + part * kind]

    def plane_w(c, idx, t, kind):
        return send(cols_of(idx, kind), cols_of(idx, kind), swp.at[kind, c, t], rwx.at[idx, 3 + kind], (c * 2 + core, q))

    def mate_w(c, idx, t, kind):
        return send(cols_of(idx, kind), cols_of(idx, kind), swm.at[kind, c, t], rwx.at[idx, 3 + kind], mate)

    def spread_w(t, kind):
        idx = d * ns + t
        for c in chips:
            plane_w(c, idx, t, kind).start()
        mate_w(chip, idx, t, kind).start()

    for copy in keep[:3]:
        copy.wait()
    spread_w(q, 0)

    for k, e in enumerate(peers):
        embeds(k, e, e).wait_recv()
    rows = modw_v.shape[0]
    here = lax.broadcasted_iota(jnp.int32, (FREQ, rows), 0)
    pick = here - lax.broadcasted_iota(jnp.int32, (FREQ, rows), 1)
    count = FREQ // (nd * ns)
    keep_col = lax.broadcasted_iota(jnp.int32, (FREQ, rows), 1) < count
    pick = jnp.where(jnp.logical_and(pick == me * count, keep_col), 1.0, 0.0).astype(BF)
    mine = jnp.dot(eland[...].reshape(nd * 16, FREQ), pick, preferred_element_type=F32).astype(BF)
    prod[...] = jnp.dot(mine, modw_v[...], preferred_element_type=F32)

    lines = prod.shape[1] // 128
    @pl.loop(0, nd)
    def _(e):
        rowp[e] = modb[...]
        for j in range(lines):
            rowp[e, j:j + 1, :] += prod[pl.ds(pl.multiple_of(e * 16, 16), 1), j * 128:(j + 1) * 128]

    def to_item(k, e, src):
        return send(rowp.at[e], land1.at[src], s1.at[k], r1.at[src], (e, q))

    for k, e in enumerate(peers):
        to_item(k, e, d).start()

    for k, t in enumerate(others):
        for copy in across(k, t, d * ns + t)[:2]:
            copy.wait_recv()
        spread_w(t, 0)

    def plane_p(c, i, t):
        return send(pack_v.at[i], pack_v.at[i], spp.at[c, t], rp.at[i], (c * 2 + core, q))

    def mate_p(c, i, t):
        return send(pack_v.at[i], pack_v.at[i], spm.at[c, t], rp.at[i], mate)

    base = lax.rem(d, spread) * ns

    @pl.when(plane == q)
    def _():
        pack_vwn.wait()
        for t in others:
            send(pack, pack_v.at[base + t], spz, rp.at[base + t], (d, plane)).wait_recv()
        for t in range(ns):
            for c in chips:
                plane_p(c, base + t, t).start()
            mate_p(chip, base + t, t).start()

    total = rowp[d]
    for k, e in enumerate(peers):
        to_item(k, e, e).wait_recv()
        total = total + land1[e]
    land2[q] = total

    def to_column(k, t, src):
        return send(land2.at[src], land2.at[src], s2.at[k], r2.at[src], (d, t))

    for k, t in enumerate(others):
        to_column(k, t, q).start()

    def relay_w(c, t, kind):
        idx = (c * 2 + core) * ns + t
        plane_w(c, idx, t, kind).wait_recv()
        mate_w(c, idx, t, kind).start()

    def holds(c):
        return (c * 2 + core) // spread == q

    def relay_p(c):
        first = lax.rem(c * 2 + core, spread) * ns
        @pl.when(holds(c))
        def _():
            for t in range(ns):
                plane_p(c, first + t, t).wait_recv()
                mate_p(c, first + t, t).start()

    def own_copies(t):
        return [pltpu.make_async_copy(src.at[t], dst.at[t], out.at[t, i]) for i, (src, dst) in enumerate(
            ((mv, md_o), (iv, inner_o), (gv, gate_o), (nv, nm_o)) if fused else ((hv, md_o),))]

    local = hv.shape[1] * hv.shape[2]
    width = hv.shape[3]

    def project(t):
        if fused:
            shift, scale = mod_o[0:1, 0:width], 1.0 + mod_o[0:1, width:2 * width]
            for s in range(nsub):
                @pl.loop(0, local // nsub // 16)
                def _(r):
                    x = hv[t, s, pl.ds(pl.multiple_of(r * 16, 16), 16), :].astype(F32)
                    x = x - jnp.mean(x, axis=1, keepdims=True)
                    x = x * lax.rsqrt(jnp.mean(x * x, axis=1, keepdims=True) + EPS)
                    to = pl.multiple_of(s * (local // nsub) + r * 16, 16)
                    nv[t, pl.ds(to, 16), :] = x.astype(BF)
                    mv[t, pl.ds(to, 16), :] = (x * scale + shift).astype(BF)
            tile = part if part % 256 else part // 2

            @pl.loop(0, part // tile)
            def _(j):
                for target, base in ((iv, 0), (gv, part)):
                    n = pl.ds(pl.multiple_of(base + j * tile, 128), tile)
                    full = jnp.dot(mv[t], wv[:, n], preferred_element_type=F32)
                    target[t, :, pl.ds(pl.multiple_of(j * tile, 128), tile)] = full.astype(target.dtype)
        for copy in own_copies(t):
            copy.start()

    relays = [(c, t) for t in [q] + others for c in chips]
    at = 0
    for s in range(nsub):
        hop(1, s)
        upto = len(relays) * (s + 1) // (2 * nsub)
        for c, t in relays[at:upto]:
            relay_w(c, t, 0)
        at = upto
    spread_w(q, 1)
    for k, t in enumerate(others):
        across(k, t, d * ns + t)[2].wait_recv()
        spread_w(t, 1)
    for c, t in relays[at:]:
        relay_w(c, t, 0)
    for c in chips:
        relay_p(c)

    for k, t in enumerate(others):
        to_column(k, t, t).wait_recv()
    total = land2[0]
    for t in range(1, ns):
        total = total + land2[t]
    mod_o[...] = jnp.zeros(mod_o.shape, F32)
    for i in range(mod_o.shape[1] // 128):
        mod_o[0:1, i * 128:(i + 1) * 128] = total[i:i + 1, :]

    twin = 1 - core
    for c in range(nc):
        for t in range(ns):
            idx = (c * 2 + twin) * ns + t
            mate_w(c, idx, t, 0).wait_recv()
    keep[3].wait()

    def project_at(t):
        @pl.when(jnp.logical_and(t >= 0, t < ns))
        def _():
            project(jnp.clip(t, 0, ns - 1))

    for k in range(2, ns):
        for s in range(nsub):
            hop(k, s)
            if k == 2 and s == 0:
                project(q)
            if s == nsub - 3:
                project_at(q - k + 1)
            if s == nsub - 2:
                project_at(q + k - 1)

    for c, t in relays:
        relay_w(c, t, 1)
    for c in range(nc):
        for t in range(ns):
            idx = (c * 2 + twin) * ns + t
            mate_w(c, idx, t, 1).wait_recv()
    wx_copy = pltpu.make_async_copy(wv, wx_o, own.at[5])
    wx_copy.start()

    for c in range(nc):
        first = lax.rem(c * 2 + twin, spread) * ns
        @pl.when((c * 2 + twin) // spread == q)
        def _():
            for t in range(ns):
                mate_p(c, first + t, t).wait_recv()
    for j in range(nd):
        here = slice(j * units, (j + 1) * units)
        select_o[here, :] = pack_v[j, 0:units, :]
        step_o[:, here] = pack_v[j, above:above + rank, 0:units]
        rate_o[0:2 * states, here] = -jnp.exp(pack_v[j, above + rank:taps_at, 0:units].astype(F32))
        fil_o[:, here] = pack_v[j, taps_at:taps_at + 16, 0:units].astype(F32)
    rate_o[2 * states:4 * states, :] = rate_o[0:2 * states, :] * LOG2E

    project_at(q - ns + 1)
    project_at(q + ns - 1)

    for k, t in enumerate(others):
        masks(k, t, t).wait_recv()
    wx_copy.wait()
    for t in range(ns):
        for copy in own_copies(t):
            copy.wait()

    for k, t in enumerate(others):
        for copy in across(k, t, me):
            copy.wait_send()
        masks(k, t, q).wait_send()
        to_column(k, t, q).wait_send()
    for k, e in enumerate(peers):
        embeds(k, e, d).wait_send()
        to_item(k, e, d).wait_send()

    @pl.when(plane != q)
    def _():
        pack_z.wait_send()

    @pl.when(plane == q)
    def _():
        for t in range(ns):
            for c in chips:
                plane_p(c, base + t, t).wait_send()
            mate_p(chip, base + t, t).wait_send()

    for kind in range(2):
        for t in range(ns):
            for c in chips:
                plane_w(c, d * ns + t, t, kind).wait_send()
                mate_w(c, (c * 2 + core) * ns + t, t, kind).wait_send()
            mate_w(chip, d * ns + t, t, kind).wait_send()
    for c in chips:
        first = lax.rem(c * 2 + core, spread) * ns
        @pl.when(holds(c))
        def _():
            for t in range(ns):
                mate_p(c, first + t, t).wait_send()
    for k in range(ns - 1):
        for s in range(nsub):
            @pl.when(jnp.logical_and(q >= k, q + 1 < ns))
            def _():
                rise(k, s).wait_send()
            @pl.when(jnp.logical_and(q + k < ns, q >= 1))
            def _():
                sink(k, s).wait_send()


def start(hidden, mask, win, wout, embedded, modw, modb, small, fused, nd, ns, cid):
    nsub = 4
    length, width = hidden.shape
    rows, inner = wout.shape
    part = inner // ns
    nc = nd // 2
    hidden = hidden.reshape(nsub, length // nsub, width)
    lines = modb.shape
    rank, units, states = small[1].shape[0], part // nd, small[2].shape[0]
    pack = (units + -units % 16 + rank + 2 * states + 16, 128)
    held = modw.shape[0] + -modw.shape[0] % 16
    runs = (ns,) + (hidden.shape if not fused else (length, width))
    return pl.pallas_call(
        functools.partial(start_kernel, nd, ns, nsub, fused),
        out_shape=[
            jax.ShapeDtypeStruct(runs, BF),
            jax.ShapeDtypeStruct((ns, length, width), BF),
            jax.ShapeDtypeStruct((ns, length, part), BF),
            jax.ShapeDtypeStruct((ns, length, part), F32),
            jax.ShapeDtypeStruct((nd * ns * rows, 3 * part), BF),
            jax.ShapeDtypeStruct((part, 128), BF),
            jax.ShapeDtypeStruct((rank, part), BF),
            jax.ShapeDtypeStruct((4 * states, part), F32),
            jax.ShapeDtypeStruct((16, part), F32),
            jax.ShapeDtypeStruct((ns, 16, 128), BF),
            jax.ShapeDtypeStruct((8, modw.shape[1]), F32),
        ],
        in_specs=[HBM, HBM, HBM] + [VMEM] * 11,
        out_specs=[HBM] * 5 + [VMEM] * 6,
        scratch_shapes=[
            pltpu.VMEM((ns,) + hidden.shape, BF), pltpu.VMEM((nd * ns * rows, 3 * part), BF),
            pltpu.VMEM((ns, length, width), BF), pltpu.VMEM((ns, length, width), BF), pltpu.VMEM((ns, length, part), BF), pltpu.VMEM((ns, length, part), F32),
            pltpu.VMEM(pack, BF), pltpu.VMEM((held, modw.shape[1]), BF), pltpu.VMEM((nd,) + pack, BF),
            pltpu.VMEM((nd, 16, FREQ), BF), pltpu.VMEM((nd * 16, modw.shape[1]), F32),
            pltpu.VMEM((nd,) + lines, F32), pltpu.VMEM((nd,) + lines, F32), pltpu.VMEM((ns,) + lines, F32),
            DMA((ns - 1, nsub)), DMA((ns - 1, nsub)), DMA((ns - 1, nsub)), DMA((ns - 1, nsub)),
            DMA((ns, 3)), DMA((nd * ns, 5)), DMA((2, nc, ns)), DMA((2, nc, ns)),
            DMA(()), DMA((nd,)), DMA((nc, ns)), DMA((nc, ns)),
            DMA((ns,)), DMA((ns,)), DMA((nd,)), DMA((nd,)),
            DMA((nd,)), DMA((nd,)), DMA((ns,)), DMA((ns,)), DMA((6,)), DMA((ns, 4)),
        ],
        compiler_params=pltpu.CompilerParams(
            collective_id=cid, has_side_effects=True, vmem_limit_bytes=56 * 2**20),
        name="start",
    )(hidden, win, wout, mask, embedded, modw, modb, *small)


def end_kernel(nd, ns, nsub, rows, turned, nfil,
               gi_h, gg_h, md_h, nm_h, wx_h, gsel, gstep, gdf, gdr, rates, hid_ref, cot_ref, mod_ref, gate_ref, emb_ref, early, *rest):
    gfil = rest[:nfil]
    (gin_o, gout_o, sel_o, step_o, df_o, dr_o, taps_o, fb_o, sb_o, gh_o, mod_o,
               gp, md, nm, wx, sm_ref, so_ref, gm, made, pair, plane, spair, splane, ssum, fro, ready, up, down, own, acc, msg, mland,
               ld, sa, ra, sb, rb, sc, rc, se, re, ta, ra2, tb, rb2, tc, rc2, su, ru, sd, rd, s1, r1, s2, r2) = rest[nfil:]
    d, q = lax.axis_index("dp"), lax.axis_index("seq")
    nc = nd // 2
    chip, core = d // 2, lax.rem(d, 2)
    mate = chip * 2 + 1 - core
    pairs = [(1, 1), (1, 0), (0, 1)] + [(a, b) for b in range(2, nc // 2) for a in (0, 1)]
    chips = [lax.rem(chip + a, 2) + 2 * lax.rem(chip // 2 + b, nc // 2) for a, b in pairs]
    others = [lax.rem(q + k, ns) for k in range(1, ns)]
    peers = [lax.rem(d + k, nd) for k in range(1, nd)]
    spread = nd // ns
    final_to = (spread * q + d // ns, lax.rem(d, ns))
    me = d * ns + q
    final_from = (lax.rem(me, nd), me // nd)
    stays = jnp.logical_and(final_to[0] == d, final_to[1] == q)
    length, cols = gp.shape
    part = cols // 2
    width = wx.shape[0]
    local = length // ns
    sub = local // nsub
    rw = pair.shape[2]
    half = ns * rw

    loads = [pltpu.make_async_copy(src, dst, ld.at[i]) for i, (src, dst) in enumerate(
        ((gi_h, gp.at[:, 0:part]), (gg_h, gp.at[:, part:cols]), (wx_h.at[:, 0:cols], wx), (nm_h, nm), (md_h, md)))]
    for copy in loads:
        copy.start()

    units = part // nd
    rank, states, taps = gstep.shape[0], gdf.shape[0], taps_o.shape[0]
    above = units + -units % 16
    taps_at = above + rank + 2 * states
    bar = pltpu.get_barrier_semaphore()
    friends = [(e, q) for e in peers] + [(d, t) for t in others]
    for to in friends:
        pl.semaphore_signal(bar, inc=1, device_id=to, device_id_type=MESH)
    @pl.when(jnp.logical_not(stays))
    def _():
        pl.semaphore_signal(bar, inc=1, device_id=final_from, device_id_type=MESH)

    def tokens(t):
        @pl.loop(0, width // 512)
        def _(j):
            here = pl.ds(pl.multiple_of(j * 512, 512), 512)
            lines = slice(t * local, (t + 1) * local)
            full = lax.dot_general(gp[lines, :], wx[here, :], NT, preferred_element_type=F32)
            acc[0:1, here] += jnp.sum(full, axis=0, keepdims=True)
            acc[1:2, here] += jnp.sum(full * nm[lines, here].astype(F32), axis=0, keepdims=True)
            full = full.astype(BF)
            for s in range(nsub):
                gm[t, s, :, here] = full[s * sub:(s + 1) * sub]

    def rise(t, s, src):
        return send(src, up.at[t, s], su.at[t, s], ru.at[t, s], (d, jnp.minimum(q + 1, ns - 1)))

    def sink(t, s, src):
        return send(src, down.at[t, s], sd.at[t, s], rd.at[t, s], (d, jnp.maximum(q - 1, 0)))

    def added(land, t, s):
        land[t, s] = (land[t, s].astype(F32) + gm[t, s].astype(F32)).astype(BF)

    def open_up(t, s):
        @pl.when(jnp.logical_and(q == 0, t > 0))
        def _():
            rise(t, s, gm.at[t, s]).start()

    def open_down(t, s):
        @pl.when(jnp.logical_and(q == ns - 1, t < ns - 1))
        def _():
            sink(t, s, gm.at[t, s]).start()

    def step(k, s):
        t = ns - 1 - k

        @pl.when(jnp.logical_and(q < t, q > 0))
        def _():
            rise(t, s, up.at[t, s]).wait_recv()
            added(up, t, s)
            rise(t, s, up.at[t, s]).start()

        @pl.when(jnp.logical_and(q > k, q < ns - 1))
        def _():
            sink(k, s, down.at[k, s]).wait_recv()
            added(down, k, s)
            sink(k, s, down.at[k, s]).start()

    def far(k):
        for t in sorted({ns - 1 - k, k}, reverse=True):
            tokens(t)
            for s in range(nsub):
                open_up(t, s)
                open_down(t, s)

    @pl.when(stays)
    def _():
        pl.semaphore_wait(bar, len(friends))

    @pl.when(jnp.logical_not(stays))
    def _():
        pl.semaphore_wait(bar, len(friends) + 1)

    def whole(t, src):
        return send(early.at[t], ready.at[src], se.at[t], re.at[src], (d, t))

    for t in others:
        whole(t, q).start()
    for copy in loads[:4]:
        copy.wait()
    acc[...] = jnp.zeros(acc.shape, F32)
    acc[2:3, :] = jnp.sum(gate_ref[...], axis=0, keepdims=True)
    acc[3:4, 0:FREQ] = emb_ref[...].astype(F32) * (1.0 / ns)
    far(0)
    steps = [(k, s) for k in range(ns - 1) for s in range(nsub)]

    def first(c):
        return send(made.at[c, 1 - core], pair.at[c], sa.at[c], ra.at[c], (mate, q))

    def first_small(c):
        return send(sm_ref.at[c * 2 + 1 - core], spair.at[c], ta.at[c], ra2.at[c], (mate, q))

    def second(c, src):
        return send(pair.at[c], plane.at[src], sb.at[c], rb.at[src], (c * 2 + core, q))

    def second_small(c, src):
        return send(spair.at[c], splane.at[src], tb.at[c], rb2.at[src], (c * 2 + core, q))

    def block(c):
        at = pl.ds(pl.multiple_of(c * 2 * half, 2 * half), 2 * half)
        tile = part if part % 256 else part // 2
        left = md[at, :] if turned else md[:, at].T

        @pl.loop(0, part // tile)
        def _(j):
            n = pl.ds(pl.multiple_of(j * tile, 128), tile)
            full = jnp.dot(left, gp[:, n], preferred_element_type=F32).astype(BF)
            for h in range(2):
                for t in range(ns):
                    line = (h * ns + t) * rw
                    made[c, h, t, :, n] = full[line:line + rw]

    sm_ref[...] = jnp.zeros(sm_ref.shape, F32)
    for j in range(nd):
        here = slice(j * units, (j + 1) * units)
        sm_ref[j, 0:units, :] = gsel[here, :]
        sm_ref[j, above:above + rank, 0:units] = gstep[:, here]
        sm_ref[j, above + rank:above + rank + states, 0:units] = gdf[:, here] * rates[0:states, here]
        sm_ref[j, above + rank + states:taps_at, 0:units] = gdr[:, here] * rates[states:2 * states, here]
        for i, line in enumerate(gfil):
            sm_ref[j, taps_at + i:taps_at + i + 1, 0:units] = jnp.sum(line[:, here], axis=0, keepdims=True)

    loads[4].wait()
    order = chips + [chip]

    def give(c):
        block(c)
        first(c).start()
        first_small(c).start()

    give(order[0])
    for k in range(1, ns // 2):
        far(k)
    msg[...] = jnp.zeros(msg.shape, F32)
    long = msg.shape[1] // 128
    for i in range(3 * width // 128 + FREQ // 128):
        r, c = divmod(i * 128, width)
        to = (i % long) * 128
        msg[i // long:i // long + 1, to:to + 128] = acc[r:r + 1, c:c + 128]
    for k, t in enumerate(others):
        send(msg, mland.at[q], s1.at[k], r1.at[q], (d, t)).start()

    for i, c in enumerate(order):
        if i + 1 < nc:
            give(order[i + 1])
        first(c).wait_recv()
        @pl.loop(0, ns)
        def _(t):
            pair[c, t] = (pair[c, t].astype(F32) + made[c, core, t].astype(F32)).astype(BF)
        first_small(c).wait_recv()
        spair[c] = spair[c] + sm_ref[c * 2 + core]
        if i < nc - 1:
            second(c, chip).start()
            second_small(c, chip).start()
        for k, s in steps[i:i + 1]:
            step(k, s)
    late = len(steps) * 3 // 4
    for k, s in steps[nc:late]:
        step(k, s)

    for c in chips:
        second(c, c).wait_recv()
        second_small(c, c).wait_recv()
    @pl.loop(0, ns)
    def _(t):
        total = pair[chip, t].astype(F32)
        for c in chips:
            total = total + plane[c, t].astype(F32)
        pair[chip, t] = total.astype(BF)
    small = spair[chip]
    for c in chips:
        small = small + splane[c]
    ssum[...] = small

    def third(t, src):
        return send(pair.at[chip, t], fro.at[src], sc.at[t], rc.at[src], (d, t))

    last = send(ssum, so_ref, tc, rc2, final_to)
    @pl.when(stays)
    def _():
        so_ref[...] = ssum[...]
    @pl.when(jnp.logical_not(stays))
    def _():
        last.start()
    for t in others:
        third(t, q).start()
    fro[q] = pair[chip, q]
    for k, s in steps[max(nc, late):]:
        step(k, s)

    total = msg[...]
    for k, t in enumerate(others):
        send(msg, mland.at[t], s1.at[k], r1.at[t], (d, t)).wait_recv()
        total = total + mland[t]
    mod_o[d] = total
    for k, e in enumerate(peers):
        send(mod_o.at[d], mod_o.at[d], s2.at[k], r2.at[d], (e, q)).start()
    scale = 1.0 + mod_ref[0:1, width:2 * width]
    for s in range(nsub):
        own[...] = gm[q, s].astype(F32)

        @pl.when(q > 0)
        def _():
            rise(q, s, gm.at[q, s]).wait_recv()
            own[...] += up[q, s].astype(F32)

        @pl.when(q < ns - 1)
        def _():
            sink(q, s, gm.at[q, s]).wait_recv()
            own[...] += down[q, s].astype(F32)

        @pl.loop(0, sub // 16)
        def _(r):
            here = pl.ds(pl.multiple_of(r * 16, 16), 16)
            grad = own[here, :]
            x = hid_ref[s, here, :].astype(F32)
            x = x - jnp.mean(x, axis=1, keepdims=True)
            inverse = lax.rsqrt(jnp.mean(x * x, axis=1, keepdims=True) + EPS)
            normed = x * inverse
            grad = grad * scale
            grad = grad - jnp.mean(grad, axis=1, keepdims=True) - normed * jnp.mean(
                grad * normed, axis=1, keepdims=True)
            gh_o[s, here, :] = (cot_ref[s, here, :].astype(F32) + inverse * grad).astype(BF)

    inner = part * ns

    def place(src, rest):
        at = src * part
        gin_o[:, pl.ds(pl.multiple_of(at, 128), part)] = fro[src, 0:rows, :].astype(F32)
        gin_o[:, pl.ds(pl.multiple_of(inner + at, 128), part)] = rest[0:rows, 0:part].astype(F32)
        gout_o[:, pl.ds(pl.multiple_of(at, 128), part)] = rest[0:rows, part:2 * part].astype(F32)

    place(q, early[q])
    for t in others:
        third(t, t).wait_recv()
        whole(t, t).wait_recv()
        place(t, ready[t])
    for k, e in enumerate(peers):
        send(mod_o.at[e], mod_o.at[e], s2.at[k], r2.at[e], (e, q)).wait_recv()
    @pl.when(jnp.logical_not(stays))
    def _():
        last.wait_recv()
        last.wait_send()

    sel_o[...] = so_ref[0:units, :]
    step_o[...] = so_ref[above:above + rank, 0:units]
    df_o[...] = so_ref[above + rank:above + rank + states, 0:units]
    dr_o[...] = so_ref[above + rank + states:taps_at, 0:units]
    taps_o[...] = so_ref[taps_at:taps_at + taps, 0:units]
    fb_o[...] = so_ref[taps_at + taps:taps_at + taps + 1, 0:units]
    sb_o[...] = so_ref[taps_at + taps + 1:taps_at + taps + 2, 0:units]
    for c in order:
        first(c).wait_send()
        first_small(c).wait_send()
    for c in chips:
        second(c, chip).wait_send()
        second_small(c, chip).wait_send()
    for k, t in enumerate(others):
        third(t, q).wait_send()
        whole(t, q).wait_send()
        send(msg, mland.at[q], s1.at[k], r1.at[q], (d, t)).wait_send()
    for k, e in enumerate(peers):
        send(mod_o.at[d], mod_o.at[d], s2.at[k], r2.at[d], (e, q)).wait_send()
    for k, s in steps:
        t = ns - 1 - k
        @pl.when(q < t)
        def _():
            rise(t, s, gm.at[t, s]).wait_send()
        @pl.when(q > k)
        def _():
            sink(k, s, gm.at[k, s]).wait_send()


def end(grad_inner, grad_gate, modded, normed, wx, early, small, fil, hidden, cot, modulation, grad_gate_scale, embedded, rows, nd, ns, cid):
    length, part = grad_inner.shape
    cols = 2 * part
    width = wx.shape[0]
    inner = part * ns
    nc, nsub = nd // 2, 4
    local = length // ns
    sub = local // nsub
    rw = rows + -rows % 16
    half = ns * rw
    turned = 2 * half % 128 != 0 or rw != rows
    if turned:
        def turn(a):
            a = a.T.reshape(nd * ns, rows, length)
            return jnp.pad(a, ((0, 0), (0, rw - rows), (0, 0))).reshape(nd * ns * rw, length)
        modded = turn(modded)
    early = jnp.pad(early.reshape(ns, rows, cols), ((0, 0), (0, rw - rows), (0, 0)))
    short = -(-(3 * width + FREQ) // 1024) * 128
    units, rank, states = part // nd, small[1].shape[0], small[2].shape[0]
    v = (units + -units % 16 + rank + 2 * states + 16, 128)
    hidden, cot = hidden.reshape(nsub, sub, width), cot.reshape(nsub, sub, width)
    blocks = pltpu.VMEM((nc, ns, rw, part), BF)
    smalls = pltpu.VMEM((nc,) + v, F32)
    runs = pltpu.VMEM((ns, nsub, sub, width), BF)
    gin, gout, *own, gh, mod = pl.pallas_call(
        functools.partial(end_kernel, nd, ns, nsub, rows, turned, len(fil)),
        out_shape=[
            jax.ShapeDtypeStruct((rows, 2 * inner), F32),
            jax.ShapeDtypeStruct((rows, inner), F32),
            jax.ShapeDtypeStruct((units, 128), F32),
            jax.ShapeDtypeStruct((rank, units), F32),
            jax.ShapeDtypeStruct((states, units), F32),
            jax.ShapeDtypeStruct((states, units), F32),
            jax.ShapeDtypeStruct((len(fil) - 2, units), F32),
            jax.ShapeDtypeStruct((1, units), F32),
            jax.ShapeDtypeStruct((1, units), F32),
            jax.ShapeDtypeStruct((nsub, sub, width), BF),
            jax.ShapeDtypeStruct((nd, 8, short), F32),
        ],
        in_specs=[HBM] * 5 + [VMEM] * (11 + len(fil)), out_specs=[VMEM] * 11,
        scratch_shapes=[
            pltpu.VMEM((length, cols), BF), pltpu.VMEM(modded.shape, BF), pltpu.VMEM(normed.shape, BF),
            pltpu.VMEM((width, cols), BF),
            pltpu.VMEM((nd,) + v, F32), pltpu.VMEM(v, F32), runs,
            pltpu.VMEM((nc, 2, ns, rw, part), BF), blocks, blocks,
            smalls, smalls, pltpu.VMEM(v, F32), pltpu.VMEM((ns, rw, part), BF), pltpu.VMEM((ns, rw, cols), BF), runs, runs,
            pltpu.VMEM((sub, width), F32), pltpu.VMEM((8, width), F32), pltpu.VMEM((8, short), F32),
            pltpu.VMEM((ns, 8, short), F32),
            DMA((5,)),
            DMA((nc,)), DMA((nc,)), DMA((nc,)), DMA((nc,)), DMA((ns,)), DMA((ns,)), DMA((ns,)), DMA((ns,)),
            DMA((nc,)), DMA((nc,)), DMA((nc,)), DMA((nc,)), DMA(()), DMA(()),
            DMA((ns, nsub)), DMA((ns, nsub)), DMA((ns, nsub)), DMA((ns, nsub)),
            DMA((ns,)), DMA((ns,)), DMA((nd,)), DMA((nd,)),
        ],
        compiler_params=pltpu.CompilerParams(
            collective_id=cid, has_side_effects=True, vmem_limit_bytes=60 * 2**20),
        name="end",
    )(grad_inner, grad_gate, modded, normed, wx, *small, hidden, cot, modulation, grad_gate_scale, embedded, early, *fil)
    return gin, gout, own, gh.reshape(local, width), mod


def frequency_embed(timestep):
    half_width = FREQ // 2
    counter = jnp.arange(half_width, dtype=F32)
    frequency = jnp.exp(counter * (-math.log(10000.0) / half_width))
    angles = timestep.astype(F32)[:, None] * frequency[None, :]
    return jnp.concatenate([jnp.cos(angles), jnp.sin(angles)], axis=1)


def dot(a, b):
    return jnp.dot(a, b, preferred_element_type=F32)


def dot_nt(a, b):
    return lax.dot_general(a, b, (((1,), (1,)), ((), ())), preferred_element_type=F32)


def dot_tn(a, b):
    return lax.dot_general(a, b, (((0,), (0,)), ((), ())), preferred_element_type=F32)


def by_eight(a):
    return jnp.sum(a.reshape(-1, 8, a.shape[1]), axis=0)


def body(
    hidden,
    pad_mask,
    timestep,
    input_weight,
    select_weight,
    step_weight,
    output_weight,
    decay_forward,
    decay_reverse,
    filter_weight,
    filter_bias,
    step_bias,
    modulation_weight,
    modulation_bias,
    cotangent,
):
    ns, nd = lax.axis_size("seq"), lax.axis_size("dp")
    q, d = lax.axis_index("seq"), lax.axis_index("dp")
    every = ("dp", "seq")
    local_len, width = hidden.shape[1:]
    length = local_len * ns
    inner = output_weight.shape[0]
    part = inner // ns
    rank = step_weight.shape[0]
    state = decay_forward.shape[1]
    taps = filter_weight.shape[0]
    rows_in = input_weight.shape[0]
    lanes = select_weight.shape[1]

    units = part // nd
    embedded = jax.nn.silu(frequency_embed(timestep)).astype(BF)
    modb = jnp.zeros((-(-3 * width // 1024) * 1024,), F32)
    modb = lax.dynamic_update_slice(modb, modulation_bias.astype(F32), ((d * ns + q) * modulation_bias.shape[0],))
    row_pad = ((0, -rows_in % 16), (0, 0))
    fused = rows_in % 16 == 0
    modded, normed, inner_part, gate_branch, wx, select_q, step_q, rates, fil, mask, modulation = start(
        hidden[0], pad_mask.reshape(-1, 128), jnp.pad(input_weight, row_pad), jnp.pad(output_weight.T, row_pad),
        embedded, modulation_weight, modb.reshape(-1, 128),
        (select_weight, step_weight, decay_forward.T, decay_reverse.T, filter_weight, filter_bias[None], step_bias[None]),
        fused, nd, ns, 4)
    wx = wx.reshape(nd * ns, -1, 3 * part)[:, :rows_in].reshape(width, 3 * part)
    win, wout = wx[:, : 2 * part], wx[:, 2 * part :]
    mask = mask[:, : local_len // 128].reshape(length, 1).astype(F32)
    rates_f, rates_r, rates_f2, rates_r2 = [rates[k * state : (k + 1) * state] for k in range(4)]
    modulation_rows, modulation = modulation, modulation[:1]
    shifts = modulation[:, :width]
    scales = modulation[:, width : 2 * width]
    gate_scale = modulation[:, 2 * width :]

    def norm(x):
        x = x.astype(F32)
        centered = x - jnp.mean(x, axis=1, keepdims=True)
        inverse = lax.rsqrt(jnp.mean(centered * centered, axis=1, keepdims=True) + EPS)
        return centered * inverse, inverse

    if fused:
        modded, normed = modded.reshape(length, width), normed.reshape(length, width)
        inner_part, gate_branch = inner_part.reshape(length, part), gate_branch.reshape(length, part)
    else:
        normed = norm(modded.reshape(length, width))[0]
        modded, normed = (normed * (1.0 + scales) + shifts).astype(BF), normed.astype(BF)
        projected = dot(modded, win)
        inner_part, gate_branch = projected[:, :part].astype(BF), projected[:, part:]
    inner_part = inner_part.astype(F32) * mask
    padded = jnp.pad(inner_part, ((taps - 1, 0), (0, 0)))
    filtered = fil[taps][None]
    for k in range(taps):
        filtered = filtered + fil[k][None] * padded[k : k + length]
    sigma_filter = jax.nn.sigmoid(filtered)
    active = (filtered * sigma_filter).astype(BF)
    active32 = active.astype(F32)
    selected = column_sum(dot(active, select_q).astype(BF), ns, BF, 0)
    cot, selected = lax.optimization_barrier((cotangent[0], selected))
    cot = lax.all_gather(cot, "seq", axis=0, tiled=True)
    low_rank = selected[:, :rank].astype(BF)
    b_rows = selected[:, rank : rank + state].astype(F32)
    c_rows = selected[:, rank + state :].astype(F32)
    pre_steps = dot(low_rank, step_q) + fil[taps + 1][None]
    steps = jax.nn.softplus(pre_steps)
    drive = steps * active32
    mixed_f, mixed_r, states_f, states_r = fwd_scan(steps, drive, rates_f2, rates_r2, b_rows.T, blockdiag(c_rows))
    merged = mixed_f + mixed_r
    sigma_gate = jax.nn.sigmoid(gate_branch)
    silu_gate = gate_branch * sigma_gate
    gated = (merged * silu_gate).astype(BF)
    branch = dot_nt(gated, wout).astype(BF)
    branch, cot = lax.optimization_barrier((branch, cot))
    branch = lax.psum_scatter(branch, "seq", scatter_dimension=0, tiled=True).astype(F32)

    mask_here = pad_mask[0].astype(F32)[:, None]
    cot_here = cotangent[0].astype(F32)
    block_out = (hidden[0].astype(F32) + gate_scale * mask_here * branch).astype(BF)
    grad_gate = by_eight(mask_here * cot_here * branch)

    grad_branch = lax.optimization_barrier((cot.astype(F32) * gate_scale * mask).astype(BF))
    grad_gated = dot(grad_branch, wout)
    grad_merged = grad_gated * silu_gate
    grad_gate_branch = grad_gated * merged * sigma_gate * (1.0 + gate_branch * (1.0 - sigma_gate))
    grad_gate_branch = grad_gate_branch.astype(BF)
    rows_first = Layout((0, 1))
    early = jnp.concatenate([
        with_layout_constraint(dot_tn(modded, grad_gate_branch).astype(BF), rows_first),
        with_layout_constraint(dot_tn(grad_branch, gated).astype(BF), rows_first)], axis=1)
    early = lax.psum_scatter(early, "dp", scatter_dimension=0, tiled=True)
    dlog_f, dlog_r, adjb_f, adjb_r, bg_f, bg_r, cg_f, cg_r, rg_f, rg_r = bwd_scan(
        steps, drive, grad_merged, rates_f2, rates_r2, c_rows.T, blockdiag(b_rows), states_f, states_r)
    adjb = adjb_f + adjb_r
    grad_steps = (dlog_f + dlog_r) * (1.0 / LOG2E) + active32 * adjb
    grad_pre = grad_steps * -jnp.expm1(-steps)
    grad_step_bias = jnp.sum(grad_pre, axis=0, keepdims=True)
    grad_pre_low = grad_pre.astype(BF)
    grad_step = dot_tn(low_rank, grad_pre_low)
    grad_selected = column_grads(grad_pre_low, step_q, bg_f, bg_r, cg_f, cg_r, ns, 1)
    grad_select = dot_tn(active, grad_selected)
    grad_active = steps * adjb + dot_nt(grad_selected, select_q)
    grad_filtered = grad_active * sigma_filter * (1.0 + filtered * (1.0 - sigma_filter))
    extended = jnp.pad(grad_filtered, ((0, taps - 1), (0, 0)))
    grad_inner = jnp.zeros_like(grad_filtered)
    filter_rows = []
    for k in range(taps):
        lead = taps - 1 - k
        grad_inner = grad_inner + fil[k][None] * extended[lead : lead + length]
        filter_rows.append(by_eight(grad_filtered * padded[k : k + length]))
    grad_filter_bias = by_eight(grad_filtered)
    grad_inner = (grad_inner * mask).astype(BF)
    g_in, g_out, own, grad_hidden, sums = end(
        grad_inner, grad_gate_branch, modded, normed, wx, early, (grad_select, grad_step, rg_f, rg_r, rates),
        filter_rows + [grad_filter_bias, grad_step_bias], hidden[0], cotangent[0], modulation_rows, grad_gate, embedded,
        rows_in, nd, ns, 2)
    gs_select, gs_step, gs_f, gs_r, gs_taps, gs_fbias, gs_sbias = own
    sums = sums.reshape(nd, -1)
    embeds = sums[:, 3 * width : 3 * width + FREQ]
    grad_mod = sums[:, : 3 * width]
    me = d * ns + q
    mine = lax.dynamic_slice_in_dim(embeds, me * modulation_weight.shape[0], modulation_weight.shape[0], 1)
    g_modw = lax.dot_general(mine, grad_mod, (((0,), (0,)), ((), ())), precision=HIGHEST)
    g_modb = lax.dynamic_slice_in_dim(
        jnp.sum(grad_mod, axis=0), me * modulation_bias.shape[0], modulation_bias.shape[0], 0)
    return (
        block_out[None],
        grad_hidden[None],
        g_in,
        gs_select,
        gs_step,
        g_out.T,
        gs_f.T,
        gs_r.T,
        gs_taps,
        gs_fbias[0],
        gs_sbias[0],
        g_modw,
        g_modb,
    )


def solution(mesh):
    return jax.shard_map(
        body,
        mesh=mesh,
        in_specs=(
            P("dp", "seq", None),
            P("dp", "seq"),
            P("dp"),
            P(("dp", "seq"), None),
            P(("dp", "seq"), None),
            P(None, ("dp", "seq")),
            P(None, ("dp", "seq")),
            P(("dp", "seq"), None),
            P(("dp", "seq"), None),
            P(None, ("dp", "seq")),
            P(("dp", "seq")),
            P(("dp", "seq")),
            P(("dp", "seq"), None),
            P(("dp", "seq")),
            P("dp", "seq", None),
        ),
        out_specs=(
            P("dp", "seq", None),
            P("dp", "seq", None),
            P(("dp", "seq"), None),
            P(("dp", "seq"), None),
            P(None, ("dp", "seq")),
            P(None, ("dp", "seq")),
            P(("dp", "seq"), None),
            P(("dp", "seq"), None),
            P(None, ("dp", "seq")),
            P(("dp", "seq")),
            P(("dp", "seq")),
            P(("dp", "seq"), None),
            P(("dp", "seq")),
        ),
        check_vma=False,
    )
```

```python
import functools
import math

import jax
import jax.numpy as jnp
from jax import lax
from jax.experimental import pallas as pl
from jax.experimental.layout import Layout, with_layout_constraint
from jax.experimental.pallas import tpu as pltpu
from jax.sharding import PartitionSpec as P

FREQ = 256
EPS = 1e-06
HIGHEST = lax.Precision.HIGHEST
LOG2E = 1.4426950408889634
SUB = 16
WF = 384
WB = 768
F32, BF = jnp.float32, jnp.bfloat16
NT = (((1,), (1,)), ((), ()))


def columns_of(rows_t, base):
    turned = pltpu.roll(rows_t, rows_t.shape[1] - base, 1)
    return [jnp.broadcast_to(turned[:, j:j + 1], (rows_t.shape[0], 128)) for j in range(SUB)]


def wide(block, lanes):
    return jnp.concatenate([block] * (lanes // 128), axis=1) if lanes > 128 else block


def states_of(base, at):
    return pl.ds(pl.multiple_of((base + at) * 16, 16), 16)


def fwd_kernel(step_f, step_r, u_f, u_r, rate_f, rate_r, bt_f, bt_r, cblk_f, cblk_r,
               y_f, y_r, s_f, s_r, carry, f0, f1, r0, r1):
    rows, lanes = step_f.shape

    @pl.when(pl.program_id(0) == 0)
    def _():
        carry[...] = jnp.zeros(carry.shape, F32)

    wide_by = min(WF, lanes)
    cuts = [slice(c, c + wide_by) for c in range(0, lanes, wide_by)]

    def walk(states, bases, kept):
        cols = [columns_of(bt[...], base) for bt, base in zip((bt_f, bt_r), bases)]
        out = []
        for cut, pair in zip(cuts, states):
            pair = list(pair)
            rates = rate_f[:, cut], rate_r[:, cut]
            for k in range(SUB):
                for z, (step, u, s, j) in enumerate(((step_f, u_f, s_f, k), (step_r, u_r, s_r, SUB - 1 - k))):
                    at = pl.ds(bases[z] + j, 1)
                    decay = jnp.exp2(step[at, cut] * rates[z])
                    pair[z] = decay * pair[z] + u[at, cut] * wide(cols[z][j], wide_by)
                    low = pair[z].astype(BF)
                    s[states_of(bases[z], j), cut] = low
                    kept[z][j * 16:(j + 1) * 16, cut] = low
            out.append(tuple(pair))
        return tuple(out)

    def mix(base, cblk, kept, y):
        here = pl.ds(base, SUB)
        y[here, :] = jnp.dot(cblk[here, :], kept[...], preferred_element_type=F32)

    def start_of(a, flip):
        a = jnp.maximum(a, 0)
        return pl.multiple_of(rows - SUB - a * SUB if flip else a * SUB, SUB)

    def two(i, states):
        for half, (fk, rk, fp, rp) in enumerate(((f0, r0, f1, r1), (f1, r1, f0, r0))):
            a = 2 * i + half
            mix(start_of(a - 1, False), cblk_f, fp, y_f)
            mix(start_of(a - 1, True), cblk_r, rp, y_r)
            states = walk(states, (start_of(a, False), start_of(a, True)), (fk, rk))
        return states

    states = tuple((carry[0, :, cut], carry[1, :, cut]) for cut in cuts)
    states = lax.fori_loop(0, rows // SUB // 2, two, states)
    mix(rows - SUB, cblk_f, f1, y_f)
    mix(0, cblk_r, r1, y_r)
    for cut, pair in zip(cuts, states):
        carry[0, :, cut], carry[1, :, cut] = pair


def fwd_scan(steps, u, rates_f, rates_r, b_t, cblk, tile=128):
    length, lanes = steps.shape
    blocks = length // tile
    specs = []
    for order in (lambda t: t, lambda t: blocks - 1 - t):
        specs.append((
            pl.BlockSpec((tile, lanes), lambda t, order=order: (order(t), 0)),
            pl.BlockSpec((16, lanes), lambda t: (0, 0)),
            pl.BlockSpec((16, tile), lambda t, order=order: (0, order(t))),
            pl.BlockSpec((tile, 256), lambda t, order=order: (order(t), 0)),
            pl.BlockSpec((tile * 16, lanes), lambda t, order=order: (order(t), 0)),
        ))
    (row_f, rate, bt_f, blk_f, s_f), (row_r, _, bt_r, blk_r, s_r) = specs
    y = jax.ShapeDtypeStruct((length, lanes), F32)
    s = jax.ShapeDtypeStruct((length * 16, lanes), BF)
    kept = pltpu.VMEM((256, lanes), BF)
    return pl.pallas_call(
        fwd_kernel,
        grid=(blocks,),
        in_specs=[row_f, row_r, row_f, row_r, rate, rate, bt_f, bt_r, blk_f, blk_r],
        out_specs=[row_f, row_r, s_f, s_r],
        out_shape=[y, y, s, s],
        scratch_shapes=[pltpu.VMEM((2, 16, lanes), F32), kept, kept, kept, kept],
        compiler_params=pltpu.CompilerParams(vmem_limit_bytes=56 * 2**20, dimension_semantics=("arbitrary",)),
        cost_estimate=pl.CostEstimate(flops=length * lanes * 16 * 3200, transcendentals=0, bytes_accessed=length * lanes * 80),
        name="fwd_scan",
    )(steps, steps, u, u, rates_f, rates_r, b_t, b_t, cblk, cblk)


def bwd_kernel(step_f, step_r, u_f, u_r, gy_f, gy_r, rate_f, rate_r, ct_f, ct_r, bblk_f, bblk_r, s_f, s_r, sp_f, sp_r,
               dlog_f, dlog_r, adjb_f, adjb_r, bg_f, bg_r, cg_f, cg_r, rg_f, rg_r, carry,
               af0, af1, ar0, ar1, lf0, lf1, lr0, lr1):
    rows, lanes = step_f.shape
    t = pl.program_id(0)
    last = pl.num_programs(0) - 1

    @pl.when(t == 0)
    def _():
        carry[...] = jnp.zeros(carry.shape, F32)
        rg_f[...] = jnp.zeros(rg_f.shape, F32)
        rg_r[...] = jnp.zeros(rg_r.shape, F32)

    ones = (lax.broadcasted_iota(jnp.int32, (SUB, 256), 0) == lax.broadcasted_iota(jnp.int32, (SUB, 256), 1) // 16)
    onesb = ones.astype(BF)
    zero = jnp.zeros((SUB, 256), F32)

    def start_of(a, down):
        a = jnp.maximum(a, 0)
        return pl.multiple_of(rows - SUB - a * SUB if down else a * SUB, SUB)

    wide_by = min(WB, lanes)
    cuts = [slice(c, c + wide_by) for c in range(0, lanes, wide_by)]

    def walk(states, bases, keep_a, keep_l):
        cols = [columns_of(ct[...], base) for ct, base in zip((ct_f, ct_r), bases)]
        out = []
        for cut, pair in zip(cuts, states):
            pair = list(pair)
            rates = rate_f[:, cut], rate_r[:, cut]
            rg = [rg_f[:, cut], rg_r[:, cut]]
            low_rates = [r.astype(BF) for r in rates]
            some = [[], []]
            for k in range(SUB):
                for z, (step, gy, s, sp, j) in enumerate((
                        (step_f, gy_f, s_f, sp_f, SUB - 1 - k), (step_r, gy_r, s_r, sp_r, k))):
                    at = pl.ds(bases[z] + j, 1)
                    row = step[at, cut]
                    adj = gy[at, cut] * wide(cols[z][j], wide_by) + pair[z]
                    pair[z] = jnp.exp2(row * rates[z]) * adj
                    before = bases[z] + (j + 1 if z else j - 1)
                    if k < SUB - 1:
                        inner = s[pl.ds(pl.multiple_of(before * 16, 16), 16), cut]
                    else:
                        inside = before < rows if z else before >= 0
                        safe = jnp.clip(before, 0, rows - 1)
                        inner = s[pl.ds(pl.multiple_of(safe * 16, 16), 16), cut]
                        outer = jnp.where(t == last, jnp.zeros_like(inner), sp[:, cut])
                        inner = jnp.where(inside, inner, outer)
                    grad = pair[z].astype(BF) * inner
                    keep_a[z][j * 16:(j + 1) * 16, cut] = adj.astype(BF)
                    keep_l[z][j * 16:(j + 1) * 16, cut] = grad * low_rates[z]
                    some[z].append(grad * jnp.broadcast_to(row, (16, wide_by)).astype(BF))
                    if len(some[z]) == 4:
                        rg[z] = rg[z] + ((some[z][0] + some[z][1]) + (some[z][2] + some[z][3])).astype(F32)
                        some[z] = []
            rg_f[:, cut], rg_r[:, cut] = rg
            out.append(tuple(pair))
        return tuple(out)

    mix_by = 256 if lanes % 256 == 0 else 128

    def mix(base, a_ref, l_ref, u, gy, bblk, s, dlog, adjb, bg, cg):
        here = pl.ds(base, SUB)
        line = pl.ds(base // SUB, 1)
        group = pl.ds(pl.multiple_of(base * 16, 256), 256)
        bgd = cgd = zero
        for c in range(0, lanes, mix_by):
            cut = slice(c, c + mix_by)
            dlog[here, cut] = jnp.dot(onesb, l_ref[:, cut], preferred_element_type=F32)
            a = a_ref[:, cut]
            adjb[here, cut] = jnp.dot(bblk[here, :], a, preferred_element_type=F32)
            bgd = bgd + lax.dot_general(u[here, cut].astype(BF), a, NT, preferred_element_type=F32)
            cgd = cgd + lax.dot_general(gy[here, cut].astype(BF), s[group, cut], NT, preferred_element_type=F32)
        bg[line, :] = jnp.sum(jnp.where(ones, bgd, zero), axis=0, keepdims=True)
        cg[line, :] = jnp.sum(jnp.where(ones, cgd, zero), axis=0, keepdims=True)

    def mix_f(base, a_ref, l_ref):
        mix(base, a_ref, l_ref, u_f, gy_f, bblk_f, s_f, dlog_f, adjb_f, bg_f, cg_f)

    def mix_r(base, a_ref, l_ref):
        mix(base, a_ref, l_ref, u_r, gy_r, bblk_r, s_r, dlog_r, adjb_r, bg_r, cg_r)

    def two(i, states):
        bufs = ((af0, lf0, ar0, lr0), (af1, lf1, ar1, lr1))
        for half in range(2):
            a = 2 * i + half
            naf, nlf, nar, nlr = bufs[half]
            paf, plf, par, plr = bufs[1 - half]
            mix_f(start_of(a - 1, True), paf, plf)
            mix_r(start_of(a - 1, False), par, plr)
            states = walk(states, (start_of(a, True), start_of(a, False)), (naf, nar), (nlf, nlr))
        return states

    states = tuple((carry[0, :, cut], carry[1, :, cut]) for cut in cuts)
    states = lax.fori_loop(0, rows // SUB // 2, two, states)
    mix_f(0, af1, lf1)
    mix_r(rows - SUB, ar1, lr1)
    for cut, pair in zip(cuts, states):
        carry[0, :, cut], carry[1, :, cut] = pair


def bwd_scan(steps, u, gy, rates_f, rates_r, c_t, bblk, states_f, states_r, tile=128):
    length, lanes = steps.shape
    blocks = length // tile
    down = lambda t: blocks - 1 - t
    up = lambda t: t

    def specs(order, before):
        return (
            pl.BlockSpec((tile, lanes), lambda t: (order(t), 0)),
            pl.BlockSpec((16, lanes), lambda t: (0, 0)),
            pl.BlockSpec((16, tile), lambda t: (0, order(t))),
            pl.BlockSpec((tile, 256), lambda t: (order(t), 0)),
            pl.BlockSpec((tile * 16, lanes), lambda t: (order(t), 0)),
            pl.BlockSpec((16, lanes), lambda t: (before(t), 0)),
            pl.BlockSpec((tile // 16, 256), lambda t: (order(t), 0)),
        )

    row_f, rate, ct_f, blk_f, s_f, sp_f, diag_f = specs(down, lambda t: jnp.maximum((blocks - 1 - t) * tile - 1, 0))
    row_r, _, ct_r, blk_r, s_r, sp_r, diag_r = specs(up, lambda t: jnp.minimum((t + 1) * tile, length - 1))
    y = jax.ShapeDtypeStruct((length, lanes), F32)
    diag = jax.ShapeDtypeStruct((length // 16, 256), F32)
    rg = jax.ShapeDtypeStruct((16, lanes), F32)
    kept = pltpu.VMEM((256, lanes), BF)
    return pl.pallas_call(
        bwd_kernel,
        grid=(blocks,),
        in_specs=[row_f, row_r, row_f, row_r, row_f, row_r, rate, rate, ct_f, ct_r, blk_f, blk_r, s_f, s_r, sp_f, sp_r],
        out_specs=[row_f, row_r, row_f, row_r, diag_f, diag_r, diag_f, diag_r, rate, rate],
        out_shape=[y, y, y, y, diag, diag, diag, diag, rg, rg],
        scratch_shapes=[pltpu.VMEM((2, 16, lanes), F32)] + [kept] * 8,
        compiler_params=pltpu.CompilerParams(vmem_limit_bytes=56 * 2**20, dimension_semantics=("arbitrary",)),
        cost_estimate=pl.CostEstimate(flops=length * lanes * 16 * 6800, transcendentals=0, bytes_accessed=length * lanes * 100),
        name="bwd_scan",
    )(steps, steps, u, u, gy, gy, rates_f, rates_r, c_t, c_t, bblk, bblk, states_f, states_r, states_f, states_r)


def blockdiag(rows):
    length = rows.shape[0]
    eye = (jnp.arange(length)[:, None] % 16) == (jnp.arange(256)[None, :] // 16)
    return jnp.where(eye, jnp.tile(rows, (1, 16)), 0).astype(BF)


MESH = pl.DeviceIdType.MESH
VMEM = pl.BlockSpec(memory_space=pltpu.VMEM)
HBM = pl.BlockSpec(memory_space=pl.ANY)
DMA = pltpu.SemaphoreType.DMA


def send(src, dst, out_sem, in_sem, to):
    return pltpu.make_async_remote_copy(
        src_ref=src, dst_ref=dst, send_sem=out_sem, recv_sem=in_sem, device_id=to, device_id_type=MESH)


def greet(devices):
    bar = pltpu.get_barrier_semaphore()
    for to in devices:
        pl.semaphore_signal(bar, inc=1, device_id=to, device_id_type=MESH)
    pl.semaphore_wait(bar, len(devices))


def column_sum_kernel(ns, p_ref, o_ref, land, s1, r1, s2, r2):
    d, q = lax.axis_index("dp"), lax.axis_index("seq")
    others = [lax.rem(q + k, ns) for k in range(1, ns)]
    greet([(d, t) for t in others])
    for k, t in enumerate(others):
        send(p_ref.at[t], land.at[q], s1.at[k], r1.at[q], (d, t)).start()
    total = p_ref[q].astype(F32)
    for k, t in enumerate(others):
        send(p_ref.at[t], land.at[t], s1.at[k], r1.at[t], (d, t)).wait_recv()
        total = total + land[t].astype(F32)
    o_ref[q] = total.astype(o_ref.dtype)
    for k, t in enumerate(others):
        send(o_ref.at[q], o_ref.at[q], s2.at[k], r2.at[q], (d, t)).start()
    for k, t in enumerate(others):
        send(o_ref.at[t], o_ref.at[t], s2.at[k], r2.at[t], (d, t)).wait_recv()
    for k, t in enumerate(others):
        send(p_ref.at[t], land.at[q], s1.at[k], r1.at[q], (d, t)).wait_send()
        send(o_ref.at[q], o_ref.at[q], s2.at[k], r2.at[q], (d, t)).wait_send()


def column_sum(partial, ns, out_dtype, cid):
    rows, lanes = partial.shape
    block = (ns, rows // ns, lanes)
    out = pl.pallas_call(
        functools.partial(column_sum_kernel, ns),
        out_shape=jax.ShapeDtypeStruct(block, out_dtype),
        in_specs=[VMEM], out_specs=VMEM,
        scratch_shapes=[pltpu.VMEM(block, partial.dtype), DMA((ns,)), DMA((ns,)), DMA((ns,)), DMA((ns,))],
        compiler_params=pltpu.CompilerParams(
            collective_id=cid, has_side_effects=True, vmem_limit_bytes=32 * 2**20),
        name="column_sum",
    )(partial.reshape(block))
    return out.reshape(rows, lanes)


def column_grads_kernel(ns, pre_ref, step_ref, bf_ref, br_ref, cf_ref, cr_ref, o_ref, state_ref, rows_ref, p_ref, *rest):
    rank = step_ref.shape[0]
    local = p_ref.shape[1]
    groups = local // 16
    rows_ref[...] = jnp.zeros(rows_ref.shape, BF)
    rows_ref[0:rank, :] = step_ref[...]
    for t in range(ns):
        lines = slice(t * groups, (t + 1) * groups)
        b, c = bf_ref[lines, :] + br_ref[lines, :], cf_ref[lines, :] + cr_ref[lines, :]
        for l in range(16):
            here = slice(l * 16, (l + 1) * 16)
            state_ref[pl.ds(l, groups, stride=16), :] = jnp.concatenate(
                [jnp.zeros((groups, rank), F32), b[:, here], c[:, here]], axis=1)
        low = lax.dot_general(pre_ref[t * local:(t + 1) * local, :], rows_ref[...], NT, preferred_element_type=F32)
        p_ref[t] = (low + state_ref[...]).astype(BF)
    column_sum_kernel(ns, p_ref, o_ref, *rest)


def column_grads(pre, step, b_f, b_r, c_f, c_r, ns, cid):
    rows, lanes = pre.shape[0], step.shape[0] + 32
    block = (ns, rows // ns, lanes)
    out = pl.pallas_call(
        functools.partial(column_grads_kernel, ns),
        out_shape=jax.ShapeDtypeStruct(block, BF),
        in_specs=[VMEM] * 6, out_specs=VMEM,
        scratch_shapes=[
            pltpu.VMEM((rows // ns, lanes), F32), pltpu.VMEM((lanes, pre.shape[1]), BF), pltpu.VMEM(block, BF),
            pltpu.VMEM(block, BF), DMA((ns,)), DMA((ns,)), DMA((ns,)), DMA((ns,))],
        compiler_params=pltpu.CompilerParams(
            collective_id=cid, has_side_effects=True, vmem_limit_bytes=32 * 2**20),
        name="column_grads",
    )(pre, step, b_f, b_r, c_f, c_r)
    return out.reshape(rows, lanes)


def start_kernel(nd, ns, nsub, fused, hid, win, wout, mask, emb, modw, modb, select, step, dec_f, dec_r, taps, fbias, sbias,
                 md_o, nm_o, inner_o, gate_o, wx_o, select_o, step_o, rate_o, fil_o, mask_o, mod_o,
                 hv, wv, mv, nv, iv, gv, pack, modw_v, pack_v, eland, prod, rowp, land1, land2,
                 su, ru, sd, rd, swz, rwx, swp, swm, spz, rp, spp, spm, sk, rk, se, re, s1, r1, s2, r2, own, out):
    d, q = lax.axis_index("dp"), lax.axis_index("seq")
    nc = nd // 2
    chip, core = d // 2, lax.rem(d, 2)
    mate = (chip * 2 + 1 - core, q)
    chips = [lax.rem(chip + k, nc) for k in range(1, nc)]
    others = [lax.rem(q + k, ns) for k in range(1, ns)]
    peers = [lax.rem(d + k, nd) for k in range(1, nd)]
    spread = nd // ns
    me = d * ns + q
    part = wout.shape[1] // ns
    rw = wout.shape[0]
    units = part // nd
    rank, states = step.shape[0], dec_f.shape[0]
    above = units + -units % 16
    taps_at = above + rank + 2 * states

    pack[...] = jnp.zeros(pack.shape, BF)
    pack[0:units, :] = select[...]
    pack[above:above + rank, 0:units] = step[...]
    pack[above + rank:above + rank + states, 0:units] = dec_f[...]
    pack[above + rank + states:taps_at, 0:units] = dec_r[...]
    pack[taps_at:taps_at + 16, 0:units] = jnp.concatenate(
        [taps[...].astype(F32), fbias[...].astype(F32), sbias[...].astype(F32),
         jnp.zeros((14 - taps.shape[0], units), F32)]).astype(BF)
    modw_v[...] = jnp.zeros(modw_v.shape, BF)
    modw_v[0:modw.shape[0], :] = modw[...]
    greet([(d, t) for t in others] + [(e, q) for e in peers])

    def column(ref, at):
        return ref.at[:, pl.ds(pl.multiple_of(at * part, 128), part)]

    def wrows(idx):
        return wv.at[pl.ds(pl.multiple_of(idx * rw, 16), rw), :]

    def pieces(t):
        return (column(win, t), column(win, ns + t), column(wout, t))

    def across(k, t, idx):
        return [
            send(src, wrows(idx).at[:, j * part:(j + 1) * part], swz.at[k, j], rwx.at[idx, j], (d, t))
            for j, src in enumerate(pieces(t))
        ]

    keep = [pltpu.make_async_copy(src, wrows(me).at[:, j * part:(j + 1) * part], own.at[j])
            for j, src in enumerate(pieces(q))]
    keep.append(pltpu.make_async_copy(hid, hv.at[q], own.at[3]))
    for copy in keep:
        copy.start()

    plane = d // spread
    slot = lax.rem(d, spread) * ns + q
    pack_z = send(pack, pack_v.at[slot], spz, rp.at[slot], (d, plane))
    pack_vwn = pltpu.make_async_copy(pack, pack_v.at[slot], own.at[4])

    @pl.when(plane == q)
    def _():
        pack_vwn.start()

    @pl.when(plane != q)
    def _():
        pack_z.start()

    def masks(k, t, src):
        return send(mask_o.at[src], mask_o.at[src], sk.at[k], rk.at[src], (d, t))

    def embeds(k, e, src):
        return send(eland.at[src], eland.at[src], se.at[k], re.at[src], (e, q))

    mask_o[q] = jnp.zeros(mask_o.shape[1:], BF)
    mask_o[q, 0:mask.shape[0], :] = mask[...].astype(F32).astype(BF)
    eland[d] = jnp.zeros(eland.shape[1:], BF)
    eland[d, 0:1, :] = emb[...]
    for k, e in enumerate(peers):
        embeds(k, e, d).start()
    for k, t in enumerate(others):
        masks(k, t, q).start()

    for k, t in enumerate(others):
        for copy in across(k, t, me)[:2]:
            copy.start()

    def rise(k, s):
        t = jnp.maximum(q - k, 0)
        src = hid.at[s] if k == 0 else hv.at[t, s]
        return send(src, hv.at[t, s], su.at[k, s], ru.at[k, s], (d, jnp.minimum(q + 1, ns - 1)))

    def sink(k, s):
        t = jnp.minimum(q + k, ns - 1)
        src = hid.at[s] if k == 0 else hv.at[t, s]
        return send(src, hv.at[t, s], sd.at[k, s], rd.at[k, s], (d, jnp.maximum(q - 1, 0)))

    def hop(k, s):
        @pl.when(q >= k)
        def _():
            if k:
                rise(k - 1, s).wait_recv()
            if k < ns - 1:
                @pl.when(q + 1 < ns)
                def _():
                    rise(k, s).start()

        @pl.when(q + k < ns)
        def _():
            if k:
                sink(k - 1, s).wait_recv()
            if k < ns - 1:
                @pl.when(q >= 1)
                def _():
                    sink(k, s).start()

    for s in range(nsub):
        hop(0, s)
    for k, t in enumerate(others):
        across(k, t, me)[2].start()

    def cols_of(idx, kind):
        return wrows(idx).at[:, 2 * part * kind:2 * part + part * kind]

    def plane_w(c, idx, t, kind):
        return send(cols_of(idx, kind), cols_of(idx, kind), swp.at[kind, c, t], rwx.at[idx, 3 + kind], (c * 2 + core, q))

    def mate_w(c, idx, t, kind):
        return send(cols_of(idx, kind), cols_of(idx, kind), swm.at[kind, c, t], rwx.at[idx, 3 + kind], mate)

    def spread_w(t, kind):
        idx = d * ns + t
        for c in chips:
            plane_w(c, idx, t, kind).start()
        mate_w(chip, idx, t, kind).start()

    for copy in keep[:3]:
        copy.wait()
    spread_w(q, 0)

    for k, e in enumerate(peers):
        embeds(k, e, e).wait_recv()
    rows = modw_v.shape[0]
    here = lax.broadcasted_iota(jnp.int32, (FREQ, rows), 0)
    pick = here - lax.broadcasted_iota(jnp.int32, (FREQ, rows), 1)
    count = FREQ // (nd * ns)
    keep_col = lax.broadcasted_iota(jnp.int32, (FREQ, rows), 1) < count
    pick = jnp.where(jnp.logical_and(pick == me * count, keep_col), 1.0, 0.0).astype(BF)
    mine = jnp.dot(eland[...].reshape(nd * 16, FREQ), pick, preferred_element_type=F32).astype(BF)
    prod[...] = jnp.dot(mine, modw_v[...], preferred_element_type=F32)

    lines = prod.shape[1] // 128
    @pl.loop(0, nd)
    def _(e):
        rowp[e] = modb[...]
        for j in range(lines):
            rowp[e, j:j + 1, :] += prod[pl.ds(pl.multiple_of(e * 16, 16), 1), j * 128:(j + 1) * 128]

    def to_item(k, e, src):
        return send(rowp.at[e], land1.at[src], s1.at[k], r1.at[src], (e, q))

    for k, e in enumerate(peers):
        to_item(k, e, d).start()

    for k, t in enumerate(others):
        for copy in across(k, t, d * ns + t)[:2]:
            copy.wait_recv()
        spread_w(t, 0)

    def plane_p(c, i, t):
        return send(pack_v.at[i], pack_v.at[i], spp.at[c, t], rp.at[i], (c * 2 + core, q))

    def mate_p(c, i, t):
        return send(pack_v.at[i], pack_v.at[i], spm.at[c, t], rp.at[i], mate)

    base = lax.rem(d, spread) * ns

    @pl.when(plane == q)
    def _():
        pack_vwn.wait()
        for t in others:
            send(pack, pack_v.at[base + t], spz, rp.at[base + t], (d, plane)).wait_recv()
        for t in range(ns):
            for c in chips:
                plane_p(c, base + t, t).start()
            mate_p(chip, base + t, t).start()

    total = rowp[d]
    for k, e in enumerate(peers):
        to_item(k, e, e).wait_recv()
        total = total + land1[e]
    land2[q] = total

    def to_column(k, t, src):
        return send(land2.at[src], land2.at[src], s2.at[k], r2.at[src], (d, t))

    for k, t in enumerate(others):
        to_column(k, t, q).start()

    def relay_w(c, t, kind):
        idx = (c * 2 + core) * ns + t
        plane_w(c, idx, t, kind).wait_recv()
        mate_w(c, idx, t, kind).start()

    def holds(c):
        return (c * 2 + core) // spread == q

    def relay_p(c):
        first = lax.rem(c * 2 + core, spread) * ns
        @pl.when(holds(c))
        def _():
            for t in range(ns):
                plane_p(c, first + t, t).wait_recv()
                mate_p(c, first + t, t).start()

    def own_copies(t):
        return [pltpu.make_async_copy(src.at[t], dst.at[t], out.at[t, i]) for i, (src, dst) in enumerate(
            ((mv, md_o), (iv, inner_o), (gv, gate_o), (nv, nm_o)) if fused else ((hv, md_o),))]

    local = hv.shape[1] * hv.shape[2]
    width = hv.shape[3]

    def project(t):
        if fused:
            shift, scale = mod_o[0:1, 0:width], 1.0 + mod_o[0:1, width:2 * width]
            for s in range(nsub):
                @pl.loop(0, local // nsub // 16)
                def _(r):
                    x = hv[t, s, pl.ds(pl.multiple_of(r * 16, 16), 16), :].astype(F32)
                    x = x - jnp.mean(x, axis=1, keepdims=True)
                    x = x * lax.rsqrt(jnp.mean(x * x, axis=1, keepdims=True) + EPS)
                    to = pl.multiple_of(s * (local // nsub) + r * 16, 16)
                    nv[t, pl.ds(to, 16), :] = x.astype(BF)
                    mv[t, pl.ds(to, 16), :] = (x * scale + shift).astype(BF)
            tile = part if part % 256 else part // 2

            @pl.loop(0, part // tile)
            def _(j):
                for target, base in ((iv, 0), (gv, part)):
                    n = pl.ds(pl.multiple_of(base + j * tile, 128), tile)
                    full = jnp.dot(mv[t], wv[:, n], preferred_element_type=F32)
                    target[t, :, pl.ds(pl.multiple_of(j * tile, 128), tile)] = full.astype(target.dtype)
        for copy in own_copies(t):
            copy.start()

    relays = [(c, t) for t in [q] + others for c in chips]
    at = 0
    for s in range(nsub):
        hop(1, s)
        upto = len(relays) * (s + 1) // (2 * nsub)
        for c, t in relays[at:upto]:
            relay_w(c, t, 0)
        at = upto
    spread_w(q, 1)
    for k, t in enumerate(others):
        across(k, t, d * ns + t)[2].wait_recv()
        spread_w(t, 1)
    for c, t in relays[at:]:
        relay_w(c, t, 0)
    for c in chips:
        relay_p(c)

    for k, t in enumerate(others):
        to_column(k, t, t).wait_recv()
    total = land2[0]
    for t in range(1, ns):
        total = total + land2[t]
    mod_o[...] = jnp.zeros(mod_o.shape, F32)
    for i in range(mod_o.shape[1] // 128):
        mod_o[0:1, i * 128:(i + 1) * 128] = total[i:i + 1, :]

    twin = 1 - core
    for c in range(nc):
        for t in range(ns):
            idx = (c * 2 + twin) * ns + t
            mate_w(c, idx, t, 0).wait_recv()
    keep[3].wait()

    def project_at(t):
        @pl.when(jnp.logical_and(t >= 0, t < ns))
        def _():
            project(jnp.clip(t, 0, ns - 1))

    for k in range(2, ns):
        for s in range(nsub):
            hop(k, s)
            if k == 2 and s == 0:
                project(q)
            if s == nsub - 3:
                project_at(q - k + 1)
            if s == nsub - 2:
                project_at(q + k - 1)

    for c, t in relays:
        relay_w(c, t, 1)
    for c in range(nc):
        for t in range(ns):
            idx = (c * 2 + twin) * ns + t
            mate_w(c, idx, t, 1).wait_recv()
    wx_copy = pltpu.make_async_copy(wv, wx_o, own.at[5])
    wx_copy.start()

    for c in range(nc):
        first = lax.rem(c * 2 + twin, spread) * ns
        @pl.when((c * 2 + twin) // spread == q)
        def _():
            for t in range(ns):
                mate_p(c, first + t, t).wait_recv()
    for j in range(nd):
        here = slice(j * units, (j + 1) * units)
        select_o[here, :] = pack_v[j, 0:units, :]
        step_o[:, here] = pack_v[j, above:above + rank, 0:units]
        rate_o[0:2 * states, here] = -jnp.exp(pack_v[j, above + rank:taps_at, 0:units].astype(F32))
        fil_o[:, here] = pack_v[j, taps_at:taps_at + 16, 0:units].astype(F32)
    rate_o[2 * states:4 * states, :] = rate_o[0:2 * states, :] * LOG2E

    project_at(q - ns + 1)
    project_at(q + ns - 1)

    for k, t in enumerate(others):
        masks(k, t, t).wait_recv()
    wx_copy.wait()
    for t in range(ns):
        for copy in own_copies(t):
            copy.wait()

    for k, t in enumerate(others):
        for copy in across(k, t, me):
            copy.wait_send()
        masks(k, t, q).wait_send()
        to_column(k, t, q).wait_send()
    for k, e in enumerate(peers):
        embeds(k, e, d).wait_send()
        to_item(k, e, d).wait_send()

    @pl.when(plane != q)
    def _():
        pack_z.wait_send()

    @pl.when(plane == q)
    def _():
        for t in range(ns):
            for c in chips:
                plane_p(c, base + t, t).wait_send()
            mate_p(chip, base + t, t).wait_send()

    for kind in range(2):
        for t in range(ns):
            for c in chips:
                plane_w(c, d * ns + t, t, kind).wait_send()
                mate_w(c, (c * 2 + core) * ns + t, t, kind).wait_send()
            mate_w(chip, d * ns + t, t, kind).wait_send()
    for c in chips:
        first = lax.rem(c * 2 + core, spread) * ns
        @pl.when(holds(c))
        def _():
            for t in range(ns):
                mate_p(c, first + t, t).wait_send()
    for k in range(ns - 1):
        for s in range(nsub):
            @pl.when(jnp.logical_and(q >= k, q + 1 < ns))
            def _():
                rise(k, s).wait_send()
            @pl.when(jnp.logical_and(q + k < ns, q >= 1))
            def _():
                sink(k, s).wait_send()


def start(hidden, mask, win, wout, embedded, modw, modb, small, fused, nd, ns, cid):
    nsub = 4
    length, width = hidden.shape
    rows, inner = wout.shape
    part = inner // ns
    nc = nd // 2
    hidden = hidden.reshape(nsub, length // nsub, width)
    lines = modb.shape
    rank, units, states = small[1].shape[0], part // nd, small[2].shape[0]
    pack = (units + -units % 16 + rank + 2 * states + 16, 128)
    held = modw.shape[0] + -modw.shape[0] % 16
    runs = (ns,) + (hidden.shape if not fused else (length, width))
    return pl.pallas_call(
        functools.partial(start_kernel, nd, ns, nsub, fused),
        out_shape=[
            jax.ShapeDtypeStruct(runs, BF),
            jax.ShapeDtypeStruct((ns, length, width), BF),
            jax.ShapeDtypeStruct((ns, length, part), BF),
            jax.ShapeDtypeStruct((ns, length, part), F32),
            jax.ShapeDtypeStruct((nd * ns * rows, 3 * part), BF),
            jax.ShapeDtypeStruct((part, 128), BF),
            jax.ShapeDtypeStruct((rank, part), BF),
            jax.ShapeDtypeStruct((4 * states, part), F32),
            jax.ShapeDtypeStruct((16, part), F32),
            jax.ShapeDtypeStruct((ns, 16, 128), BF),
            jax.ShapeDtypeStruct((8, modw.shape[1]), F32),
        ],
        in_specs=[HBM, HBM, HBM] + [VMEM] * 11,
        out_specs=[HBM] * 5 + [VMEM] * 6,
        scratch_shapes=[
            pltpu.VMEM((ns,) + hidden.shape, BF), pltpu.VMEM((nd * ns * rows, 3 * part), BF),
            pltpu.VMEM((ns, length, width), BF), pltpu.VMEM((ns, length, width), BF), pltpu.VMEM((ns, length, part), BF), pltpu.VMEM((ns, length, part), F32),
            pltpu.VMEM(pack, BF), pltpu.VMEM((held, modw.shape[1]), BF), pltpu.VMEM((nd,) + pack, BF),
            pltpu.VMEM((nd, 16, FREQ), BF), pltpu.VMEM((nd * 16, modw.shape[1]), F32),
            pltpu.VMEM((nd,) + lines, F32), pltpu.VMEM((nd,) + lines, F32), pltpu.VMEM((ns,) + lines, F32),
            DMA((ns - 1, nsub)), DMA((ns - 1, nsub)), DMA((ns - 1, nsub)), DMA((ns - 1, nsub)),
            DMA((ns, 3)), DMA((nd * ns, 5)), DMA((2, nc, ns)), DMA((2, nc, ns)),
            DMA(()), DMA((nd,)), DMA((nc, ns)), DMA((nc, ns)),
            DMA((ns,)), DMA((ns,)), DMA((nd,)), DMA((nd,)),
            DMA((nd,)), DMA((nd,)), DMA((ns,)), DMA((ns,)), DMA((6,)), DMA((ns, 4)),
        ],
        compiler_params=pltpu.CompilerParams(
            collective_id=cid, has_side_effects=True, vmem_limit_bytes=56 * 2**20),
        name="start",
    )(hidden, win, wout, mask, embedded, modw, modb, *small)


def end_kernel(nd, ns, nsub, rows, turned, nfil,
               gi_h, gg_h, md_h, nm_h, wx_h, gsel, gstep, gdf, gdr, rates, hid_ref, cot_ref, mod_ref, gate_ref, emb_ref, early, *rest):
    gfil = rest[:nfil]
    (gin_o, gout_o, sel_o, step_o, df_o, dr_o, taps_o, fb_o, sb_o, gh_o, mod_o,
               gp, md, nm, wx, sm_ref, so_ref, gm, made, pair, plane, spair, splane, ssum, fro, ready, up, down, own, acc, msg, mland,
               ld, sa, ra, sb, rb, sc, rc, se, re, ta, ra2, tb, rb2, tc, rc2, su, ru, sd, rd, s1, r1, s2, r2) = rest[nfil:]
    d, q = lax.axis_index("dp"), lax.axis_index("seq")
    nc = nd // 2
    chip, core = d // 2, lax.rem(d, 2)
    mate = chip * 2 + 1 - core
    pairs = [(1, 1), (1, 0), (0, 1)] + [(a, b) for b in range(2, nc // 2) for a in (0, 1)]
    chips = [lax.rem(chip + a, 2) + 2 * lax.rem(chip // 2 + b, nc // 2) for a, b in pairs]
    others = [lax.rem(q + k, ns) for k in range(1, ns)]
    peers = [lax.rem(d + k, nd) for k in range(1, nd)]
    spread = nd // ns
    final_to = (spread * q + d // ns, lax.rem(d, ns))
    me = d * ns + q
    final_from = (lax.rem(me, nd), me // nd)
    stays = jnp.logical_and(final_to[0] == d, final_to[1] == q)
    length, cols = gp.shape
    part = cols // 2
    width = wx.shape[0]
    local = length // ns
    sub = local // nsub
    rw = pair.shape[2]
    half = ns * rw

    loads = [pltpu.make_async_copy(src, dst, ld.at[i]) for i, (src, dst) in enumerate(
        ((gi_h, gp.at[:, 0:part]), (gg_h, gp.at[:, part:cols]), (wx_h.at[:, 0:cols], wx), (nm_h, nm), (md_h, md)))]
    for copy in loads:
        copy.start()

    units = part // nd
    rank, states, taps = gstep.shape[0], gdf.shape[0], taps_o.shape[0]
    above = units + -units % 16
    taps_at = above + rank + 2 * states
    bar = pltpu.get_barrier_semaphore()
    friends = [(e, q) for e in peers] + [(d, t) for t in others]
    for to in friends:
        pl.semaphore_signal(bar, inc=1, device_id=to, device_id_type=MESH)
    @pl.when(jnp.logical_not(stays))
    def _():
        pl.semaphore_signal(bar, inc=1, device_id=final_from, device_id_type=MESH)

    def tokens(t):
        @pl.loop(0, width // 512)
        def _(j):
            here = pl.ds(pl.multiple_of(j * 512, 512), 512)
            lines = slice(t * local, (t + 1) * local)
            full = lax.dot_general(gp[lines, :], wx[here, :], NT, preferred_element_type=F32)
            acc[0:1, here] += jnp.sum(full, axis=0, keepdims=True)
            acc[1:2, here] += jnp.sum(full * nm[lines, here].astype(F32), axis=0, keepdims=True)
            full = full.astype(BF)
            for s in range(nsub):
                gm[t, s, :, here] = full[s * sub:(s + 1) * sub]

    def rise(t, s, src):
        return send(src, up.at[t, s], su.at[t, s], ru.at[t, s], (d, jnp.minimum(q + 1, ns - 1)))

    def sink(t, s, src):
        return send(src, down.at[t, s], sd.at[t, s], rd.at[t, s], (d, jnp.maximum(q - 1, 0)))

    def added(land, t, s):
        land[t, s] = (land[t, s].astype(F32) + gm[t, s].astype(F32)).astype(BF)

    def open_up(t, s):
        @pl.when(jnp.logical_and(q == 0, t > 0))
        def _():
            rise(t, s, gm.at[t, s]).start()

    def open_down(t, s):
        @pl.when(jnp.logical_and(q == ns - 1, t < ns - 1))
        def _():
            sink(t, s, gm.at[t, s]).start()

    def step(k, s):
        t = ns - 1 - k

        @pl.when(jnp.logical_and(q < t, q > 0))
        def _():
            rise(t, s, up.at[t, s]).wait_recv()
            added(up, t, s)
            rise(t, s, up.at[t, s]).start()

        @pl.when(jnp.logical_and(q > k, q < ns - 1))
        def _():
            sink(k, s, down.at[k, s]).wait_recv()
            added(down, k, s)
            sink(k, s, down.at[k, s]).start()

    def far(k):
        for t in sorted({ns - 1 - k, k}, reverse=True):
            tokens(t)
            for s in range(nsub):
                open_up(t, s)
                open_down(t, s)

    @pl.when(stays)
    def _():
        pl.semaphore_wait(bar, len(friends))

    @pl.when(jnp.logical_not(stays))
    def _():
        pl.semaphore_wait(bar, len(friends) + 1)

    def whole(t, src):
        return send(early.at[t], ready.at[src], se.at[t], re.at[src], (d, t))

    for t in others:
        whole(t, q).start()
    for copy in loads[:4]:
        copy.wait()
    acc[...] = jnp.zeros(acc.shape, F32)
    acc[2:3, :] = jnp.sum(gate_ref[...], axis=0, keepdims=True)
    acc[3:4, 0:FREQ] = emb_ref[...].astype(F32) * (1.0 / ns)
    far(0)
    steps = [(k, s) for k in range(ns - 1) for s in range(nsub)]

    def first(c):
        return send(made.at[c, 1 - core], pair.at[c], sa.at[c], ra.at[c], (mate, q))

    def first_small(c):
        return send(sm_ref.at[c * 2 + 1 - core], spair.at[c], ta.at[c], ra2.at[c], (mate, q))

    def second(c, src):
        return send(pair.at[c], plane.at[src], sb.at[c], rb.at[src], (c * 2 + core, q))

    def second_small(c, src):
        return send(spair.at[c], splane.at[src], tb.at[c], rb2.at[src], (c * 2 + core, q))

    def block(c):
        at = pl.ds(pl.multiple_of(c * 2 * half, 2 * half), 2 * half)
        tile = part if part % 256 else part // 2
        left = md[at, :] if turned else md[:, at].T

        @pl.loop(0, part // tile)
        def _(j):
            n = pl.ds(pl.multiple_of(j * tile, 128), tile)
            full = jnp.dot(left, gp[:, n], preferred_element_type=F32).astype(BF)
            for h in range(2):
                for t in range(ns):
                    line = (h * ns + t) * rw
                    made[c, h, t, :, n] = full[line:line + rw]

    sm_ref[...] = jnp.zeros(sm_ref.shape, F32)
    for j in range(nd):
        here = slice(j * units, (j + 1) * units)
        sm_ref[j, 0:units, :] = gsel[here, :]
        sm_ref[j, above:above + rank, 0:units] = gstep[:, here]
        sm_ref[j, above + rank:above + rank + states, 0:units] = gdf[:, here] * rates[0:states, here]
        sm_ref[j, above + rank + states:taps_at, 0:units] = gdr[:, here] * rates[states:2 * states, here]
        for i, line in enumerate(gfil):
            sm_ref[j, taps_at + i:taps_at + i + 1, 0:units] = jnp.sum(line[:, here], axis=0, keepdims=True)

    loads[4].wait()
    order = chips + [chip]

    def give(c):
        block(c)
        first(c).start()
        first_small(c).start()

    give(order[0])
    for k in range(1, ns // 2):
        far(k)
    msg[...] = jnp.zeros(msg.shape, F32)
    long = msg.shape[1] // 128
    for i in range(3 * width // 128 + FREQ // 128):
        r, c = divmod(i * 128, width)
        to = (i % long) * 128
        msg[i // long:i // long + 1, to:to + 128] = acc[r:r + 1, c:c + 128]
    for k, t in enumerate(others):
        send(msg, mland.at[q], s1.at[k], r1.at[q], (d, t)).start()

    for i, c in enumerate(order):
        if i + 1 < nc:
            give(order[i + 1])
        first(c).wait_recv()
        @pl.loop(0, ns)
        def _(t):
            pair[c, t] = (pair[c, t].astype(F32) + made[c, core, t].astype(F32)).astype(BF)
        first_small(c).wait_recv()
        spair[c] = spair[c] + sm_ref[c * 2 + core]
        if i < nc - 1:
            second(c, chip).start()
            second_small(c, chip).start()
        for k, s in steps[2 * i:2 * i + 2]:
            step(k, s)
    late = len(steps) * 3 // 4
    for k, s in steps[2 * nc:late]:
        step(k, s)

    for c in chips:
        second(c, c).wait_recv()
        second_small(c, c).wait_recv()
    @pl.loop(0, ns)
    def _(t):
        total = pair[chip, t].astype(F32)
        for c in chips:
            total = total + plane[c, t].astype(F32)
        pair[chip, t] = total.astype(BF)
    small = spair[chip]
    for c in chips:
        small = small + splane[c]
    ssum[...] = small

    def third(t, src):
        return send(pair.at[chip, t], fro.at[src], sc.at[t], rc.at[src], (d, t))

    last = send(ssum, so_ref, tc, rc2, final_to)
    @pl.when(stays)
    def _():
        so_ref[...] = ssum[...]
    @pl.when(jnp.logical_not(stays))
    def _():
        last.start()
    for t in others:
        third(t, q).start()
    fro[q] = pair[chip, q]
    for k, s in steps[max(2 * nc, late):]:
        step(k, s)

    total = msg[...]
    for k, t in enumerate(others):
        send(msg, mland.at[t], s1.at[k], r1.at[t], (d, t)).wait_recv()
        total = total + mland[t]
    mod_o[d] = total
    for k, e in enumerate(peers):
        send(mod_o.at[d], mod_o.at[d], s2.at[k], r2.at[d], (e, q)).start()
    scale = 1.0 + mod_ref[0:1, width:2 * width]
    for s in range(nsub):
        own[...] = gm[q, s].astype(F32)

        @pl.when(q > 0)
        def _():
            rise(q, s, gm.at[q, s]).wait_recv()
            own[...] += up[q, s].astype(F32)

        @pl.when(q < ns - 1)
        def _():
            sink(q, s, gm.at[q, s]).wait_recv()
            own[...] += down[q, s].astype(F32)

        @pl.loop(0, sub // 16)
        def _(r):
            here = pl.ds(pl.multiple_of(r * 16, 16), 16)
            grad = own[here, :]
            x = hid_ref[s, here, :].astype(F32)
            x = x - jnp.mean(x, axis=1, keepdims=True)
            inverse = lax.rsqrt(jnp.mean(x * x, axis=1, keepdims=True) + EPS)
            normed = x * inverse
            grad = grad * scale
            grad = grad - jnp.mean(grad, axis=1, keepdims=True) - normed * jnp.mean(
                grad * normed, axis=1, keepdims=True)
            gh_o[s, here, :] = (cot_ref[s, here, :].astype(F32) + inverse * grad).astype(BF)

    inner = part * ns

    def place(src, rest):
        at = src * part
        gin_o[:, pl.ds(pl.multiple_of(at, 128), part)] = fro[src, 0:rows, :].astype(F32)
        gin_o[:, pl.ds(pl.multiple_of(inner + at, 128), part)] = rest[0:rows, 0:part].astype(F32)
        gout_o[:, pl.ds(pl.multiple_of(at, 128), part)] = rest[0:rows, part:2 * part].astype(F32)

    place(q, early[q])
    for t in others:
        third(t, t).wait_recv()
        whole(t, t).wait_recv()
        place(t, ready[t])
    for k, e in enumerate(peers):
        send(mod_o.at[e], mod_o.at[e], s2.at[k], r2.at[e], (e, q)).wait_recv()
    @pl.when(jnp.logical_not(stays))
    def _():
        last.wait_recv()
        last.wait_send()

    sel_o[...] = so_ref[0:units, :]
    step_o[...] = so_ref[above:above + rank, 0:units]
    df_o[...] = so_ref[above + rank:above + rank + states, 0:units]
    dr_o[...] = so_ref[above + rank + states:taps_at, 0:units]
    taps_o[...] = so_ref[taps_at:taps_at + taps, 0:units]
    fb_o[...] = so_ref[taps_at + taps:taps_at + taps + 1, 0:units]
    sb_o[...] = so_ref[taps_at + taps + 1:taps_at + taps + 2, 0:units]
    for c in order:
        first(c).wait_send()
        first_small(c).wait_send()
    for c in chips:
        second(c, chip).wait_send()
        second_small(c, chip).wait_send()
    for k, t in enumerate(others):
        third(t, q).wait_send()
        whole(t, q).wait_send()
        send(msg, mland.at[q], s1.at[k], r1.at[q], (d, t)).wait_send()
    for k, e in enumerate(peers):
        send(mod_o.at[d], mod_o.at[d], s2.at[k], r2.at[d], (e, q)).wait_send()
    for k, s in steps:
        t = ns - 1 - k
        @pl.when(q < t)
        def _():
            rise(t, s, gm.at[t, s]).wait_send()
        @pl.when(q > k)
        def _():
            sink(k, s, gm.at[k, s]).wait_send()


def end(grad_inner, grad_gate, modded, normed, wx, early, small, fil, hidden, cot, modulation, grad_gate_scale, embedded, rows, nd, ns, cid):
    length, part = grad_inner.shape
    cols = 2 * part
    width = wx.shape[0]
    inner = part * ns
    nc, nsub = nd // 2, 8
    local = length // ns
    sub = local // nsub
    rw = rows + -rows % 16
    half = ns * rw
    turned = 2 * half % 128 != 0 or rw != rows
    if turned:
        def turn(a):
            a = a.T.reshape(nd * ns, rows, length)
            return jnp.pad(a, ((0, 0), (0, rw - rows), (0, 0))).reshape(nd * ns * rw, length)
        modded = turn(modded)
    early = jnp.pad(early.reshape(ns, rows, cols), ((0, 0), (0, rw - rows), (0, 0)))
    short = -(-(3 * width + FREQ) // 1024) * 128
    units, rank, states = part // nd, small[1].shape[0], small[2].shape[0]
    v = (units + -units % 16 + rank + 2 * states + 16, 128)
    hidden, cot = hidden.reshape(nsub, sub, width), cot.reshape(nsub, sub, width)
    blocks = pltpu.VMEM((nc, ns, rw, part), BF)
    smalls = pltpu.VMEM((nc,) + v, F32)
    runs = pltpu.VMEM((ns, nsub, sub, width), BF)
    gin, gout, *own, gh, mod = pl.pallas_call(
        functools.partial(end_kernel, nd, ns, nsub, rows, turned, len(fil)),
        out_shape=[
            jax.ShapeDtypeStruct((rows, 2 * inner), F32),
            jax.ShapeDtypeStruct((rows, inner), F32),
            jax.ShapeDtypeStruct((units, 128), F32),
            jax.ShapeDtypeStruct((rank, units), F32),
            jax.ShapeDtypeStruct((states, units), F32),
            jax.ShapeDtypeStruct((states, units), F32),
            jax.ShapeDtypeStruct((len(fil) - 2, units), F32),
            jax.ShapeDtypeStruct((1, units), F32),
            jax.ShapeDtypeStruct((1, units), F32),
            jax.ShapeDtypeStruct((nsub, sub, width), BF),
            jax.ShapeDtypeStruct((nd, 8, short), F32),
        ],
        in_specs=[HBM] * 5 + [VMEM] * (11 + len(fil)), out_specs=[VMEM] * 11,
        scratch_shapes=[
            pltpu.VMEM((length, cols), BF), pltpu.VMEM(modded.shape, BF), pltpu.VMEM(normed.shape, BF),
            pltpu.VMEM((width, cols), BF),
            pltpu.VMEM((nd,) + v, F32), pltpu.VMEM(v, F32), runs,
            pltpu.VMEM((nc, 2, ns, rw, part), BF), blocks, blocks,
            smalls, smalls, pltpu.VMEM(v, F32), pltpu.VMEM((ns, rw, part), BF), pltpu.VMEM((ns, rw, cols), BF), runs, runs,
            pltpu.VMEM((sub, width), F32), pltpu.VMEM((8, width), F32), pltpu.VMEM((8, short), F32),
            pltpu.VMEM((ns, 8, short), F32),
            DMA((5,)),
            DMA((nc,)), DMA((nc,)), DMA((nc,)), DMA((nc,)), DMA((ns,)), DMA((ns,)), DMA((ns,)), DMA((ns,)),
            DMA((nc,)), DMA((nc,)), DMA((nc,)), DMA((nc,)), DMA(()), DMA(()),
            DMA((ns, nsub)), DMA((ns, nsub)), DMA((ns, nsub)), DMA((ns, nsub)),
            DMA((ns,)), DMA((ns,)), DMA((nd,)), DMA((nd,)),
        ],
        compiler_params=pltpu.CompilerParams(
            collective_id=cid, has_side_effects=True, vmem_limit_bytes=60 * 2**20),
        name="end",
    )(grad_inner, grad_gate, modded, normed, wx, *small, hidden, cot, modulation, grad_gate_scale, embedded, early, *fil)
    return gin, gout, own, gh.reshape(local, width), mod


def frequency_embed(timestep):
    half_width = FREQ // 2
    counter = jnp.arange(half_width, dtype=F32)
    frequency = jnp.exp(counter * (-math.log(10000.0) / half_width))
    angles = timestep.astype(F32)[:, None] * frequency[None, :]
    return jnp.concatenate([jnp.cos(angles), jnp.sin(angles)], axis=1)


def dot(a, b):
    return jnp.dot(a, b, preferred_element_type=F32)


def dot_nt(a, b):
    return lax.dot_general(a, b, (((1,), (1,)), ((), ())), preferred_element_type=F32)


def dot_tn(a, b):
    return lax.dot_general(a, b, (((0,), (0,)), ((), ())), preferred_element_type=F32)


def by_eight(a):
    return jnp.sum(a.reshape(-1, 8, a.shape[1]), axis=0)


def body(
    hidden,
    pad_mask,
    timestep,
    input_weight,
    select_weight,
    step_weight,
    output_weight,
    decay_forward,
    decay_reverse,
    filter_weight,
    filter_bias,
    step_bias,
    modulation_weight,
    modulation_bias,
    cotangent,
):
    ns, nd = lax.axis_size("seq"), lax.axis_size("dp")
    q, d = lax.axis_index("seq"), lax.axis_index("dp")
    every = ("dp", "seq")
    local_len, width = hidden.shape[1:]
    length = local_len * ns
    inner = output_weight.shape[0]
    part = inner // ns
    rank = step_weight.shape[0]
    state = decay_forward.shape[1]
    taps = filter_weight.shape[0]
    rows_in = input_weight.shape[0]
    lanes = select_weight.shape[1]

    units = part // nd
    embedded = jax.nn.silu(frequency_embed(timestep)).astype(BF)
    modb = jnp.zeros((-(-3 * width // 1024) * 1024,), F32)
    modb = lax.dynamic_update_slice(modb, modulation_bias.astype(F32), ((d * ns + q) * modulation_bias.shape[0],))
    row_pad = ((0, -rows_in % 16), (0, 0))
    fused = rows_in % 16 == 0
    modded, normed, inner_part, gate_branch, wx, select_q, step_q, rates, fil, mask, modulation = start(
        hidden[0], pad_mask.reshape(-1, 128), jnp.pad(input_weight, row_pad), jnp.pad(output_weight.T, row_pad),
        embedded, modulation_weight, modb.reshape(-1, 128),
        (select_weight, step_weight, decay_forward.T, decay_reverse.T, filter_weight, filter_bias[None], step_bias[None]),
        fused, nd, ns, 4)
    wx = wx.reshape(nd * ns, -1, 3 * part)[:, :rows_in].reshape(width, 3 * part)
    win, wout = wx[:, : 2 * part], wx[:, 2 * part :]
    mask = mask[:, : local_len // 128].reshape(length, 1).astype(F32)
    rates_f, rates_r, rates_f2, rates_r2 = [rates[k * state : (k + 1) * state] for k in range(4)]
    modulation_rows, modulation = modulation, modulation[:1]
    shifts = modulation[:, :width]
    scales = modulation[:, width : 2 * width]
    gate_scale = modulation[:, 2 * width :]

    def norm(x):
        x = x.astype(F32)
        centered = x - jnp.mean(x, axis=1, keepdims=True)
        inverse = lax.rsqrt(jnp.mean(centered * centered, axis=1, keepdims=True) + EPS)
        return centered * inverse, inverse

    if fused:
        modded, normed = modded.reshape(length, width), normed.reshape(length, width)
        inner_part, gate_branch = inner_part.reshape(length, part), gate_branch.reshape(length, part)
    else:
        normed = norm(modded.reshape(length, width))[0]
        modded, normed = (normed * (1.0 + scales) + shifts).astype(BF), normed.astype(BF)
        projected = dot(modded, win)
        inner_part, gate_branch = projected[:, :part].astype(BF), projected[:, part:]
    inner_part = inner_part.astype(F32) * mask
    padded = jnp.pad(inner_part, ((taps - 1, 0), (0, 0)))
    filtered = fil[taps][None]
    for k in range(taps):
        filtered = filtered + fil[k][None] * padded[k : k + length]
    sigma_filter = jax.nn.sigmoid(filtered)
    active = (filtered * sigma_filter).astype(BF)
    active32 = active.astype(F32)
    selected = column_sum(dot(active, select_q).astype(BF), ns, BF, 0)
    cot, selected = lax.optimization_barrier((cotangent[0], selected))
    cot = lax.all_gather(cot, "seq", axis=0, tiled=True)
    low_rank = selected[:, :rank].astype(BF)
    b_rows = selected[:, rank : rank + state].astype(F32)
    c_rows = selected[:, rank + state :].astype(F32)
    pre_steps = dot(low_rank, step_q) + fil[taps + 1][None]
    steps = jax.nn.softplus(pre_steps)
    drive = steps * active32
    mixed_f, mixed_r, states_f, states_r = fwd_scan(steps, drive, rates_f2, rates_r2, b_rows.T, blockdiag(c_rows))
    merged = mixed_f + mixed_r
    sigma_gate = jax.nn.sigmoid(gate_branch)
    silu_gate = gate_branch * sigma_gate
    gated = (merged * silu_gate).astype(BF)
    branch = dot_nt(gated, wout).astype(BF)
    branch, cot = lax.optimization_barrier((branch, cot))
    branch = lax.psum_scatter(branch, "seq", scatter_dimension=0, tiled=True).astype(F32)

    mask_here = pad_mask[0].astype(F32)[:, None]
    cot_here = cotangent[0].astype(F32)
    block_out = (hidden[0].astype(F32) + gate_scale * mask_here * branch).astype(BF)
    grad_gate = by_eight(mask_here * cot_here * branch)

    grad_branch = lax.optimization_barrier((cot.astype(F32) * gate_scale * mask).astype(BF))
    grad_gated = dot(grad_branch, wout)
    grad_merged = grad_gated * silu_gate
    grad_gate_branch = grad_gated * merged * sigma_gate * (1.0 + gate_branch * (1.0 - sigma_gate))
    grad_gate_branch = grad_gate_branch.astype(BF)
    rows_first = Layout((0, 1))
    early = jnp.concatenate([
        with_layout_constraint(dot_tn(modded, grad_gate_branch).astype(BF), rows_first),
        with_layout_constraint(dot_tn(grad_branch, gated).astype(BF), rows_first)], axis=1)
    early = lax.psum_scatter(early, "dp", scatter_dimension=0, tiled=True)
    dlog_f, dlog_r, adjb_f, adjb_r, bg_f, bg_r, cg_f, cg_r, rg_f, rg_r = bwd_scan(
        steps, drive, grad_merged, rates_f2, rates_r2, c_rows.T, blockdiag(b_rows), states_f, states_r)
    adjb = adjb_f + adjb_r
    grad_steps = (dlog_f + dlog_r) * (1.0 / LOG2E) + active32 * adjb
    grad_pre = grad_steps * -jnp.expm1(-steps)
    grad_step_bias = jnp.sum(grad_pre, axis=0, keepdims=True)
    grad_pre_low = grad_pre.astype(BF)
    grad_step = dot_tn(low_rank, grad_pre_low)
    grad_selected = column_grads(grad_pre_low, step_q, bg_f, bg_r, cg_f, cg_r, ns, 1)
    grad_select = dot_tn(active, grad_selected)
    grad_active = steps * adjb + dot_nt(grad_selected, select_q)
    grad_filtered = grad_active * sigma_filter * (1.0 + filtered * (1.0 - sigma_filter))
    extended = jnp.pad(grad_filtered, ((0, taps - 1), (0, 0)))
    grad_inner = jnp.zeros_like(grad_filtered)
    filter_rows = []
    for k in range(taps):
        lead = taps - 1 - k
        grad_inner = grad_inner + fil[k][None] * extended[lead : lead + length]
        filter_rows.append(by_eight(grad_filtered * padded[k : k + length]))
    grad_filter_bias = by_eight(grad_filtered)
    grad_inner = (grad_inner * mask).astype(BF)
    g_in, g_out, own, grad_hidden, sums = end(
        grad_inner, grad_gate_branch, modded, normed, wx, early, (grad_select, grad_step, rg_f, rg_r, rates),
        filter_rows + [grad_filter_bias, grad_step_bias], hidden[0], cotangent[0], modulation_rows, grad_gate, embedded,
        rows_in, nd, ns, 2)
    gs_select, gs_step, gs_f, gs_r, gs_taps, gs_fbias, gs_sbias = own
    sums = sums.reshape(nd, -1)
    embeds = sums[:, 3 * width : 3 * width + FREQ]
    grad_mod = sums[:, : 3 * width]
    me = d * ns + q
    mine = lax.dynamic_slice_in_dim(embeds, me * modulation_weight.shape[0], modulation_weight.shape[0], 1)
    g_modw = lax.dot_general(mine, grad_mod, (((0,), (0,)), ((), ())), precision=HIGHEST)
    g_modb = lax.dynamic_slice_in_dim(
        jnp.sum(grad_mod, axis=0), me * modulation_bias.shape[0], modulation_bias.shape[0], 0)
    return (
        block_out[None],
        grad_hidden[None],
        g_in,
        gs_select,
        gs_step,
        g_out.T,
        gs_f.T,
        gs_r.T,
        gs_taps,
        gs_fbias[0],
        gs_sbias[0],
        g_modw,
        g_modb,
    )


def solution(mesh):
    return jax.shard_map(
        body,
        mesh=mesh,
        in_specs=(
            P("dp", "seq", None),
            P("dp", "seq"),
            P("dp"),
            P(("dp", "seq"), None),
            P(("dp", "seq"), None),
            P(None, ("dp", "seq")),
            P(None, ("dp", "seq")),
            P(("dp", "seq"), None),
            P(("dp", "seq"), None),
            P(None, ("dp", "seq")),
            P(("dp", "seq")),
            P(("dp", "seq")),
            P(("dp", "seq"), None),
            P(("dp", "seq")),
            P("dp", "seq", None),
        ),
        out_specs=(
            P("dp", "seq", None),
            P("dp", "seq", None),
            P(("dp", "seq"), None),
            P(("dp", "seq"), None),
            P(None, ("dp", "seq")),
            P(None, ("dp", "seq")),
            P(("dp", "seq"), None),
            P(("dp", "seq"), None),
            P(None, ("dp", "seq")),
            P(("dp", "seq")),
            P(("dp", "seq")),
            P(("dp", "seq"), None),
            P(("dp", "seq")),
        ),
        check_vma=False,
    )
```
